32 devices in a mesh: node: 8 (over y, x, core), local: 4 (over z).
Axes of the slice: x: 2, y: 2, z: 4, core: 2. Of those that a mesh axis runs over, the one named last changes fastest.
Arguments:
- grad_out: bfloat16 [4096, 32, 384], P(('node', 'local')), may hold values from -6 to 6
- pooled: bfloat16 [4096, 32, 256], P(('node', 'local')), may hold values from -6 to 6
- proj: bfloat16 [32, 256, 128], P(('node', 'local')), may hold values from -0.5 to 0.5
- assign: int32 [32], replicated, may hold values from 0 to 31, each once
- indices: int32 [32, 4096, 3, 8], P(('node', 'local')), may hold values from 0 to 511
- lengths: int32 [32, 4096, 3], P(('node', 'local')), may hold values from 1 to 8
Outputs:
- table_grad: float32 [32, 512, 256], P(('node', 'local'))
- proj_grad: float32 [32, 256, 128], P(('node', 'local'))
The draws below stay inside these ranges and needn't reach their ends.
Inputs may be any that keep to these rules, and one draw needn't show every extreme that they name: assign holds every group id once.
All inputs are finite; a program needn't handle non-finite values.
Results may differ from the reference program's by a relative error of at most 0.0029.
Values may be sent and summed in bfloat16 or wider, within the bound.
No kernel may reach another device: no remote copies, remote signals or barrier semaphores. Data moves between devices by JAX's collectives and lax.ppermute only.
A program may use at most 192 MiB of HBM per device.

```python
import math
import jax
import jax.numpy as jnp
import numpy as np
from jax import lax

ROWS = 512
BAG = 8
W1 = 16
W2 = 48
W3 = 192
PD = 128
WSUM = 256
CAT = 384
GROUPS = 32
BATCH = 4096


def with_ends(result, rng, smallest, high):
    place = [jax.random.randint(jax.random.fold_in(rng, axis), (), 0, length) for axis, length in enumerate(result.shape)]
    widest = result.shape.index(max(result.shape))
    beside = place[:widest] + [(place[widest] + 1) % result.shape[widest]] + place[widest + 1:]
    return result.at[tuple(place)].set(smallest).at[tuple(beside)].set(high)


def raised(drawn, key, source, target, parts, factor):
    def block_of(position):
        return (jnp.arange(drawn.shape[position]) // (drawn.shape[position] // parts)).reshape((-1,) + (1,) * (drawn.ndim - 1 - position))

    one_side = jax.random.permutation(key, parts)[block_of(target)]
    second = (block_of(target) + parts // 2) % parts
    return jnp.where((block_of(source) == one_side) | (block_of(source) == second), factor * drawn, drawn)


def levels(stream_key, dims, pieces, low, high):
    def one(axis_at, shards_of):
        heights = jax.random.uniform(jax.random.fold_in(jax.random.fold_in(stream_key, 6), axis_at), (shards_of,), jnp.float32, low / len(pieces), high / len(pieces))
        return jnp.repeat(jnp.exp(heights), dims[axis_at] // shards_of).reshape((-1,) + (1,) * (len(dims) - axis_at - 1))

    loudness = one(*pieces[0])
    for cut in pieces[1:]:
        loudness = loudness * one(*cut)
    return loudness


def rank_table(number_of, lean):
    loads = [(1 << 20) // math.isqrt(standing ** lean) + 1 for standing in range(1, number_of + 1)]
    scale = 1 + sum(loads) // (1 << 30)
    return np.cumsum(np.array([max(1, weight // scale) for weight in loads]))


def ranked(key, dims, amount, lean):
    table = rank_table(amount, lean)
    lot = jax.random.randint(jax.random.fold_in(key, 1), dims, 0, int(table[amount - 1]))
    grade = jnp.searchsorted(jnp.asarray(table, jnp.int32), lot, side="right")
    return jax.random.permutation(jax.random.fold_in(key, 2), amount)[grade].astype(jnp.int32)


def gaussian(stream_key, shape, scale, reach, shards=(), kind=jnp.bfloat16):
    result = jax.random.normal(stream_key, shape, jnp.float32) * scale
    if len(shards) > 0:
        result = levels(stream_key, shape, shards, -0.22, 0.18) * result
    return jnp.clip(result, min=-reach, max=reach).astype(kind)


def bell_draw_with(rng, extent, scale, reach, shards, heavy, held_as=jnp.bfloat16):
    result = scale * jax.random.normal(rng, extent, jnp.float32)
    if shards:
        result = result * levels(rng, extent, shards, -0.22, 0.18)
    return jnp.clip(raised(result, jax.random.fold_in(rng, 3), *heavy), -reach, reach).astype(held_as)


def setup_inputs(seed: int = 0) -> dict:
    seeds = jax.random.split(jax.random.key(seed), 7)
    grad_out = bell_draw_with(seeds[0], (BATCH, GROUPS, CAT), 1.0, 6.0, ((0, 32),), (0, 1, 32, 2.75))
    pooled = bell_draw_with(seeds[1], (BATCH, GROUPS, WSUM), 1.0, 6.0, ((0, 32),), (0, 1, 32, 2.75))
    proj = gaussian(seeds[2], (GROUPS, WSUM, PD), PD ** -0.5, 0.5, ((0, 32),))
    assign = jax.random.permutation(seeds[3], GROUPS).astype(jnp.int32)
    indices = with_ends(ranked(seeds[4], (GROUPS, BATCH, 3, BAG), ROWS, 2), jax.random.fold_in(seeds[4], 3), 0, ROWS - 1).astype(jnp.int32)
    lengths = with_ends(jax.random.randint(seeds[5], (GROUPS, BATCH, 3), 1, BAG + 1), jax.random.fold_in(seeds[5], 1), 1, BAG).astype(jnp.int32)
    return {"grad_out": grad_out, "pooled": pooled, "proj": proj, "assign": assign, "indices": indices, "lengths": lengths}


def reference(grad_out, pooled, proj, assign, indices, lengths):
    widths = (W1, W2, W3)
    scale = 1.0 / math.sqrt(BATCH)

    def one_slot(slot):
        group = assign[slot]
        grads = lax.dynamic_index_in_dim(grad_out, group, 1, keepdims=False)
        saved = lax.dynamic_index_in_dim(pooled, group, 1, keepdims=False)
        weights = proj[slot]
        lookups = indices[slot]
        counts = lengths[slot]
        tables = []
        projections = []
        offset = 0
        for table, width in enumerate(widths):
            grad_part = grads[:, table * PD:(table + 1) * PD]
            rounded = jnp.dot(grad_part, weights[offset:offset + width].T, preferred_element_type=jnp.float32).astype(jnp.bfloat16)
            dpool = lax.optimization_barrier(rounded).astype(jnp.float32)
            projections.append(jnp.dot(saved[:, offset:offset + width].T, grad_part, preferred_element_type=jnp.float32) * scale)
            total = jnp.zeros((ROWS, width), jnp.float32)
            for lookup in range(BAG):
                keep = (counts[:, table] > lookup).astype(jnp.float32)
                total = total + jax.ops.segment_sum(dpool * keep[:, None], lookups[:, table, lookup], num_segments=ROWS)
            tables.append(total)
            offset = offset + width
        return (jnp.concatenate(tables, axis=1), jnp.concatenate(projections, axis=0))
    table_grad, proj_grad = lax.map(one_slot, jnp.arange(GROUPS, dtype=jnp.int32))
    return (table_grad, proj_grad)
```

```python
import functools
import math

import jax
import jax.numpy as jnp
from jax import lax
from jax.experimental import pallas as pl
from jax.experimental.pallas import tpu as pltpu
from jax.sharding import PartitionSpec as P

ROWS = 512
W1 = 16
W2 = 48
W3 = 192
PD = 128
W12 = W1 + W2
WSUM = W12 + W3
AXES = ("node", "local")
EB = 16
VMEM = 60 * 1024 * 1024


def params(*semantics):
    return pltpu.CompilerParams(dimension_semantics=semantics, vmem_limit_bytes=VMEM)


def cost(flops, nbytes):
    return pl.CostEstimate(flops=flops, bytes_accessed=nbytes, transcendentals=0)


def fill_permutation(assign_ref, perm_ref, slots):
    width = EB * slots
    lane = lax.broadcasted_iota(jnp.int32, (EB, width), 1)
    first = lax.broadcasted_iota(jnp.int32, (EB, width), 0) * slots

    def one(s, carry):
        start = pl.multiple_of(s * EB, EB)
        perm_ref[pl.ds(start, EB), :] = jnp.where(lane == first + assign_ref[s], 1.0, 0.0).astype(jnp.bfloat16)
        return carry

    lax.fori_loop(0, slots, one, 0)


def permute_one_kernel(slots, assign_ref, x_ref, out_ref, perm_ref):
    @pl.when(pl.program_id(0) == 0)
    def _():
        fill_permutation(assign_ref, perm_ref, slots)

    block = x_ref[...].reshape(EB * slots, x_ref.shape[2])
    moved = jnp.dot(perm_ref[...], block, preferred_element_type=jnp.float32)
    out_ref[...] = moved.astype(jnp.bfloat16).reshape(slots, EB, x_ref.shape[2])


def permute_one(assign, x, width, column):
    count, slots, _ = x.shape
    return pl.pallas_call(
        functools.partial(permute_one_kernel, slots),
        out_shape=jax.ShapeDtypeStruct((slots, count, width), x.dtype),
        grid_spec=pltpu.PrefetchScalarGridSpec(
            num_scalar_prefetch=1,
            grid=(count // EB,),
            in_specs=[pl.BlockSpec((EB, slots, width), lambda i, a: (i, 0, column))],
            out_specs=pl.BlockSpec((slots, EB, width), lambda i, a: (0, i, 0)),
            scratch_shapes=[pltpu.VMEM((EB * slots, EB * slots), jnp.bfloat16)],
        ),
        compiler_params=params("arbitrary"),
        cost_estimate=cost(2 * count * slots * EB * slots * width, 4 * count * slots * width),
        name="permute_sent",
    )(assign, x)


def permute_two_kernel(slots, assign_ref, x_ref, y_ref, xo_ref, yo_ref, perm_ref):
    @pl.when(pl.program_id(0) == 0)
    def _():
        fill_permutation(assign_ref, perm_ref, slots)

    for ref, out in ((x_ref, xo_ref), (y_ref, yo_ref)):
        block = ref[...].reshape(EB * slots, ref.shape[2])
        moved = jnp.dot(perm_ref[...], block, preferred_element_type=jnp.float32)
        out[...] = moved.astype(jnp.bfloat16).reshape(slots, EB, ref.shape[2])


def permute_two(assign, x, xw, y, yw):
    count, slots, _ = x.shape
    return pl.pallas_call(
        functools.partial(permute_two_kernel, slots),
        out_shape=(
            jax.ShapeDtypeStruct((slots, count, xw), x.dtype),
            jax.ShapeDtypeStruct((slots, count, yw), y.dtype),
        ),
        grid_spec=pltpu.PrefetchScalarGridSpec(
            num_scalar_prefetch=1,
            grid=(count // EB,),
            in_specs=[
                pl.BlockSpec((EB, slots, xw), lambda i, a: (i, 0, 0)),
                pl.BlockSpec((EB, slots, yw), lambda i, a: (i, 0, 0)),
            ],
            out_specs=[
                pl.BlockSpec((slots, EB, xw), lambda i, a: (0, i, 0)),
                pl.BlockSpec((slots, EB, yw), lambda i, a: (0, i, 0)),
            ],
            scratch_shapes=[pltpu.VMEM((EB * slots, EB * slots), jnp.bfloat16)],
        ),
        compiler_params=params("arbitrary"),
        cost_estimate=cost(2 * count * slots * EB * slots * (xw + yw), 4 * count * slots * (xw + yw)),
        name="permute_rest",
    )(assign, x, y)


def narrow_kernel(slots_step, g_ref, w_ref, out_ref):
    half = g_ref.shape[1] // 2
    row = lax.broadcasted_iota(jnp.int32, (W12, PD), 0)
    for s in range(slots_step):
        w = w_ref[s].astype(jnp.float32)
        first = jnp.where(row < W1, w, 0.0).astype(jnp.bfloat16)
        second = jnp.where(row < W1, 0.0, w).astype(jnp.bfloat16)
        weights = jnp.concatenate([first, second], axis=1)
        d = lax.dot_general(g_ref[s], weights, (((1,), (1,)), ((), ())), preferred_element_type=jnp.float32)
        out_ref[s] = jnp.concatenate([d[:half], d[half:]], axis=1).astype(jnp.bfloat16)


def narrow_dpool(g12, w12):
    slots, count, _ = g12.shape
    step = 4
    return pl.pallas_call(
        functools.partial(narrow_kernel, step),
        out_shape=jax.ShapeDtypeStruct((slots, count // 2, 2 * W12), jnp.bfloat16),
        grid=(slots // step,),
        in_specs=[
            pl.BlockSpec((step, count, 2 * PD), lambda i: (i, 0, 0)),
            pl.BlockSpec((step, W12, PD), lambda i: (i, 0, 0)),
        ],
        out_specs=pl.BlockSpec((step, count // 2, 2 * W12), lambda i: (i, 0, 0)),
        compiler_params=params("arbitrary"),
        cost_estimate=cost(4 * slots * count * W12 * PD, slots * count * 6 * PD),
        name="narrow_dpool",
    )(g12, w12)


def partial_kernel(order_ref, q_ref, g12_ref, g3_ref, out_ref):
    step = out_ref.shape[0]
    for p in range(step):
        slot = order_ref[pl.program_id(0) * step + p]
        q = q_ref[slot]
        g = jnp.concatenate([g12_ref[slot], g3_ref[slot]], axis=1)
        dims = (((0,), (0,)), ((), ()))
        full = lax.dot_general(q, g, dims, preferred_element_type=jnp.float32)
        out_ref[p, :W1] = full[:W1, :PD]
        out_ref[p, W1:W12] = full[W1:W12, PD : 2 * PD]
        out_ref[p, W12:] = full[W12:, 2 * PD :]


def partial_proj(order, q, g12, g3):
    slots, count, _ = q.shape
    chosen = order.shape[0]
    step = 4
    return pl.pallas_call(
        partial_kernel,
        out_shape=jax.ShapeDtypeStruct((chosen, WSUM, PD), jnp.float32),
        grid_spec=pltpu.PrefetchScalarGridSpec(
            num_scalar_prefetch=1,
            grid=(chosen // step,),
            in_specs=[
                pl.BlockSpec((slots, count, WSUM), lambda i, o: (0, 0, 0)),
                pl.BlockSpec((slots, count, 2 * PD), lambda i, o: (0, 0, 0)),
                pl.BlockSpec((slots, count, PD), lambda i, o: (0, 0, 0)),
            ],
            out_specs=pl.BlockSpec((step, WSUM, PD), lambda i, o: (i, 0, 0)),
        ),
        compiler_params=params("arbitrary"),
        cost_estimate=cost(2 * chosen * count * WSUM * 3 * PD, slots * count * 1280 + chosen * WSUM * PD * 4),
        name="partial_proj",
    )(order, q, g12, g3)


def hits_kernel(index_ref, length_ref, out_ref):
    lookups, block = index_ref.shape[1], index_ref.shape[2]
    rows = out_ref.shape[1]
    half = rows // 2
    chunk = 16
    index = index_ref[0]
    which = lax.broadcasted_iota(jnp.int32, (lookups, block), 0)
    index = jnp.where(which < length_ref[0], index, -1)
    ids = lax.broadcasted_iota(jnp.int32, (chunk, block), 0).astype(jnp.float32).astype(jnp.bfloat16)
    for part in range(2):
        wanted = (index - part * half).astype(jnp.float32)
        wide = [
            jnp.broadcast_to(wanted[j : j + 1], (chunk, block)).astype(jnp.bfloat16) for j in range(lookups)
        ]
        for r in range(half // chunk):
            row = ids + jnp.bfloat16(r * chunk)
            total = jnp.zeros((chunk, block), jnp.bfloat16)
            for j in range(lookups):
                total = total + jnp.where(wide[j] == row, jnp.bfloat16(1), jnp.bfloat16(0))
            start = part * half + r * chunk
            out_ref[0, start : start + chunk, :] = total


def count_hits(lookups, counts):
    tables, bag, examples = lookups.shape
    block = 512
    return pl.pallas_call(
        hits_kernel,
        out_shape=jax.ShapeDtypeStruct((tables, ROWS, examples), jnp.bfloat16),
        grid=(tables, examples // block),
        in_specs=[
            pl.BlockSpec((1, bag, block), lambda k, i: (k, 0, i)),
            pl.BlockSpec((1, 1, block), lambda k, i: (k, 0, i)),
        ],
        out_specs=pl.BlockSpec((1, ROWS, block), lambda k, i: (k, 0, i)),
        compiler_params=params("arbitrary", "arbitrary"),
        cost_estimate=cost(tables * ROWS * examples * bag * 3, tables * examples * (ROWS * 2 + 36)),
        name="count_hits",
    )(lookups, counts)


def table_kernel(hits_ref, g3_ref, narrow_ref, w_ref, out_ref):
    block = g3_ref.shape[0]
    sources, half, _ = narrow_ref.shape

    @pl.when(pl.program_id(0) == 0)
    def _():
        out_ref[...] = jnp.zeros_like(out_ref)

    column = lax.broadcasted_iota(jnp.int32, (block, WSUM), 1)
    d3 = lax.dot_general(g3_ref[...], w_ref[...], (((1,), (1,)), ((), ())), preferred_element_type=jnp.float32)
    d3 = jnp.where(column < W12, 0.0, d3).astype(jnp.bfloat16)
    pieces = []
    for d in range(sources):
        packed = narrow_ref[d].astype(jnp.float32)
        pieces += [packed[:, :W12], packed[:, W12:]]
    d12 = jnp.concatenate(pieces, axis=0)
    d12 = jnp.concatenate([d12, jnp.zeros((block, WSUM - W12), jnp.float32)], axis=1)
    d1 = jnp.where(column < W1, d12, 0.0).astype(jnp.bfloat16)
    d2 = jnp.where(column < W1, 0.0, d12).astype(jnp.bfloat16)
    out_ref[...] += (
        jnp.dot(hits_ref[0], d1, preferred_element_type=jnp.float32)
        + jnp.dot(hits_ref[1], d2, preferred_element_type=jnp.float32)
        + jnp.dot(hits_ref[2], d3, preferred_element_type=jnp.float32)
    )


def table_sum(hits, g3, narrow, weights):
    tables, rows, examples = hits.shape
    sources, half, _ = narrow.shape
    block = 512
    per = block // (2 * half)
    return pl.pallas_call(
        table_kernel,
        out_shape=jax.ShapeDtypeStruct((rows, WSUM), jnp.float32),
        grid=(examples // block,),
        in_specs=[
            pl.BlockSpec((tables, rows, block), lambda i: (0, 0, i)),
            pl.BlockSpec((block, PD), lambda i: (i, 0)),
            pl.BlockSpec((per, half, 2 * W12), lambda i: (i, 0, 0)),
            pl.BlockSpec((WSUM, PD), lambda i: (0, 0)),
        ],
        out_specs=pl.BlockSpec((rows, WSUM), lambda i: (0, 0)),
        compiler_params=params("arbitrary"),
        cost_estimate=cost(6 * rows * examples * WSUM, hits.size * 2 + examples * 400 + rows * WSUM * 4),
        name="table_sum",
    )(hits, g3, narrow, weights)


def bits_of(size):
    return [1 << b for b in range(size.bit_length() - 1)]


def swap(x, axis, size, bit):
    return lax.ppermute(x, axis, [(d, d ^ bit) for d in range(size)])


def halve(kept, sent, path, sizes):
    for n, (axis, bit) in enumerate(path):
        got = swap(sent, axis, sizes[axis], bit)
        half = kept.shape[0] // 2
        if n + 1 < len(path):
            sent = kept[half:] + got[half:]
            kept = kept[:half] + got[:half]
        else:
            kept = kept + got
    return kept


def local(sizes, grad_out, pooled, proj, assign, indices, lengths):
    count, slots, _ = grad_out.shape
    scale = 1.0 / math.sqrt(count * slots)
    n_node, n_local = sizes["node"], sizes["local"]

    w12 = lax.all_gather(proj[0, :W12], AXES, axis=0, tiled=False)
    g3 = permute_one(assign, grad_out, PD, 2)
    g3_got = lax.all_to_all(g3, AXES, split_axis=0, concat_axis=0, tiled=True).reshape(-1, PD)
    g12, q = permute_two(assign, grad_out, 2 * PD, pooled, WSUM)
    narrow = narrow_dpool(g12, w12)
    narrow_got = lax.all_to_all(narrow, AXES, split_axis=0, concat_axis=0, tiled=True)

    node, loc = lax.axis_index("node"), lax.axis_index("local")
    core = [("node", 1)]
    nodes = [("node", b) for b in bits_of(n_node)[1:]]
    locals_ = [("local", b) for b in bits_of(n_local)]
    path_a = core + nodes + locals_

    def slot_order(path):
        position = jnp.arange(slots, dtype=jnp.int32)
        flip = jnp.zeros((slots,), jnp.int32)
        for n, (axis, bit) in enumerate(path):
            on = (position >> (len(path) - 1 - n)) & 1
            flip = flip + on * bit * (n_local if axis == "node" else 1)
        return flip ^ (node * n_local + loc).astype(jnp.int32)

    order = slot_order(path_a)
    sent = partial_proj(order[slots // 2 :], q, g12, g3)
    kept = partial_proj(order[: slots // 2], q, g12, g3)
    got = swap(sent, "node", n_node, 1)
    rows = WSUM // 2
    shape = [2] * len(nodes) + [n_local, rows, PD]
    back = list(range(len(nodes)))[::-1] + [len(nodes), len(nodes) + 1, len(nodes) + 2]
    halves = []
    for part in range(2):
        cut = slice(part * rows, (part + 1) * rows)

        def laid(x):
            x = x[:, cut]
            if part:
                x = x.reshape(shape).transpose(back).reshape(x.shape)
            return x

        total = laid(kept) + laid(got)
        path = (nodes if part == 0 else nodes[::-1]) + locals_
        half = total.shape[0] // 2
        halves.append(halve(total[:half], total[half:], path, sizes))
    proj_grad = jnp.concatenate(halves, axis=1) * scale

    lookups = indices[0].transpose(1, 2, 0)
    counts = lengths[0].T[:, None, :]
    hits = count_hits(lookups, counts)
    table_grad = table_sum(hits, g3_got, narrow_got, proj[0])[None]
    return (table_grad, proj_grad)


def solution(mesh):
    placed = (
        P(AXES, None, None),
        P(AXES, None, None),
        P(AXES, None, None),
        P(),
        P(AXES, None, None, None),
        P(AXES, None, None),
    )
    return jax.shard_map(
        functools.partial(local, dict(mesh.shape)),
        mesh=mesh,
        in_specs=placed,
        out_specs=(P(AXES, None, None), P(AXES, None, None)),
        check_vma=False,
    )
```

```python
import functools
import math

import jax
import jax.numpy as jnp
from jax import lax
from jax.experimental import pallas as pl
from jax.experimental.pallas import tpu as pltpu
from jax.sharding import PartitionSpec as P

ROWS = 512
W1 = 16
W2 = 48
W3 = 192
PD = 128
W12 = W1 + W2
WSUM = W12 + W3
AXES = ("node", "local")
EB = 8
STEP = 32
MIB = 1024 * 1024


def params(grid, mib):
    return pltpu.CompilerParams(dimension_semantics=("arbitrary",) * grid, vmem_limit_bytes=mib * MIB)


def cost(micros, nbytes):
    return pl.CostEstimate(flops=int(micros * 1e9), bytes_accessed=int(nbytes), transcendentals=0)


def permute_kernel(slots, parts, assign_ref, *refs):
    ins, outs, perm_ref = refs[:parts], refs[parts : 2 * parts], refs[2 * parts]

    @pl.when(pl.program_id(0) == 0)
    def _():
        width = EB * slots
        lane = lax.broadcasted_iota(jnp.int32, (2 * EB, width), 1)
        row = lax.broadcasted_iota(jnp.int32, (2 * EB, width), 0)
        for s in range(0, slots, 2):
            group = jnp.where(row < EB, assign_ref[s], assign_ref[s + 1])
            hit = lane == (row % EB) * slots + group
            perm_ref[s * EB : (s + 2) * EB, :] = jnp.where(hit, 1.0, 0.0).astype(jnp.bfloat16)

    for ref, out in zip(ins, outs):
        width = ref.shape[2]
        for start in range(0, STEP, 2 * EB):
            pair = []
            for at in (start, start + EB):
                block = ref[at : at + EB].reshape(EB * slots, width)
                moved = jnp.dot(perm_ref[...], block, preferred_element_type=jnp.float32)
                pair.append(moved.reshape(slots, EB, width))
            out[:, start : start + 2 * EB, :] = jnp.concatenate(pair, axis=1).astype(jnp.bfloat16)


def permute(assign, name, *parts):
    count, slots, _ = parts[0][0].shape
    total = sum(width for _, width, _ in parts)

    def taken(column):
        return lambda i, a: (i, 0, column)

    return pl.pallas_call(
        functools.partial(permute_kernel, slots, len(parts)),
        out_shape=[jax.ShapeDtypeStruct((slots, count, width), x.dtype) for x, width, _ in parts],
        grid_spec=pltpu.PrefetchScalarGridSpec(
            num_scalar_prefetch=1,
            grid=(count // STEP,),
            in_specs=[pl.BlockSpec((STEP, slots, width), taken(column)) for _, width, column in parts],
            out_specs=[pl.BlockSpec((slots, STEP, width), lambda i, a: (0, i, 0)) for _, width, _ in parts],
            scratch_shapes=[pltpu.VMEM((EB * slots, EB * slots), jnp.bfloat16)],
        ),
        compiler_params=params(1, 40),
        cost_estimate=cost(total / 100, 4 * count * slots * total),
        name=name,
    )(assign, *[x for x, _, _ in parts])


def narrow_kernel(place_ref, g_ref, w_ref, out_ref):
    step, count, _ = g_ref.shape
    half = count // 2
    column = lax.broadcasted_iota(jnp.int32, (count, W12), 1)
    dims = (((1,), (1,)), ((), ()))
    for s in range(step):
        w = w_ref[place_ref[pl.program_id(0) * step + s]]
        first = lax.dot_general(g_ref[s, :, :PD], w, dims, preferred_element_type=jnp.float32)
        second = lax.dot_general(g_ref[s, :, PD:], w, dims, preferred_element_type=jnp.float32)
        d = jnp.where(column < W1, first, second)
        out_ref[s] = jnp.concatenate([d[:half], d[half:]], axis=1).astype(jnp.bfloat16)


def narrow_dpool(place, g12, w12):
    slots, count, _ = g12.shape
    step = 8
    return pl.pallas_call(
        narrow_kernel,
        out_shape=jax.ShapeDtypeStruct((slots, count // 2, 2 * W12), jnp.bfloat16),
        grid_spec=pltpu.PrefetchScalarGridSpec(
            num_scalar_prefetch=1,
            grid=(slots // step,),
            in_specs=[
                pl.BlockSpec((step, count, 2 * PD), lambda i, o: (i, 0, 0)),
                pl.BlockSpec((slots, W12, PD), lambda i, o: (0, 0, 0)),
            ],
            out_specs=pl.BlockSpec((step, count // 2, 2 * W12), lambda i, o: (i, 0, 0)),
        ),
        compiler_params=params(1, 24),
        cost_estimate=cost(4, slots * count * 6 * PD),
        name="narrow_dpool",
    )(place, g12, w12)


def partial_kernel(order_ref, q_ref, g12_ref, g3_ref, out_ref):
    step = out_ref.shape[0]
    dims = (((0,), (0,)), ((), ()))
    for p in range(step):
        slot = order_ref[pl.program_id(0) * step + p]
        narrow = lax.dot_general(q_ref[slot, :, :PD], g12_ref[slot], dims, preferred_element_type=jnp.float32)
        wide = lax.dot_general(q_ref[slot], g3_ref[slot], dims, preferred_element_type=jnp.float32)
        out_ref[p, :W1] = narrow[:W1, :PD]
        out_ref[p, W1:W12] = narrow[W1:W12, PD:]
        out_ref[p, W12:] = wide[W12:]


def partial_proj(order, q, g12, g3):
    slots, count, _ = q.shape
    chosen = order.shape[0]
    step = 8
    return pl.pallas_call(
        partial_kernel,
        out_shape=jax.ShapeDtypeStruct((chosen, WSUM, PD), jnp.float32),
        grid_spec=pltpu.PrefetchScalarGridSpec(
            num_scalar_prefetch=1,
            grid=(chosen // step,),
            in_specs=[
                pl.BlockSpec((slots, count, WSUM), lambda i, o: (0, 0, 0)),
                pl.BlockSpec((slots, count, 2 * PD), lambda i, o: (0, 0, 0)),
                pl.BlockSpec((slots, count, PD), lambda i, o: (0, 0, 0)),
            ],
            out_specs=pl.BlockSpec((step, WSUM, PD), lambda i, o: (i, 0, 0)),
        ),
        compiler_params=params(1, 48),
        cost_estimate=cost(4, slots * count * 1280 + chosen * WSUM * PD * 4),
        name="partial_proj",
    )(order, q, g12, g3)


def hits_kernel(index_ref, length_ref, out_ref):
    bag, block = index_ref.shape[1], index_ref.shape[2]
    lanes, chunk, low = 256, 16, ROWS // 8

    def one(i, carry):
        at = pl.ds(pl.multiple_of(i * lanes, lanes), lanes)
        index = index_ref[0, :, at]
        which = lax.broadcasted_iota(jnp.int32, (bag, lanes), 0)
        key = jnp.where(which < length_ref[0, :, at], index & (low - 1), -1)
        unit = jnp.left_shift(jnp.int32(1), jnp.right_shift(index, 6) * 4)
        ids = lax.broadcasted_iota(jnp.int32, (chunk, lanes), 0)
        for c in range(low // chunk):
            total = jnp.zeros((chunk, lanes), jnp.int32)
            for j in range(bag):
                total = total + jnp.where(key[j : j + 1] == ids + c * chunk, unit[j : j + 1], 0)
            for n in range(8):
                count = lax.shift_right_logical(total, jnp.int32(4 * n)) & 15
                start = n * low + c * chunk
                out_ref[0, start : start + chunk, at] = count.astype(jnp.float32).astype(jnp.bfloat16)
        return carry

    lax.fori_loop(0, block // lanes, one, 0)


def count_hits(lookups, counts):
    tables, bag, examples = lookups.shape
    block = 1024
    return pl.pallas_call(
        hits_kernel,
        out_shape=jax.ShapeDtypeStruct((tables, ROWS, examples), jnp.bfloat16),
        grid=(tables, examples // block),
        in_specs=[
            pl.BlockSpec((1, bag, block), lambda k, i: (k, 0, i)),
            pl.BlockSpec((1, 1, block), lambda k, i: (k, 0, i)),
        ],
        out_specs=pl.BlockSpec((1, ROWS, block), lambda k, i: (k, 0, i)),
        compiler_params=params(2, 16),
        cost_estimate=cost(10, tables * examples * (ROWS * 2 + 36)),
        name="count_hits",
    )(lookups, counts)


def wide_kernel(hits_ref, g_ref, w_ref, out_ref):
    @pl.when(pl.program_id(0) == 0)
    def _():
        out_ref[...] = jnp.zeros_like(out_ref)

    block = g_ref.shape[0]
    column = lax.broadcasted_iota(jnp.int32, (block, WSUM), 1)
    d = lax.dot_general(g_ref[...], w_ref[...], (((1,), (1,)), ((), ())), preferred_element_type=jnp.float32)
    d = jnp.where(column < W12, 0.0, d).astype(jnp.bfloat16)
    out_ref[...] += jnp.dot(hits_ref[0], d, preferred_element_type=jnp.float32)


def wide_sum(hits, g3, weights):
    _, rows, examples = hits.shape
    block = 1024
    return pl.pallas_call(
        wide_kernel,
        out_shape=jax.ShapeDtypeStruct((rows, WSUM), jnp.float32),
        grid=(examples // block,),
        in_specs=[
            pl.BlockSpec((1, rows, block), lambda i: (2, 0, i)),
            pl.BlockSpec((block, PD), lambda i: (i, 0)),
            pl.BlockSpec((WSUM, PD), lambda i: (0, 0)),
        ],
        out_specs=pl.BlockSpec((rows, WSUM), lambda i: (0, 0)),
        compiler_params=params(1, 24),
        cost_estimate=cost(5, rows * examples * 2 + examples * 256 + rows * WSUM * 4),
        name="wide_sum",
    )(hits, g3, weights)


def narrow_sum_kernel(hits_ref, d_ref, wide_ref, out_ref):
    @pl.when(pl.program_id(0) == 0)
    def _():
        out_ref[...] = wide_ref[...]

    sources = d_ref.shape[0]
    block = hits_ref.shape[2]
    column = lax.broadcasted_iota(jnp.int32, (block, PD), 1)
    pieces = []
    for d in range(sources):
        packed = d_ref[d].astype(jnp.float32)
        pieces += [packed, pltpu.roll(packed, PD - W12, 1)]
    both = jnp.concatenate(pieces, axis=0)
    d1 = jnp.where(column < W1, both, 0.0).astype(jnp.bfloat16)
    d2 = jnp.where((column >= W1) & (column < W12), both, 0.0).astype(jnp.bfloat16)
    out_ref[...] += jnp.dot(hits_ref[0], d1, preferred_element_type=jnp.float32) + jnp.dot(
        hits_ref[1], d2, preferred_element_type=jnp.float32
    )


def narrow_sum(hits, narrow, wide):
    _, rows, examples = hits.shape
    sources, half, _ = narrow.shape
    block = 1024
    per = block // (2 * half)
    return pl.pallas_call(
        narrow_sum_kernel,
        out_shape=jax.ShapeDtypeStruct((rows, WSUM), jnp.float32),
        grid=(examples // block,),
        in_specs=[
            pl.BlockSpec((2, rows, block), lambda i: (0, 0, i)),
            pl.BlockSpec((per, half, 2 * W12), lambda i: (i, 0, 0)),
            pl.BlockSpec((rows, PD), lambda i: (0, 0)),
        ],
        out_specs=pl.BlockSpec((rows, PD), lambda i: (0, 0)),
        input_output_aliases={2: 0},
        compiler_params=params(1, 24),
        cost_estimate=cost(6, rows * examples * 4 + examples * 128 + rows * PD * 8),
        name="narrow_sum",
    )(hits, narrow, wide)


def bits_of(size):
    return [1 << b for b in range(size.bit_length() - 1)]


def swap(x, axis, size, bit):
    return lax.ppermute(x, axis, [(d, d ^ bit) for d in range(size)])


def halve(kept, sent, path, sizes):
    for n, (axis, bit) in enumerate(path):
        got = swap(sent, axis, sizes[axis], bit)
        half = kept.shape[0] // 2
        if n + 1 < len(path):
            sent = kept[half:] + got[half:]
            kept = kept[:half] + got[:half]
        else:
            kept = kept + got
    return kept


def gather_rows(mine, path, sizes):
    for axis, bit in path:
        mine = jnp.concatenate([mine, swap(mine, axis, sizes[axis], bit)], axis=0)
    return mine


def local(sizes, grad_out, pooled, proj, assign, indices, lengths):
    count, slots, _ = grad_out.shape
    scale = 1.0 / math.sqrt(count * slots)
    n_node, n_local = sizes["node"], sizes["local"]
    node, loc = lax.axis_index("node"), lax.axis_index("local")
    me = (node * n_local + loc).astype(jnp.int32)

    def step_of(axis, bit):
        return bit * (n_local if axis == "node" else 1)

    core = [("node", 1)]
    nodes = [("node", b) for b in bits_of(n_node)[1:]]
    locals_ = [("local", b) for b in bits_of(n_local)]
    ids = jnp.arange(slots, dtype=jnp.int32)

    gather_path = locals_ + nodes + core
    w12 = gather_rows(proj[:, :W12], gather_path, sizes)
    place = sum(((((ids ^ me) // step_of(*hop)) & 1) << n) for n, hop in enumerate(gather_path))

    (g3,) = permute(assign, "permute_sent", (grad_out, PD, 2))
    g3_got = lax.all_to_all(g3, AXES, split_axis=0, concat_axis=0, tiled=True)
    g12, q = permute(assign, "permute_rest", (grad_out, 2 * PD, 0), (pooled, WSUM, 0))
    narrow = narrow_dpool(place, g12, w12)
    narrow, g3_got = lax.optimization_barrier((narrow, g3_got))
    narrow_got = lax.all_to_all(narrow, AXES, split_axis=0, concat_axis=0, tiled=True)

    path = core + nodes + locals_
    flip = sum(((ids >> (len(path) - 1 - n)) & 1) * step_of(*hop) for n, hop in enumerate(path))
    order = flip ^ me
    sent = partial_proj(order[slots // 2 :], q, g12, g3)
    got = swap(sent, "node", n_node, 1)
    kept = partial_proj(order[: slots // 2], q, g12, g3)
    rows = WSUM // 2
    shape = [2] * len(nodes) + [n_local, rows, PD]
    back = list(range(len(nodes)))[::-1] + [len(nodes), len(nodes) + 1, len(nodes) + 2]
    halves = []
    for part in range(2):
        cut = slice(part * rows, (part + 1) * rows)

        def laid(x):
            x = x[:, cut]
            if part:
                x = x.reshape(shape).transpose(back).reshape(x.shape)
            return x

        total = laid(kept) + laid(got)
        path = (nodes if part == 0 else nodes[::-1]) + locals_
        half = total.shape[0] // 2
        halves.append(halve(total[:half], total[half:], path, sizes))
    proj_grad = jnp.concatenate(halves, axis=1) * scale

    hits = count_hits(indices[0].transpose(1, 2, 0), lengths[0].T[:, None, :])
    wide = wide_sum(hits, g3_got.reshape(-1, PD), proj[0])
    table_grad = narrow_sum(hits, narrow_got, wide)[None]
    return (table_grad, proj_grad)


def solution(mesh):
    placed = (
        P(AXES, None, None),
        P(AXES, None, None),
        P(AXES, None, None),
        P(),
        P(AXES, None, None, None),
        P(AXES, None, None),
    )
    return jax.shard_map(
        functools.partial(local, dict(mesh.shape)),
        mesh=mesh,
        in_specs=placed,
        out_specs=(P(AXES, None, None), P(AXES, None, None)),
        check_vma=False,
    )
```

```python
import functools
import math

import jax
import jax.numpy as jnp
from jax import lax
from jax.experimental import pallas as pl
from jax.experimental.pallas import tpu as pltpu
from jax.sharding import PartitionSpec as P

ROWS = 512
W1 = 16
W2 = 48
W3 = 192
PD = 128
W12 = W1 + W2
WSUM = W12 + W3
AXES = ("node", "local")
EB = 8
STEP = 32
MIB = 1024 * 1024


def params(grid):
    return pltpu.CompilerParams(dimension_semantics=("arbitrary",) * grid, vmem_limit_bytes=60 * MIB)


ANY = pl.BlockSpec(memory_space=pl.ANY)


def cost(micros, nbytes):
    return pl.CostEstimate(flops=int(micros * 1e9), bytes_accessed=int(nbytes), transcendentals=0)


def permute_kernel(slots, parts, assign_ref, *refs):
    ins, outs, perm_ref = refs[:parts], refs[-1 - parts : -1], refs[-1]

    @pl.when(pl.program_id(0) == 0)
    def _():
        width = EB * slots
        lane = lax.broadcasted_iota(jnp.int32, (2 * EB, width), 1)
        row = lax.broadcasted_iota(jnp.int32, (2 * EB, width), 0)
        for s in range(0, slots, 2):
            group = jnp.where(row < EB, assign_ref[s], assign_ref[s + 1])
            hit = lane == (row % EB) * slots + group
            perm_ref[s * EB : (s + 2) * EB, :] = jnp.where(hit, 1.0, 0.0).astype(jnp.bfloat16)

    for ref, out in zip(ins, outs):
        width = ref.shape[2]
        for start in range(0, STEP, 2 * EB):
            pair = []
            for at in (start, start + EB):
                block = ref[at : at + EB].reshape(EB * slots, width)
                moved = jnp.dot(perm_ref[...], block, preferred_element_type=jnp.float32)
                pair.append(moved.reshape(slots, EB, width))
            out[:, start : start + 2 * EB, :] = jnp.concatenate(pair, axis=1).astype(jnp.bfloat16)


def permute(assign, name, *parts, after=()):
    count, slots, _ = parts[0][0].shape
    total = sum(width for _, width, _ in parts)

    def taken(column):
        return lambda i, a: (i, 0, column)

    return pl.pallas_call(
        functools.partial(permute_kernel, slots, len(parts)),
        out_shape=[jax.ShapeDtypeStruct((slots, count, width), x.dtype) for x, width, _ in parts],
        grid_spec=pltpu.PrefetchScalarGridSpec(
            num_scalar_prefetch=1,
            grid=(count // STEP,),
            in_specs=[pl.BlockSpec((STEP, slots, width), taken(column)) for _, width, column in parts]
            + [ANY] * len(after),
            out_specs=[pl.BlockSpec((slots, STEP, width), lambda i, a: (0, i, 0)) for _, width, _ in parts],
            scratch_shapes=[pltpu.VMEM((EB * slots, EB * slots), jnp.bfloat16)],
        ),
        compiler_params=params(1),
        cost_estimate=cost(total / 100, 4 * count * slots * total),
        name=name,
    )(assign, *[x for x, _, _ in parts], *after)


def narrow_kernel(place_ref, g_ref, w_ref, out_ref):
    step, count, _ = g_ref.shape
    half = count // 2
    column = lax.broadcasted_iota(jnp.int32, (count, W12), 1)
    dims = (((1,), (1,)), ((), ()))
    for s in range(step):
        w = w_ref[place_ref[pl.program_id(0) * step + s]]
        first = lax.dot_general(g_ref[s, :, :PD], w, dims, preferred_element_type=jnp.float32)
        second = lax.dot_general(g_ref[s, :, PD:], w, dims, preferred_element_type=jnp.float32)
        d = jnp.where(column < W1, first, second)
        out_ref[s] = jnp.concatenate([d[:half], d[half:]], axis=1).astype(jnp.bfloat16)


def narrow_dpool(place, g12, w12):
    slots, count, _ = g12.shape
    step = 8
    return pl.pallas_call(
        narrow_kernel,
        out_shape=jax.ShapeDtypeStruct((slots, count // 2, 2 * W12), jnp.bfloat16),
        grid_spec=pltpu.PrefetchScalarGridSpec(
            num_scalar_prefetch=1,
            grid=(slots // step,),
            in_specs=[
                pl.BlockSpec((step, count, 2 * PD), lambda i, o: (i, 0, 0)),
                pl.BlockSpec((slots, W12, PD), lambda i, o: (0, 0, 0)),
            ],
            out_specs=pl.BlockSpec((step, count // 2, 2 * W12), lambda i, o: (i, 0, 0)),
        ),
        compiler_params=params(1),
        cost_estimate=cost(4, slots * count * 6 * PD),
        name="narrow_dpool",
    )(place, g12, w12)


def partial_kernel(add, order_ref, q_ref, g12_ref, g3_ref, *refs):
    out_ref = refs[-1]
    step = out_ref.shape[0]
    dims = (((0,), (0,)), ((), ()))
    for p in range(step):
        slot = order_ref[pl.program_id(0) * step + p]
        narrow = lax.dot_general(q_ref[slot, :, :PD], g12_ref[slot], dims, preferred_element_type=jnp.float32)
        wide = lax.dot_general(q_ref[slot], g3_ref[slot], dims, preferred_element_type=jnp.float32)
        pieces = ((0, W1, narrow[:W1, :PD]), (W1, W12, narrow[W1:W12, PD:]), (W12, WSUM, wide[W12:]))
        for start, end, piece in pieces:
            out_ref[p, start:end] = piece + refs[0][p, start:end] if add else piece


def partial_proj(order, q, g12, g3, other=None, after=()):
    slots, count, _ = q.shape
    chosen = order.shape[0]
    step = 8
    added = () if other is None else (other,)
    block = pl.BlockSpec((step, WSUM, PD), lambda i, o: (i, 0, 0))
    return pl.pallas_call(
        functools.partial(partial_kernel, other is not None),
        out_shape=jax.ShapeDtypeStruct((chosen, WSUM, PD), jnp.float32),
        grid_spec=pltpu.PrefetchScalarGridSpec(
            num_scalar_prefetch=1,
            grid=(chosen // step,),
            in_specs=[
                pl.BlockSpec((slots, count, WSUM), lambda i, o: (0, 0, 0)),
                pl.BlockSpec((slots, count, 2 * PD), lambda i, o: (0, 0, 0)),
                pl.BlockSpec((slots, count, PD), lambda i, o: (0, 0, 0)),
            ]
            + [block] * len(added)
            + [ANY] * len(after),
            out_specs=block,
        ),
        compiler_params=params(1),
        cost_estimate=cost(4, slots * count * 1280 + chosen * WSUM * PD * 4),
        name="partial_proj",
    )(order, q, g12, g3, *added, *after)


def hits_kernel(index_ref, length_ref, *refs):
    out_ref = refs[-1]
    bag, block = index_ref.shape[1], index_ref.shape[2]
    lanes, chunk, low = 256, 16, ROWS // 8

    def one(i, carry):
        at = pl.ds(pl.multiple_of(i * lanes, lanes), lanes)
        index = index_ref[0, :, at]
        which = lax.broadcasted_iota(jnp.int32, (bag, lanes), 0)
        key = jnp.where(which < length_ref[0, :, at], index & (low - 1), -1)
        unit = jnp.left_shift(jnp.int32(1), jnp.right_shift(index, 6) * 4)
        ids = lax.broadcasted_iota(jnp.int32, (chunk, lanes), 0)
        for c in range(low // chunk):
            total = jnp.zeros((chunk, lanes), jnp.int32)
            for j in range(bag):
                total = total + jnp.where(key[j : j + 1] == ids + c * chunk, unit[j : j + 1], 0)
            for n in range(8):
                count = lax.shift_right_logical(total, jnp.int32(4 * n)) & 15
                start = n * low + c * chunk
                out_ref[0, start : start + chunk, at] = count.astype(jnp.float32).astype(jnp.bfloat16)
        return carry

    lax.fori_loop(0, block // lanes, one, 0)


def count_hits(lookups, counts, after=()):
    tables, bag, examples = lookups.shape
    block = 1024
    return pl.pallas_call(
        hits_kernel,
        out_shape=jax.ShapeDtypeStruct((tables, ROWS, examples), jnp.bfloat16),
        grid=(tables, examples // block),
        in_specs=[
            pl.BlockSpec((1, bag, block), lambda k, i: (k, 0, i)),
            pl.BlockSpec((1, 1, block), lambda k, i: (k, 0, i)),
        ]
        + [ANY] * len(after),
        out_specs=pl.BlockSpec((1, ROWS, block), lambda k, i: (k, 0, i)),
        compiler_params=params(2),
        cost_estimate=cost(10, tables * examples * (ROWS * 2 + 36)),
        name="count_hits",
    )(lookups, counts, *after)


def wide_kernel(hits_ref, g_ref, w_ref, out_ref):
    @pl.when(pl.program_id(0) == 0)
    def _():
        out_ref[...] = jnp.zeros_like(out_ref)

    block = g_ref.shape[0]
    column = lax.broadcasted_iota(jnp.int32, (block, WSUM), 1)
    d = lax.dot_general(g_ref[...], w_ref[...], (((1,), (1,)), ((), ())), preferred_element_type=jnp.float32)
    d = jnp.where(column < W12, 0.0, d).astype(jnp.bfloat16)
    out_ref[...] += jnp.dot(hits_ref[0], d, preferred_element_type=jnp.float32)


def wide_sum(hits, g3, weights):
    _, rows, examples = hits.shape
    block = 1024
    return pl.pallas_call(
        wide_kernel,
        out_shape=jax.ShapeDtypeStruct((rows, WSUM), jnp.float32),
        grid=(examples // block,),
        in_specs=[
            pl.BlockSpec((1, rows, block), lambda i: (2, 0, i)),
            pl.BlockSpec((block, PD), lambda i: (i, 0)),
            pl.BlockSpec((WSUM, PD), lambda i: (0, 0)),
        ],
        out_specs=pl.BlockSpec((rows, WSUM), lambda i: (0, 0)),
        compiler_params=params(1),
        cost_estimate=cost(5, rows * examples * 2 + examples * 256 + rows * WSUM * 4),
        name="wide_sum",
    )(hits, g3, weights)


def narrow_sum_kernel(hits_ref, d_ref, wide_ref, out_ref):
    @pl.when(pl.program_id(0) == 0)
    def _():
        out_ref[...] = wide_ref[...]

    sources = d_ref.shape[0]
    block = hits_ref.shape[2]
    column = lax.broadcasted_iota(jnp.int32, (block, PD), 1)
    pieces = []
    for d in range(sources):
        packed = d_ref[d].astype(jnp.float32)
        pieces += [packed, pltpu.roll(packed, PD - W12, 1)]
    both = jnp.concatenate(pieces, axis=0)
    d1 = jnp.where(column < W1, both, 0.0).astype(jnp.bfloat16)
    d2 = jnp.where((column >= W1) & (column < W12), both, 0.0).astype(jnp.bfloat16)
    out_ref[...] += jnp.dot(hits_ref[0], d1, preferred_element_type=jnp.float32) + jnp.dot(
        hits_ref[1], d2, preferred_element_type=jnp.float32
    )


def narrow_sum(hits, narrow, wide):
    _, rows, examples = hits.shape
    sources, half, _ = narrow.shape
    block = 1024
    per = block // (2 * half)
    return pl.pallas_call(
        narrow_sum_kernel,
        out_shape=jax.ShapeDtypeStruct((rows, WSUM), jnp.float32),
        grid=(examples // block,),
        in_specs=[
            pl.BlockSpec((2, rows, block), lambda i: (0, 0, i)),
            pl.BlockSpec((per, half, 2 * W12), lambda i: (i, 0, 0)),
            pl.BlockSpec((rows, PD), lambda i: (0, 0)),
        ],
        out_specs=pl.BlockSpec((rows, PD), lambda i: (0, 0)),
        input_output_aliases={2: 0},
        compiler_params=params(1),
        cost_estimate=cost(6, rows * examples * 4 + examples * 128 + rows * PD * 8),
        name="narrow_sum",
    )(hits, narrow, wide)


def bits_of(size):
    return [1 << b for b in range(size.bit_length() - 1)]


def swap(x, axis, size, bit):
    return lax.ppermute(x, axis, [(d, d ^ bit) for d in range(size)])


def gather_rows(mine, path, sizes):
    steps = []
    for axis, bit in path:
        steps.append(swap(mine, axis, sizes[axis], bit))
        mine = jnp.concatenate([mine, steps[-1]], axis=0)
    return mine, steps


def local(sizes, grad_out, pooled, proj, assign, indices, lengths):
    count, slots, _ = grad_out.shape
    scale = 1.0 / math.sqrt(count * slots)
    n_node, n_local = sizes["node"], sizes["local"]
    node, loc = lax.axis_index("node"), lax.axis_index("local")
    me = (node * n_local + loc).astype(jnp.int32)

    def step_of(axis, bit):
        return bit * (n_local if axis == "node" else 1)

    ids = jnp.arange(slots, dtype=jnp.int32)
    path = [("local", b) for b in bits_of(n_local)] + [("node", b) for b in bits_of(n_node)[1:]] + [("node", 1)]
    w12, steps = gather_rows(proj[:, :W12], path, sizes)
    place = sum(((((ids ^ me) // step_of(*hop)) & 1) << n) for n, hop in enumerate(path))

    half = jnp.arange(slots // 2, dtype=jnp.int32)
    here = (half // n_local * 2 + node % 2) * n_local + half % n_local
    there = (half // n_local * 2 + 1 - node % 2) * n_local + half % n_local

    (g3,) = permute(assign, "permute_sent", (grad_out, PD, 2))
    g3_got = lax.all_to_all(g3, AXES, split_axis=0, concat_axis=0, tiled=True)
    g12, q = permute(
        assign, "permute_rest", (grad_out, 2 * PD, 0), (pooled, WSUM, 0), after=steps[0:1]
    )
    sent = partial_proj(there, q, g12, g3, after=steps[1:2])
    got = swap(sent, "node", n_node, 1)
    hits = count_hits(indices[0].transpose(1, 2, 0), lengths[0].T[:, None, :], after=[sent] + steps[2:3])
    kept = partial_proj(here, q, g12, g3, got, after=[hits] + steps[3:4])
    narrow = narrow_dpool(place, g12, w12)
    narrow, g3_got = lax.optimization_barrier((narrow, g3_got))
    narrow_got = lax.all_to_all(narrow, AXES, split_axis=0, concat_axis=0, tiled=True)

    groups = [list(range(c, n_node, 2)) for c in range(2)]
    plane = lax.all_to_all(kept, "node", split_axis=0, concat_axis=0, tiled=True, axis_index_groups=groups)
    plane = plane.reshape(n_node // 2, n_local, WSUM, PD).sum(axis=0)
    line = lax.all_to_all(plane, "local", split_axis=0, concat_axis=0, tiled=True)
    proj_grad = line.sum(axis=0, keepdims=True) * scale

    wide = wide_sum(hits, g3_got.reshape(-1, PD), proj[0])
    table_grad = narrow_sum(hits, narrow_got, wide)[None]
    return (table_grad, proj_grad)


def solution(mesh):
    placed = (
        P(AXES, None, None),
        P(AXES, None, None),
        P(AXES, None, None),
        P(),
        P(AXES, None, None, None),
        P(AXES, None, None),
    )
    return jax.shard_map(
        functools.partial(local, dict(mesh.shape)),
        mesh=mesh,
        in_specs=placed,
        out_specs=(P(AXES, None, None), P(AXES, None, None)),
        check_vma=False,
    )
```

```python
import functools
import math

import jax
import jax.numpy as jnp
from jax import lax
from jax.experimental import pallas as pl
from jax.experimental.pallas import tpu as pltpu
from jax.sharding import PartitionSpec as P

ROWS = 512
W1 = 16
W2 = 48
W3 = 192
PD = 128
W12 = W1 + W2
WSUM = W12 + W3
AXES = ("node", "local")
EB = 8
STEP = 32
MIB = 1024 * 1024


def params(grid, mib, slots=32):
    mib = min(60, mib * max(slots, 32) // 32)
    return pltpu.CompilerParams(dimension_semantics=("arbitrary",) * grid, vmem_limit_bytes=mib * MIB)


ANY = pl.BlockSpec(memory_space=pl.ANY)


def cost(flops):
    return pl.CostEstimate(flops=int(flops), bytes_accessed=1024, transcendentals=0)


def permute_kernel(slots, pieces, assign_ref, *refs):
    ins, outs, perm_ref = refs[:2], refs[2:-1], refs[-1]

    @pl.when(pl.program_id(0) == 0)
    def _():
        width = EB * slots
        lane = lax.broadcasted_iota(jnp.int32, (2 * EB, width), 1)
        row = lax.broadcasted_iota(jnp.int32, (2 * EB, width), 0)
        for s in range(0, slots, 2):
            group = jnp.where(row < EB, assign_ref[s], assign_ref[s + 1])
            hit = lane == (row % EB) * slots + group
            perm_ref[s * EB : (s + 2) * EB, :] = jnp.where(hit, 1.0, 0.0).astype(jnp.bfloat16)

    for ref, cuts in zip(ins, pieces):
        width = ref.shape[2]
        for start in range(0, STEP, 2 * EB):
            pair = []
            for at in (start, start + EB):
                block = ref[at : at + EB].reshape(EB * slots, width)
                moved = jnp.dot(perm_ref[...], block, preferred_element_type=jnp.float32)
                pair.append(moved.reshape(slots, EB, width))
            both = jnp.concatenate(pair, axis=1).astype(jnp.bfloat16)
            for n, low, high in cuts:
                outs[n][:, start : start + 2 * EB, :] = both[:, :, low:high]


def permute(assign, grad_out, pooled):
    count, slots, _ = grad_out.shape
    widths = (2 * PD, PD, WSUM)
    pieces = (((0, 0, 2 * PD), (1, 2 * PD, 3 * PD)), ((2, 0, WSUM),))
    return pl.pallas_call(
        functools.partial(permute_kernel, slots, pieces),
        out_shape=[jax.ShapeDtypeStruct((slots, count, width), jnp.bfloat16) for width in widths],
        grid_spec=pltpu.PrefetchScalarGridSpec(
            num_scalar_prefetch=1,
            grid=(count // STEP,),
            in_specs=[pl.BlockSpec((STEP, slots, x.shape[2]), lambda i, a: (i, 0, 0)) for x in (grad_out, pooled)],
            out_specs=[pl.BlockSpec((slots, STEP, width), lambda i, a: (0, i, 0)) for width in widths],
            scratch_shapes=[pltpu.VMEM((EB * slots, EB * slots), jnp.bfloat16)],
        ),
        compiler_params=params(1, 16, slots),
        cost_estimate=cost(1e9),
        name="permute_groups",
    )(assign, grad_out, pooled)


def narrow_kernel(g_ref, w_ref, out_ref):
    step, count, _ = g_ref.shape
    half = count // 2
    column = lax.broadcasted_iota(jnp.int32, (count, W12), 1)
    dims = (((1,), (1,)), ((), ()))
    for s in range(step):
        w = w_ref[s]
        first = lax.dot_general(g_ref[s, :, :PD], w, dims, preferred_element_type=jnp.float32)
        second = lax.dot_general(g_ref[s, :, PD:], w, dims, preferred_element_type=jnp.float32)
        d = jnp.where(column < W1, first, second)
        out_ref[s] = jnp.concatenate([d[:half], d[half:]], axis=1).astype(jnp.bfloat16)


def narrow_dpool(g12, w12):
    slots, count, _ = g12.shape
    step = 8
    return pl.pallas_call(
        narrow_kernel,
        out_shape=jax.ShapeDtypeStruct((slots, count // 2, 2 * W12), jnp.bfloat16),
        grid=(slots // step,),
        in_specs=[
            pl.BlockSpec((step, count, 2 * PD), lambda i: (i, 0, 0)),
            pl.BlockSpec((step, W12, PD), lambda i: (i, 0, 0)),
        ],
        out_specs=pl.BlockSpec((step, count // 2, 2 * W12), lambda i: (i, 0, 0)),
        compiler_params=params(1, 12),
        cost_estimate=cost(1e9),
        name="narrow_dpool",
    )(g12, w12)


def partial_kernel(step, chunks, add, order_ref, q_ref, g12_ref, g3_ref, *refs):
    outs = refs[len(refs) - chunks :]
    dims = (((0,), (0,)), ((), ()))
    size = outs[0].shape[0]

    def one(c, i, at):
        slot = order_ref[c * size + at]
        narrow = lax.dot_general(q_ref[slot, :, :PD], g12_ref[slot], dims, preferred_element_type=jnp.float32)
        wide = lax.dot_general(q_ref[slot], g3_ref[slot], dims, preferred_element_type=jnp.float32)
        pieces = ((0, W1, narrow[:W1, :PD]), (W1, W12, narrow[W1:W12, PD:]), (W12, WSUM, wide[W12:]))
        for start, end, piece in pieces:
            if add:
                piece = piece + refs[0][i, start:end]
            outs[c][at, start:end] = piece

    per = size // step
    for c in range(chunks):

        @pl.when(pl.program_id(0) // per == c)
        def _():
            for i in range(step):
                one(c, i, pl.program_id(0) % per * step + i)


def partial_proj(order, chunks, q, g12, g3, other=None):
    slots, count, _ = q.shape
    chosen = order.shape[0]
    size = chosen // chunks
    step = math.gcd(size, 8)
    added = () if other is None else (other,)
    whole = pl.BlockSpec((size, WSUM, PD), lambda i, o: (0, 0, 0))
    return pl.pallas_call(
        functools.partial(partial_kernel, step, chunks, other is not None),
        out_shape=[jax.ShapeDtypeStruct((size, WSUM, PD), jnp.float32)] * chunks,
        grid_spec=pltpu.PrefetchScalarGridSpec(
            num_scalar_prefetch=1,
            grid=(chosen // step,),
            in_specs=[
                pl.BlockSpec((slots, count, WSUM), lambda i, o: (0, 0, 0), pipeline_mode=pl.Buffered(1)),
                pl.BlockSpec((slots, count, 2 * PD), lambda i, o: (0, 0, 0), pipeline_mode=pl.Buffered(1)),
                pl.BlockSpec((slots, count, PD), lambda i, o: (0, 0, 0), pipeline_mode=pl.Buffered(1)),
            ]
            + [pl.BlockSpec((step, WSUM, PD), lambda i, o: (i, 0, 0))] * len(added),
            out_specs=[whole] * chunks,
        ),
        compiler_params=params(1, 18, slots),
        cost_estimate=cost(1e9),
        name="partial_proj",
    )(order, q, g12, g3, *added)


def hits_kernel(index_ref, length_ref, *refs):
    out_ref = refs[-1]
    bag, block = index_ref.shape[1], index_ref.shape[2]
    lanes, chunk, low = 256, 16, ROWS // 8

    def one(i, carry):
        at = pl.ds(pl.multiple_of(i * lanes, lanes), lanes)
        index = index_ref[0, :, at]
        which = lax.broadcasted_iota(jnp.int32, (bag, lanes), 0)
        key = jnp.where(which < length_ref[0, :, at], index & (low - 1), -1)
        unit = jnp.left_shift(jnp.int32(1), jnp.right_shift(index, 6) * 4)
        ids = lax.broadcasted_iota(jnp.int32, (chunk, lanes), 0)
        for c in range(low // chunk):
            total = jnp.zeros((chunk, lanes), jnp.int32)
            for j in range(bag):
                total = total + jnp.where(key[j : j + 1] == ids + c * chunk, unit[j : j + 1], 0)
            for n in range(8):
                count = lax.shift_right_logical(total, jnp.int32(4 * n)) & 15
                start = n * low + c * chunk
                out_ref[0, start : start + chunk, at] = count.astype(jnp.float32).astype(jnp.bfloat16)
        return carry

    lax.fori_loop(0, block // lanes, one, 0)


def count_hits(lookups, counts, after=()):
    tables, bag, examples = lookups.shape
    block = 1024
    return pl.pallas_call(
        hits_kernel,
        out_shape=jax.ShapeDtypeStruct((tables, ROWS, examples), jnp.bfloat16),
        grid=(tables, examples // block),
        in_specs=[
            pl.BlockSpec((1, bag, block), lambda k, i: (k, 0, i)),
            pl.BlockSpec((1, 1, block), lambda k, i: (k, 0, i)),
        ]
        + [ANY] * len(after),
        out_specs=pl.BlockSpec((1, ROWS, block), lambda k, i: (k, 0, i)),
        compiler_params=params(2, 12),
        cost_estimate=cost(1e9),
        name="count_hits",
    )(lookups, counts, *after)


def wide_kernel(hits_ref, g_ref, w_ref, out_ref):
    @pl.when(pl.program_id(0) == 0)
    def _():
        out_ref[...] = jnp.zeros_like(out_ref)

    block = g_ref.shape[0]
    column = lax.broadcasted_iota(jnp.int32, (block, WSUM), 1)
    d = lax.dot_general(g_ref[...], w_ref[...], (((1,), (1,)), ((), ())), preferred_element_type=jnp.float32)
    d = jnp.where(column < W12, 0.0, d).astype(jnp.bfloat16)
    out_ref[...] += jnp.dot(hits_ref[0], d, preferred_element_type=jnp.float32)


def wide_sum(hits, g3, weights):
    _, rows, examples = hits.shape
    block = 1024
    return pl.pallas_call(
        wide_kernel,
        out_shape=jax.ShapeDtypeStruct((rows, WSUM), jnp.float32),
        grid=(examples // block,),
        in_specs=[
            pl.BlockSpec((1, rows, block), lambda i: (2, 0, i)),
            pl.BlockSpec((block, PD), lambda i: (i, 0)),
            pl.BlockSpec((WSUM, PD), lambda i: (0, 0)),
        ],
        out_specs=pl.BlockSpec((rows, WSUM), lambda i: (0, 0)),
        compiler_params=params(1, 12),
        cost_estimate=cost(1e9),
        name="wide_sum",
    )(hits, g3, weights)


def narrow_sum_kernel(hits_ref, d_ref, wide_ref, out_ref):
    @pl.when(pl.program_id(0) == 0)
    def _():
        out_ref[...] = wide_ref[...]

    sources = d_ref.shape[0]
    block = hits_ref.shape[2]
    column = lax.broadcasted_iota(jnp.int32, (block, PD), 1)
    pieces = []
    for d in range(sources):
        packed = d_ref[d].astype(jnp.float32)
        pieces += [packed, pltpu.roll(packed, PD - W12, 1)]
    both = jnp.concatenate(pieces, axis=0)
    d1 = jnp.where(column < W1, both, 0.0).astype(jnp.bfloat16)
    d2 = jnp.where((column >= W1) & (column < W12), both, 0.0).astype(jnp.bfloat16)
    out_ref[...] += jnp.dot(hits_ref[0], d1, preferred_element_type=jnp.float32) + jnp.dot(
        hits_ref[1], d2, preferred_element_type=jnp.float32
    )


def narrow_sum(hits, narrow, wide):
    _, rows, examples = hits.shape
    sources, half, _ = narrow.shape
    block = 1024
    per = block // (2 * half)
    return pl.pallas_call(
        narrow_sum_kernel,
        out_shape=jax.ShapeDtypeStruct((rows, WSUM), jnp.float32),
        grid=(examples // block,),
        in_specs=[
            pl.BlockSpec((2, rows, block), lambda i: (0, 0, i)),
            pl.BlockSpec((per, half, 2 * W12), lambda i: (i, 0, 0)),
            pl.BlockSpec((rows, PD), lambda i: (0, 0)),
        ],
        out_specs=pl.BlockSpec((rows, PD), lambda i: (0, 0)),
        input_output_aliases={2: 0},
        compiler_params=params(1, 12),
        cost_estimate=cost(1e9),
        name="narrow_sum",
    )(hits, narrow, wide)


def swap(x, axis, size, bits):
    return lax.ppermute(x, axis, [(d, d ^ bits) for d in range(size)])


def local(sizes, grad_out, pooled, proj, assign, indices, lengths):
    count, slots, _ = grad_out.shape
    scale = 1.0 / math.sqrt(count * slots)
    n_node, n_local = sizes["node"], sizes["local"]
    n_plane = n_node // 2
    node, loc = lax.axis_index("node"), lax.axis_index("local")

    w12 = jnp.broadcast_to(proj[:, :W12], (slots, W12, PD))
    w12 = lax.all_to_all(w12, AXES, split_axis=0, concat_axis=0, tiled=True)

    g12, g3, q = permute(assign, grad_out, pooled)
    g3_sent, w12 = lax.optimization_barrier((g3, w12))
    g3_got = lax.all_to_all(g3_sent, AXES, split_axis=0, concat_axis=0, tiled=True)
    narrow = narrow_dpool(g12, w12)
    narrow_sent, g3_got = lax.optimization_barrier((narrow, g3_got))
    narrow_got = lax.all_to_all(narrow_sent, AXES, split_axis=0, concat_axis=0, tiled=True)

    place = jnp.arange(slots // 2, dtype=jnp.int32)
    plane, line = (place // n_local) ^ (node // 2), (place % n_local) ^ loc
    here = (plane * 2 + node % 2) * n_local + line
    there = (plane * 2 + 1 - node % 2) * n_local + line
    (sent,) = partial_proj(there, 1, q, g12, g3)
    got = swap(sent, "node", n_node, 1)
    kept = partial_proj(here, n_plane, q, g12, g3, got)
    total = kept[0]
    for d in range(1, n_plane):
        total = total + swap(kept[d], "node", n_node, 2 * d)
    proj_grad = total[:1]
    for d in range(1, n_local):
        proj_grad = proj_grad + swap(total[d : d + 1], "local", n_local, d)
    proj_grad = proj_grad * scale

    hits = count_hits(indices[0].transpose(1, 2, 0), lengths[0].T[:, None, :], after=[narrow])
    wide = wide_sum(hits, g3_got.reshape(-1, PD), proj[0])
    table_grad = narrow_sum(hits, narrow_got, wide)[None]
    return (table_grad, proj_grad)


def solution(mesh):
    placed = (
        P(AXES, None, None),
        P(AXES, None, None),
        P(AXES, None, None),
        P(),
        P(AXES, None, None, None),
        P(AXES, None, None),
    )
    return jax.shard_map(
        functools.partial(local, dict(mesh.shape)),
        mesh=mesh,
        in_specs=placed,
        out_specs=(P(AXES, None, None), P(AXES, None, None)),
        check_vma=False,
    )
```

```python
import functools
import math

import jax
import jax.numpy as jnp
from jax import lax
from jax.experimental import pallas as pl
from jax.experimental.pallas import tpu as pltpu
from jax.sharding import PartitionSpec as P

ROWS = 512
W1 = 16
W2 = 48
W3 = 192
PD = 128
W12 = W1 + W2
WSUM = W12 + W3
AXES = ("node", "local")
EB = 8
STEP = 32
MIB = 1024 * 1024


def params(grid, mib, slots=32):
    mib = min(60, mib * max(slots, 32) // 32)
    return pltpu.CompilerParams(dimension_semantics=("arbitrary",) * grid, vmem_limit_bytes=mib * MIB)


ANY = pl.BlockSpec(memory_space=pl.ANY)


def cost(flops):
    return pl.CostEstimate(flops=int(flops), bytes_accessed=1024, transcendentals=0)


def permute_kernel(slots, pieces, assign_ref, grad_ref, pool_ref, *refs):
    outs, (perm_ref, grad_held, pool_held, sems) = refs[:3], refs[3:]
    step = pl.program_id(0)
    sources = ((grad_ref, grad_held), (pool_ref, pool_held))

    def copies(i):
        at = pl.ds(i * STEP, STEP)
        return [
            pltpu.make_async_copy(ref.at[at], held.at[at], sems.at[n, i]) for n, (ref, held) in enumerate(sources)
        ]

    @pl.when(step == 0)
    def _():
        for i in range(grad_ref.shape[0] // STEP):
            for copy in copies(i):
                copy.start()
        width = EB * slots
        lane = lax.broadcasted_iota(jnp.int32, (2 * EB, width), 1)
        row = lax.broadcasted_iota(jnp.int32, (2 * EB, width), 0)
        for s in range(0, slots, 2):
            group = jnp.where(row < EB, assign_ref[s], assign_ref[s + 1])
            hit = lane == (row % EB) * slots + group
            perm_ref[s * EB : (s + 2) * EB, :] = jnp.where(hit, 1.0, 0.0).astype(jnp.bfloat16)

    for copy, (_, held), cuts in zip(copies(step), sources, pieces):
        copy.wait()
        width = held.shape[2]
        for start in range(0, STEP, 2 * EB):
            pair = []
            for at in (start, start + EB):
                block = held[pl.ds(step * STEP + at, EB)].reshape(EB * slots, width)
                moved = jnp.dot(perm_ref[...], block, preferred_element_type=jnp.float32)
                pair.append(moved.reshape(slots, EB, width))
            both = jnp.concatenate(pair, axis=1).astype(jnp.bfloat16)
            for n, low, high in cuts:
                outs[n][:, start : start + 2 * EB, :] = both[:, :, low:high]


def permute(assign, grad_out, pooled):
    count, slots, _ = grad_out.shape
    widths = (2 * PD, PD, WSUM)
    pieces = (((0, 0, 2 * PD), (1, 2 * PD, 3 * PD)), ((2, 0, WSUM),))
    return pl.pallas_call(
        functools.partial(permute_kernel, slots, pieces),
        out_shape=[jax.ShapeDtypeStruct((slots, count, width), jnp.bfloat16) for width in widths],
        grid_spec=pltpu.PrefetchScalarGridSpec(
            num_scalar_prefetch=1,
            grid=(count // STEP,),
            in_specs=[pl.BlockSpec(memory_space=pltpu.HBM)] * 2,
            out_specs=[pl.BlockSpec((slots, STEP, width), lambda i, a: (0, i, 0)) for width in widths],
            scratch_shapes=[
                pltpu.VMEM((EB * slots, EB * slots), jnp.bfloat16),
                pltpu.VMEM(grad_out.shape, jnp.bfloat16),
                pltpu.VMEM(pooled.shape, jnp.bfloat16),
                pltpu.SemaphoreType.DMA((2, count // STEP)),
            ],
        ),
        compiler_params=params(1, 15, slots),
        cost_estimate=cost(1e9),
        name="permute_groups",
    )(assign, grad_out, pooled)


def narrow_kernel(place_ref, g_ref, w_ref, out_ref):
    step, count, _ = g_ref.shape
    half = count // 2
    column = lax.broadcasted_iota(jnp.int32, (count, W12), 1)
    dims = (((1,), (1,)), ((), ()))
    for s in range(step):
        w = w_ref[place_ref[pl.program_id(0) * step + s]]
        first = lax.dot_general(g_ref[s, :, :PD], w, dims, preferred_element_type=jnp.float32)
        second = lax.dot_general(g_ref[s, :, PD:], w, dims, preferred_element_type=jnp.float32)
        d = jnp.where(column < W1, first, second)
        out_ref[s] = jnp.concatenate([d[:half], d[half:]], axis=1).astype(jnp.bfloat16)


def narrow_dpool(place, g12, w12):
    slots, count, _ = g12.shape
    step = 8
    return pl.pallas_call(
        narrow_kernel,
        out_shape=jax.ShapeDtypeStruct((slots, count // 2, 2 * W12), jnp.bfloat16),
        grid_spec=pltpu.PrefetchScalarGridSpec(
            num_scalar_prefetch=1,
            grid=(slots // step,),
            in_specs=[
                pl.BlockSpec((step, count, 2 * PD), lambda i, o: (i, 0, 0)),
                pl.BlockSpec((slots, W12, PD), lambda i, o: (0, 0, 0)),
            ],
            out_specs=pl.BlockSpec((step, count // 2, 2 * W12), lambda i, o: (i, 0, 0)),
        ),
        compiler_params=params(1, 12),
        cost_estimate=cost(1e9),
        name="narrow_dpool",
    )(place, g12, w12)


def partial_kernel(step, chunks, add, order_ref, q_ref, g12_ref, g3_ref, *refs):
    outs = refs[len(refs) - chunks :]
    size = outs[0].shape[0]

    def one(c, i, at):
        slot = order_ref[c * size + at]
        q = q_ref[slot].T
        narrow = jnp.dot(q[:W12], g12_ref[slot], preferred_element_type=jnp.float32)
        wide = jnp.dot(q[W12:], g3_ref[slot], preferred_element_type=jnp.float32)
        pieces = ((0, W1, narrow[:W1, :PD]), (W1, W12, narrow[W1:, PD:]), (W12, WSUM, wide))
        for start, end, piece in pieces:
            if add:
                piece = piece + refs[0][i, start:end]
            outs[c][at, start:end] = piece.astype(outs[c].dtype)

    per = size // step
    for c in range(chunks):

        @pl.when(pl.program_id(0) // per == c)
        def _():
            for i in range(step):
                one(c, i, pl.program_id(0) % per * step + i)


def partial_proj(order, chunks, q, g12, g3, other=None):
    slots, count, _ = q.shape
    chosen = order.shape[0]
    size = chosen // chunks
    step = math.gcd(size, 8)
    added = () if other is None else (other,)
    whole = pl.BlockSpec((size, WSUM, PD), lambda i, o: (0, 0, 0))
    return pl.pallas_call(
        functools.partial(partial_kernel, step, chunks, other is not None),
        out_shape=[
            jax.ShapeDtypeStruct((size, WSUM, PD), jnp.bfloat16 if c else jnp.float32) for c in range(chunks)
        ],
        grid_spec=pltpu.PrefetchScalarGridSpec(
            num_scalar_prefetch=1,
            grid=(chosen // step,),
            in_specs=[
                pl.BlockSpec((slots, count, WSUM), lambda i, o: (0, 0, 0), pipeline_mode=pl.Buffered(1)),
                pl.BlockSpec((slots, count, 2 * PD), lambda i, o: (0, 0, 0), pipeline_mode=pl.Buffered(1)),
                pl.BlockSpec((slots, count, PD), lambda i, o: (0, 0, 0), pipeline_mode=pl.Buffered(1)),
            ]
            + [pl.BlockSpec((step, WSUM, PD), lambda i, o: (i, 0, 0))] * len(added),
            out_specs=[whole] * chunks,
        ),
        compiler_params=params(1, 18, slots),
        cost_estimate=cost(1e9),
        name="partial_proj",
    )(order, q, g12, g3, *added)


def hits_kernel(index_ref, length_ref, *refs):
    out_ref = refs[-1]
    bag, block = index_ref.shape[1], index_ref.shape[2]
    lanes, chunk, low = 256, 16, ROWS // 8

    def one(i, carry):
        at = pl.ds(pl.multiple_of(i * lanes, lanes), lanes)
        index = index_ref[0, :, at]
        which = lax.broadcasted_iota(jnp.int32, (bag, lanes), 0)
        key = jnp.where(which < length_ref[0, :, at], index & (low - 1), -1)
        unit = jnp.left_shift(jnp.int32(1), jnp.right_shift(index, 6) * 4)
        ids = lax.broadcasted_iota(jnp.int32, (chunk, lanes), 0)
        for c in range(low // chunk):
            total = jnp.zeros((chunk, lanes), jnp.int32)
            for j in range(bag):
                total = total + jnp.where(key[j : j + 1] == ids + c * chunk, unit[j : j + 1], 0)
            for n in range(8):
                count = lax.shift_right_logical(total, jnp.int32(4 * n)) & 15
                start = n * low + c * chunk
                out_ref[0, start : start + chunk, at] = count.astype(jnp.float32).astype(jnp.bfloat16)
        return carry

    lax.fori_loop(0, block // lanes, one, 0)


def count_hits(lookups, counts, first, tables, after=()):
    _, bag, examples = lookups.shape
    block = 1024
    return pl.pallas_call(
        hits_kernel,
        out_shape=jax.ShapeDtypeStruct((tables, ROWS, examples), jnp.bfloat16),
        grid=(tables, examples // block),
        in_specs=[
            pl.BlockSpec((1, bag, block), lambda k, i: (k + first, 0, i)),
            pl.BlockSpec((1, 1, block), lambda k, i: (k + first, 0, i)),
        ]
        + [ANY] * len(after),
        out_specs=pl.BlockSpec((1, ROWS, block), lambda k, i: (k, 0, i)),
        compiler_params=params(2, 12),
        cost_estimate=cost(1e9),
        name="count_hits",
    )(lookups, counts, *after)


def wide_kernel(hits_ref, g_ref, w_ref, out_ref):
    @pl.when(pl.program_id(0) == 0)
    def _():
        out_ref[...] = jnp.zeros_like(out_ref)

    block = g_ref.shape[0]
    column = lax.broadcasted_iota(jnp.int32, (block, WSUM), 1)
    d = lax.dot_general(g_ref[...], w_ref[...], (((1,), (1,)), ((), ())), preferred_element_type=jnp.float32)
    d = jnp.where(column < W12, 0.0, d).astype(jnp.bfloat16)
    out_ref[...] += jnp.dot(hits_ref[0], d, preferred_element_type=jnp.float32)


def wide_sum(hits, g3, weights):
    _, rows, examples = hits.shape
    block = 1024
    return pl.pallas_call(
        wide_kernel,
        out_shape=jax.ShapeDtypeStruct((rows, WSUM), jnp.float32),
        grid=(examples // block,),
        in_specs=[
            pl.BlockSpec((1, rows, block), lambda i: (0, 0, i)),
            pl.BlockSpec((block, PD), lambda i: (i, 0)),
            pl.BlockSpec((WSUM, PD), lambda i: (0, 0)),
        ],
        out_specs=pl.BlockSpec((rows, WSUM), lambda i: (0, 0)),
        compiler_params=params(1, 12),
        cost_estimate=cost(1e9),
        name="wide_sum",
    )(hits, g3, weights)


def narrow_sum_kernel(hits_ref, d_ref, wide_ref, out_ref):
    @pl.when(pl.program_id(0) == 0)
    def _():
        out_ref[...] = wide_ref[...]

    sources = d_ref.shape[0]
    block = hits_ref.shape[2]
    column = lax.broadcasted_iota(jnp.int32, (block, PD), 1)
    pieces = []
    for d in range(sources):
        packed = d_ref[d].astype(jnp.float32)
        pieces += [packed, pltpu.roll(packed, PD - W12, 1)]
    both = jnp.concatenate(pieces, axis=0)
    d1 = jnp.where(column < W1, both, 0.0).astype(jnp.bfloat16)
    d2 = jnp.where((column >= W1) & (column < W12), both, 0.0).astype(jnp.bfloat16)
    out_ref[...] += jnp.dot(hits_ref[0], d1, preferred_element_type=jnp.float32) + jnp.dot(
        hits_ref[1], d2, preferred_element_type=jnp.float32
    )


def narrow_sum(hits, narrow, wide):
    _, rows, examples = hits.shape
    sources, half, _ = narrow.shape
    block = 1024
    per = block // (2 * half)
    return pl.pallas_call(
        narrow_sum_kernel,
        out_shape=jax.ShapeDtypeStruct((rows, WSUM), jnp.float32),
        grid=(examples // block,),
        in_specs=[
            pl.BlockSpec((2, rows, block), lambda i: (0, 0, i)),
            pl.BlockSpec((per, half, 2 * W12), lambda i: (i, 0, 0)),
            pl.BlockSpec((rows, PD), lambda i: (0, 0)),
        ],
        out_specs=pl.BlockSpec((rows, PD), lambda i: (0, 0)),
        input_output_aliases={2: 0},
        compiler_params=params(1, 12),
        cost_estimate=cost(1e9),
        name="narrow_sum",
    )(hits, narrow, wide)


def swap(x, axis, size, bits):
    return lax.ppermute(x, axis, [(d, d ^ bits) for d in range(size)])


def local(sizes, grad_out, pooled, proj, assign, indices, lengths):
    count, slots, _ = grad_out.shape
    scale = 1.0 / math.sqrt(count * slots)
    n_node, n_local = sizes["node"], sizes["local"]
    n_plane = n_node // 2
    node, loc = lax.axis_index("node"), lax.axis_index("local")

    place = jnp.arange(slots // 2, dtype=jnp.int32)
    plane, line = (place // n_local) ^ (node // 2), (place % n_local) ^ loc
    here = (plane * 2 + node % 2) * n_local + line
    there = (plane * 2 + 1 - node % 2) * n_local + line

    rows = proj[:, :W12]
    rows = jnp.concatenate([rows] + [swap(rows, "local", n_local, d) for d in range(1, n_local)])

    g12, g3, q = permute(assign, grad_out, pooled)
    (sent,) = partial_proj(there, 1, q, g12, g3)
    got = swap(sent, "node", n_node, 1)

    rows, sent = lax.optimization_barrier((rows, sent))
    rows = jnp.concatenate([rows] + [swap(rows, "node", n_node, 2 * d) for d in range(1, n_plane)])
    g3_sent, rows = lax.optimization_barrier((g3, rows))
    g3_got = lax.all_to_all(g3_sent, AXES, split_axis=0, concat_axis=0, tiled=True)
    rows = jnp.concatenate([rows, swap(rows, "node", n_node, 1)])
    slot = jnp.arange(slots, dtype=jnp.int32)
    slot_node = slot // n_local ^ node
    slot_place = slot_node % 2 * (slots // 2) + slot_node // 2 * n_local + (slot % n_local ^ loc)
    narrow = narrow_dpool(slot_place, g12, rows)
    narrow_sent, g3_got = lax.optimization_barrier((narrow, g3_got))
    narrow_got = lax.all_to_all(narrow_sent, AXES, split_axis=0, concat_axis=0, tiled=True)

    lookups, counts = indices[0].transpose(1, 2, 0), lengths[0].T[:, None, :]
    hits3 = count_hits(lookups, counts, 2, 1, after=[narrow])
    wide = wide_sum(hits3, g3_got.reshape(-1, PD), proj[0])

    kept = partial_proj(here, n_plane, q, g12, g3, got)
    arrived = [swap(kept[d], "node", n_node, 2 * d) for d in range(1, n_plane)]
    arrived, wide = lax.optimization_barrier((arrived, wide))
    total = kept[0]
    for term in arrived:
        total = total + term.astype(jnp.float32)
    proj_grad = total[:1]
    for d in range(1, n_local):
        proj_grad = proj_grad + swap(total[d : d + 1], "local", n_local, d)
    proj_grad = proj_grad * scale

    hits12 = count_hits(lookups, counts, 0, 2, after=[wide])
    table_grad = narrow_sum(hits12, narrow_got, wide)[None]
    return (table_grad, proj_grad)


def solution(mesh):
    placed = (
        P(AXES, None, None),
        P(AXES, None, None),
        P(AXES, None, None),
        P(),
        P(AXES, None, None, None),
        P(AXES, None, None),
    )
    return jax.shard_map(
        functools.partial(local, dict(mesh.shape)),
        mesh=mesh,
        in_specs=placed,
        out_specs=(P(AXES, None, None), P(AXES, None, None)),
        check_vma=False,
    )
```

```python
import functools
import math

import jax
import jax.numpy as jnp
from jax import lax
from jax.experimental import pallas as pl
from jax.experimental.pallas import tpu as pltpu
from jax.sharding import PartitionSpec as P

ROWS = 512
W1 = 16
W2 = 48
W3 = 192
PD = 128
W12 = W1 + W2
WSUM = W12 + W3
AXES = ("node", "local")
EB = 8
STEP = 32
MIB = 1024 * 1024


def params(grid):
    return pltpu.CompilerParams(dimension_semantics=("arbitrary",) * grid, vmem_limit_bytes=58 * MIB)


ANY = pl.BlockSpec(memory_space=pl.ANY)


def cost(flops):
    return pl.CostEstimate(flops=int(flops), bytes_accessed=1024, transcendentals=0)


def permute_kernel(slots, pieces, assign_ref, grad_ref, pool_ref, *refs):
    outs, (perm_ref, grad_held, pool_held, sems) = refs[:3], refs[3:]
    step = pl.program_id(0)
    sources = ((grad_ref, grad_held), (pool_ref, pool_held))

    def copies(i):
        at = pl.ds(i * STEP, STEP)
        return [
            pltpu.make_async_copy(ref.at[at], held.at[at], sems.at[n, i]) for n, (ref, held) in enumerate(sources)
        ]

    @pl.when(step == 0)
    def _():
        for i in range(grad_ref.shape[0] // STEP):
            for copy in copies(i):
                copy.start()
        width = EB * slots
        lane = lax.broadcasted_iota(jnp.int32, (2 * EB, width), 1)
        row = lax.broadcasted_iota(jnp.int32, (2 * EB, width), 0)
        for s in range(0, slots, 2):
            group = jnp.where(row < EB, assign_ref[s], assign_ref[s + 1])
            hit = lane == (row % EB) * slots + group
            perm_ref[s * EB : (s + 2) * EB, :] = jnp.where(hit, 1.0, 0.0).astype(jnp.bfloat16)

    for copy, (_, held), cuts in zip(copies(step), sources, pieces):
        copy.wait()
        width = held.shape[2]
        for start in range(0, STEP, 2 * EB):
            pair = []
            for at in (start, start + EB):
                block = held[pl.ds(step * STEP + at, EB)].reshape(EB * slots, width)
                moved = jnp.dot(perm_ref[...], block, preferred_element_type=jnp.float32)
                pair.append(moved.reshape(slots, EB, width))
            both = jnp.concatenate(pair, axis=1).astype(jnp.bfloat16)
            for n, low, high in cuts:
                outs[n][:, start : start + 2 * EB, :] = both[:, :, low:high]


def permute(assign, grad_out, pooled):
    count, slots, _ = grad_out.shape
    widths = (2 * PD, PD, WSUM)
    pieces = (((0, 0, 2 * PD), (1, 2 * PD, 3 * PD)), ((2, 0, WSUM),))
    return pl.pallas_call(
        functools.partial(permute_kernel, slots, pieces),
        out_shape=[jax.ShapeDtypeStruct((slots, count, width), jnp.bfloat16) for width in widths],
        grid_spec=pltpu.PrefetchScalarGridSpec(
            num_scalar_prefetch=1,
            grid=(count // STEP,),
            in_specs=[pl.BlockSpec(memory_space=pltpu.HBM)] * 2,
            out_specs=[pl.BlockSpec((slots, STEP, width), lambda i, a: (0, i, 0)) for width in widths],
            scratch_shapes=[
                pltpu.VMEM((EB * slots, EB * slots), jnp.bfloat16),
                pltpu.VMEM(grad_out.shape, jnp.bfloat16),
                pltpu.VMEM(pooled.shape, jnp.bfloat16),
                pltpu.SemaphoreType.DMA((2, count // STEP)),
            ],
        ),
        compiler_params=params(1),
        cost_estimate=cost(1e9),
        name="permute_groups",
    )(assign, grad_out, pooled)


def narrow_kernel(place_ref, g_ref, w_ref, out_ref):
    step, count, _ = g_ref.shape
    half = count // 2
    column = lax.broadcasted_iota(jnp.int32, (count, W12), 1)
    dims = (((1,), (1,)), ((), ()))
    for s in range(step):
        w = w_ref[place_ref[pl.program_id(0) * step + s]]
        first = lax.dot_general(g_ref[s, :, :PD], w, dims, preferred_element_type=jnp.float32)
        second = lax.dot_general(g_ref[s, :, PD:], w, dims, preferred_element_type=jnp.float32)
        d = jnp.where(column < W1, first, second)
        out_ref[s] = jnp.concatenate([d[:half], d[half:]], axis=1).astype(jnp.bfloat16)


def narrow_dpool(place, g12, w12):
    slots, count, _ = g12.shape
    step = 8
    return pl.pallas_call(
        narrow_kernel,
        out_shape=jax.ShapeDtypeStruct((slots, count // 2, 2 * W12), jnp.bfloat16),
        grid_spec=pltpu.PrefetchScalarGridSpec(
            num_scalar_prefetch=1,
            grid=(slots // step,),
            in_specs=[
                pl.BlockSpec((step, count, 2 * PD), lambda i, o: (i, 0, 0)),
                pl.BlockSpec((slots, W12, PD), lambda i, o: (0, 0, 0)),
            ],
            out_specs=pl.BlockSpec((step, count // 2, 2 * W12), lambda i, o: (i, 0, 0)),
        ),
        compiler_params=params(1),
        cost_estimate=cost(1e9),
        name="narrow_dpool",
    )(place, g12, w12)


def partial_kernel(chunks, add, node_ref, line_ref, q_ref, g12_ref, g3_ref, *refs):
    outs = refs[len(refs) - chunks :]
    size = outs[0].shape[0]

    def fill(out):
        for i in range(size):
            slot = line_ref[i]
            q = q_ref[slot].T
            narrow = jnp.dot(q[:W12], g12_ref[slot], preferred_element_type=jnp.float32)
            wide = jnp.dot(q[W12:], g3_ref[slot], preferred_element_type=jnp.float32)
            pieces = ((0, W1, narrow[:W1, :PD]), (W1, W12, narrow[W1:, PD:]), (W12, WSUM, wide))
            for start, end, piece in pieces:
                if add:
                    piece = piece + refs[0][i, start:end]
                out[i, start:end] = piece.astype(out.dtype)

    if chunks == 1:
        fill(outs[0])
    else:
        for c in range(chunks):
            pl.when(pl.program_id(0) == c)(functools.partial(fill, outs[c]))


def partial_proj(nodes, lines, q, g12, g3, other=None, after=()):
    slots, count, _ = q.shape
    chunks, size = nodes.shape[0], lines.shape[0]
    block = pl.BlockSpec((size, WSUM, PD), lambda i, n, o: (i, 0, 0))
    if other is None:
        added, outs, out_specs = (), 1, [block]
        out_shape = [jax.ShapeDtypeStruct((chunks * size, WSUM, PD), jnp.float32)]
    else:
        added, outs = (other,), chunks
        out_specs = [pl.BlockSpec((size, WSUM, PD), lambda i, n, o: (0, 0, 0))] * chunks
        out_shape = [
            jax.ShapeDtypeStruct((size, WSUM, PD), jnp.bfloat16 if c else jnp.float32) for c in range(chunks)
        ]
    return pl.pallas_call(
        functools.partial(partial_kernel, outs, other is not None),
        out_shape=out_shape,
        grid_spec=pltpu.PrefetchScalarGridSpec(
            num_scalar_prefetch=2,
            grid=(chunks,),
            in_specs=[
                pl.BlockSpec((size, count, width), lambda i, n, o: (n[i], 0, 0)) for width in (WSUM, 2 * PD, PD)
            ]
            + [block] * len(added)
            + [ANY] * len(after),
            out_specs=out_specs,
        ),
        compiler_params=params(1),
        cost_estimate=cost(1e9),
        name="partial_proj",
    )(nodes, lines, q, g12, g3, *added, *after)


def count_kernel(index_ref, length_ref, *refs):
    out_ref = refs[-1]
    bag, block = index_ref.shape[1], index_ref.shape[2]
    lanes, chunk, low = 256, 16, ROWS // 8

    def one(i, carry):
        at = pl.ds(pl.multiple_of(i * lanes, lanes), lanes)
        index = index_ref[0, :, at]
        which = lax.broadcasted_iota(jnp.int32, (bag, lanes), 0)
        key = jnp.where(which < length_ref[0, :, at], index & (low - 1), -1)
        unit = jnp.left_shift(jnp.int32(1), jnp.right_shift(index, 6) * 4)
        ids = lax.broadcasted_iota(jnp.int32, (chunk, lanes), 0)
        for c in range(low // chunk):
            total = jnp.zeros((chunk, lanes), jnp.int32)
            for j in range(bag):
                total = total + jnp.where(key[j : j + 1] == ids + c * chunk, unit[j : j + 1], 0)
            out_ref[0, c * chunk : (c + 1) * chunk, at] = total
        return carry

    lax.fori_loop(0, block // lanes, one, 0)


def count_hits(lookups, counts, after=()):
    tables, bag, examples = lookups.shape
    block = 2048
    return pl.pallas_call(
        count_kernel,
        out_shape=jax.ShapeDtypeStruct((tables, ROWS // 8, examples), jnp.int32),
        grid=(tables, examples // block),
        in_specs=[
            pl.BlockSpec((1, bag, block), lambda k, i: (k, 0, i)),
            pl.BlockSpec((1, 1, block), lambda k, i: (k, 0, i)),
        ]
        + [ANY] * len(after),
        out_specs=pl.BlockSpec((1, ROWS // 8, block), lambda k, i: (k, 0, i)),
        compiler_params=params(2),
        cost_estimate=cost(1e9),
        name="count_hits",
    )(lookups, counts, *after)


def unpacked(words):
    rows = [lax.shift_right_logical(words, jnp.int32(4 * n)) & 15 for n in range(8)]
    return jnp.concatenate([r.astype(jnp.float32).astype(jnp.bfloat16) for r in rows], axis=0)


def wide_kernel(hits_ref, g_ref, w_ref, out_ref):
    @pl.when(pl.program_id(0) == 0)
    def _():
        out_ref[...] = jnp.zeros_like(out_ref)

    block = g_ref.shape[0]
    column = lax.broadcasted_iota(jnp.int32, (block, WSUM), 1)
    d = lax.dot_general(g_ref[...], w_ref[...], (((1,), (1,)), ((), ())), preferred_element_type=jnp.float32)
    d = jnp.where(column < W12, 0.0, d).astype(jnp.bfloat16)
    out_ref[...] += jnp.dot(unpacked(hits_ref[0]), d, preferred_element_type=jnp.float32)


def wide_sum(hits, g3, weights):
    _, words, examples = hits.shape
    block = 1024
    return pl.pallas_call(
        wide_kernel,
        out_shape=jax.ShapeDtypeStruct((ROWS, WSUM), jnp.float32),
        grid=(examples // block,),
        in_specs=[
            pl.BlockSpec((1, words, block), lambda i: (2, 0, i)),
            pl.BlockSpec((block, PD), lambda i: (i, 0)),
            pl.BlockSpec((WSUM, PD), lambda i: (0, 0)),
        ],
        out_specs=pl.BlockSpec((ROWS, WSUM), lambda i: (0, 0)),
        compiler_params=params(1),
        cost_estimate=cost(1e9),
        name="wide_sum",
    )(hits, g3, weights)


def narrow_sum_kernel(hits_ref, d_ref, wide_ref, out_ref):
    @pl.when(pl.program_id(0) == 0)
    def _():
        out_ref[...] = wide_ref[...]

    sources = d_ref.shape[0]
    block = hits_ref.shape[2]
    column = lax.broadcasted_iota(jnp.int32, (block, PD), 1)
    pieces = []
    for d in range(sources):
        packed = d_ref[d].astype(jnp.float32)
        pieces += [packed, pltpu.roll(packed, PD - W12, 1)]
    both = jnp.concatenate(pieces, axis=0)
    d1 = jnp.where(column < W1, both, 0.0).astype(jnp.bfloat16)
    d2 = jnp.where((column >= W1) & (column < W12), both, 0.0).astype(jnp.bfloat16)
    out_ref[...] += jnp.dot(unpacked(hits_ref[0]), d1, preferred_element_type=jnp.float32) + jnp.dot(
        unpacked(hits_ref[1]), d2, preferred_element_type=jnp.float32
    )


def narrow_sum(hits, narrow, wide):
    _, words, examples = hits.shape
    sources, half, _ = narrow.shape
    block = 1024
    per = block // (2 * half)
    return pl.pallas_call(
        narrow_sum_kernel,
        out_shape=jax.ShapeDtypeStruct((ROWS, WSUM), jnp.float32),
        grid=(examples // block,),
        in_specs=[
            pl.BlockSpec((2, words, block), lambda i: (0, 0, i)),
            pl.BlockSpec((per, half, 2 * W12), lambda i: (i, 0, 0)),
            pl.BlockSpec((ROWS, PD), lambda i: (0, 0)),
        ],
        out_specs=pl.BlockSpec((ROWS, PD), lambda i: (0, 0)),
        input_output_aliases={2: 0},
        compiler_params=params(1),
        cost_estimate=cost(1e9),
        name="narrow_sum",
    )(hits, narrow, wide)


def swap(x, axis, size, bits):
    return lax.ppermute(x, axis, [(d, d ^ bits) for d in range(size)])


def local(sizes, grad_out, pooled, proj, assign, indices, lengths):
    count, slots, _ = grad_out.shape
    scale = 1.0 / math.sqrt(count * slots)
    n_node, n_local = sizes["node"], sizes["local"]
    n_plane = n_node // 2
    node, loc = lax.axis_index("node"), lax.axis_index("local")

    rows = proj[:, :W12]
    rows = jnp.concatenate([rows] + [swap(rows, "local", n_local, d) for d in range(1, n_local)])

    g12, g3, q = permute(assign, grad_out, pooled)

    rows, g3 = lax.optimization_barrier((rows, g3))
    rows = jnp.concatenate([rows] + [swap(rows, "node", n_node, 2 * d) for d in range(1, n_plane)])
    g3_got = lax.all_to_all(g3, AXES, split_axis=0, concat_axis=0, tiled=True)

    plane = jnp.arange(n_plane, dtype=jnp.int32) ^ (node // 2)
    lines = jnp.arange(n_local, dtype=jnp.int32) ^ loc
    (sent,) = partial_proj(plane * 2 + 1 - node % 2, lines, q, g12, g3, after=[rows])
    got = swap(sent, "node", n_node, 1)

    rows = jnp.concatenate([rows, swap(rows, "node", n_node, 1)])
    slot = jnp.arange(slots, dtype=jnp.int32)
    slot_node = slot // n_local ^ node
    slot_place = slot_node % 2 * (slots // 2) + slot_node // 2 * n_local + (slot % n_local ^ loc)
    narrow = narrow_dpool(slot_place, g12, rows)

    kept = partial_proj(plane * 2 + node % 2, lines, q, g12, g3, got, after=[narrow])
    arrived = [swap(kept[d], "node", n_node, 2 * d) for d in range(1, n_plane)]
    hits = count_hits(indices[0].transpose(1, 2, 0), lengths[0].T[:, None, :], after=kept[:1])

    narrow_sent, g3_got = lax.optimization_barrier((narrow, g3_got))
    narrow_got = lax.all_to_all(narrow_sent, AXES, split_axis=0, concat_axis=0, tiled=True)
    wide = wide_sum(hits, g3_got.reshape(-1, PD), proj[0])

    arrived, wide = lax.optimization_barrier((arrived, wide))
    total = kept[0]
    for term in arrived:
        total = total + term.astype(jnp.float32)
    proj_grad = total[:1]
    for d in range(1, n_local):
        proj_grad = proj_grad + swap(total[d : d + 1], "local", n_local, d)
    proj_grad = proj_grad * scale

    table_grad = narrow_sum(hits, narrow_got, wide)[None]
    return (table_grad, proj_grad)


def solution(mesh):
    placed = (
        P(AXES, None, None),
        P(AXES, None, None),
        P(AXES, None, None),
        P(),
        P(AXES, None, None, None),
        P(AXES, None, None),
    )
    return jax.shard_map(
        functools.partial(local, dict(mesh.shape)),
        mesh=mesh,
        in_specs=placed,
        out_specs=(P(AXES, None, None), P(AXES, None, None)),
        check_vma=False,
    )
```

```python
import functools
import math

import jax
import jax.numpy as jnp
from jax import lax
from jax.experimental import pallas as pl
from jax.experimental.pallas import tpu as pltpu
from jax.sharding import PartitionSpec as P

ROWS = 512
W1 = 16
W2 = 48
W3 = 192
PD = 128
W12 = W1 + W2
WSUM = W12 + W3
AXES = ("node", "local")
EB = 8
STEP = 16
MIB = 1024 * 1024


def params(grid):
    return pltpu.CompilerParams(dimension_semantics=("arbitrary",) * grid, vmem_limit_bytes=58 * MIB)


HBM = pl.BlockSpec(memory_space=pltpu.HBM)
ANY = pl.BlockSpec(memory_space=pl.ANY)


def cost(flops):
    return pl.CostEstimate(flops=int(flops), bytes_accessed=1024, transcendentals=0)


def permute_kernel(slots, pieces, assign_ref, grad_ref, pool_ref, *refs):
    outs, (perm_ref, grad_held, pool_held, sems) = refs[:3], refs[3:]
    step = pl.program_id(0)
    sources = ((grad_ref, grad_held), (pool_ref, pool_held))

    def copies(i):
        at = pl.ds(i * STEP, STEP)
        return [
            pltpu.make_async_copy(ref.at[at], held.at[at], sems.at[n, i]) for n, (ref, held) in enumerate(sources)
        ]

    @pl.when(step == 0)
    def _():
        for i in range(grad_ref.shape[0] // STEP):
            for copy in copies(i):
                copy.start()
        width = EB * slots
        lane = lax.broadcasted_iota(jnp.int32, (2 * EB, width), 1)
        row = lax.broadcasted_iota(jnp.int32, (2 * EB, width), 0)
        for s in range(0, slots, 2):
            group = jnp.where(row < EB, assign_ref[s], assign_ref[s + 1])
            hit = lane == (row % EB) * slots + group
            perm_ref[s * EB : (s + 2) * EB, :] = jnp.where(hit, 1.0, 0.0).astype(jnp.bfloat16)

    for copy, (_, held), cuts in zip(copies(step), sources, pieces):
        copy.wait()
        width = held.shape[2]
        for start in range(0, STEP, 2 * EB):
            pair = []
            for at in (start, start + EB):
                block = held[pl.ds(step * STEP + at, EB)].reshape(EB * slots, width)
                moved = jnp.dot(perm_ref[...], block, preferred_element_type=jnp.float32)
                pair.append(moved.reshape(slots, EB, width))
            both = jnp.concatenate(pair, axis=1).astype(jnp.bfloat16)
            for n, low, high in cuts:
                outs[n][:, start : start + 2 * EB, :] = both[:, :, low:high]


def permute(assign, grad_out, pooled):
    count, slots, _ = grad_out.shape
    widths = (2 * PD, PD, WSUM)
    pieces = (((0, 0, 2 * PD), (1, 2 * PD, 3 * PD)), ((2, 0, WSUM),))
    return pl.pallas_call(
        functools.partial(permute_kernel, slots, pieces),
        out_shape=[jax.ShapeDtypeStruct((slots, count, width), jnp.bfloat16) for width in widths],
        grid_spec=pltpu.PrefetchScalarGridSpec(
            num_scalar_prefetch=1,
            grid=(count // STEP,),
            in_specs=[HBM] * 2,
            out_specs=[pl.BlockSpec((slots, STEP, width), lambda i, a: (0, i, 0)) for width in widths],
            scratch_shapes=[
                pltpu.VMEM((EB * slots, EB * slots), jnp.bfloat16),
                pltpu.VMEM(grad_out.shape, jnp.bfloat16),
                pltpu.VMEM(pooled.shape, jnp.bfloat16),
                pltpu.SemaphoreType.DMA((2, count // STEP)),
            ],
        ),
        compiler_params=params(1),
        cost_estimate=cost(1e7),
        name="permute_groups",
    )(assign, grad_out, pooled)


def fetch(ref, held, sems, blocks, pick=lambda i: i):
    size = held.shape[0] // blocks
    copies = [
        pltpu.make_async_copy(ref.at[pl.ds(pick(i) * size, size)], held.at[pl.ds(i * size, size)], sems.at[i])
        for i in range(blocks)
    ]
    for copy in copies:
        copy.start()
    return copies


def narrow_kernel(blocks, place_ref, g_ref, w_ref, out_ref, g_held, w_held, out_held, g_sems, w_sems, out_sems):
    weights = fetch(w_ref, w_held, w_sems, 1)
    loads = fetch(g_ref, g_held, g_sems, blocks)
    slots, count, _ = g_held.shape
    step, half = slots // blocks, count // 2
    column = lax.broadcasted_iota(jnp.int32, (count, W12), 1)
    dims = (((1,), (1,)), ((), ()))
    weights[0].wait()
    stores = []
    for i, load in enumerate(loads):
        load.wait()
        for s in range(i * step, (i + 1) * step):
            w = w_held[place_ref[s]]
            first = lax.dot_general(g_held[s, :, :PD], w, dims, preferred_element_type=jnp.float32)
            second = lax.dot_general(g_held[s, :, PD:], w, dims, preferred_element_type=jnp.float32)
            d = jnp.where(column < W1, first, second)
            out_held[s] = jnp.concatenate([d[:half], d[half:]], axis=1).astype(jnp.bfloat16)
        at = pl.ds(i * step, step)
        stores.append(pltpu.make_async_copy(out_held.at[at], out_ref.at[at], out_sems.at[i]))
        stores[-1].start()
    for store in stores:
        store.wait()


def narrow_dpool(place, g12, w12):
    slots, count, _ = g12.shape
    blocks = 4
    shape = (slots, count // 2, 2 * W12)
    return pl.pallas_call(
        functools.partial(narrow_kernel, blocks),
        out_shape=jax.ShapeDtypeStruct(shape, jnp.bfloat16),
        grid_spec=pltpu.PrefetchScalarGridSpec(
            num_scalar_prefetch=1,
            grid=(1,),
            in_specs=[HBM] * 2,
            out_specs=HBM,
            scratch_shapes=[
                pltpu.VMEM(g12.shape, jnp.bfloat16),
                pltpu.VMEM(w12.shape, jnp.bfloat16),
                pltpu.VMEM(shape, jnp.bfloat16),
                pltpu.SemaphoreType.DMA((blocks,)),
                pltpu.SemaphoreType.DMA((1,)),
                pltpu.SemaphoreType.DMA((blocks,)),
            ],
        ),
        compiler_params=params(1),
        cost_estimate=cost(1e7),
        name="narrow_dpool",
    )(place, g12, w12)


def partial_kernel(ins, waits, outs, node_ref, line_ref, *refs):
    operands, results = refs[:ins], refs[ins + waits : ins + waits + outs]
    held, out_held = refs[-2 - ins - outs : -2 - outs], refs[-2 - outs : -2]
    in_sems, out_sems = refs[-2:]
    blocks, size = node_ref.shape[0], line_ref.shape[0]
    loads = [
        fetch(ref, at, in_sems.at[n], blocks, (lambda i: node_ref[i]) if n < 3 else (lambda i: i))
        for n, (ref, at) in enumerate(zip(operands, held))
    ]
    stores = []
    for i in range(blocks):
        for copies in loads:
            copies[i].wait()
        if outs == 1:
            at = pl.ds(i * size, size)
            result, out = results[0].at[at], out_held[0].at[at]
        else:
            result, out = results[i], out_held[i]
        for l in range(size):
            slot = i * size + line_ref[l]
            q = held[0][slot].T
            narrow = jnp.dot(q[:W12], held[1][slot], preferred_element_type=jnp.float32)
            wide = jnp.dot(q[W12:], held[2][slot], preferred_element_type=jnp.float32)
            pieces = ((0, W1, narrow[:W1, :PD]), (W1, W12, narrow[W1:, PD:]), (W12, WSUM, wide))
            for start, end, piece in pieces:
                if ins == 4:
                    piece = piece + held[3][i * size + l, start:end]
                out[l, start:end] = piece.astype(out.dtype)
        stores.append(pltpu.make_async_copy(out, result, out_sems.at[i]))
        stores[-1].start()
    for store in stores:
        store.wait()


def partial_proj(nodes, lines, q, g12, g3, other=None, after=()):
    _, count, _ = q.shape
    blocks, size = nodes.shape[0], lines.shape[0]
    every = (blocks * size, WSUM, PD)
    if other is None:
        added, shapes = (), [jax.ShapeDtypeStruct(every, jnp.float32)]
    else:
        kinds = [jnp.float32] + [jnp.bfloat16] * (blocks - 1)
        added, shapes = (other,), [jax.ShapeDtypeStruct((size, WSUM, PD), kind) for kind in kinds]
    ins = 3 + len(added)
    return pl.pallas_call(
        functools.partial(partial_kernel, ins, len(after), len(shapes)),
        out_shape=shapes,
        grid_spec=pltpu.PrefetchScalarGridSpec(
            num_scalar_prefetch=2,
            grid=(1,),
            in_specs=[HBM] * ins + [ANY] * len(after),
            out_specs=[HBM] * len(shapes),
            scratch_shapes=[pltpu.VMEM((blocks * size, count, x.shape[2]), jnp.bfloat16) for x in (q, g12, g3)]
            + [pltpu.VMEM(every, jnp.float32)] * len(added)
            + [pltpu.VMEM(x.shape, x.dtype) for x in shapes]
            + [pltpu.SemaphoreType.DMA((ins, blocks)), pltpu.SemaphoreType.DMA((blocks,))],
        ),
        compiler_params=params(1),
        cost_estimate=cost(1e7),
        name="partial_proj",
    )(nodes, lines, q, g12, g3, *added, *after)


def count_kernel(index_ref, length_ref, *refs):
    out_ref = refs[-1]
    bag, block = index_ref.shape[1], index_ref.shape[2]
    lanes, chunk, low = 256, 16, ROWS // 8

    def one(i, carry):
        at = pl.ds(pl.multiple_of(i * lanes, lanes), lanes)
        index = index_ref[0, :, at]
        which = lax.broadcasted_iota(jnp.int32, (bag, lanes), 0)
        key = jnp.where(which < length_ref[0, :, at], index & (low - 1), -1)
        unit = jnp.left_shift(jnp.int32(1), jnp.right_shift(index, 6) * 4)
        ids = lax.broadcasted_iota(jnp.int32, (chunk, lanes), 0)
        for c in range(low // chunk):
            total = jnp.zeros((chunk, lanes), jnp.int32)
            for j in range(bag):
                total = total + jnp.where(key[j : j + 1] == ids + c * chunk, unit[j : j + 1], 0)
            out_ref[0, c * chunk : (c + 1) * chunk, at] = total
        return carry

    lax.fori_loop(0, block // lanes, one, 0)


def count_hits(lookups, counts, after=()):
    tables, bag, examples = lookups.shape
    block = 4096
    return pl.pallas_call(
        count_kernel,
        out_shape=jax.ShapeDtypeStruct((tables, ROWS // 8, examples), jnp.int32),
        grid=(tables, examples // block),
        in_specs=[
            pl.BlockSpec((1, bag, block), lambda k, i: (k, 0, i)),
            pl.BlockSpec((1, 1, block), lambda k, i: (k, 0, i)),
        ]
        + [ANY] * len(after),
        out_specs=pl.BlockSpec((1, ROWS // 8, block), lambda k, i: (k, 0, i)),
        compiler_params=params(2),
        cost_estimate=cost(1e7),
        name="count_hits",
    )(lookups, counts, *after)


def unpacked(words):
    rows = [lax.shift_right_logical(words, jnp.int32(4 * n)) & 15 for n in range(8)]
    return jnp.concatenate([r.astype(jnp.float32).astype(jnp.bfloat16) for r in rows], axis=0)


def fetch_words(ref, held, sems, tables, blocks):
    size = ref.shape[2] // blocks
    copies = []
    for i in range(blocks):
        at = pl.ds(i * size, size)
        copies.append(
            [pltpu.make_async_copy(ref.at[k, :, at], held.at[n, :, at], sems.at[n, i]) for n, k in enumerate(tables)]
        )
        for copy in copies[-1]:
            copy.start()
    return copies


def wide_kernel(blocks, hits_ref, g_ref, w_ref, *refs):
    out_ref, hits_held, g_held, hits_sems, g_sems = refs[-5:]
    hits = fetch_words(hits_ref, hits_held, hits_sems, (2,), blocks)
    loads = fetch(g_ref, g_held, g_sems, blocks)
    block = g_held.shape[0] // blocks
    column = lax.broadcasted_iota(jnp.int32, (block, WSUM), 1)
    for i in range(blocks):
        at = slice(i * block, (i + 1) * block)
        loads[i].wait()
        d = lax.dot_general(g_held[at], w_ref[...], (((1,), (1,)), ((), ())), preferred_element_type=jnp.float32)
        d = jnp.where(column < W12, 0.0, d).astype(jnp.bfloat16)
        hits[i][0].wait()
        term = jnp.dot(unpacked(hits_held[0, :, at]), d, preferred_element_type=jnp.float32)
        out_ref[...] = term if i == 0 else out_ref[...] + term


def wide_sum(hits, g3, weights, after=()):
    _, words, examples = hits.shape
    blocks = 4
    return pl.pallas_call(
        functools.partial(wide_kernel, blocks),
        out_shape=jax.ShapeDtypeStruct((ROWS, WSUM), jnp.float32),
        in_specs=[HBM, HBM, pl.BlockSpec(memory_space=pltpu.VMEM)] + [ANY] * len(after),
        out_specs=pl.BlockSpec(memory_space=pltpu.VMEM),
        scratch_shapes=[
            pltpu.VMEM((1, words, examples), jnp.int32),
            pltpu.VMEM(g3.shape, jnp.bfloat16),
            pltpu.SemaphoreType.DMA((1, blocks)),
            pltpu.SemaphoreType.DMA((blocks,)),
        ],
        compiler_params=params(0),
        cost_estimate=cost(1e7),
        name="wide_sum",
    )(hits, g3, weights, *after)


def narrow_sum_kernel(blocks, hits_ref, d_ref, wide_ref, out_ref, hits_held, d_held, hits_sems, d_sems):
    hits = fetch_words(hits_ref, hits_held, hits_sems, (0, 1), blocks)
    loads = fetch(d_ref, d_held, d_sems, blocks)
    sources, block = d_held.shape[0] // blocks, hits_held.shape[2] // blocks
    column = lax.broadcasted_iota(jnp.int32, (block, PD), 1)
    out_ref[...] = wide_ref[...]
    for i in range(blocks):
        at = slice(i * block, (i + 1) * block)
        loads[i].wait()
        pieces = []
        for d in range(i * sources, (i + 1) * sources):
            packed = d_held[d].astype(jnp.float32)
            pieces += [packed, pltpu.roll(packed, PD - W12, 1)]
        both = jnp.concatenate(pieces, axis=0)
        d1 = jnp.where(column < W1, both, 0.0).astype(jnp.bfloat16)
        d2 = jnp.where((column >= W1) & (column < W12), both, 0.0).astype(jnp.bfloat16)
        for n, d in enumerate((d1, d2)):
            hits[i][n].wait()
            out_ref[...] += jnp.dot(unpacked(hits_held[n, :, at]), d, preferred_element_type=jnp.float32)


def narrow_sum(hits, narrow, wide):
    _, words, examples = hits.shape
    blocks = 4
    return pl.pallas_call(
        functools.partial(narrow_sum_kernel, blocks),
        out_shape=jax.ShapeDtypeStruct((ROWS, WSUM), jnp.float32),
        grid=(1,),
        in_specs=[HBM, HBM, pl.BlockSpec((ROWS, PD), lambda i: (0, 0))],
        out_specs=pl.BlockSpec((ROWS, PD), lambda i: (0, 0)),
        scratch_shapes=[
            pltpu.VMEM((2, words, examples), jnp.int32),
            pltpu.VMEM(narrow.shape, jnp.bfloat16),
            pltpu.SemaphoreType.DMA((2, blocks)),
            pltpu.SemaphoreType.DMA((blocks,)),
        ],
        input_output_aliases={2: 0},
        compiler_params=params(1),
        cost_estimate=cost(1e7),
        name="narrow_sum",
    )(hits, narrow, wide)


def swap(x, axis, size, bits):
    return lax.ppermute(x, axis, [(d, d ^ bits) for d in range(size)])


def local(sizes, grad_out, pooled, proj, assign, indices, lengths):
    count, slots, _ = grad_out.shape
    scale = 1.0 / math.sqrt(count * slots)
    n_node, n_local = sizes["node"], sizes["local"]
    n_plane = n_node // 2
    node, loc = lax.axis_index("node"), lax.axis_index("local")

    rows = proj[:, :W12]
    rows = jnp.concatenate([rows] + [swap(rows, "local", n_local, d) for d in range(1, n_local)])

    g12, g3, q = permute(assign, grad_out, pooled)

    rows, g3 = lax.optimization_barrier((rows, g3))
    rows = jnp.concatenate([rows] + [swap(rows, "node", n_node, 2 * d) for d in range(1, n_plane)])
    g3_got = lax.all_to_all(g3, AXES, split_axis=0, concat_axis=0, tiled=True)

    plane = jnp.arange(n_plane, dtype=jnp.int32) ^ (node // 2)
    lines = jnp.arange(n_local, dtype=jnp.int32) ^ loc
    (sent,) = partial_proj(plane * 2 + 1 - node % 2, lines, q, g12, g3, after=[rows])
    got = swap(sent, "node", n_node, 1)

    rows = jnp.concatenate([rows, swap(rows, "node", n_node, 1)])
    slot = jnp.arange(slots, dtype=jnp.int32)
    slot_node = slot // n_local ^ node
    slot_place = slot_node % 2 * (slots // 2) + slot_node // 2 * n_local + (slot % n_local ^ loc)
    narrow = narrow_dpool(slot_place, g12, rows)

    kept = partial_proj(plane * 2 + node % 2, lines, q, g12, g3, got, after=[narrow])
    arrived = [swap(kept[d], "node", n_node, 2 * d) for d in range(1, n_plane)]
    hits = count_hits(indices[0].transpose(1, 2, 0), lengths[0].T[:, None, :], after=kept[:1])

    narrow_sent, g3_got, hits = lax.optimization_barrier((narrow, g3_got, hits))
    narrow_got = lax.all_to_all(narrow_sent, AXES, split_axis=0, concat_axis=0, tiled=True)

    arrived, g3_got = lax.optimization_barrier((arrived, g3_got))
    total = kept[0]
    for term in arrived:
        total = total + term.astype(jnp.float32)
    own, terms = total[:1], [swap(total[d : d + 1], "local", n_local, d) for d in range(1, n_local)]

    wide = wide_sum(hits, g3_got.reshape(-1, PD), proj[0], after=[own])
    table_grad = narrow_sum(hits, narrow_got, wide)[None]
    terms, table_grad = lax.optimization_barrier((terms, table_grad))
    proj_grad = sum(terms, own) * scale
    return (table_grad, proj_grad)


def solution(mesh):
    placed = (
        P(AXES, None, None),
        P(AXES, None, None),
        P(AXES, None, None),
        P(),
        P(AXES, None, None, None),
        P(AXES, None, None),
    )
    return jax.shard_map(
        functools.partial(local, dict(mesh.shape)),
        mesh=mesh,
        in_specs=placed,
        out_specs=(P(AXES, None, None), P(AXES, None, None)),
        check_vma=False,
    )
```

```python
import functools
import math

import jax
import jax.numpy as jnp
from jax import lax
from jax.experimental import pallas as pl
from jax.experimental.pallas import tpu as pltpu
from jax.sharding import PartitionSpec as P

ROWS = 512
W1 = 16
W2 = 48
W3 = 192
PD = 128
W12 = W1 + W2
WSUM = W12 + W3
AXES = ("node", "local")
EB = 8
STEP = 32
MIB = 1024 * 1024


def params(grid):
    return pltpu.CompilerParams(dimension_semantics=("arbitrary",) * grid, vmem_limit_bytes=58 * MIB)


HBM = pl.BlockSpec(memory_space=pltpu.HBM)
ANY = pl.BlockSpec(memory_space=pl.ANY)


def cost(flops):
    return pl.CostEstimate(flops=int(flops), bytes_accessed=1024, transcendentals=0)


def permute_kernel(slots, pieces, assign_ref, grad_ref, pool_ref, *refs):
    outs, (perm_ref, grad_held, pool_held, sems) = refs[:3], refs[3:]
    step = pl.program_id(0)
    sources = ((grad_ref, grad_held), (pool_ref, pool_held))

    def copies(i):
        at = pl.ds(i * STEP, STEP)
        return [
            pltpu.make_async_copy(ref.at[at], held.at[at], sems.at[n, i]) for n, (ref, held) in enumerate(sources)
        ]

    @pl.when(step == 0)
    def _():
        for i in range(grad_ref.shape[0] // STEP):
            for copy in copies(i):
                copy.start()
        width = EB * slots
        lane = lax.broadcasted_iota(jnp.int32, (2 * EB, width), 1)
        row = lax.broadcasted_iota(jnp.int32, (2 * EB, width), 0)
        for s in range(0, slots, 2):
            group = jnp.where(row < EB, assign_ref[s], assign_ref[s + 1])
            hit = lane == (row % EB) * slots + group
            perm_ref[s * EB : (s + 2) * EB, :] = jnp.where(hit, 1.0, 0.0).astype(jnp.bfloat16)

    for copy, (_, held), cuts in zip(copies(step), sources, pieces):
        copy.wait()
        width = held.shape[2]
        for start in range(0, STEP, 2 * EB):
            pair = []
            for at in (start, start + EB):
                block = held[pl.ds(step * STEP + at, EB)].reshape(EB * slots, width)
                moved = jnp.dot(perm_ref[...], block, preferred_element_type=jnp.float32)
                pair.append(moved.reshape(slots, EB, width))
            both = jnp.concatenate(pair, axis=1).astype(jnp.bfloat16)
            for n, low, high in cuts:
                outs[n][:, start : start + 2 * EB, :] = both[:, :, low:high]


def permute(assign, grad_out, pooled):
    count, slots, _ = grad_out.shape
    widths = (2 * PD, PD, WSUM)
    pieces = (((0, 0, 2 * PD), (1, 2 * PD, 3 * PD)), ((2, 0, WSUM),))
    return pl.pallas_call(
        functools.partial(permute_kernel, slots, pieces),
        out_shape=[jax.ShapeDtypeStruct((slots, count, width), jnp.bfloat16) for width in widths],
        grid_spec=pltpu.PrefetchScalarGridSpec(
            num_scalar_prefetch=1,
            grid=(count // STEP,),
            in_specs=[HBM] * 2,
            out_specs=[pl.BlockSpec((slots, STEP, width), lambda i, a: (0, i, 0)) for width in widths],
            scratch_shapes=[
                pltpu.VMEM((EB * slots, EB * slots), jnp.bfloat16),
                pltpu.VMEM(grad_out.shape, jnp.bfloat16),
                pltpu.VMEM(pooled.shape, jnp.bfloat16),
                pltpu.SemaphoreType.DMA((2, count // STEP)),
            ],
        ),
        compiler_params=params(1),
        cost_estimate=cost(1e7),
        name="permute_groups",
    )(assign, grad_out, pooled)


def fetch(ref, held, sems, blocks, pick=lambda i: i):
    size = held.shape[0] // blocks
    copies = [
        pltpu.make_async_copy(ref.at[pl.ds(pick(i) * size, size)], held.at[pl.ds(i * size, size)], sems.at[i])
        for i in range(blocks)
    ]
    for copy in copies:
        copy.start()
    return copies


def narrow_kernel(blocks, place_ref, g_ref, w_ref, *refs):
    out_ref, g_held, w_held, out_held, g_sems, w_sems, out_sems = refs[-7:]
    weights = fetch(w_ref, w_held, w_sems, 1)
    loads = fetch(g_ref, g_held, g_sems, blocks)
    slots, count, _ = g_held.shape
    step, half = slots // blocks, count // 2
    column = lax.broadcasted_iota(jnp.int32, (count, W12), 1)
    dims = (((1,), (1,)), ((), ()))
    weights[0].wait()
    stores = []
    for i, load in enumerate(loads):
        load.wait()
        for s in range(i * step, (i + 1) * step):
            w = w_held[place_ref[s]]
            first = lax.dot_general(g_held[s, :, :PD], w, dims, preferred_element_type=jnp.float32)
            second = lax.dot_general(g_held[s, :, PD:], w, dims, preferred_element_type=jnp.float32)
            d = jnp.where(column < W1, first, second)
            out_held[s] = jnp.concatenate([d[:half], d[half:]], axis=1).astype(jnp.bfloat16)
        at = pl.ds(i * step, step)
        stores.append(pltpu.make_async_copy(out_held.at[at], out_ref.at[at], out_sems.at[i]))
        stores[-1].start()
    for store in stores:
        store.wait()


def narrow_dpool(place, g12, w12, after=()):
    slots, count, _ = g12.shape
    blocks = 4
    shape = (slots, count // 2, 2 * W12)
    return pl.pallas_call(
        functools.partial(narrow_kernel, blocks),
        out_shape=jax.ShapeDtypeStruct(shape, jnp.bfloat16),
        grid_spec=pltpu.PrefetchScalarGridSpec(
            num_scalar_prefetch=1,
            grid=(1,),
            in_specs=[HBM] * 2 + [ANY] * len(after),
            out_specs=HBM,
            scratch_shapes=[
                pltpu.VMEM(g12.shape, jnp.bfloat16),
                pltpu.VMEM(w12.shape, jnp.bfloat16),
                pltpu.VMEM(shape, jnp.bfloat16),
                pltpu.SemaphoreType.DMA((blocks,)),
                pltpu.SemaphoreType.DMA((1,)),
                pltpu.SemaphoreType.DMA((blocks,)),
            ],
        ),
        compiler_params=params(1),
        cost_estimate=cost(1e7),
        name="narrow_dpool",
    )(place, g12, w12, *after)


def partial_kernel(ins, waits, outs, node_ref, line_ref, *refs):
    operands, results = refs[:ins], refs[ins + waits : ins + waits + outs]
    held, out_held = refs[-2 - ins - outs : -2 - outs], refs[-2 - outs : -2]
    in_sems, out_sems = refs[-2:]
    blocks, size = node_ref.shape[0], line_ref.shape[0]
    loads = [
        fetch(ref, at, in_sems.at[n], blocks, (lambda i: node_ref[i]) if n < 3 else (lambda i: i))
        for n, (ref, at) in enumerate(zip(operands, held))
    ]
    stores = []
    for i in range(blocks):
        for copies in loads:
            copies[i].wait()
        if outs == 1:
            at = pl.ds(i * size, size)
            result, out = results[0].at[at], out_held[0].at[at]
        else:
            result, out = results[i], out_held[i]
        for l in range(size):
            slot = i * size + line_ref[l]
            q = held[0][slot].T
            narrow = jnp.dot(q[:W12], held[1][slot], preferred_element_type=jnp.float32)
            wide = jnp.dot(q[W12:], held[2][slot], preferred_element_type=jnp.float32)
            pieces = ((0, W1, narrow[:W1, :PD]), (W1, W12, narrow[W1:, PD:]), (W12, WSUM, wide))
            for start, end, piece in pieces:
                if ins == 4:
                    piece = piece + held[3][i * size + l, start:end]
                out[l, start:end] = piece.astype(out.dtype)
        stores.append(pltpu.make_async_copy(out, result, out_sems.at[i]))
        stores[-1].start()
    for store in stores:
        store.wait()


def partial_proj(nodes, lines, q, g12, g3, other=None, after=()):
    _, count, _ = q.shape
    blocks, size = nodes.shape[0], lines.shape[0]
    every = (blocks * size, WSUM, PD)
    if other is None:
        added, shapes = (), [jax.ShapeDtypeStruct(every, jnp.float32)]
    else:
        kinds = [jnp.float32] + [jnp.bfloat16] * (blocks - 1)
        added, shapes = (other,), [jax.ShapeDtypeStruct((size, WSUM, PD), kind) for kind in kinds]
    ins = 3 + len(added)
    return pl.pallas_call(
        functools.partial(partial_kernel, ins, len(after), len(shapes)),
        out_shape=shapes,
        grid_spec=pltpu.PrefetchScalarGridSpec(
            num_scalar_prefetch=2,
            grid=(1,),
            in_specs=[HBM] * ins + [ANY] * len(after),
            out_specs=[HBM] * len(shapes),
            scratch_shapes=[pltpu.VMEM((blocks * size, count, x.shape[2]), jnp.bfloat16) for x in (q, g12, g3)]
            + [pltpu.VMEM(every, jnp.float32)] * len(added)
            + [pltpu.VMEM(x.shape, x.dtype) for x in shapes]
            + [pltpu.SemaphoreType.DMA((ins, blocks)), pltpu.SemaphoreType.DMA((blocks,))],
        ),
        compiler_params=params(1),
        cost_estimate=cost(1e7),
        name="partial_proj",
    )(nodes, lines, q, g12, g3, *added, *after)


def count_kernel(index_ref, length_ref, *refs):
    out_ref = refs[-1]
    bag, block = index_ref.shape[1], index_ref.shape[2]
    lanes, chunk, low = 256, 16, ROWS // 8

    def one(i, carry):
        at = pl.ds(pl.multiple_of(i * lanes, lanes), lanes)
        index = index_ref[0, :, at]
        which = lax.broadcasted_iota(jnp.int32, (bag, lanes), 0)
        key = jnp.where(which < length_ref[0, :, at], index & (low - 1), -1)
        unit = jnp.left_shift(jnp.int32(1), jnp.right_shift(index, 6) * 4)
        ids = lax.broadcasted_iota(jnp.int32, (chunk, lanes), 0)
        for c in range(low // chunk):
            total = jnp.zeros((chunk, lanes), jnp.int32)
            for j in range(bag):
                total = total + jnp.where(key[j : j + 1] == ids + c * chunk, unit[j : j + 1], 0)
            out_ref[0, c * chunk : (c + 1) * chunk, at] = total
        return carry

    lax.fori_loop(0, block // lanes, one, 0)


def count_hits(lookups, counts, after=()):
    tables, bag, examples = lookups.shape
    block = 4096
    return pl.pallas_call(
        count_kernel,
        out_shape=jax.ShapeDtypeStruct((tables, ROWS // 8, examples), jnp.int32),
        grid=(tables, examples // block),
        in_specs=[
            pl.BlockSpec((1, bag, block), lambda k, i: (k, 0, i)),
            pl.BlockSpec((1, 1, block), lambda k, i: (k, 0, i)),
        ]
        + [ANY] * len(after),
        out_specs=pl.BlockSpec((1, ROWS // 8, block), lambda k, i: (k, 0, i)),
        compiler_params=params(2),
        cost_estimate=cost(1e7),
        name="count_hits",
    )(lookups, counts, *after)


def unpacked(words):
    rows = [lax.shift_right_logical(words, jnp.int32(4 * n)) & 15 for n in range(8)]
    return jnp.concatenate([r.astype(jnp.float32).astype(jnp.bfloat16) for r in rows], axis=0)


def wide_kernel(hits_ref, g_ref, w_ref, out_ref):
    @pl.when(pl.program_id(0) == 0)
    def _():
        out_ref[...] = jnp.zeros_like(out_ref)

    block = g_ref.shape[0]
    column = lax.broadcasted_iota(jnp.int32, (block, WSUM), 1)
    d = lax.dot_general(g_ref[...], w_ref[...], (((1,), (1,)), ((), ())), preferred_element_type=jnp.float32)
    d = jnp.where(column < W12, 0.0, d).astype(jnp.bfloat16)
    out_ref[...] += jnp.dot(unpacked(hits_ref[0]), d, preferred_element_type=jnp.float32)


def wide_sum(hits, g3, weights):
    _, words, examples = hits.shape
    block = 1024
    return pl.pallas_call(
        wide_kernel,
        out_shape=jax.ShapeDtypeStruct((ROWS, WSUM), jnp.float32),
        grid=(examples // block,),
        in_specs=[
            pl.BlockSpec((1, words, block), lambda i: (2, 0, i)),
            pl.BlockSpec((block, PD), lambda i: (i, 0)),
            pl.BlockSpec((WSUM, PD), lambda i: (0, 0)),
        ],
        out_specs=pl.BlockSpec((ROWS, WSUM), lambda i: (0, 0)),
        compiler_params=params(1),
        cost_estimate=cost(1e7),
        name="wide_sum",
    )(hits, g3, weights)


def narrow_sum_kernel(hits_ref, d_ref, wide_ref, out_ref):
    @pl.when(pl.program_id(0) == 0)
    def _():
        out_ref[...] = wide_ref[...]

    sources = d_ref.shape[0]
    block = hits_ref.shape[2]
    column = lax.broadcasted_iota(jnp.int32, (block, PD), 1)
    pieces = []
    for d in range(sources):
        packed = d_ref[d].astype(jnp.float32)
        pieces += [packed, pltpu.roll(packed, PD - W12, 1)]
    both = jnp.concatenate(pieces, axis=0)
    d1 = jnp.where(column < W1, both, 0.0).astype(jnp.bfloat16)
    d2 = jnp.where((column >= W1) & (column < W12), both, 0.0).astype(jnp.bfloat16)
    out_ref[...] += jnp.dot(unpacked(hits_ref[0]), d1, preferred_element_type=jnp.float32) + jnp.dot(
        unpacked(hits_ref[1]), d2, preferred_element_type=jnp.float32
    )


def narrow_sum(hits, narrow, wide):
    _, words, examples = hits.shape
    sources, half, _ = narrow.shape
    block = 1024
    per = block // (2 * half)
    return pl.pallas_call(
        narrow_sum_kernel,
        out_shape=jax.ShapeDtypeStruct((ROWS, WSUM), jnp.float32),
        grid=(examples // block,),
        in_specs=[
            pl.BlockSpec((2, words, block), lambda i: (0, 0, i)),
            pl.BlockSpec((per, half, 2 * W12), lambda i: (i, 0, 0)),
            pl.BlockSpec((ROWS, PD), lambda i: (0, 0)),
        ],
        out_specs=pl.BlockSpec((ROWS, PD), lambda i: (0, 0)),
        input_output_aliases={2: 0},
        compiler_params=params(1),
        cost_estimate=cost(1e7),
        name="narrow_sum",
    )(hits, narrow, wide)


def swap(x, axis, size, bits):
    return lax.ppermute(x, axis, [(d, d ^ bits) for d in range(size)])


def local(sizes, grad_out, pooled, proj, assign, indices, lengths):
    count, slots, _ = grad_out.shape
    scale = 1.0 / math.sqrt(count * slots)
    n_node, n_local = sizes["node"], sizes["local"]
    n_plane = n_node // 2
    node, loc = lax.axis_index("node"), lax.axis_index("local")

    g12, g3, q = permute(assign, grad_out, pooled)
    plane = jnp.arange(n_plane, dtype=jnp.int32) ^ (node // 2)
    lines = jnp.arange(n_local, dtype=jnp.int32) ^ loc
    (sent,) = partial_proj(plane * 2 + 1 - node % 2, lines, q, g12, g3)
    got = swap(sent, "node", n_node, 1)

    rows, g3 = lax.optimization_barrier((proj[:, :W12], g3))
    rows = jnp.concatenate([rows] + [swap(rows, "local", n_local, d) for d in range(1, n_local)])
    rows = jnp.concatenate([rows] + [swap(rows, "node", n_node, 2 * d) for d in range(1, n_plane)])
    g3_got = lax.all_to_all(g3, AXES, split_axis=0, concat_axis=0, tiled=True)
    rows = jnp.concatenate([rows, swap(rows, "node", n_node, 1)])

    kept = partial_proj(plane * 2 + node % 2, lines, q, g12, g3, got)
    arrived = [swap(kept[d], "node", n_node, 2 * d) for d in range(1, n_plane)]

    slot = jnp.arange(slots, dtype=jnp.int32)
    slot_node = slot // n_local ^ node
    slot_place = slot_node % 2 * (slots // 2) + slot_node // 2 * n_local + (slot % n_local ^ loc)
    narrow = narrow_dpool(slot_place, g12, rows, after=kept[:1])
    hits = count_hits(indices[0].transpose(1, 2, 0), lengths[0].T[:, None, :], after=[narrow])

    narrow_sent, g3_got, hits = lax.optimization_barrier((narrow, g3_got, hits))
    narrow_got = lax.all_to_all(narrow_sent, AXES, split_axis=0, concat_axis=0, tiled=True)
    wide = wide_sum(hits, g3_got.reshape(-1, PD), proj[0])

    arrived, wide = lax.optimization_barrier((arrived, wide))
    total = kept[0]
    for term in arrived:
        total = total + term.astype(jnp.float32)
    own, terms = total[:1], [swap(total[d : d + 1], "local", n_local, d) for d in range(1, n_local)]

    table_grad = narrow_sum(hits, narrow_got, wide)[None]
    terms, table_grad = lax.optimization_barrier((terms, table_grad))
    proj_grad = sum(terms, own) * scale
    return (table_grad, proj_grad)


def solution(mesh):
    placed = (
        P(AXES, None, None),
        P(AXES, None, None),
        P(AXES, None, None),
        P(),
        P(AXES, None, None, None),
        P(AXES, None, None),
    )
    return jax.shard_map(
        functools.partial(local, dict(mesh.shape)),
        mesh=mesh,
        in_specs=placed,
        out_specs=(P(AXES, None, None), P(AXES, None, None)),
        check_vma=False,
    )
```

```python
import functools
import math

import jax
import jax.numpy as jnp
from jax import lax
from jax.experimental import pallas as pl
from jax.experimental.pallas import tpu as pltpu
from jax.sharding import PartitionSpec as P

ROWS = 512
W1 = 16
W2 = 48
W3 = 192
PD = 128
W12 = W1 + W2
WSUM = W12 + W3
AXES = ("node", "local")
EB = 8
STEP = 32
MIB = 1024 * 1024


def params(grid):
    return pltpu.CompilerParams(dimension_semantics=("arbitrary",) * grid, vmem_limit_bytes=58 * MIB)


HBM = pl.BlockSpec(memory_space=pltpu.HBM)
ANY = pl.BlockSpec(memory_space=pl.ANY)


def cost(flops):
    return pl.CostEstimate(flops=int(flops), bytes_accessed=1024, transcendentals=0)


def permute_kernel(slots, pieces, assign_ref, grad_ref, pool_ref, *refs):
    outs, (perm_ref, grad_held, pool_held, sems) = refs[:3], refs[3:]
    step = pl.program_id(0)
    sources = ((grad_ref, grad_held), (pool_ref, pool_held))

    def copies(i):
        at = pl.ds(i * STEP, STEP)
        return [
            pltpu.make_async_copy(ref.at[at], held.at[at], sems.at[n, i]) for n, (ref, held) in enumerate(sources)
        ]

    @pl.when(step == 0)
    def _():
        for i in range(grad_ref.shape[0] // STEP):
            for copy in copies(i):
                copy.start()
        width = EB * slots
        lane = lax.broadcasted_iota(jnp.int32, (2 * EB, width), 1)
        row = lax.broadcasted_iota(jnp.int32, (2 * EB, width), 0)
        for s in range(0, slots, 2):
            group = jnp.where(row < EB, assign_ref[s], assign_ref[s + 1])
            hit = lane == (row % EB) * slots + group
            perm_ref[s * EB : (s + 2) * EB, :] = jnp.where(hit, 1.0, 0.0).astype(jnp.bfloat16)

    for copy, (_, held), cuts in zip(copies(step), sources, pieces):
        copy.wait()
        width = held.shape[2]
        for start in range(0, STEP, 2 * EB):
            pair = []
            for at in (start, start + EB):
                block = held[pl.ds(step * STEP + at, EB)].reshape(EB * slots, width)
                moved = jnp.dot(perm_ref[...], block, preferred_element_type=jnp.float32)
                pair.append(moved.reshape(slots, EB, width))
            both = jnp.concatenate(pair, axis=1).astype(jnp.bfloat16)
            for n, low, high in cuts:
                outs[n][:, start : start + 2 * EB, :] = both[:, :, low:high]


def permute(assign, grad_out, pooled):
    count, slots, _ = grad_out.shape
    widths = (2 * PD, PD, WSUM)
    pieces = (((0, 0, 2 * PD), (1, 2 * PD, 3 * PD)), ((2, 0, WSUM),))
    return pl.pallas_call(
        functools.partial(permute_kernel, slots, pieces),
        out_shape=[jax.ShapeDtypeStruct((slots, count, width), jnp.bfloat16) for width in widths],
        grid_spec=pltpu.PrefetchScalarGridSpec(
            num_scalar_prefetch=1,
            grid=(count // STEP,),
            in_specs=[HBM] * 2,
            out_specs=[pl.BlockSpec((slots, STEP, width), lambda i, a: (0, i, 0)) for width in widths],
            scratch_shapes=[
                pltpu.VMEM((EB * slots, EB * slots), jnp.bfloat16),
                pltpu.VMEM(grad_out.shape, jnp.bfloat16),
                pltpu.VMEM(pooled.shape, jnp.bfloat16),
                pltpu.SemaphoreType.DMA((2, count // STEP)),
            ],
        ),
        compiler_params=params(1),
        cost_estimate=cost(1e7),
        name="permute_groups",
    )(assign, grad_out, pooled)


def fetch(ref, held, sems, blocks, pick=lambda i: i):
    size = held.shape[0] // blocks
    copies = [
        pltpu.make_async_copy(ref.at[pl.ds(pick(i) * size, size)], held.at[pl.ds(i * size, size)], sems.at[i])
        for i in range(blocks)
    ]
    for copy in copies:
        copy.start()
    return copies


def narrow_kernel(blocks, place_ref, g_ref, w_ref, *refs):
    out_ref, g_held, w_held, out_held, g_sems, w_sems, out_sems = refs[-7:]
    weights = fetch(w_ref, w_held, w_sems, 1)
    loads = fetch(g_ref, g_held, g_sems, blocks)
    slots, count, _ = g_held.shape
    step, half = slots // blocks, count // 2
    column = lax.broadcasted_iota(jnp.int32, (count, W12), 1)
    dims = (((1,), (1,)), ((), ()))
    weights[0].wait()
    stores = []
    for i, load in enumerate(loads):
        load.wait()
        for s in range(i * step, (i + 1) * step):
            w = w_held[place_ref[s]]
            first = lax.dot_general(g_held[s, :, :PD], w, dims, preferred_element_type=jnp.float32)
            second = lax.dot_general(g_held[s, :, PD:], w, dims, preferred_element_type=jnp.float32)
            d = jnp.where(column < W1, first, second)
            out_held[s] = jnp.concatenate([d[:half], d[half:]], axis=1).astype(jnp.bfloat16)
        at = pl.ds(i * step, step)
        stores.append(pltpu.make_async_copy(out_held.at[at], out_ref.at[at], out_sems.at[i]))
        stores[-1].start()
    for store in stores:
        store.wait()


def narrow_dpool(place, g12, w12, after=()):
    slots, count, _ = g12.shape
    blocks = 4
    shape = (slots, count // 2, 2 * W12)
    return pl.pallas_call(
        functools.partial(narrow_kernel, blocks),
        out_shape=jax.ShapeDtypeStruct(shape, jnp.bfloat16),
        grid_spec=pltpu.PrefetchScalarGridSpec(
            num_scalar_prefetch=1,
            grid=(1,),
            in_specs=[HBM] * 2 + [ANY] * len(after),
            out_specs=HBM,
            scratch_shapes=[
                pltpu.VMEM(g12.shape, jnp.bfloat16),
                pltpu.VMEM(w12.shape, jnp.bfloat16),
                pltpu.VMEM(shape, jnp.bfloat16),
                pltpu.SemaphoreType.DMA((blocks,)),
                pltpu.SemaphoreType.DMA((1,)),
                pltpu.SemaphoreType.DMA((blocks,)),
            ],
        ),
        compiler_params=params(1),
        cost_estimate=cost(1e7),
        name="narrow_dpool",
    )(place, g12, w12, *after)


def partial_kernel(ins, waits, outs, node_ref, line_ref, *refs):
    operands, results = refs[:ins], refs[ins + waits : ins + waits + outs]
    held, out_held = refs[-2 - ins - outs : -2 - outs], refs[-2 - outs : -2]
    in_sems, out_sems = refs[-2:]
    blocks, size = node_ref.shape[0], line_ref.shape[0]
    loads = [
        fetch(ref, at, in_sems.at[n], blocks, (lambda i: node_ref[i]) if n < 3 else (lambda i: i))
        for n, (ref, at) in enumerate(zip(operands, held))
    ]
    stores = []
    for i in range(blocks):
        for copies in loads:
            copies[i].wait()
        if outs == 1:
            at = pl.ds(i * size, size)
            result, out = results[0].at[at], out_held[0].at[at]
        else:
            result, out = results[i], out_held[i]
        for l in range(size):
            slot = i * size + line_ref[l]
            q = held[0][slot].T
            narrow = jnp.dot(q[:W12], held[1][slot], preferred_element_type=jnp.float32)
            wide = jnp.dot(q[W12:], held[2][slot], preferred_element_type=jnp.float32)
            pieces = ((0, W1, narrow[:W1, :PD]), (W1, W12, narrow[W1:, PD:]), (W12, WSUM, wide))
            for start, end, piece in pieces:
                if ins == 4:
                    piece = piece + held[3][i * size + l, start:end]
                out[l, start:end] = piece.astype(out.dtype)
        stores.append(pltpu.make_async_copy(out, result, out_sems.at[i]))
        stores[-1].start()
    for store in stores:
        store.wait()


def partial_proj(nodes, lines, q, g12, g3, other=None, after=()):
    _, count, _ = q.shape
    blocks, size = nodes.shape[0], lines.shape[0]
    every = (blocks * size, WSUM, PD)
    if other is None:
        added, shapes = (), [jax.ShapeDtypeStruct(every, jnp.float32)]
    else:
        kinds = [jnp.float32] + [jnp.bfloat16] * (blocks - 1)
        added, shapes = (other,), [jax.ShapeDtypeStruct((size, WSUM, PD), kind) for kind in kinds]
    ins = 3 + len(added)
    return pl.pallas_call(
        functools.partial(partial_kernel, ins, len(after), len(shapes)),
        out_shape=shapes,
        grid_spec=pltpu.PrefetchScalarGridSpec(
            num_scalar_prefetch=2,
            grid=(1,),
            in_specs=[HBM] * ins + [ANY] * len(after),
            out_specs=[HBM] * len(shapes),
            scratch_shapes=[pltpu.VMEM((blocks * size, count, x.shape[2]), jnp.bfloat16) for x in (q, g12, g3)]
            + [pltpu.VMEM(every, jnp.float32)] * len(added)
            + [pltpu.VMEM(x.shape, x.dtype) for x in shapes]
            + [pltpu.SemaphoreType.DMA((ins, blocks)), pltpu.SemaphoreType.DMA((blocks,))],
        ),
        compiler_params=params(1),
        cost_estimate=cost(1e7),
        name="partial_proj",
    )(nodes, lines, q, g12, g3, *added, *after)


def count_kernel(index_ref, length_ref, *refs):
    out_ref = refs[-1]
    bag, block = index_ref.shape[1], index_ref.shape[2]
    lanes, chunk, low = 256, 16, ROWS // 8

    def one(i, carry):
        at = pl.ds(pl.multiple_of(i * lanes, lanes), lanes)
        index = index_ref[0, :, at]
        which = lax.broadcasted_iota(jnp.int32, (bag, lanes), 0)
        key = jnp.where(which < length_ref[0, :, at], index & (low - 1), -1)
        unit = jnp.left_shift(jnp.int32(1), jnp.right_shift(index, 6) * 4)
        ids = lax.broadcasted_iota(jnp.int32, (chunk, lanes), 0)
        for c in range(low // chunk):
            total = jnp.zeros((chunk, lanes), jnp.int32)
            for j in range(bag):
                total = total + jnp.where(key[j : j + 1] == ids + c * chunk, unit[j : j + 1], 0)
            out_ref[0, c * chunk : (c + 1) * chunk, at] = total
        return carry

    lax.fori_loop(0, block // lanes, one, 0)


def count_hits(lookups, counts, after=()):
    tables, bag, examples = lookups.shape
    block = 4096
    return pl.pallas_call(
        count_kernel,
        out_shape=jax.ShapeDtypeStruct((tables, ROWS // 8, examples), jnp.int32),
        grid=(tables, examples // block),
        in_specs=[
            pl.BlockSpec((1, bag, block), lambda k, i: (k, 0, i)),
            pl.BlockSpec((1, 1, block), lambda k, i: (k, 0, i)),
        ]
        + [ANY] * len(after),
        out_specs=pl.BlockSpec((1, ROWS // 8, block), lambda k, i: (k, 0, i)),
        compiler_params=params(2),
        cost_estimate=cost(1e7),
        name="count_hits",
    )(lookups, counts, *after)


def unpacked(words):
    rows = [lax.shift_right_logical(words, jnp.int32(4 * n)) & 15 for n in range(8)]
    return jnp.concatenate([r.astype(jnp.float32).astype(jnp.bfloat16) for r in rows], axis=0)


def wide_kernel(hits_ref, g_ref, w_ref, *refs):
    out_ref = refs[-1]

    @pl.when(pl.program_id(0) == 0)
    def _():
        out_ref[...] = jnp.zeros_like(out_ref)

    block = g_ref.shape[0]
    column = lax.broadcasted_iota(jnp.int32, (block, WSUM), 1)
    d = lax.dot_general(g_ref[...], w_ref[...], (((1,), (1,)), ((), ())), preferred_element_type=jnp.float32)
    d = jnp.where(column < W12, 0.0, d).astype(jnp.bfloat16)
    out_ref[...] += jnp.dot(unpacked(hits_ref[0]), d, preferred_element_type=jnp.float32)


def wide_sum(hits, g3, weights, after=()):
    _, words, examples = hits.shape
    block = 1024
    return pl.pallas_call(
        wide_kernel,
        out_shape=jax.ShapeDtypeStruct((ROWS, WSUM), jnp.float32),
        grid=(examples // block,),
        in_specs=[
            pl.BlockSpec((1, words, block), lambda i: (2, 0, i)),
            pl.BlockSpec((block, PD), lambda i: (i, 0)),
            pl.BlockSpec((WSUM, PD), lambda i: (0, 0)),
        ]
        + [ANY] * len(after),
        out_specs=pl.BlockSpec((ROWS, WSUM), lambda i: (0, 0)),
        compiler_params=params(1),
        cost_estimate=cost(1e7),
        name="wide_sum",
    )(hits, g3, weights, *after)


def narrow_sum_kernel(hits_ref, d_ref, wide_ref, out_ref):
    @pl.when(pl.program_id(0) == 0)
    def _():
        out_ref[...] = wide_ref[...]

    sources = d_ref.shape[0]
    block = hits_ref.shape[2]
    column = lax.broadcasted_iota(jnp.int32, (block, PD), 1)
    pieces = []
    for d in range(sources):
        packed = d_ref[d].astype(jnp.float32)
        pieces += [packed, pltpu.roll(packed, PD - W12, 1)]
    both = jnp.concatenate(pieces, axis=0)
    d1 = jnp.where(column < W1, both, 0.0).astype(jnp.bfloat16)
    d2 = jnp.where((column >= W1) & (column < W12), both, 0.0).astype(jnp.bfloat16)
    out_ref[...] += jnp.dot(unpacked(hits_ref[0]), d1, preferred_element_type=jnp.float32) + jnp.dot(
        unpacked(hits_ref[1]), d2, preferred_element_type=jnp.float32
    )


def narrow_sum(hits, narrow, wide):
    _, words, examples = hits.shape
    sources, half, _ = narrow.shape
    block = 1024
    per = block // (2 * half)
    return pl.pallas_call(
        narrow_sum_kernel,
        out_shape=jax.ShapeDtypeStruct((ROWS, WSUM), jnp.float32),
        grid=(examples // block,),
        in_specs=[
            pl.BlockSpec((2, words, block), lambda i: (0, 0, i)),
            pl.BlockSpec((per, half, 2 * W12), lambda i: (i, 0, 0)),
            pl.BlockSpec((ROWS, PD), lambda i: (0, 0)),
        ],
        out_specs=pl.BlockSpec((ROWS, PD), lambda i: (0, 0)),
        input_output_aliases={2: 0},
        compiler_params=params(1),
        cost_estimate=cost(1e7),
        name="narrow_sum",
    )(hits, narrow, wide)


def swap(x, axis, size, bits):
    return lax.ppermute(x, axis, [(d, d ^ bits) for d in range(size)])


def local(sizes, grad_out, pooled, proj, assign, indices, lengths):
    count, slots, _ = grad_out.shape
    scale = 1.0 / math.sqrt(count * slots)
    n_node, n_local = sizes["node"], sizes["local"]
    n_plane = n_node // 2
    node, loc = lax.axis_index("node"), lax.axis_index("local")

    g12, g3, q = permute(assign, grad_out, pooled)
    plane = jnp.arange(n_plane, dtype=jnp.int32) ^ (node // 2)
    lines = jnp.arange(n_local, dtype=jnp.int32) ^ loc
    (sent,) = partial_proj(plane * 2 + 1 - node % 2, lines, q, g12, g3)
    got = swap(sent, "node", n_node, 1)

    rows, g3 = lax.optimization_barrier((proj[:, :W12], g3))
    rows = jnp.concatenate([rows] + [swap(rows, "local", n_local, d) for d in range(1, n_local)])
    rows = jnp.concatenate([rows] + [swap(rows, "node", n_node, 2 * d) for d in range(1, n_plane)])
    g3, rows = lax.optimization_barrier((g3, rows))
    g3_got = lax.all_to_all(g3, AXES, split_axis=0, concat_axis=0, tiled=True)
    rows = jnp.concatenate([rows, swap(rows, "node", n_node, 1)])

    kept = partial_proj(plane * 2 + node % 2, lines, q, g12, g3, got)
    arrived = [swap(kept[d], "node", n_node, 2 * d) for d in range(1, n_plane)]

    slot = jnp.arange(slots, dtype=jnp.int32)
    slot_node = slot // n_local ^ node
    slot_place = slot_node % 2 * (slots // 2) + slot_node // 2 * n_local + (slot % n_local ^ loc)
    narrow = narrow_dpool(slot_place, g12, rows, after=kept[:1])
    hits = count_hits(indices[0].transpose(1, 2, 0), lengths[0].T[:, None, :], after=[narrow])

    narrow_sent, g3_got, hits, arrived = lax.optimization_barrier((narrow, g3_got, hits, arrived))
    narrow_got = lax.all_to_all(narrow_sent, AXES, split_axis=0, concat_axis=0, tiled=True)
    total = kept[0]
    for term in arrived:
        total = total + term.astype(jnp.float32)
    own, terms = total[:1], [swap(total[d : d + 1], "local", n_local, d) for d in range(1, n_local)]

    wide = wide_sum(hits, g3_got.reshape(-1, PD), proj[0], after=[own])
    table_grad = narrow_sum(hits, narrow_got, wide)[None]
    terms, table_grad = lax.optimization_barrier((terms, table_grad))
    proj_grad = sum(terms, own) * scale
    return (table_grad, proj_grad)


def solution(mesh):
    placed = (
        P(AXES, None, None),
        P(AXES, None, None),
        P(AXES, None, None),
        P(),
        P(AXES, None, None, None),
        P(AXES, None, None),
    )
    return jax.shard_map(
        functools.partial(local, dict(mesh.shape)),
        mesh=mesh,
        in_specs=placed,
        out_specs=(P(AXES, None, None), P(AXES, None, None)),
        check_vma=False,
    )
```

```python
import functools
import math

import jax
import jax.numpy as jnp
from jax import lax
from jax.experimental import pallas as pl
from jax.experimental.pallas import tpu as pltpu
from jax.sharding import PartitionSpec as P

ROWS = 512
W1 = 16
W2 = 48
W3 = 192
PD = 128
W12 = W1 + W2
WSUM = W12 + W3
AXES = ("node", "local")
EB = 8
STEP = 32
MIB = 1024 * 1024


def params(grid):
    return pltpu.CompilerParams(dimension_semantics=("arbitrary",) * grid, vmem_limit_bytes=58 * MIB)


HBM = pl.BlockSpec(memory_space=pltpu.HBM)
ANY = pl.BlockSpec(memory_space=pl.ANY)


def cost(flops):
    return pl.CostEstimate(flops=int(flops), bytes_accessed=1024, transcendentals=0)


def permute_kernel(slots, pieces, assign_ref, grad_ref, pool_ref, *refs):
    outs, (perm_ref, grad_held, pool_held, sems) = refs[-7:-4], refs[-4:]
    step = pl.program_id(0)
    sources = ((grad_ref, grad_held), (pool_ref, pool_held))

    def copies(i):
        at = pl.ds(i * STEP, STEP)
        return [
            pltpu.make_async_copy(ref.at[at], held.at[at], sems.at[n, i]) for n, (ref, held) in enumerate(sources)
        ]

    @pl.when(step == 0)
    def _():
        for i in range(grad_ref.shape[0] // STEP):
            for copy in copies(i):
                copy.start()
        width = EB * slots
        lane = lax.broadcasted_iota(jnp.int32, (2 * EB, width), 1)
        row = lax.broadcasted_iota(jnp.int32, (2 * EB, width), 0)
        for s in range(0, slots, 2):
            group = jnp.where(row < EB, assign_ref[s], assign_ref[s + 1])
            hit = lane == (row % EB) * slots + group
            perm_ref[s * EB : (s + 2) * EB, :] = jnp.where(hit, 1.0, 0.0).astype(jnp.bfloat16)

    for copy, (_, held), cuts in zip(copies(step), sources, pieces):
        copy.wait()
        width = held.shape[2]
        for start in range(0, STEP, 2 * EB):
            pair = []
            for at in (start, start + EB):
                block = held[pl.ds(step * STEP + at, EB)].reshape(EB * slots, width)
                moved = jnp.dot(perm_ref[...], block, preferred_element_type=jnp.float32)
                pair.append(moved.reshape(slots, EB, width))
            both = jnp.concatenate(pair, axis=1).astype(jnp.bfloat16)
            for n, low, high in cuts:
                outs[n][:, start : start + 2 * EB, :] = both[:, :, low:high]


def permute(assign, grad_out, pooled, after=()):
    count, slots, _ = grad_out.shape
    widths = (2 * PD, PD, WSUM)
    pieces = (((0, 0, 2 * PD), (1, 2 * PD, 3 * PD)), ((2, 0, WSUM),))
    return pl.pallas_call(
        functools.partial(permute_kernel, slots, pieces),
        out_shape=[jax.ShapeDtypeStruct((slots, count, width), jnp.bfloat16) for width in widths],
        grid_spec=pltpu.PrefetchScalarGridSpec(
            num_scalar_prefetch=1,
            grid=(count // STEP,),
            in_specs=[HBM] * 2 + [ANY] * len(after),
            out_specs=[pl.BlockSpec((slots, STEP, width), lambda i, a: (0, i, 0)) for width in widths],
            scratch_shapes=[
                pltpu.VMEM((EB * slots, EB * slots), jnp.bfloat16),
                pltpu.VMEM(grad_out.shape, jnp.bfloat16),
                pltpu.VMEM(pooled.shape, jnp.bfloat16),
                pltpu.SemaphoreType.DMA((2, count // STEP)),
            ],
        ),
        compiler_params=params(1),
        cost_estimate=cost(1e7),
        name="permute_groups",
    )(assign, grad_out, pooled, *after)


def fetch(ref, held, sems, blocks, pick=lambda i: i):
    size = held.shape[0] // blocks
    copies = [
        pltpu.make_async_copy(ref.at[pl.ds(pick(i) * size, size)], held.at[pl.ds(i * size, size)], sems.at[i])
        for i in range(blocks)
    ]
    for copy in copies:
        copy.start()
    return copies


def narrow_kernel(blocks, place_ref, g_ref, w_ref, *refs):
    out_ref, g_held, w_held, out_held, g_sems, w_sems, out_sems = refs[-7:]
    weights = fetch(w_ref, w_held, w_sems, 1)
    loads = fetch(g_ref, g_held, g_sems, blocks)
    slots, count, _ = g_held.shape
    step, half = slots // blocks, count // 2
    column = lax.broadcasted_iota(jnp.int32, (count, W12), 1)
    dims = (((1,), (1,)), ((), ()))
    weights[0].wait()
    stores = []
    for i, load in enumerate(loads):
        load.wait()
        for s in range(i * step, (i + 1) * step):
            w = w_held[place_ref[s]]
            first = lax.dot_general(g_held[s, :, :PD], w, dims, preferred_element_type=jnp.float32)
            second = lax.dot_general(g_held[s, :, PD:], w, dims, preferred_element_type=jnp.float32)
            d = jnp.where(column < W1, first, second)
            out_held[s] = jnp.concatenate([d[:half], d[half:]], axis=1).astype(jnp.bfloat16)
        at = pl.ds(i * step, step)
        stores.append(pltpu.make_async_copy(out_held.at[at], out_ref.at[at], out_sems.at[i]))
        stores[-1].start()
    for store in stores:
        store.wait()


def narrow_dpool(place, g12, w12, after=()):
    slots, count, _ = g12.shape
    blocks = 4
    shape = (slots, count // 2, 2 * W12)
    return pl.pallas_call(
        functools.partial(narrow_kernel, blocks),
        out_shape=jax.ShapeDtypeStruct(shape, jnp.bfloat16),
        grid_spec=pltpu.PrefetchScalarGridSpec(
            num_scalar_prefetch=1,
            grid=(1,),
            in_specs=[HBM] * 2 + [ANY] * len(after),
            out_specs=HBM,
            scratch_shapes=[
                pltpu.VMEM(g12.shape, jnp.bfloat16),
                pltpu.VMEM(w12.shape, jnp.bfloat16),
                pltpu.VMEM(shape, jnp.bfloat16),
                pltpu.SemaphoreType.DMA((blocks,)),
                pltpu.SemaphoreType.DMA((1,)),
                pltpu.SemaphoreType.DMA((blocks,)),
            ],
        ),
        compiler_params=params(1),
        cost_estimate=cost(1e7),
        name="narrow_dpool",
    )(place, g12, w12, *after)


def partial_kernel(ins, waits, outs, node_ref, line_ref, *refs):
    operands, results = refs[:ins], refs[ins + waits : ins + waits + outs]
    held, out_held = refs[-2 - ins - outs : -2 - outs], refs[-2 - outs : -2]
    in_sems, out_sems = refs[-2:]
    blocks, size = node_ref.shape[0], line_ref.shape[0]
    loads = [
        fetch(ref, at, in_sems.at[n], blocks, (lambda i: node_ref[i]) if n < 3 else (lambda i: i))
        for n, (ref, at) in enumerate(zip(operands, held))
    ]
    stores = []
    for i in range(blocks):
        for copies in loads:
            copies[i].wait()
        if outs == 1:
            at = pl.ds(i * size, size)
            result, out = results[0].at[at], out_held[0].at[at]
        else:
            result, out = results[i], out_held[i]
        for l in range(size):
            slot = i * size + line_ref[l]
            q = held[0][slot].T
            narrow = jnp.dot(q[:W12], held[1][slot], preferred_element_type=jnp.float32)
            wide = jnp.dot(q[W12:], held[2][slot], preferred_element_type=jnp.float32)
            pieces = ((0, W1, narrow[:W1, :PD]), (W1, W12, narrow[W1:, PD:]), (W12, WSUM, wide))
            for start, end, piece in pieces:
                if ins == 4:
                    piece = piece + held[3][i * size + l, start:end]
                out[l, start:end] = piece.astype(out.dtype)
        stores.append(pltpu.make_async_copy(out, result, out_sems.at[i]))
        stores[-1].start()
    for store in stores:
        store.wait()


def partial_proj(nodes, lines, q, g12, g3, other=None, after=()):
    _, count, _ = q.shape
    blocks, size = nodes.shape[0], lines.shape[0]
    every = (blocks * size, WSUM, PD)
    if other is None:
        added, shapes = (), [jax.ShapeDtypeStruct(every, jnp.float32)]
    else:
        kinds = [jnp.float32] + [jnp.bfloat16] * (blocks - 1)
        added, shapes = (other,), [jax.ShapeDtypeStruct((size, WSUM, PD), kind) for kind in kinds]
    ins = 3 + len(added)
    return pl.pallas_call(
        functools.partial(partial_kernel, ins, len(after), len(shapes)),
        out_shape=shapes,
        grid_spec=pltpu.PrefetchScalarGridSpec(
            num_scalar_prefetch=2,
            grid=(1,),
            in_specs=[HBM] * ins + [ANY] * len(after),
            out_specs=[HBM] * len(shapes),
            scratch_shapes=[pltpu.VMEM((blocks * size, count, x.shape[2]), jnp.bfloat16) for x in (q, g12, g3)]
            + [pltpu.VMEM(every, jnp.float32)] * len(added)
            + [pltpu.VMEM(x.shape, x.dtype) for x in shapes]
            + [pltpu.SemaphoreType.DMA((ins, blocks)), pltpu.SemaphoreType.DMA((blocks,))],
        ),
        compiler_params=params(1),
        cost_estimate=cost(1e7),
        name="partial_proj",
    )(nodes, lines, q, g12, g3, *added, *after)


def count_kernel(index_ref, length_ref, *refs):
    out_ref = refs[-1]
    bag, block = index_ref.shape[1], index_ref.shape[2]
    lanes, chunk, low = 256, 16, ROWS // 8

    def one(i, carry):
        at = pl.ds(pl.multiple_of(i * lanes, lanes), lanes)
        index = index_ref[0, :, at]
        which = lax.broadcasted_iota(jnp.int32, (bag, lanes), 0)
        key = jnp.where(which < length_ref[0, :, at], index & (low - 1), -1)
        unit = jnp.left_shift(jnp.int32(1), jnp.right_shift(index, 6) * 4)
        ids = lax.broadcasted_iota(jnp.int32, (chunk, lanes), 0)
        for c in range(low // chunk):
            total = jnp.zeros((chunk, lanes), jnp.int32)
            for j in range(bag):
                total = total + jnp.where(key[j : j + 1] == ids + c * chunk, unit[j : j + 1], 0)
            out_ref[0, c * chunk : (c + 1) * chunk, at] = total
        return carry

    lax.fori_loop(0, block // lanes, one, 0)


def count_hits(lookups, counts, after=()):
    tables, bag, examples = lookups.shape
    block = 4096
    return pl.pallas_call(
        count_kernel,
        out_shape=jax.ShapeDtypeStruct((tables, ROWS // 8, examples), jnp.int32),
        grid=(tables, examples // block),
        in_specs=[
            pl.BlockSpec((1, bag, block), lambda k, i: (k, 0, i)),
            pl.BlockSpec((1, 1, block), lambda k, i: (k, 0, i)),
        ]
        + [ANY] * len(after),
        out_specs=pl.BlockSpec((1, ROWS // 8, block), lambda k, i: (k, 0, i)),
        compiler_params=params(2),
        cost_estimate=cost(1e7),
        name="count_hits",
    )(lookups, counts, *after)


def unpacked(words):
    rows = [lax.shift_right_logical(words, jnp.int32(4 * n)) & 15 for n in range(8)]
    return jnp.concatenate([r.astype(jnp.float32).astype(jnp.bfloat16) for r in rows], axis=0)


def wide_kernel(hits_ref, g_ref, w_ref, *refs):
    out_ref = refs[-1]

    @pl.when(pl.program_id(0) == 0)
    def _():
        out_ref[...] = jnp.zeros_like(out_ref)

    block = g_ref.shape[0]
    column = lax.broadcasted_iota(jnp.int32, (block, WSUM), 1)
    d = lax.dot_general(g_ref[...], w_ref[...], (((1,), (1,)), ((), ())), preferred_element_type=jnp.float32)
    d = jnp.where(column < W12, 0.0, d).astype(jnp.bfloat16)
    out_ref[...] += jnp.dot(unpacked(hits_ref[0]), d, preferred_element_type=jnp.float32)


def wide_sum(hits, g3, weights, after=()):
    _, words, examples = hits.shape
    block = 1024
    return pl.pallas_call(
        wide_kernel,
        out_shape=jax.ShapeDtypeStruct((ROWS, WSUM), jnp.float32),
        grid=(examples // block,),
        in_specs=[
            pl.BlockSpec((1, words, block), lambda i: (2, 0, i)),
            pl.BlockSpec((block, PD), lambda i: (i, 0)),
            pl.BlockSpec((WSUM, PD), lambda i: (0, 0)),
        ]
        + [ANY] * len(after),
        out_specs=pl.BlockSpec((ROWS, WSUM), lambda i: (0, 0)),
        compiler_params=params(1),
        cost_estimate=cost(1e7),
        name="wide_sum",
    )(hits, g3, weights, *after)


def narrow_sum_kernel(hits_ref, d_ref, wide_ref, out_ref):
    @pl.when(pl.program_id(0) == 0)
    def _():
        out_ref[...] = wide_ref[...]

    sources = d_ref.shape[0]
    block = hits_ref.shape[2]
    column = lax.broadcasted_iota(jnp.int32, (block, PD), 1)
    pieces = []
    for d in range(sources):
        packed = d_ref[d].astype(jnp.float32)
        pieces += [packed, pltpu.roll(packed, PD - W12, 1)]
    both = jnp.concatenate(pieces, axis=0)
    d1 = jnp.where(column < W1, both, 0.0).astype(jnp.bfloat16)
    d2 = jnp.where((column >= W1) & (column < W12), both, 0.0).astype(jnp.bfloat16)
    out_ref[...] += jnp.dot(unpacked(hits_ref[0]), d1, preferred_element_type=jnp.float32) + jnp.dot(
        unpacked(hits_ref[1]), d2, preferred_element_type=jnp.float32
    )


def narrow_sum(hits, narrow, wide):
    _, words, examples = hits.shape
    sources, half, _ = narrow.shape
    block = 1024
    per = block // (2 * half)
    return pl.pallas_call(
        narrow_sum_kernel,
        out_shape=jax.ShapeDtypeStruct((ROWS, WSUM), jnp.float32),
        grid=(examples // block,),
        in_specs=[
            pl.BlockSpec((2, words, block), lambda i: (0, 0, i)),
            pl.BlockSpec((per, half, 2 * W12), lambda i: (i, 0, 0)),
            pl.BlockSpec((ROWS, PD), lambda i: (0, 0)),
        ],
        out_specs=pl.BlockSpec((ROWS, PD), lambda i: (0, 0)),
        input_output_aliases={2: 0},
        compiler_params=params(1),
        cost_estimate=cost(1e7),
        name="narrow_sum",
    )(hits, narrow, wide)


def swap(x, axis, size, bits):
    return lax.ppermute(x, axis, [(d, d ^ bits) for d in range(size)])


def local(sizes, grad_out, pooled, proj, assign, indices, lengths):
    count, slots, _ = grad_out.shape
    scale = 1.0 / math.sqrt(count * slots)
    n_node, n_local = sizes["node"], sizes["local"]
    n_plane = n_node // 2
    node, loc = lax.axis_index("node"), lax.axis_index("local")

    rows = proj[:, :W12]
    rows = jnp.concatenate([rows] + [swap(rows, "local", n_local, d) for d in range(1, n_local)])
    rows = jnp.concatenate([rows] + [swap(rows, "node", n_node, 2 * d) for d in range(1, n_plane)])

    g12, g3, q = permute(assign, grad_out, pooled, after=[rows])
    g3, rows = lax.optimization_barrier((g3, rows))
    g3_got = lax.all_to_all(g3, AXES, split_axis=0, concat_axis=0, tiled=True)
    rows = jnp.concatenate([rows, swap(rows, "node", n_node, 1)])

    plane = jnp.arange(n_plane, dtype=jnp.int32) ^ (node // 2)
    lines = jnp.arange(n_local, dtype=jnp.int32) ^ loc
    (sent,) = partial_proj(plane * 2 + 1 - node % 2, lines, q, g12, g3, after=[rows])
    got = swap(sent, "node", n_node, 1)

    kept = partial_proj(plane * 2 + node % 2, lines, q, g12, g3, got)
    arrived = [swap(kept[d], "node", n_node, 2 * d) for d in range(1, n_plane)]

    slot = jnp.arange(slots, dtype=jnp.int32)
    slot_node = slot // n_local ^ node
    slot_place = slot_node % 2 * (slots // 2) + slot_node // 2 * n_local + (slot % n_local ^ loc)
    narrow = narrow_dpool(slot_place, g12, rows, after=kept[:1])
    hits = count_hits(indices[0].transpose(1, 2, 0), lengths[0].T[:, None, :], after=[narrow])

    narrow_sent, g3_got, hits, arrived = lax.optimization_barrier((narrow, g3_got, hits, arrived))
    narrow_got = lax.all_to_all(narrow_sent, AXES, split_axis=0, concat_axis=0, tiled=True)
    total = kept[0]
    for term in arrived:
        total = total + term.astype(jnp.float32)
    rounded = total.astype(jnp.bfloat16)
    own, terms = total[:1], [swap(rounded[d : d + 1], "local", n_local, d) for d in range(1, n_local)]

    wide = wide_sum(hits, g3_got.reshape(-1, PD), proj[0], after=[own])
    table_grad = narrow_sum(hits, narrow_got, wide)[None]
    terms, table_grad = lax.optimization_barrier((terms, table_grad))
    proj_grad = sum((term.astype(jnp.float32) for term in terms), own) * scale
    return (table_grad, proj_grad)


def solution(mesh):
    placed = (
        P(AXES, None, None),
        P(AXES, None, None),
        P(AXES, None, None),
        P(),
        P(AXES, None, None, None),
        P(AXES, None, None),
    )
    return jax.shard_map(
        functools.partial(local, dict(mesh.shape)),
        mesh=mesh,
        in_specs=placed,
        out_specs=(P(AXES, None, None), P(AXES, None, None)),
        check_vma=False,
    )
```

```python
import functools
import math

import jax
import jax.numpy as jnp
from jax import lax
from jax.experimental import pallas as pl
from jax.experimental.pallas import tpu as pltpu
from jax.sharding import PartitionSpec as P

ROWS = 512
W1 = 16
W2 = 48
W3 = 192
PD = 128
W12 = W1 + W2
WSUM = W12 + W3
AXES = ("node", "local")
EB = 8
STEP = 32
MIB = 1024 * 1024


def params(grid):
    return pltpu.CompilerParams(dimension_semantics=("arbitrary",) * grid, vmem_limit_bytes=58 * MIB)


HBM = pl.BlockSpec(memory_space=pltpu.HBM)
ANY = pl.BlockSpec(memory_space=pl.ANY)


def cost(flops):
    return pl.CostEstimate(flops=int(flops), bytes_accessed=1024, transcendentals=0)


def permute_kernel(slots, pieces, assign_ref, grad_ref, pool_ref, *refs):
    outs, (perm_ref, grad_held, pool_held, sems) = refs[-7:-4], refs[-4:]
    step = pl.program_id(0)
    sources = ((grad_ref, grad_held), (pool_ref, pool_held))

    def copies(i):
        at = pl.ds(i * STEP, STEP)
        return [
            pltpu.make_async_copy(ref.at[at], held.at[at], sems.at[n, i]) for n, (ref, held) in enumerate(sources)
        ]

    @pl.when(step == 0)
    def _():
        for i in range(grad_ref.shape[0] // STEP):
            for copy in copies(i):
                copy.start()
        width = EB * slots
        lane = lax.broadcasted_iota(jnp.int32, (2 * EB, width), 1)
        row = lax.broadcasted_iota(jnp.int32, (2 * EB, width), 0)
        for s in range(0, slots, 2):
            group = jnp.where(row < EB, assign_ref[s], assign_ref[s + 1])
            hit = lane == (row % EB) * slots + group
            perm_ref[s * EB : (s + 2) * EB, :] = jnp.where(hit, 1.0, 0.0).astype(jnp.bfloat16)

    for copy, (_, held), cuts in zip(copies(step), sources, pieces):
        copy.wait()
        width = held.shape[2]
        for start in range(0, STEP, 2 * EB):
            pair = []
            for at in (start, start + EB):
                block = held[pl.ds(step * STEP + at, EB)].reshape(EB * slots, width)
                moved = jnp.dot(perm_ref[...], block, preferred_element_type=jnp.float32)
                pair.append(moved.reshape(slots, EB, width))
            both = jnp.concatenate(pair, axis=1).astype(jnp.bfloat16)
            for n, low, high in cuts:
                outs[n][:, start : start + 2 * EB, :] = both[:, :, low:high]


def permute(assign, grad_out, pooled, after=()):
    count, slots, _ = grad_out.shape
    widths = (2 * PD, PD, WSUM)
    pieces = (((0, 0, 2 * PD), (1, 2 * PD, 3 * PD)), ((2, 0, WSUM),))
    return pl.pallas_call(
        functools.partial(permute_kernel, slots, pieces),
        out_shape=[jax.ShapeDtypeStruct((slots, count, width), jnp.bfloat16) for width in widths],
        grid_spec=pltpu.PrefetchScalarGridSpec(
            num_scalar_prefetch=1,
            grid=(count // STEP,),
            in_specs=[HBM] * 2 + [ANY] * len(after),
            out_specs=[pl.BlockSpec((slots, STEP, width), lambda i, a: (0, i, 0)) for width in widths],
            scratch_shapes=[
                pltpu.VMEM((EB * slots, EB * slots), jnp.bfloat16),
                pltpu.VMEM(grad_out.shape, jnp.bfloat16),
                pltpu.VMEM(pooled.shape, jnp.bfloat16),
                pltpu.SemaphoreType.DMA((2, count // STEP)),
            ],
        ),
        compiler_params=params(1),
        cost_estimate=cost(1e7),
        name="permute_groups",
    )(assign, grad_out, pooled, *after)


def fetch(ref, held, sems, blocks, pick=lambda i: i):
    size = held.shape[0] // blocks
    copies = [
        pltpu.make_async_copy(ref.at[pl.ds(pick(i) * size, size)], held.at[pl.ds(i * size, size)], sems.at[i])
        for i in range(blocks)
    ]
    for copy in copies:
        copy.start()
    return copies


def narrow_kernel(blocks, g_ref, w_ref, *refs):
    out_ref, g_held, w_held, out_held, g_sems, w_sems, out_sems = refs[-7:]
    weights = fetch(w_ref, w_held, w_sems, 1)
    loads = fetch(g_ref, g_held, g_sems, blocks)
    slots, count, _ = g_held.shape
    step, half = slots // blocks, count // 2
    column = lax.broadcasted_iota(jnp.int32, (count, W12), 1)
    dims = (((1,), (1,)), ((), ()))
    weights[0].wait()
    stores = []
    for i, load in enumerate(loads):
        load.wait()
        for s in range(i * step, (i + 1) * step):
            w = w_held[s]
            first = lax.dot_general(g_held[s, :, :PD], w, dims, preferred_element_type=jnp.float32)
            second = lax.dot_general(g_held[s, :, PD:], w, dims, preferred_element_type=jnp.float32)
            d = jnp.where(column < W1, first, second)
            out_held[s] = jnp.concatenate([d[:half], d[half:]], axis=1).astype(jnp.bfloat16)
        at = pl.ds(i * step, step)
        stores.append(pltpu.make_async_copy(out_held.at[at], out_ref.at[at], out_sems.at[i]))
        stores[-1].start()
    for store in stores:
        store.wait()


def narrow_dpool(g12, w12, after=()):
    slots, count, _ = g12.shape
    blocks = 4
    shape = (slots, count // 2, 2 * W12)
    return pl.pallas_call(
        functools.partial(narrow_kernel, blocks),
        out_shape=jax.ShapeDtypeStruct(shape, jnp.bfloat16),
        in_specs=[HBM] * 2 + [ANY] * len(after),
        out_specs=HBM,
        scratch_shapes=[
            pltpu.VMEM(g12.shape, jnp.bfloat16),
            pltpu.VMEM(w12.shape, jnp.bfloat16),
            pltpu.VMEM(shape, jnp.bfloat16),
            pltpu.SemaphoreType.DMA((blocks,)),
            pltpu.SemaphoreType.DMA((1,)),
            pltpu.SemaphoreType.DMA((blocks,)),
        ],
        compiler_params=params(0),
        cost_estimate=cost(1e7),
        name="narrow_dpool",
    )(g12, w12, *after)


def partial_kernel(ins, waits, outs, node_ref, line_ref, *refs):
    operands, results = refs[:ins], refs[ins + waits : ins + waits + outs]
    held, out_held = refs[-2 - ins - outs : -2 - outs], refs[-2 - outs : -2]
    in_sems, out_sems = refs[-2:]
    blocks, size = node_ref.shape[0], line_ref.shape[0]
    loads = [
        fetch(ref, at, in_sems.at[n], blocks, (lambda i: node_ref[i]) if n < 3 else (lambda i: i))
        for n, (ref, at) in enumerate(zip(operands, held))
    ]
    stores = []
    for i in range(blocks):
        for copies in loads:
            copies[i].wait()
        if outs == 1:
            at = pl.ds(i * size, size)
            result, out = results[0].at[at], out_held[0].at[at]
        else:
            result, out = results[i], out_held[i]
        for l in range(size):
            slot = i * size + line_ref[l]
            q = held[0][slot].T
            narrow = jnp.dot(q[:W12], held[1][slot], preferred_element_type=jnp.float32)
            wide = jnp.dot(q[W12:], held[2][slot], preferred_element_type=jnp.float32)
            pieces = ((0, W1, narrow[:W1, :PD]), (W1, W12, narrow[W1:, PD:]), (W12, WSUM, wide))
            for start, end, piece in pieces:
                if ins == 4:
                    piece = piece + held[3][i * size + l, start:end]
                out[l, start:end] = piece.astype(out.dtype)
        stores.append(pltpu.make_async_copy(out, result, out_sems.at[i]))
        stores[-1].start()
    for store in stores:
        store.wait()


def partial_proj(nodes, lines, q, g12, g3, other=None, after=()):
    _, count, _ = q.shape
    blocks, size = nodes.shape[0], lines.shape[0]
    every = (blocks * size, WSUM, PD)
    if other is None:
        added, shapes = (), [jax.ShapeDtypeStruct(every, jnp.float32)]
    else:
        kinds = [jnp.float32] + [jnp.bfloat16] * (blocks - 1)
        added, shapes = (other,), [jax.ShapeDtypeStruct((size, WSUM, PD), kind) for kind in kinds]
    ins = 3 + len(added)
    return pl.pallas_call(
        functools.partial(partial_kernel, ins, len(after), len(shapes)),
        out_shape=shapes,
        grid_spec=pltpu.PrefetchScalarGridSpec(
            num_scalar_prefetch=2,
            grid=(1,),
            in_specs=[HBM] * ins + [ANY] * len(after),
            out_specs=[HBM] * len(shapes),
            scratch_shapes=[pltpu.VMEM((blocks * size, count, x.shape[2]), jnp.bfloat16) for x in (q, g12, g3)]
            + [pltpu.VMEM(every, jnp.float32)] * len(added)
            + [pltpu.VMEM(x.shape, x.dtype) for x in shapes]
            + [pltpu.SemaphoreType.DMA((ins, blocks)), pltpu.SemaphoreType.DMA((blocks,))],
        ),
        compiler_params=params(1),
        cost_estimate=cost(1e7),
        name="partial_proj",
    )(nodes, lines, q, g12, g3, *added, *after)


def count_kernel(index_ref, length_ref, *refs):
    out_ref = refs[-1]
    bag, block = index_ref.shape[1], index_ref.shape[2]
    lanes, chunk, low = 256, 16, ROWS // 8

    def one(i, carry):
        at = pl.ds(pl.multiple_of(i * lanes, lanes), lanes)
        index = index_ref[0, :, at]
        which = lax.broadcasted_iota(jnp.int32, (bag, lanes), 0)
        key = jnp.where(which < length_ref[0, :, at], index & (low - 1), -1)
        unit = jnp.left_shift(jnp.int32(1), jnp.right_shift(index, 6) * 4)
        ids = lax.broadcasted_iota(jnp.int32, (chunk, lanes), 0)
        for c in range(low // chunk):
            total = jnp.zeros((chunk, lanes), jnp.int32)
            for j in range(bag):
                total = total + jnp.where(key[j : j + 1] == ids + c * chunk, unit[j : j + 1], 0)
            out_ref[0, c * chunk : (c + 1) * chunk, at] = total
        return carry

    lax.fori_loop(0, block // lanes, one, 0)


def count_hits(lookups, counts, after=()):
    tables, bag, examples = lookups.shape
    block = 4096
    return pl.pallas_call(
        count_kernel,
        out_shape=jax.ShapeDtypeStruct((tables, ROWS // 8, examples), jnp.int32),
        grid=(tables, examples // block),
        in_specs=[
            pl.BlockSpec((1, bag, block), lambda k, i: (k, 0, i)),
            pl.BlockSpec((1, 1, block), lambda k, i: (k, 0, i)),
        ]
        + [ANY] * len(after),
        out_specs=pl.BlockSpec((1, ROWS // 8, block), lambda k, i: (k, 0, i)),
        compiler_params=params(2),
        cost_estimate=cost(1e7),
        name="count_hits",
    )(lookups, counts, *after)


def unpacked(words):
    rows = [lax.shift_right_logical(words, jnp.int32(4 * n)) & 15 for n in range(8)]
    return jnp.concatenate([r.astype(jnp.float32).astype(jnp.bfloat16) for r in rows], axis=0)


def wide_kernel(hits_ref, g_ref, w_ref, *refs):
    out_ref = refs[-1]

    @pl.when(pl.program_id(0) == 0)
    def _():
        out_ref[...] = jnp.zeros_like(out_ref)

    block = g_ref.shape[0]
    column = lax.broadcasted_iota(jnp.int32, (block, WSUM), 1)
    d = lax.dot_general(g_ref[...], w_ref[...], (((1,), (1,)), ((), ())), preferred_element_type=jnp.float32)
    d = jnp.where(column < W12, 0.0, d).astype(jnp.bfloat16)
    out_ref[...] += jnp.dot(unpacked(hits_ref[0]), d, preferred_element_type=jnp.float32)


def wide_sum(hits, g3, weights, after=()):
    _, words, examples = hits.shape
    block = 1024
    return pl.pallas_call(
        wide_kernel,
        out_shape=jax.ShapeDtypeStruct((ROWS, WSUM), jnp.float32),
        grid=(examples // block,),
        in_specs=[
            pl.BlockSpec((1, words, block), lambda i: (2, 0, i)),
            pl.BlockSpec((block, PD), lambda i: (i, 0)),
            pl.BlockSpec((WSUM, PD), lambda i: (0, 0)),
        ]
        + [ANY] * len(after),
        out_specs=pl.BlockSpec((ROWS, WSUM), lambda i: (0, 0)),
        compiler_params=params(1),
        cost_estimate=cost(1e7),
        name="wide_sum",
    )(hits, g3, weights, *after)


def narrow_sum_kernel(hits_ref, d_ref, wide_ref, out_ref):
    @pl.when(pl.program_id(0) == 0)
    def _():
        out_ref[...] = wide_ref[...]

    sources = d_ref.shape[0]
    block = hits_ref.shape[2]
    column = lax.broadcasted_iota(jnp.int32, (block, PD), 1)
    pieces = []
    for d in range(sources):
        packed = d_ref[d].astype(jnp.float32)
        pieces += [packed, pltpu.roll(packed, PD - W12, 1)]
    both = jnp.concatenate(pieces, axis=0)
    d1 = jnp.where(column < W1, both, 0.0).astype(jnp.bfloat16)
    d2 = jnp.where((column >= W1) & (column < W12), both, 0.0).astype(jnp.bfloat16)
    out_ref[...] += jnp.dot(unpacked(hits_ref[0]), d1, preferred_element_type=jnp.float32) + jnp.dot(
        unpacked(hits_ref[1]), d2, preferred_element_type=jnp.float32
    )


def narrow_sum(hits, narrow, wide):
    _, words, examples = hits.shape
    sources, half, _ = narrow.shape
    block = 1024
    per = block // (2 * half)
    return pl.pallas_call(
        narrow_sum_kernel,
        out_shape=jax.ShapeDtypeStruct((ROWS, WSUM), jnp.float32),
        grid=(examples // block,),
        in_specs=[
            pl.BlockSpec((2, words, block), lambda i: (0, 0, i)),
            pl.BlockSpec((per, half, 2 * W12), lambda i: (i, 0, 0)),
            pl.BlockSpec((ROWS, PD), lambda i: (0, 0)),
        ],
        out_specs=pl.BlockSpec((ROWS, PD), lambda i: (0, 0)),
        input_output_aliases={2: 0},
        compiler_params=params(1),
        cost_estimate=cost(1e7),
        name="narrow_sum",
    )(hits, narrow, wide)


def swap(x, axis, size, bits):
    return lax.ppermute(x, axis, [(d, d ^ bits) for d in range(size)])


def local(sizes, grad_out, pooled, proj, assign, indices, lengths):
    count, slots, _ = grad_out.shape
    scale = 1.0 / math.sqrt(count * slots)
    n_node, n_local = sizes["node"], sizes["local"]
    n_plane = n_node // 2
    node, loc = lax.axis_index("node"), lax.axis_index("local")

    rows = jnp.broadcast_to(proj[:, :W12], (slots, W12, PD))
    rows = lax.all_to_all(rows, AXES, split_axis=0, concat_axis=0, tiled=True)

    g12, g3, q = permute(assign, grad_out, pooled)
    plane = jnp.arange(n_plane, dtype=jnp.int32) ^ (node // 2)
    lines = jnp.arange(n_local, dtype=jnp.int32) ^ loc
    (sent,) = partial_proj(plane * 2 + 1 - node % 2, lines, q, g12, g3)
    got = swap(sent, "node", n_node, 1)

    g3, rows = lax.optimization_barrier((g3, rows))
    g3_got = lax.all_to_all(g3, AXES, split_axis=0, concat_axis=0, tiled=True)

    kept = partial_proj(plane * 2 + node % 2, lines, q, g12, g3, got)
    arrived = [swap(kept[d], "node", n_node, 2 * d) for d in range(1, n_plane)]

    narrow = narrow_dpool(g12, rows, after=kept[:1])
    hits = count_hits(indices[0].transpose(1, 2, 0), lengths[0].T[:, None, :], after=[narrow])

    narrow_sent, g3_got, hits = lax.optimization_barrier((narrow, g3_got, hits))
    narrow_got = lax.all_to_all(narrow_sent, AXES, split_axis=0, concat_axis=0, tiled=True)
    total = kept[0]
    for term in arrived:
        total = total + term.astype(jnp.float32)
    rounded = total.astype(jnp.bfloat16)
    own, terms = total[:1], [swap(rounded[d : d + 1], "local", n_local, d) for d in range(1, n_local)]

    wide = wide_sum(hits, g3_got.reshape(-1, PD), proj[0], after=[own])
    table_grad = narrow_sum(hits, narrow_got, wide)[None]
    terms, table_grad = lax.optimization_barrier((terms, table_grad))
    proj_grad = sum((term.astype(jnp.float32) for term in terms), own) * scale
    return (table_grad, proj_grad)


def solution(mesh):
    placed = (
        P(AXES, None, None),
        P(AXES, None, None),
        P(AXES, None, None),
        P(),
        P(AXES, None, None, None),
        P(AXES, None, None),
    )
    return jax.shard_map(
        functools.partial(local, dict(mesh.shape)),
        mesh=mesh,
        in_specs=placed,
        out_specs=(P(AXES, None, None), P(AXES, None, None)),
        check_vma=False,
    )
```

```python
import functools
import math

import jax
import jax.numpy as jnp
from jax import lax
from jax.experimental import pallas as pl
from jax.experimental.pallas import tpu as pltpu
from jax.sharding import PartitionSpec as P

ROWS = 512
W1 = 16
W2 = 48
W3 = 192
PD = 128
W12 = W1 + W2
WSUM = W12 + W3
AXES = ("node", "local")
EB = 8
STEP = 32
MIB = 1024 * 1024


def params(grid):
    return pltpu.CompilerParams(dimension_semantics=("arbitrary",) * grid, vmem_limit_bytes=58 * MIB)


HBM = pl.BlockSpec(memory_space=pltpu.HBM)
ANY = pl.BlockSpec(memory_space=pl.ANY)


def cost(flops):
    return pl.CostEstimate(flops=int(flops), bytes_accessed=1024, transcendentals=0)


def permute_kernel(slots, pieces, assign_ref, grad_ref, pool_ref, rows_ref, *refs):
    outs, (perm_ref, grad_held, pool_held, sems) = refs[:3], refs[3:]
    step = pl.program_id(0)
    sources = ((grad_ref, grad_held), (pool_ref, pool_held))

    def copies(i):
        at = pl.ds(i * STEP, STEP)
        return [
            pltpu.make_async_copy(ref.at[at], held.at[at], sems.at[n, i]) for n, (ref, held) in enumerate(sources)
        ]

    @pl.when(step == 0)
    def _():
        for i in range(grad_ref.shape[0] // STEP):
            for copy in copies(i):
                copy.start()
        width = EB * slots
        lane = lax.broadcasted_iota(jnp.int32, (2 * EB, width), 1)
        row = lax.broadcasted_iota(jnp.int32, (2 * EB, width), 0)
        for s in range(0, slots, 2):
            group = jnp.where(row < EB, assign_ref[s], assign_ref[s + 1])
            hit = lane == (row % EB) * slots + group
            perm_ref[s * EB : (s + 2) * EB, :] = jnp.where(hit, 1.0, 0.0).astype(jnp.bfloat16)

    steps = grad_ref.shape[0] // STEP

    @pl.when(step < steps)
    def _():
        for copy, (_, held), cuts in zip(copies(step), sources, pieces):
            copy.wait()
            width = held.shape[2]
            for start in range(0, STEP, 2 * EB):
                pair = []
                for at in (start, start + EB):
                    block = held[pl.ds(step * STEP + at, EB)].reshape(EB * slots, width)
                    moved = jnp.dot(perm_ref[...], block, preferred_element_type=jnp.float32)
                    pair.append(moved.reshape(slots, EB, width))
                both = jnp.concatenate(pair, axis=1).astype(jnp.bfloat16)
                for n, low, high in cuts:
                    outs[n][:, start : start + 2 * EB, :] = both[:, :, low:high]

    @pl.when(step >= steps)
    def _():
        rows = rows_ref[0, pl.ds(pl.multiple_of((step - steps) * STEP, STEP), STEP)]
        outs[1][...] = jnp.broadcast_to(rows[None], (slots, STEP, PD))


def permute(assign, grad_out, pooled, rows):
    count, slots, _ = grad_out.shape
    widths, lengths = (2 * PD, PD, WSUM), (count, count + rows.shape[1], count)
    pieces = (((0, 0, 2 * PD), (1, 2 * PD, 3 * PD)), ((2, 0, WSUM),))

    def place(length):
        last = length // STEP - 1
        return lambda i, a: (0, jnp.minimum(i, last), 0)

    return pl.pallas_call(
        functools.partial(permute_kernel, slots, pieces),
        out_shape=[
            jax.ShapeDtypeStruct((slots, length, width), jnp.bfloat16) for width, length in zip(widths, lengths)
        ],
        grid_spec=pltpu.PrefetchScalarGridSpec(
            num_scalar_prefetch=1,
            grid=(max(lengths) // STEP,),
            in_specs=[HBM] * 2 + [pl.BlockSpec(rows.shape, lambda i, a: (0, 0, 0))],
            out_specs=[
                pl.BlockSpec((slots, STEP, width), place(length)) for width, length in zip(widths, lengths)
            ],
            scratch_shapes=[
                pltpu.VMEM((EB * slots, EB * slots), jnp.bfloat16),
                pltpu.VMEM(grad_out.shape, jnp.bfloat16),
                pltpu.VMEM(pooled.shape, jnp.bfloat16),
                pltpu.SemaphoreType.DMA((2, count // STEP)),
            ],
        ),
        compiler_params=params(1),
        cost_estimate=cost(1e7),
        name="permute_groups",
    )(assign, grad_out, pooled, rows)


def fetch(ref, held, sems, blocks, pick=lambda i: i, first=0):
    size, rows = held.shape[0] // blocks, pl.ds(first, held.shape[1])
    copies = [
        pltpu.make_async_copy(
            ref.at[pl.ds(pick(i) * size, size), rows], held.at[pl.ds(i * size, size)], sems.at[i]
        )
        for i in range(blocks)
    ]
    for copy in copies:
        copy.start()
    return copies


def narrow_kernel(blocks, g_ref, w_ref, *refs):
    out_ref, g_held, w_held, out_held, g_sems, w_sems, out_sems = refs[-7:]
    weights = fetch(w_ref, w_held, w_sems, 1, first=w_ref.shape[1] - W12)
    loads = fetch(g_ref, g_held, g_sems, blocks)
    slots, count, _ = g_held.shape
    step, half = slots // blocks, count // 2
    column = lax.broadcasted_iota(jnp.int32, (count, W12), 1)
    dims = (((1,), (1,)), ((), ()))
    weights[0].wait()
    stores = []
    for i, load in enumerate(loads):
        load.wait()
        for s in range(i * step, (i + 1) * step):
            w = w_held[s]
            first = lax.dot_general(g_held[s, :, :PD], w, dims, preferred_element_type=jnp.float32)
            second = lax.dot_general(g_held[s, :, PD:], w, dims, preferred_element_type=jnp.float32)
            d = jnp.where(column < W1, first, second)
            out_held[s] = jnp.concatenate([d[:half], d[half:]], axis=1).astype(jnp.bfloat16)
        at = pl.ds(i * step, step)
        stores.append(pltpu.make_async_copy(out_held.at[at], out_ref.at[at], out_sems.at[i]))
        stores[-1].start()
    for store in stores:
        store.wait()


def narrow_dpool(g12, w12, after=()):
    slots, count, _ = g12.shape
    blocks = 4
    shape = (slots, count // 2, 2 * W12)
    return pl.pallas_call(
        functools.partial(narrow_kernel, blocks),
        out_shape=jax.ShapeDtypeStruct(shape, jnp.bfloat16),
        in_specs=[HBM] * 2 + [ANY] * len(after),
        out_specs=HBM,
        scratch_shapes=[
            pltpu.VMEM(g12.shape, jnp.bfloat16),
            pltpu.VMEM((slots, W12, PD), jnp.bfloat16),
            pltpu.VMEM(shape, jnp.bfloat16),
            pltpu.SemaphoreType.DMA((blocks,)),
            pltpu.SemaphoreType.DMA((1,)),
            pltpu.SemaphoreType.DMA((blocks,)),
        ],
        compiler_params=params(0),
        cost_estimate=cost(1e7),
        name="narrow_dpool",
    )(g12, w12, *after)


def partial_kernel(ins, waits, outs, node_ref, line_ref, *refs):
    operands, results = refs[:ins], refs[ins + waits : ins + waits + outs]
    held, out_held = refs[-2 - ins - outs : -2 - outs], refs[-2 - outs : -2]
    in_sems, out_sems = refs[-2:]
    blocks, size = node_ref.shape[0], line_ref.shape[0]
    loads = [
        fetch(ref, at, in_sems.at[n], blocks, (lambda i: node_ref[i]) if n < 3 else (lambda i: i))
        for n, (ref, at) in enumerate(zip(operands, held))
    ]
    stores = []
    for i in range(blocks):
        for copies in loads:
            copies[i].wait()
        if outs == 1:
            at = pl.ds(i * size, size)
            result, out = results[0].at[at], out_held[0].at[at]
        else:
            result, out = results[i], out_held[i]
        for l in range(size):
            slot = i * size + line_ref[l]
            q = held[0][slot].T
            narrow = jnp.dot(q[:W12], held[1][slot], preferred_element_type=jnp.float32)
            wide = jnp.dot(q[W12:], held[2][slot], preferred_element_type=jnp.float32)
            pieces = ((0, W1, narrow[:W1, :PD]), (W1, W12, narrow[W1:, PD:]), (W12, WSUM, wide))
            for start, end, piece in pieces:
                if ins == 4:
                    piece = piece + held[3][i * size + l, start:end]
                out[l, start:end] = piece.astype(out.dtype)
        stores.append(pltpu.make_async_copy(out, result, out_sems.at[i]))
        stores[-1].start()
    for store in stores:
        store.wait()


def partial_proj(nodes, lines, q, g12, g3, other=None, after=()):
    _, count, _ = q.shape
    blocks, size = nodes.shape[0], lines.shape[0]
    every = (blocks * size, WSUM, PD)
    if other is None:
        added, shapes = (), [jax.ShapeDtypeStruct(every, jnp.float32)]
    else:
        kinds = [jnp.float32] + [jnp.bfloat16] * (blocks - 1)
        added, shapes = (other,), [jax.ShapeDtypeStruct((size, WSUM, PD), kind) for kind in kinds]
    ins = 3 + len(added)
    return pl.pallas_call(
        functools.partial(partial_kernel, ins, len(after), len(shapes)),
        out_shape=shapes,
        grid_spec=pltpu.PrefetchScalarGridSpec(
            num_scalar_prefetch=2,
            grid=(1,),
            in_specs=[HBM] * ins + [ANY] * len(after),
            out_specs=[HBM] * len(shapes),
            scratch_shapes=[pltpu.VMEM((blocks * size, count, x.shape[2]), jnp.bfloat16) for x in (q, g12, g3)]
            + [pltpu.VMEM(every, jnp.float32)] * len(added)
            + [pltpu.VMEM(x.shape, x.dtype) for x in shapes]
            + [pltpu.SemaphoreType.DMA((ins, blocks)), pltpu.SemaphoreType.DMA((blocks,))],
        ),
        compiler_params=params(1),
        cost_estimate=cost(1e7),
        name="partial_proj",
    )(nodes, lines, q, g12, g3, *added, *after)


def count_kernel(index_ref, length_ref, *refs):
    out_ref = refs[-1]
    bag, block = index_ref.shape[1], index_ref.shape[2]
    lanes, chunk, low = 256, 16, ROWS // 8

    def one(i, carry):
        at = pl.ds(pl.multiple_of(i * lanes, lanes), lanes)
        index = index_ref[0, :, at]
        which = lax.broadcasted_iota(jnp.int32, (bag, lanes), 0)
        key = jnp.where(which < length_ref[0, :, at], index & (low - 1), -1)
        unit = jnp.left_shift(jnp.int32(1), jnp.right_shift(index, 6) * 4)
        ids = lax.broadcasted_iota(jnp.int32, (chunk, lanes), 0)
        for c in range(low // chunk):
            total = jnp.zeros((chunk, lanes), jnp.int32)
            for j in range(bag):
                total = total + jnp.where(key[j : j + 1] == ids + c * chunk, unit[j : j + 1], 0)
            out_ref[0, c * chunk : (c + 1) * chunk, at] = total
        return carry

    lax.fori_loop(0, block // lanes, one, 0)


def count_hits(lookups, counts, after=()):
    tables, bag, examples = lookups.shape
    block = 4096
    return pl.pallas_call(
        count_kernel,
        out_shape=jax.ShapeDtypeStruct((tables, ROWS // 8, examples), jnp.int32),
        grid=(tables, examples // block),
        in_specs=[
            pl.BlockSpec((1, bag, block), lambda k, i: (k, 0, i)),
            pl.BlockSpec((1, 1, block), lambda k, i: (k, 0, i)),
        ]
        + [ANY] * len(after),
        out_specs=pl.BlockSpec((1, ROWS // 8, block), lambda k, i: (k, 0, i)),
        compiler_params=params(2),
        cost_estimate=cost(1e7),
        name="count_hits",
    )(lookups, counts, *after)


def unpacked(words):
    rows = [lax.shift_right_logical(words, jnp.int32(4 * n)) & 15 for n in range(8)]
    return jnp.concatenate([r.astype(jnp.float32).astype(jnp.bfloat16) for r in rows], axis=0)


def wide_kernel(hits_ref, g_ref, w_ref, *refs):
    out_ref = refs[-1]

    @pl.when(pl.program_id(0) == 0)
    def _():
        out_ref[...] = jnp.zeros_like(out_ref)

    block = hits_ref.shape[2]
    column = lax.broadcasted_iota(jnp.int32, (block, WSUM), 1)
    d = lax.dot_general(g_ref[...].reshape(block, PD), w_ref[...], (((1,), (1,)), ((), ())), preferred_element_type=jnp.float32)
    d = jnp.where(column < W12, 0.0, d).astype(jnp.bfloat16)
    out_ref[...] += jnp.dot(unpacked(hits_ref[0]), d, preferred_element_type=jnp.float32)


def wide_sum(hits, g3, weights, after=()):
    _, words, examples = hits.shape
    block = 1024
    count = examples // g3.shape[0]
    return pl.pallas_call(
        wide_kernel,
        out_shape=jax.ShapeDtypeStruct((ROWS, WSUM), jnp.float32),
        grid=(examples // block,),
        in_specs=[
            pl.BlockSpec((1, words, block), lambda i: (2, 0, i)),
            pl.BlockSpec((block // count, count, PD), lambda i: (i, 0, 0)),
            pl.BlockSpec((WSUM, PD), lambda i: (0, 0)),
        ]
        + [ANY] * len(after),
        out_specs=pl.BlockSpec((ROWS, WSUM), lambda i: (0, 0)),
        compiler_params=params(1),
        cost_estimate=cost(1e7),
        name="wide_sum",
    )(hits, g3, weights, *after)


def narrow_sum_kernel(hits_ref, d_ref, wide_ref, out_ref):
    @pl.when(pl.program_id(0) == 0)
    def _():
        out_ref[...] = wide_ref[...]

    sources = d_ref.shape[0]
    block = hits_ref.shape[2]
    column = lax.broadcasted_iota(jnp.int32, (block, PD), 1)
    pieces = []
    for d in range(sources):
        packed = d_ref[d].astype(jnp.float32)
        pieces += [packed, pltpu.roll(packed, PD - W12, 1)]
    both = jnp.concatenate(pieces, axis=0)
    d1 = jnp.where(column < W1, both, 0.0).astype(jnp.bfloat16)
    d2 = jnp.where((column >= W1) & (column < W12), both, 0.0).astype(jnp.bfloat16)
    out_ref[...] += jnp.dot(unpacked(hits_ref[0]), d1, preferred_element_type=jnp.float32) + jnp.dot(
        unpacked(hits_ref[1]), d2, preferred_element_type=jnp.float32
    )


def narrow_sum(hits, narrow, wide):
    _, words, examples = hits.shape
    sources, half, _ = narrow.shape
    block = 1024
    per = block // (2 * half)
    return pl.pallas_call(
        narrow_sum_kernel,
        out_shape=jax.ShapeDtypeStruct((ROWS, WSUM), jnp.float32),
        grid=(examples // block,),
        in_specs=[
            pl.BlockSpec((2, words, block), lambda i: (0, 0, i)),
            pl.BlockSpec((per, half, 2 * W12), lambda i: (i, 0, 0)),
            pl.BlockSpec((ROWS, PD), lambda i: (0, 0)),
        ],
        out_specs=pl.BlockSpec((ROWS, PD), lambda i: (0, 0)),
        input_output_aliases={2: 0},
        compiler_params=params(1),
        cost_estimate=cost(1e7),
        name="narrow_sum",
    )(hits, narrow, wide)


def swap(x, axis, size, bits):
    return lax.ppermute(x, axis, [(d, d ^ bits) for d in range(size)])


def local(sizes, grad_out, pooled, proj, assign, indices, lengths):
    count, slots, _ = grad_out.shape
    scale = 1.0 / math.sqrt(count * slots)
    n_node, n_local = sizes["node"], sizes["local"]
    n_plane = n_node // 2
    node, loc = lax.axis_index("node"), lax.axis_index("local")

    g12, g3, q = permute(assign, grad_out, pooled, proj[:, :W12])
    g3_got = lax.all_to_all(g3, AXES, split_axis=0, concat_axis=0, tiled=True)

    plane = jnp.arange(n_plane, dtype=jnp.int32) ^ (node // 2)
    lines = jnp.arange(n_local, dtype=jnp.int32) ^ loc
    (sent,) = partial_proj(plane * 2 + 1 - node % 2, lines, q, g12, g3)
    got = swap(sent, "node", n_node, 1)

    kept = partial_proj(plane * 2 + node % 2, lines, q, g12, g3, got)
    arrived = [swap(kept[d], "node", n_node, 2 * d) for d in range(1, n_plane)]

    narrow = narrow_dpool(g12, g3_got)
    hits = count_hits(indices[0].transpose(1, 2, 0), lengths[0].T[:, None, :], after=kept[:1])

    narrow_sent, hits, arrived = lax.optimization_barrier((narrow, hits, arrived))
    narrow_got = lax.all_to_all(narrow_sent, AXES, split_axis=0, concat_axis=0, tiled=True)
    total = kept[0]
    for term in arrived:
        total = total + term.astype(jnp.float32)
    rounded = total.astype(jnp.bfloat16)
    own, terms = total[:1], [swap(rounded[d : d + 1], "local", n_local, d) for d in range(1, n_local)]

    wide = wide_sum(hits, g3_got, proj[0], after=[own])
    table_grad = narrow_sum(hits, narrow_got, wide)[None]
    terms, table_grad = lax.optimization_barrier((terms, table_grad))
    proj_grad = sum((term.astype(jnp.float32) for term in terms), own) * scale
    return (table_grad, proj_grad)


def solution(mesh):
    placed = (
        P(AXES, None, None),
        P(AXES, None, None),
        P(AXES, None, None),
        P(),
        P(AXES, None, None, None),
        P(AXES, None, None),
    )
    return jax.shard_map(
        functools.partial(local, dict(mesh.shape)),
        mesh=mesh,
        in_specs=placed,
        out_specs=(P(AXES, None, None), P(AXES, None, None)),
        check_vma=False,
    )
```

```python
import functools
import math

import jax
import jax.numpy as jnp
from jax import lax
from jax.experimental import pallas as pl
from jax.experimental.pallas import tpu as pltpu
from jax.sharding import PartitionSpec as P

ROWS = 512
W1 = 16
W2 = 48
W3 = 192
PD = 128
W12 = W1 + W2
WSUM = W12 + W3
AXES = ("node", "local")
EB = 8
STEP = 32
MIB = 1024 * 1024


def params(grid):
    return pltpu.CompilerParams(dimension_semantics=("arbitrary",) * grid, vmem_limit_bytes=58 * MIB)


HBM = pl.BlockSpec(memory_space=pltpu.HBM)
ANY = pl.BlockSpec(memory_space=pl.ANY)


def cost(flops):
    return pl.CostEstimate(flops=int(flops), bytes_accessed=1024, transcendentals=0)


def permute_kernel(slots, pieces, assign_ref, grad_ref, pool_ref, rows_ref, *refs):
    outs, (perm_ref, grad_held, pool_held, sems) = refs[:3], refs[3:]
    step = pl.program_id(0)
    sources = ((grad_ref, grad_held), (pool_ref, pool_held))

    def copies(i):
        at = pl.ds(i * STEP, STEP)
        return [
            pltpu.make_async_copy(ref.at[at], held.at[at], sems.at[n, i]) for n, (ref, held) in enumerate(sources)
        ]

    @pl.when(step == 0)
    def _():
        for i in range(grad_ref.shape[0] // STEP):
            for copy in copies(i):
                copy.start()
        width = EB * slots
        lane = lax.broadcasted_iota(jnp.int32, (2 * EB, width), 1)
        row = lax.broadcasted_iota(jnp.int32, (2 * EB, width), 0)
        for s in range(0, slots, 2):
            group = jnp.where(row < EB, assign_ref[s], assign_ref[s + 1])
            hit = lane == (row % EB) * slots + group
            perm_ref[s * EB : (s + 2) * EB, :] = jnp.where(hit, 1.0, 0.0).astype(jnp.bfloat16)

    steps = grad_ref.shape[0] // STEP

    @pl.when(step < steps)
    def _():
        for copy, (_, held), cuts in zip(copies(step), sources, pieces):
            copy.wait()
            width = held.shape[2]
            for start in range(0, STEP, 2 * EB):
                pair = []
                for at in (start, start + EB):
                    block = held[pl.ds(step * STEP + at, EB)].reshape(EB * slots, width)
                    moved = jnp.dot(perm_ref[...], block, preferred_element_type=jnp.float32)
                    pair.append(moved.reshape(slots, EB, width))
                both = jnp.concatenate(pair, axis=1).astype(jnp.bfloat16)
                for n, low, high in cuts:
                    outs[n][:, start : start + 2 * EB, :] = both[:, :, low:high]

    @pl.when(step >= steps)
    def _():
        rows = rows_ref[0, pl.ds(pl.multiple_of((step - steps) * STEP, STEP), STEP)]
        outs[1][...] = jnp.broadcast_to(rows[None], (slots, STEP, PD))


def permute(assign, grad_out, pooled, proj):
    count, slots, _ = grad_out.shape
    widths, lengths = (2 * PD, PD, WSUM), (count, count + W12, count)
    pieces = (((0, 0, 2 * PD), (1, 2 * PD, 3 * PD)), ((2, 0, WSUM),))

    def place(length):
        last = length // STEP - 1
        return lambda i, a: (0, jnp.minimum(i, last), 0)

    return pl.pallas_call(
        functools.partial(permute_kernel, slots, pieces),
        out_shape=[
            jax.ShapeDtypeStruct((slots, length, width), jnp.bfloat16) for width, length in zip(widths, lengths)
        ],
        grid_spec=pltpu.PrefetchScalarGridSpec(
            num_scalar_prefetch=1,
            grid=(max(lengths) // STEP,),
            in_specs=[HBM] * 2 + [pl.BlockSpec((1, W12, PD), lambda i, a: (0, 0, 0))],
            out_specs=[
                pl.BlockSpec((slots, STEP, width), place(length)) for width, length in zip(widths, lengths)
            ],
            scratch_shapes=[
                pltpu.VMEM((EB * slots, EB * slots), jnp.bfloat16),
                pltpu.VMEM(grad_out.shape, jnp.bfloat16),
                pltpu.VMEM(pooled.shape, jnp.bfloat16),
                pltpu.SemaphoreType.DMA((2, count // STEP)),
            ],
        ),
        compiler_params=params(1),
        cost_estimate=cost(1e7),
        name="permute_groups",
    )(assign, grad_out, pooled, proj)


def fetch(ref, held, sems, blocks, pick=lambda i: i, first=0):
    size, rows = held.shape[0] // blocks, pl.ds(first, held.shape[1])
    copies = [
        pltpu.make_async_copy(
            ref.at[pl.ds(pick(i) * size, size), rows], held.at[pl.ds(i * size, size)], sems.at[i]
        )
        for i in range(blocks)
    ]
    for copy in copies:
        copy.start()
    return copies


def narrow_kernel(blocks, g_ref, w_ref, *refs):
    out_ref, g_held, w_held, out_held, g_sems, w_sems, out_sems = refs[-7:]
    weights = fetch(w_ref, w_held, w_sems, 1, first=w_ref.shape[1] - W12)
    loads = fetch(g_ref, g_held, g_sems, blocks)
    slots, count, _ = g_held.shape
    step, half = slots // blocks, count // 2
    column = lax.broadcasted_iota(jnp.int32, (count, W12), 1)
    dims = (((1,), (1,)), ((), ()))
    weights[0].wait()
    stores = []
    for i, load in enumerate(loads):
        load.wait()
        for s in range(i * step, (i + 1) * step):
            w = w_held[s]
            first = lax.dot_general(g_held[s, :, :PD], w, dims, preferred_element_type=jnp.float32)
            second = lax.dot_general(g_held[s, :, PD:], w, dims, preferred_element_type=jnp.float32)
            d = jnp.where(column < W1, first, second)
            out_held[s] = jnp.concatenate([d[:half], d[half:]], axis=1).astype(jnp.bfloat16)
        at = pl.ds(i * step, step)
        stores.append(pltpu.make_async_copy(out_held.at[at], out_ref.at[at], out_sems.at[i]))
        stores[-1].start()
    for store in stores:
        store.wait()


def narrow_dpool(g12, w12, after=()):
    slots, count, _ = g12.shape
    blocks = 4
    shape = (slots, count // 2, 2 * W12)
    return pl.pallas_call(
        functools.partial(narrow_kernel, blocks),
        out_shape=jax.ShapeDtypeStruct(shape, jnp.bfloat16),
        in_specs=[HBM] * 2 + [ANY] * len(after),
        out_specs=HBM,
        scratch_shapes=[
            pltpu.VMEM(g12.shape, jnp.bfloat16),
            pltpu.VMEM((slots, W12, PD), jnp.bfloat16),
            pltpu.VMEM(shape, jnp.bfloat16),
            pltpu.SemaphoreType.DMA((blocks,)),
            pltpu.SemaphoreType.DMA((1,)),
            pltpu.SemaphoreType.DMA((blocks,)),
        ],
        compiler_params=params(0),
        cost_estimate=cost(1e7),
        name="narrow_dpool",
    )(g12, w12, *after)


def partial_kernel(ins, waits, outs, node_ref, line_ref, *refs):
    operands, results = refs[:ins], refs[ins + waits : ins + waits + outs]
    held, out_held = refs[-2 - ins - outs : -2 - outs], refs[-2 - outs : -2]
    in_sems, out_sems = refs[-2:]
    blocks, size = node_ref.shape[0], line_ref.shape[0]
    loads = [
        fetch(ref, at, in_sems.at[n], blocks, (lambda i: node_ref[i]) if n < 3 else (lambda i: i))
        for n, (ref, at) in enumerate(zip(operands, held))
    ]
    stores = []
    for i in range(blocks):
        for copies in loads:
            copies[i].wait()
        if outs == 1:
            at = pl.ds(i * size, size)
            result, out = results[0].at[at], out_held[0].at[at]
        else:
            result, out = results[i], out_held[i]
        for l in range(size):
            slot = i * size + line_ref[l]
            q = held[0][slot].T
            narrow = jnp.dot(q[:W12], held[1][slot], preferred_element_type=jnp.float32)
            wide = jnp.dot(q[W12:], held[2][slot], preferred_element_type=jnp.float32)
            pieces = ((0, W1, narrow[:W1, :PD]), (W1, W12, narrow[W1:, PD:]), (W12, WSUM, wide))
            for start, end, piece in pieces:
                if ins == 4:
                    piece = piece + held[3][i * size + l, start:end]
                out[l, start:end] = piece.astype(out.dtype)
        stores.append(pltpu.make_async_copy(out, result, out_sems.at[i]))
        stores[-1].start()
    for store in stores:
        store.wait()


def partial_proj(nodes, lines, q, g12, g3, other=None, after=()):
    _, count, _ = q.shape
    blocks, size = nodes.shape[0], lines.shape[0]
    every = (blocks * size, WSUM, PD)
    if other is None:
        added, shapes = (), [jax.ShapeDtypeStruct(every, jnp.float32)]
    else:
        kinds = [jnp.float32] + [jnp.bfloat16] * (blocks - 1)
        added, shapes = (other,), [jax.ShapeDtypeStruct((size, WSUM, PD), kind) for kind in kinds]
    ins = 3 + len(added)
    return pl.pallas_call(
        functools.partial(partial_kernel, ins, len(after), len(shapes)),
        out_shape=shapes,
        grid_spec=pltpu.PrefetchScalarGridSpec(
            num_scalar_prefetch=2,
            grid=(1,),
            in_specs=[HBM] * ins + [ANY] * len(after),
            out_specs=[HBM] * len(shapes),
            scratch_shapes=[pltpu.VMEM((blocks * size, count, x.shape[2]), jnp.bfloat16) for x in (q, g12, g3)]
            + [pltpu.VMEM(every, jnp.float32)] * len(added)
            + [pltpu.VMEM(x.shape, x.dtype) for x in shapes]
            + [pltpu.SemaphoreType.DMA((ins, blocks)), pltpu.SemaphoreType.DMA((blocks,))],
        ),
        compiler_params=params(1),
        cost_estimate=cost(1e7),
        name="partial_proj",
    )(nodes, lines, q, g12, g3, *added, *after)


def count_kernel(index_ref, length_ref, *refs):
    out_ref = refs[-1]
    bag, block = index_ref.shape[1], index_ref.shape[2]
    lanes, chunk, low = 256, 16, ROWS // 8

    def one(i, carry):
        at = pl.ds(pl.multiple_of(i * lanes, lanes), lanes)
        index = index_ref[0, :, at]
        which = lax.broadcasted_iota(jnp.int32, (bag, lanes), 0)
        key = jnp.where(which < length_ref[0, :, at], index & (low - 1), -1)
        unit = jnp.left_shift(jnp.int32(1), jnp.right_shift(index, 6) * 4)
        ids = lax.broadcasted_iota(jnp.int32, (chunk, lanes), 0)
        for c in range(low // chunk):
            total = jnp.zeros((chunk, lanes), jnp.int32)
            for j in range(bag):
                total = total + jnp.where(key[j : j + 1] == ids + c * chunk, unit[j : j + 1], 0)
            out_ref[0, c * chunk : (c + 1) * chunk, at] = total
        return carry

    lax.fori_loop(0, block // lanes, one, 0)


def count_hits(lookups, counts, after=()):
    tables, bag, examples = lookups.shape
    block = 4096
    return pl.pallas_call(
        count_kernel,
        out_shape=jax.ShapeDtypeStruct((tables, ROWS // 8, examples), jnp.int32),
        grid=(tables, examples // block),
        in_specs=[
            pl.BlockSpec((1, bag, block), lambda k, i: (k, 0, i)),
            pl.BlockSpec((1, 1, block), lambda k, i: (k, 0, i)),
        ]
        + [ANY] * len(after),
        out_specs=pl.BlockSpec((1, ROWS // 8, block), lambda k, i: (k, 0, i)),
        compiler_params=params(2),
        cost_estimate=cost(1e7),
        name="count_hits",
    )(lookups, counts, *after)


def unpacked(words):
    rows = [lax.shift_right_logical(words, jnp.int32(4 * n)) & 15 for n in range(8)]
    return jnp.concatenate([r.astype(jnp.float32).astype(jnp.bfloat16) for r in rows], axis=0)


def wide_kernel(hits_ref, g_ref, w_ref, *refs):
    out_ref = refs[-1]

    @pl.when(pl.program_id(0) == 0)
    def _():
        out_ref[...] = jnp.zeros_like(out_ref)

    block = hits_ref.shape[2]
    column = lax.broadcasted_iota(jnp.int32, (block, WSUM), 1)
    d = lax.dot_general(g_ref[...].reshape(block, PD), w_ref[...], (((1,), (1,)), ((), ())), preferred_element_type=jnp.float32)
    d = jnp.where(column < W12, 0.0, d).astype(jnp.bfloat16)
    out_ref[...] += jnp.dot(unpacked(hits_ref[0]), d, preferred_element_type=jnp.float32)


def wide_sum(hits, g3, weights, after=()):
    _, words, examples = hits.shape
    block = 1024
    count = examples // g3.shape[0]
    return pl.pallas_call(
        wide_kernel,
        out_shape=jax.ShapeDtypeStruct((ROWS, WSUM), jnp.float32),
        grid=(examples // block,),
        in_specs=[
            pl.BlockSpec((1, words, block), lambda i: (2, 0, i)),
            pl.BlockSpec((block // count, count, PD), lambda i: (i, 0, 0)),
            pl.BlockSpec((WSUM, PD), lambda i: (0, 0)),
        ]
        + [ANY] * len(after),
        out_specs=pl.BlockSpec((ROWS, WSUM), lambda i: (0, 0)),
        compiler_params=params(1),
        cost_estimate=cost(1e7),
        name="wide_sum",
    )(hits, g3, weights, *after)


def narrow_sum_kernel(hits_ref, d_ref, wide_ref, out_ref):
    @pl.when(pl.program_id(0) == 0)
    def _():
        out_ref[...] = wide_ref[...]

    sources = d_ref.shape[0]
    block = hits_ref.shape[2]
    column = lax.broadcasted_iota(jnp.int32, (block, PD), 1)
    pieces = []
    for d in range(sources):
        packed = d_ref[d].astype(jnp.float32)
        pieces += [packed, pltpu.roll(packed, PD - W12, 1)]
    both = jnp.concatenate(pieces, axis=0)
    d1 = jnp.where(column < W1, both, 0.0).astype(jnp.bfloat16)
    d2 = jnp.where((column >= W1) & (column < W12), both, 0.0).astype(jnp.bfloat16)
    out_ref[...] += jnp.dot(unpacked(hits_ref[0]), d1, preferred_element_type=jnp.float32) + jnp.dot(
        unpacked(hits_ref[1]), d2, preferred_element_type=jnp.float32
    )


def narrow_sum(hits, narrow, wide):
    _, words, examples = hits.shape
    sources, half, _ = narrow.shape
    block = 1024
    per = block // (2 * half)
    return pl.pallas_call(
        narrow_sum_kernel,
        out_shape=jax.ShapeDtypeStruct((ROWS, WSUM), jnp.float32),
        grid=(examples // block,),
        in_specs=[
            pl.BlockSpec((2, words, block), lambda i: (0, 0, i)),
            pl.BlockSpec((per, half, 2 * W12), lambda i: (i, 0, 0)),
            pl.BlockSpec((ROWS, PD), lambda i: (0, 0)),
        ],
        out_specs=pl.BlockSpec((ROWS, PD), lambda i: (0, 0)),
        input_output_aliases={2: 0},
        compiler_params=params(1),
        cost_estimate=cost(1e7),
        name="narrow_sum",
    )(hits, narrow, wide)


def swap(x, axis, size, bits):
    return lax.ppermute(x, axis, [(d, d ^ bits) for d in range(size)])


def local(sizes, grad_out, pooled, proj, assign, indices, lengths):
    count, slots, _ = grad_out.shape
    scale = 1.0 / math.sqrt(count * slots)
    n_node, n_local = sizes["node"], sizes["local"]
    n_plane = n_node // 2
    node, loc = lax.axis_index("node"), lax.axis_index("local")

    g12, g3, q = permute(assign, grad_out, pooled, proj)
    g3_got = lax.all_to_all(g3, AXES, split_axis=0, concat_axis=0, tiled=True)

    plane = jnp.arange(n_plane, dtype=jnp.int32) ^ (node // 2)
    lines = jnp.arange(n_local, dtype=jnp.int32) ^ loc
    (sent,) = partial_proj(plane * 2 + 1 - node % 2, lines, q, g12, g3)
    got = swap(sent, "node", n_node, 1)

    kept = partial_proj(plane * 2 + node % 2, lines, q, g12, g3, got)
    arrived = [swap(kept[d], "node", n_node, 2 * d) for d in range(1, n_plane)]

    total = kept[0]
    for term in arrived:
        total = total + term.astype(jnp.float32)
    rounded = total.astype(jnp.bfloat16)
    terms = [swap(rounded[d : d + 1], "local", n_local, d) for d in range(1, n_local)]
    g3_got, terms = lax.optimization_barrier((g3_got, terms))
    proj_grad = sum((term.astype(jnp.float32) for term in terms), total[:1]) * scale

    narrow = narrow_dpool(g12, g3_got)
    narrow_got = lax.all_to_all(narrow, AXES, split_axis=0, concat_axis=0, tiled=True)
    hits = count_hits(indices[0].transpose(1, 2, 0), lengths[0].T[:, None, :], after=[narrow])
    wide = wide_sum(hits, g3_got, proj[0], after=[proj_grad])
    table_grad = narrow_sum(hits, narrow_got, wide)[None]
    return (table_grad, proj_grad)


def solution(mesh):
    placed = (
        P(AXES, None, None),
        P(AXES, None, None),
        P(AXES, None, None),
        P(),
        P(AXES, None, None, None),
        P(AXES, None, None),
    )
    return jax.shard_map(
        functools.partial(local, dict(mesh.shape)),
        mesh=mesh,
        in_specs=placed,
        out_specs=(P(AXES, None, None), P(AXES, None, None)),
        check_vma=False,
    )
```

```python
import functools
import math

import jax
import jax.numpy as jnp
from jax import lax
from jax.experimental import pallas as pl
from jax.experimental.pallas import tpu as pltpu
from jax.sharding import PartitionSpec as P

ROWS = 512
W1 = 16
W2 = 48
W3 = 192
PD = 128
W12 = W1 + W2
WSUM = W12 + W3
AXES = ("node", "local")
EB = 8
STEP = 32
MIB = 1024 * 1024


def params(grid):
    return pltpu.CompilerParams(dimension_semantics=("arbitrary",) * grid, vmem_limit_bytes=58 * MIB)


HBM = pl.BlockSpec(memory_space=pltpu.HBM)
ANY = pl.BlockSpec(memory_space=pl.ANY)


def cost(flops):
    return pl.CostEstimate(flops=int(flops), bytes_accessed=1024, transcendentals=0)


def permute_kernel(slots, pieces, assign_ref, grad_ref, pool_ref, *refs):
    outs, (perm_ref, grad_held, pool_held, sems) = refs[:3], refs[3:]
    step = pl.program_id(0)
    sources = ((grad_ref, grad_held), (pool_ref, pool_held))

    def copies(i):
        at = pl.ds(i * STEP, STEP)
        return [
            pltpu.make_async_copy(ref.at[at], held.at[at], sems.at[n, i]) for n, (ref, held) in enumerate(sources)
        ]

    @pl.when(step == 0)
    def _():
        for i in range(grad_ref.shape[0] // STEP):
            for copy in copies(i):
                copy.start()
        width = EB * slots
        lane = lax.broadcasted_iota(jnp.int32, (2 * EB, width), 1)
        row = lax.broadcasted_iota(jnp.int32, (2 * EB, width), 0)
        for s in range(0, slots, 2):
            group = jnp.where(row < EB, assign_ref[s], assign_ref[s + 1])
            hit = lane == (row % EB) * slots + group
            perm_ref[s * EB : (s + 2) * EB, :] = jnp.where(hit, 1.0, 0.0).astype(jnp.bfloat16)

    for copy, (_, held), cuts in zip(copies(step), sources, pieces):
        copy.wait()
        width = held.shape[2]
        for start in range(0, STEP, 2 * EB):
            pair = []
            for at in (start, start + EB):
                block = held[pl.ds(step * STEP + at, EB)].reshape(EB * slots, width)
                moved = jnp.dot(perm_ref[...], block, preferred_element_type=jnp.float32)
                pair.append(moved.reshape(slots, EB, width))
            both = jnp.concatenate(pair, axis=1).astype(jnp.bfloat16)
            for n, low, high in cuts:
                outs[n][:, start : start + 2 * EB, :] = both[:, :, low:high]


def permute(assign, grad_out, pooled):
    count, slots, _ = grad_out.shape
    widths = (2 * PD, PD, WSUM)
    pieces = (((0, 0, 2 * PD), (1, 2 * PD, 3 * PD)), ((2, 0, WSUM),))
    return pl.pallas_call(
        functools.partial(permute_kernel, slots, pieces),
        out_shape=[jax.ShapeDtypeStruct((slots, count, width), jnp.bfloat16) for width in widths],
        grid_spec=pltpu.PrefetchScalarGridSpec(
            num_scalar_prefetch=1,
            grid=(count // STEP,),
            in_specs=[HBM] * 2,
            out_specs=[pl.BlockSpec((slots, STEP, width), lambda i, a: (0, i, 0)) for width in widths],
            scratch_shapes=[
                pltpu.VMEM((EB * slots, EB * slots), jnp.bfloat16),
                pltpu.VMEM(grad_out.shape, jnp.bfloat16),
                pltpu.VMEM(pooled.shape, jnp.bfloat16),
                pltpu.SemaphoreType.DMA((2, count // STEP)),
            ],
        ),
        compiler_params=params(1),
        cost_estimate=cost(1e7),
        name="permute_groups",
    )(assign, grad_out, pooled)


def fetch(ref, held, sems, blocks, pick=lambda i: i):
    size = held.shape[0] // blocks
    copies = [
        pltpu.make_async_copy(ref.at[pl.ds(pick(i) * size, size)], held.at[pl.ds(i * size, size)], sems.at[i])
        for i in range(blocks)
    ]
    for copy in copies:
        copy.start()
    return copies


def narrow_kernel(blocks, place_ref, g_ref, w_ref, *refs):
    out_ref, g_held, w_held, out_held, g_sems, w_sems, out_sems = refs[-7:]
    weights = fetch(w_ref, w_held, w_sems, 1)
    loads = fetch(g_ref, g_held, g_sems, blocks)
    slots, count, _ = g_held.shape
    step, half = slots // blocks, count // 2
    column = lax.broadcasted_iota(jnp.int32, (count, W12), 1)
    dims = (((1,), (1,)), ((), ()))
    weights[0].wait()
    stores = []
    for i, load in enumerate(loads):
        load.wait()
        for s in range(i * step, (i + 1) * step):
            w = w_held[place_ref[s]]
            first = lax.dot_general(g_held[s, :, :PD], w, dims, preferred_element_type=jnp.float32)
            second = lax.dot_general(g_held[s, :, PD:], w, dims, preferred_element_type=jnp.float32)
            d = jnp.where(column < W1, first, second)
            out_held[s] = jnp.concatenate([d[:half], d[half:]], axis=1).astype(jnp.bfloat16)
        at = pl.ds(i * step, step)
        stores.append(pltpu.make_async_copy(out_held.at[at], out_ref.at[at], out_sems.at[i]))
        stores[-1].start()
    for store in stores:
        store.wait()


def narrow_dpool(place, g12, w12, after=()):
    slots, count, _ = g12.shape
    blocks = 4
    shape = (slots, count // 2, 2 * W12)
    return pl.pallas_call(
        functools.partial(narrow_kernel, blocks),
        out_shape=jax.ShapeDtypeStruct(shape, jnp.bfloat16),
        grid_spec=pltpu.PrefetchScalarGridSpec(
            num_scalar_prefetch=1,
            grid=(1,),
            in_specs=[HBM] * 2 + [ANY] * len(after),
            out_specs=HBM,
            scratch_shapes=[
                pltpu.VMEM(g12.shape, jnp.bfloat16),
                pltpu.VMEM(w12.shape, jnp.bfloat16),
                pltpu.VMEM(shape, jnp.bfloat16),
                pltpu.SemaphoreType.DMA((blocks,)),
                pltpu.SemaphoreType.DMA((1,)),
                pltpu.SemaphoreType.DMA((blocks,)),
            ],
        ),
        compiler_params=params(1),
        cost_estimate=cost(1e7),
        name="narrow_dpool",
    )(place, g12, w12, *after)


def partial_kernel(ins, add, node_ref, line_ref, *refs):
    blocks, size = node_ref.shape[0], line_ref.shape[0]
    added = blocks * add
    operands, others, results = refs[:ins], refs[ins : ins + added], refs[ins + added : ins + added + blocks]
    refs = refs[ins + added + blocks :]
    held, other_held, out_held = refs[:ins], refs[ins : ins + added], refs[ins + added : ins + added + blocks]
    in_sems, other_sems, out_sems = refs[-3:]
    loads = [fetch(ref, at, in_sems.at[n], blocks, lambda i: node_ref[i]) for n, (ref, at) in enumerate(zip(operands, held))]
    for i in range(added):
        loads.append(pltpu.make_async_copy(others[i], other_held[i], other_sems.at[i]))
        loads[-1].start()
    stores = []
    for i in range(blocks):
        for copies in loads[:ins]:
            copies[i].wait()
        if add:
            loads[ins + i].wait()
        for l in range(size):
            slot = i * size + line_ref[l]
            q = held[0][slot].T
            narrow = jnp.dot(q[:W12], held[1][slot], preferred_element_type=jnp.float32)
            wide = jnp.dot(q[W12:], held[2][slot], preferred_element_type=jnp.float32)
            pieces = ((0, W1, narrow[:W1, :PD]), (W1, W12, narrow[W1:, PD:]), (W12, WSUM, wide))
            for start, end, piece in pieces:
                if add:
                    piece = piece + other_held[i][l, start:end]
                out_held[i][l, start:end] = piece.astype(out_held[i].dtype)
        stores.append(pltpu.make_async_copy(out_held[i], results[i], out_sems.at[i]))
        stores[-1].start()
    for store in stores:
        store.wait()


def partial_proj(nodes, lines, q, g12, g3, others=()):
    _, count, _ = q.shape
    blocks, size = nodes.shape[0], lines.shape[0]
    kinds = [jnp.bfloat16 if others and i else jnp.float32 for i in range(blocks)]
    shapes = [jax.ShapeDtypeStruct((size, WSUM, PD), kind) for kind in kinds]
    operands = (q, g12, g3)
    return pl.pallas_call(
        functools.partial(partial_kernel, len(operands), len(others) > 0),
        out_shape=shapes,
        grid_spec=pltpu.PrefetchScalarGridSpec(
            num_scalar_prefetch=2,
            grid=(1,),
            in_specs=[HBM] * (len(operands) + len(others)),
            out_specs=[HBM] * blocks,
            scratch_shapes=[pltpu.VMEM((blocks * size, count, x.shape[2]), jnp.bfloat16) for x in operands]
            + [pltpu.VMEM(x.shape, x.dtype) for x in others]
            + [pltpu.VMEM(x.shape, x.dtype) for x in shapes]
            + [
                pltpu.SemaphoreType.DMA((len(operands), blocks)),
                pltpu.SemaphoreType.DMA((blocks,)),
                pltpu.SemaphoreType.DMA((blocks,)),
            ],
        ),
        compiler_params=params(1),
        cost_estimate=cost(1e7),
        name="partial_proj",
    )(nodes, lines, *operands, *others)


def count_kernel(index_ref, length_ref, *refs):
    out_ref = refs[-1]
    bag, block = index_ref.shape[1], index_ref.shape[2]
    lanes, chunk, low = 256, 16, ROWS // 8

    def one(i, carry):
        at = pl.ds(pl.multiple_of(i * lanes, lanes), lanes)
        index = index_ref[0, :, at]
        which = lax.broadcasted_iota(jnp.int32, (bag, lanes), 0)
        key = jnp.where(which < length_ref[0, :, at], index & (low - 1), -1)
        unit = jnp.left_shift(jnp.int32(1), jnp.right_shift(index, 6) * 4)
        ids = lax.broadcasted_iota(jnp.int32, (chunk, lanes), 0)
        for c in range(low // chunk):
            total = jnp.zeros((chunk, lanes), jnp.int32)
            for j in range(bag):
                total = total + jnp.where(key[j : j + 1] == ids + c * chunk, unit[j : j + 1], 0)
            out_ref[0, c * chunk : (c + 1) * chunk, at] = total
        return carry

    lax.fori_loop(0, block // lanes, one, 0)


def count_hits(lookups, counts, after=()):
    tables, bag, examples = lookups.shape
    block = 4096
    return pl.pallas_call(
        count_kernel,
        out_shape=jax.ShapeDtypeStruct((tables, ROWS // 8, examples), jnp.int32),
        grid=(tables, examples // block),
        in_specs=[
            pl.BlockSpec((1, bag, block), lambda k, i: (k, 0, i)),
            pl.BlockSpec((1, 1, block), lambda k, i: (k, 0, i)),
        ]
        + [ANY] * len(after),
        out_specs=pl.BlockSpec((1, ROWS // 8, block), lambda k, i: (k, 0, i)),
        compiler_params=params(2),
        cost_estimate=cost(1e7),
        name="count_hits",
    )(lookups, counts, *after)


def unpacked(words):
    rows = [lax.shift_right_logical(words, jnp.int32(4 * n)) & 15 for n in range(8)]
    return jnp.concatenate([r.astype(jnp.float32).astype(jnp.bfloat16) for r in rows], axis=0)


def wide_kernel(hits_ref, g_ref, w_ref, *refs):
    out_ref = refs[-1]

    @pl.when(pl.program_id(0) == 0)
    def _():
        out_ref[...] = jnp.zeros_like(out_ref)

    block = g_ref.shape[0]
    column = lax.broadcasted_iota(jnp.int32, (block, WSUM), 1)
    d = lax.dot_general(g_ref[...], w_ref[...], (((1,), (1,)), ((), ())), preferred_element_type=jnp.float32)
    d = jnp.where(column < W12, 0.0, d).astype(jnp.bfloat16)
    out_ref[...] += jnp.dot(unpacked(hits_ref[0]), d, preferred_element_type=jnp.float32)


def wide_sum(hits, g3, weights, after=()):
    _, words, examples = hits.shape
    block = 1024
    return pl.pallas_call(
        wide_kernel,
        out_shape=jax.ShapeDtypeStruct((ROWS, WSUM), jnp.float32),
        grid=(examples // block,),
        in_specs=[
            pl.BlockSpec((1, words, block), lambda i: (2, 0, i)),
            pl.BlockSpec((block, PD), lambda i: (i, 0)),
            pl.BlockSpec((WSUM, PD), lambda i: (0, 0)),
        ]
        + [ANY] * len(after),
        out_specs=pl.BlockSpec((ROWS, WSUM), lambda i: (0, 0)),
        compiler_params=params(1),
        cost_estimate=cost(1e7),
        name="wide_sum",
    )(hits, g3, weights, *after)


def narrow_sum_kernel(hits_ref, d_ref, wide_ref, *refs):
    out_ref = refs[-1]

    @pl.when(pl.program_id(0) == 0)
    def _():
        out_ref[...] = wide_ref[...]

    sources = d_ref.shape[0]
    block = hits_ref.shape[2]
    column = lax.broadcasted_iota(jnp.int32, (block, PD), 1)
    pieces = []
    for d in range(sources):
        packed = d_ref[d].astype(jnp.float32)
        pieces += [packed, pltpu.roll(packed, PD - W12, 1)]
    both = jnp.concatenate(pieces, axis=0)
    d1 = jnp.where(column < W1, both, 0.0).astype(jnp.bfloat16)
    d2 = jnp.where((column >= W1) & (column < W12), both, 0.0).astype(jnp.bfloat16)
    out_ref[...] += jnp.dot(unpacked(hits_ref[0]), d1, preferred_element_type=jnp.float32) + jnp.dot(
        unpacked(hits_ref[1]), d2, preferred_element_type=jnp.float32
    )


def narrow_sum(hits, narrow, wide, after=()):
    _, words, examples = hits.shape
    sources, half, _ = narrow.shape
    block = 1024
    per = block // (2 * half)
    return pl.pallas_call(
        narrow_sum_kernel,
        out_shape=jax.ShapeDtypeStruct((ROWS, WSUM), jnp.float32),
        grid=(examples // block,),
        in_specs=[
            pl.BlockSpec((2, words, block), lambda i: (0, 0, i)),
            pl.BlockSpec((per, half, 2 * W12), lambda i: (i, 0, 0)),
            pl.BlockSpec((ROWS, PD), lambda i: (0, 0)),
        ]
        + [ANY] * len(after),
        out_specs=pl.BlockSpec((ROWS, PD), lambda i: (0, 0)),
        input_output_aliases={2: 0},
        compiler_params=params(1),
        cost_estimate=cost(1e7),
        name="narrow_sum",
    )(hits, narrow, wide, *after)


def swap(x, axis, size, bits):
    return lax.ppermute(x, axis, [(d, d ^ bits) for d in range(size)])


def local(sizes, grad_out, pooled, proj, assign, indices, lengths):
    count, slots, _ = grad_out.shape
    scale = 1.0 / math.sqrt(count * slots)
    n_node, n_local = sizes["node"], sizes["local"]
    n_plane = n_node // 2
    node, loc = lax.axis_index("node"), lax.axis_index("local")

    rows = proj[:, :W12]
    rows = jnp.concatenate([rows] + [swap(rows, "local", n_local, d) for d in range(1, n_local)])
    g12, g3, q = permute(assign, grad_out, pooled)
    rows, g3 = lax.optimization_barrier((rows, g3))
    g3_got = lax.all_to_all(g3, AXES, split_axis=0, concat_axis=0, tiled=True)
    rows = jnp.concatenate([rows] + [swap(rows, "node", n_node, 2 * d) for d in range(1, n_plane)])
    rows = jnp.concatenate([rows, swap(rows, "node", n_node, 1)])
    slot = jnp.arange(slots, dtype=jnp.int32)
    slot_node = slot // n_local ^ node
    slot_place = slot_node % 2 * (slots // 2) + slot_node // 2 * n_local + (slot % n_local ^ loc)
    narrow = narrow_dpool(slot_place, g12, rows)

    plane = jnp.arange(n_plane, dtype=jnp.int32) ^ (node // 2)
    lines = jnp.arange(n_local, dtype=jnp.int32) ^ loc
    sent = partial_proj(plane * 2 + 1 - node % 2, lines, q, g12, g3)
    got = [swap(x, "node", n_node, 1) for x in sent]
    kept = partial_proj(plane * 2 + node % 2, lines, q, g12, g3, got)
    arrived = [swap(kept[d], "node", n_node, 2 * d) for d in range(1, n_plane)]

    narrow, g3_got, arrived = lax.optimization_barrier((narrow, g3_got, arrived))
    narrow_got = lax.all_to_all(narrow, AXES, split_axis=0, concat_axis=0, tiled=True)
    total = kept[0]
    for term in arrived:
        total = total + term.astype(jnp.float32)
    rounded = total.astype(jnp.bfloat16)
    own, terms = total[:1], [swap(rounded[d : d + 1], "local", n_local, d) for d in range(1, n_local)]
    proj_grad = sum((term.astype(jnp.float32) for term in terms), own) * scale

    hits = count_hits(indices[0].transpose(1, 2, 0), lengths[0].T[:, None, :], after=[narrow])
    wide = wide_sum(hits, g3_got.reshape(-1, PD), proj[0], after=[own])
    table_grad = narrow_sum(hits, narrow_got, wide, after=[proj_grad])[None]
    return (table_grad, proj_grad)


def solution(mesh):
    placed = (
        P(AXES, None, None),
        P(AXES, None, None),
        P(AXES, None, None),
        P(),
        P(AXES, None, None, None),
        P(AXES, None, None),
    )
    return jax.shard_map(
        functools.partial(local, dict(mesh.shape)),
        mesh=mesh,
        in_specs=placed,
        out_specs=(P(AXES, None, None), P(AXES, None, None)),
        check_vma=False,
    )
```

```python
import functools
import math

import jax
import jax.numpy as jnp
from jax import lax
from jax.experimental import pallas as pl
from jax.experimental.pallas import tpu as pltpu
from jax.sharding import PartitionSpec as P

ROWS = 512
W1 = 16
W2 = 48
W3 = 192
PD = 128
W12 = W1 + W2
WSUM = W12 + W3
AXES = ("node", "local")
EB = 8
STEP = 32
MIB = 1024 * 1024


def params(grid):
    return pltpu.CompilerParams(dimension_semantics=("arbitrary",) * grid, vmem_limit_bytes=58 * MIB)


HBM = pl.BlockSpec(memory_space=pltpu.HBM)
ANY = pl.BlockSpec(memory_space=pl.ANY)


def cost(flops):
    return pl.CostEstimate(flops=int(flops), bytes_accessed=1024, transcendentals=0)


def permute_kernel(slots, pieces, assign_ref, grad_ref, pool_ref, *refs):
    outs, (perm_ref, grad_held, pool_held, sems) = refs[:3], refs[3:]
    step = pl.program_id(0)
    sources = ((grad_ref, grad_held), (pool_ref, pool_held))

    def copies(i):
        at = pl.ds(i * STEP, STEP)
        return [
            pltpu.make_async_copy(ref.at[at], held.at[at], sems.at[n, i]) for n, (ref, held) in enumerate(sources)
        ]

    @pl.when(step == 0)
    def _():
        for i in range(grad_ref.shape[0] // STEP):
            for copy in copies(i):
                copy.start()
        width = EB * slots
        lane = lax.broadcasted_iota(jnp.int32, (2 * EB, width), 1)
        row = lax.broadcasted_iota(jnp.int32, (2 * EB, width), 0)
        for s in range(0, slots, 2):
            group = jnp.where(row < EB, assign_ref[s], assign_ref[s + 1])
            hit = lane == (row % EB) * slots + group
            perm_ref[s * EB : (s + 2) * EB, :] = jnp.where(hit, 1.0, 0.0).astype(jnp.bfloat16)

    for copy, (_, held), cuts in zip(copies(step), sources, pieces):
        copy.wait()
        width = held.shape[2]
        for start in range(0, STEP, 2 * EB):
            pair = []
            for at in (start, start + EB):
                block = held[pl.ds(step * STEP + at, EB)].reshape(EB * slots, width)
                moved = jnp.dot(perm_ref[...], block, preferred_element_type=jnp.float32)
                pair.append(moved.reshape(slots, EB, width))
            both = jnp.concatenate(pair, axis=1).astype(jnp.bfloat16)
            for n, low, high in cuts:
                outs[n][:, start : start + 2 * EB, :] = both[:, :, low:high]


def permute(assign, grad_out, pooled):
    count, slots, _ = grad_out.shape
    widths = (2 * PD, PD, WSUM)
    pieces = (((0, 0, 2 * PD), (1, 2 * PD, 3 * PD)), ((2, 0, WSUM),))
    return pl.pallas_call(
        functools.partial(permute_kernel, slots, pieces),
        out_shape=[jax.ShapeDtypeStruct((slots, count, width), jnp.bfloat16) for width in widths],
        grid_spec=pltpu.PrefetchScalarGridSpec(
            num_scalar_prefetch=1,
            grid=(count // STEP,),
            in_specs=[HBM] * 2,
            out_specs=[pl.BlockSpec((slots, STEP, width), lambda i, a: (0, i, 0)) for width in widths],
            scratch_shapes=[
                pltpu.VMEM((EB * slots, EB * slots), jnp.bfloat16),
                pltpu.VMEM(grad_out.shape, jnp.bfloat16),
                pltpu.VMEM(pooled.shape, jnp.bfloat16),
                pltpu.SemaphoreType.DMA((2, count // STEP)),
            ],
        ),
        compiler_params=params(1),
        cost_estimate=cost(1e7),
        name="permute_groups",
    )(assign, grad_out, pooled)


def fetch(ref, held, sems, blocks, pick=lambda i: i):
    size = held.shape[0] // blocks
    copies = [
        pltpu.make_async_copy(ref.at[pl.ds(pick(i) * size, size)], held.at[pl.ds(i * size, size)], sems.at[i])
        for i in range(blocks)
    ]
    for copy in copies:
        copy.start()
    return copies


def narrow_kernel(blocks, place_ref, g_ref, w_ref, *refs):
    out_ref, g_held, w_held, out_held, g_sems, w_sems, out_sems = refs[-7:]
    weights = fetch(w_ref, w_held, w_sems, 1)
    loads = fetch(g_ref, g_held, g_sems, blocks)
    slots, count, _ = g_held.shape
    step, half = slots // blocks, count // 2
    column = lax.broadcasted_iota(jnp.int32, (count, W12), 1)
    dims = (((1,), (1,)), ((), ()))
    weights[0].wait()
    stores = []
    for i, load in enumerate(loads):
        load.wait()
        for s in range(i * step, (i + 1) * step):
            w = w_held[place_ref[s]]
            first = lax.dot_general(g_held[s, :, :PD], w, dims, preferred_element_type=jnp.float32)
            second = lax.dot_general(g_held[s, :, PD:], w, dims, preferred_element_type=jnp.float32)
            d = jnp.where(column < W1, first, second)
            out_held[s] = jnp.concatenate([d[:half], d[half:]], axis=1).astype(jnp.bfloat16)
        at = pl.ds(i * step, step)
        stores.append(pltpu.make_async_copy(out_held.at[at], out_ref.at[at], out_sems.at[i]))
        stores[-1].start()
    for store in stores:
        store.wait()


def narrow_dpool(place, g12, w12, after=()):
    slots, count, _ = g12.shape
    blocks = 4
    shape = (slots, count // 2, 2 * W12)
    return pl.pallas_call(
        functools.partial(narrow_kernel, blocks),
        out_shape=jax.ShapeDtypeStruct(shape, jnp.bfloat16),
        grid_spec=pltpu.PrefetchScalarGridSpec(
            num_scalar_prefetch=1,
            grid=(1,),
            in_specs=[HBM] * 2 + [ANY] * len(after),
            out_specs=HBM,
            scratch_shapes=[
                pltpu.VMEM(g12.shape, jnp.bfloat16),
                pltpu.VMEM(w12.shape, jnp.bfloat16),
                pltpu.VMEM(shape, jnp.bfloat16),
                pltpu.SemaphoreType.DMA((blocks,)),
                pltpu.SemaphoreType.DMA((1,)),
                pltpu.SemaphoreType.DMA((blocks,)),
            ],
        ),
        compiler_params=params(1),
        cost_estimate=cost(1e7),
        name="narrow_dpool",
    )(place, g12, w12, *after)


def partial_kernel(ins, added, results, node_ref, line_ref, *refs):
    blocks, size = node_ref.shape[0], line_ref.shape[0]
    operands, others = refs[:ins], refs[ins : ins + added]
    outs, scratch = refs[-3 - 2 * results - ins - added :][:results], refs[-3 - results - ins - added :]
    held, other_held, out_held = scratch[:ins], scratch[ins : ins + added], scratch[ins + added : -3]
    in_sems, other_sems, out_sems = scratch[-3:]

    def block(arrays, i):
        per = blocks // len(arrays)
        return arrays[i // per].at[pl.ds(i % per * size, size)]

    loads = [
        fetch(ref, at, in_sems.at[n], blocks, lambda i: node_ref[i])
        for n, (ref, at) in enumerate(zip(operands, held))
    ]
    if added:
        loads.append(
            [
                pltpu.make_async_copy(block(others, i), block(other_held, i), other_sems.at[i])
                for i in range(blocks)
            ]
        )
        for copy in loads[-1]:
            copy.start()
    stores = []
    for i in range(blocks):
        for copies in loads:
            copies[i].wait()
        out = block(out_held, i)
        for l in range(size):
            slot = i * size + line_ref[l]
            q = held[0][slot].T
            narrow = jnp.dot(q[:W12], held[1][slot], preferred_element_type=jnp.float32)
            wide = jnp.dot(q[W12:], held[2][slot], preferred_element_type=jnp.float32)
            pieces = ((0, W1, narrow[:W1, :PD]), (W1, W12, narrow[W1:, PD:]), (W12, WSUM, wide))
            for start, end, piece in pieces:
                if added:
                    piece = piece + block(other_held, i)[l, start:end]
                out[l, start:end] = piece.astype(out.dtype)
        stores.append(pltpu.make_async_copy(out, block(outs, i), out_sems.at[i]))
        stores[-1].start()
    for store in stores:
        store.wait()


def partial_proj(nodes, lines, q, g12, g3, results, others=(), after=()):
    _, count, _ = q.shape
    blocks, size = nodes.shape[0], lines.shape[0]
    kinds = [jnp.bfloat16 if others and i else jnp.float32 for i in range(results)]
    shapes = [jax.ShapeDtypeStruct((blocks // results * size, WSUM, PD), kind) for kind in kinds]
    operands = (q, g12, g3)
    return pl.pallas_call(
        functools.partial(partial_kernel, len(operands), len(others), results),
        out_shape=shapes,
        grid_spec=pltpu.PrefetchScalarGridSpec(
            num_scalar_prefetch=2,
            grid=(1,),
            in_specs=[HBM] * (len(operands) + len(others)) + [ANY] * len(after),
            out_specs=[HBM] * results,
            scratch_shapes=[pltpu.VMEM((blocks * size, count, x.shape[2]), jnp.bfloat16) for x in operands]
            + [pltpu.VMEM(x.shape, x.dtype) for x in others]
            + [pltpu.VMEM(x.shape, x.dtype) for x in shapes]
            + [
                pltpu.SemaphoreType.DMA((len(operands), blocks)),
                pltpu.SemaphoreType.DMA((blocks,)),
                pltpu.SemaphoreType.DMA((blocks,)),
            ],
        ),
        compiler_params=params(1),
        cost_estimate=cost(1e7),
        name="partial_proj",
    )(nodes, lines, *operands, *others, *after)


def count_kernel(index_ref, length_ref, *refs):
    out_ref = refs[-1]
    bag, block = index_ref.shape[1], index_ref.shape[2]
    lanes, chunk, low = 256, 16, ROWS // 8

    def one(i, carry):
        at = pl.ds(pl.multiple_of(i * lanes, lanes), lanes)
        index = index_ref[0, :, at]
        which = lax.broadcasted_iota(jnp.int32, (bag, lanes), 0)
        key = jnp.where(which < length_ref[0, :, at], index & (low - 1), -1)
        unit = jnp.left_shift(jnp.int32(1), jnp.right_shift(index, 6) * 4)
        ids = lax.broadcasted_iota(jnp.int32, (chunk, lanes), 0)
        for c in range(low // chunk):
            total = jnp.zeros((chunk, lanes), jnp.int32)
            for j in range(bag):
                total = total + jnp.where(key[j : j + 1] == ids + c * chunk, unit[j : j + 1], 0)
            out_ref[0, c * chunk : (c + 1) * chunk, at] = total
        return carry

    lax.fori_loop(0, block // lanes, one, 0)


def count_hits(lookups, counts, after=()):
    tables, bag, examples = lookups.shape
    block = 4096
    return pl.pallas_call(
        count_kernel,
        out_shape=jax.ShapeDtypeStruct((tables, ROWS // 8, examples), jnp.int32),
        grid=(tables, examples // block),
        in_specs=[
            pl.BlockSpec((1, bag, block), lambda k, i: (k, 0, i)),
            pl.BlockSpec((1, 1, block), lambda k, i: (k, 0, i)),
        ]
        + [ANY] * len(after),
        out_specs=pl.BlockSpec((1, ROWS // 8, block), lambda k, i: (k, 0, i)),
        compiler_params=params(2),
        cost_estimate=cost(1e7),
        name="count_hits",
    )(lookups, counts, *after)


def unpacked(words):
    rows = [lax.shift_right_logical(words, jnp.int32(4 * n)) & 15 for n in range(8)]
    return jnp.concatenate([r.astype(jnp.float32).astype(jnp.bfloat16) for r in rows], axis=0)


def wide_kernel(hits_ref, g_ref, w_ref, *refs):
    out_ref = refs[-1]

    @pl.when(pl.program_id(0) == 0)
    def _():
        out_ref[...] = jnp.zeros_like(out_ref)

    block = g_ref.shape[0]
    column = lax.broadcasted_iota(jnp.int32, (block, WSUM), 1)
    d = lax.dot_general(g_ref[...], w_ref[...], (((1,), (1,)), ((), ())), preferred_element_type=jnp.float32)
    d = jnp.where(column < W12, 0.0, d).astype(jnp.bfloat16)
    out_ref[...] += jnp.dot(unpacked(hits_ref[0]), d, preferred_element_type=jnp.float32)


def wide_sum(hits, g3, weights, after=()):
    _, words, examples = hits.shape
    block = 1024
    return pl.pallas_call(
        wide_kernel,
        out_shape=jax.ShapeDtypeStruct((ROWS, WSUM), jnp.float32),
        grid=(examples // block,),
        in_specs=[
            pl.BlockSpec((1, words, block), lambda i: (2, 0, i)),
            pl.BlockSpec((block, PD), lambda i: (i, 0)),
            pl.BlockSpec((WSUM, PD), lambda i: (0, 0)),
        ]
        + [ANY] * len(after),
        out_specs=pl.BlockSpec((ROWS, WSUM), lambda i: (0, 0)),
        compiler_params=params(1),
        cost_estimate=cost(1e7),
        name="wide_sum",
    )(hits, g3, weights, *after)


def narrow_sum_kernel(hits_ref, d_ref, wide_ref, *refs):
    out_ref = refs[-1]

    @pl.when(pl.program_id(0) == 0)
    def _():
        out_ref[...] = wide_ref[...]

    sources = d_ref.shape[0]
    block = hits_ref.shape[2]
    column = lax.broadcasted_iota(jnp.int32, (block, PD), 1)
    pieces = []
    for d in range(sources):
        packed = d_ref[d].astype(jnp.float32)
        pieces += [packed, pltpu.roll(packed, PD - W12, 1)]
    both = jnp.concatenate(pieces, axis=0)
    d1 = jnp.where(column < W1, both, 0.0).astype(jnp.bfloat16)
    d2 = jnp.where((column >= W1) & (column < W12), both, 0.0).astype(jnp.bfloat16)
    out_ref[...] += jnp.dot(unpacked(hits_ref[0]), d1, preferred_element_type=jnp.float32) + jnp.dot(
        unpacked(hits_ref[1]), d2, preferred_element_type=jnp.float32
    )


def narrow_sum(hits, narrow, wide, after=()):
    _, words, examples = hits.shape
    sources, half, _ = narrow.shape
    block = 1024
    per = block // (2 * half)
    return pl.pallas_call(
        narrow_sum_kernel,
        out_shape=jax.ShapeDtypeStruct((ROWS, WSUM), jnp.float32),
        grid=(examples // block,),
        in_specs=[
            pl.BlockSpec((2, words, block), lambda i: (0, 0, i)),
            pl.BlockSpec((per, half, 2 * W12), lambda i: (i, 0, 0)),
            pl.BlockSpec((ROWS, PD), lambda i: (0, 0)),
        ]
        + [ANY] * len(after),
        out_specs=pl.BlockSpec((ROWS, PD), lambda i: (0, 0)),
        input_output_aliases={2: 0},
        compiler_params=params(1),
        cost_estimate=cost(1e7),
        name="narrow_sum",
    )(hits, narrow, wide, *after)


def swap(x, axis, size, bits):
    return lax.ppermute(x, axis, [(d, d ^ bits) for d in range(size)])


def local(sizes, grad_out, pooled, proj, assign, indices, lengths):
    count, slots, _ = grad_out.shape
    scale = 1.0 / math.sqrt(count * slots)
    n_node, n_local = sizes["node"], sizes["local"]
    n_plane = n_node // 2
    node, loc = lax.axis_index("node"), lax.axis_index("local")

    rows = proj[:, :W12]
    rows = jnp.concatenate([rows] + [swap(rows, "local", n_local, d) for d in range(1, n_local)])
    g12, g3, q = permute(assign, grad_out, pooled)
    rows, g3 = lax.optimization_barrier((rows, g3))
    g3_got = lax.all_to_all(g3, AXES, split_axis=0, concat_axis=0, tiled=True)

    plane = jnp.arange(n_plane, dtype=jnp.int32) ^ (node // 2)
    lines = jnp.arange(n_local, dtype=jnp.int32) ^ loc
    sent = partial_proj(plane * 2 + 1 - node % 2, lines, q, g12, g3, 2)
    got = [swap(x, "node", n_node, 1) for x in sent]

    rows, sent = lax.optimization_barrier((rows, sent))
    rows = jnp.concatenate([rows] + [swap(rows, "node", n_node, 2 * d) for d in range(1, n_plane)])
    kept = partial_proj(plane * 2 + node % 2, lines, q, g12, g3, n_plane, got, after=[rows])
    arrived = [swap(kept[d], "node", n_node, 2 * d) for d in range(1, n_plane)]

    rows = jnp.concatenate([rows, swap(rows, "node", n_node, 1)])
    slot = jnp.arange(slots, dtype=jnp.int32)
    slot_node = slot // n_local ^ node
    slot_place = slot_node % 2 * (slots // 2) + slot_node // 2 * n_local + (slot % n_local ^ loc)
    narrow = narrow_dpool(slot_place, g12, rows, after=kept[:1])
    hits = count_hits(indices[0].transpose(1, 2, 0), lengths[0].T[:, None, :], after=[narrow])

    narrow, hits, g3_got, arrived = lax.optimization_barrier((narrow, hits, g3_got, arrived))
    narrow_got = lax.all_to_all(narrow, AXES, split_axis=0, concat_axis=0, tiled=True)
    total = kept[0]
    for term in arrived:
        total = total + term.astype(jnp.float32)
    rounded = total.astype(jnp.bfloat16)
    own, terms = total[:1], [swap(rounded[d : d + 1], "local", n_local, d) for d in range(1, n_local)]

    wide = wide_sum(hits, g3_got.reshape(-1, PD), proj[0], after=[own])
    terms, wide = lax.optimization_barrier((terms, wide))
    proj_grad = sum((term.astype(jnp.float32) for term in terms), own) * scale
    table_grad = narrow_sum(hits, narrow_got, wide, after=[proj_grad])[None]
    return (table_grad, proj_grad)


def solution(mesh):
    placed = (
        P(AXES, None, None),
        P(AXES, None, None),
        P(AXES, None, None),
        P(),
        P(AXES, None, None, None),
        P(AXES, None, None),
    )
    return jax.shard_map(
        functools.partial(local, dict(mesh.shape)),
        mesh=mesh,
        in_specs=placed,
        out_specs=(P(AXES, None, None), P(AXES, None, None)),
        check_vma=False,
    )
```

```python
import functools
import math

import jax
import jax.numpy as jnp
from jax import lax
from jax.experimental import pallas as pl
from jax.experimental.pallas import tpu as pltpu
from jax.sharding import PartitionSpec as P

ROWS = 512
W1 = 16
W2 = 48
W3 = 192
PD = 128
W12 = W1 + W2
WSUM = W12 + W3
AXES = ("node", "local")
EB = 8
STEP = 32
MIB = 1024 * 1024


def params(grid):
    return pltpu.CompilerParams(dimension_semantics=("arbitrary",) * grid, vmem_limit_bytes=58 * MIB)


HBM = pl.BlockSpec(memory_space=pltpu.HBM)
ANY = pl.BlockSpec(memory_space=pl.ANY)


def cost(flops):
    return pl.CostEstimate(flops=int(flops), bytes_accessed=1024, transcendentals=0)


def permute_kernel(slots, pieces, assign_ref, grad_ref, pool_ref, *refs):
    outs, (perm_ref, grad_held, pool_held, sems) = refs[:3], refs[3:]
    step = pl.program_id(0)
    sources = ((grad_ref, grad_held), (pool_ref, pool_held))

    def copies(i):
        at = pl.ds(i * STEP, STEP)
        return [
            pltpu.make_async_copy(ref.at[at], held.at[at], sems.at[n, i]) for n, (ref, held) in enumerate(sources)
        ]

    @pl.when(step == 0)
    def _():
        for i in range(grad_ref.shape[0] // STEP):
            for copy in copies(i):
                copy.start()
        width = EB * slots
        lane = lax.broadcasted_iota(jnp.int32, (2 * EB, width), 1)
        row = lax.broadcasted_iota(jnp.int32, (2 * EB, width), 0)
        for s in range(0, slots, 2):
            group = jnp.where(row < EB, assign_ref[s], assign_ref[s + 1])
            hit = lane == (row % EB) * slots + group
            perm_ref[s * EB : (s + 2) * EB, :] = jnp.where(hit, 1.0, 0.0).astype(jnp.bfloat16)

    for copy, (_, held), cuts in zip(copies(step), sources, pieces):
        copy.wait()
        width = held.shape[2]
        for start in range(0, STEP, 2 * EB):
            pair = []
            for at in (start, start + EB):
                block = held[pl.ds(step * STEP + at, EB)].reshape(EB * slots, width)
                moved = jnp.dot(perm_ref[...], block, preferred_element_type=jnp.float32)
                pair.append(moved.reshape(slots, EB, width))
            both = jnp.concatenate(pair, axis=1).astype(jnp.bfloat16)
            for n, low, high in cuts:
                outs[n][:, start : start + 2 * EB, :] = both[:, :, low:high]


def permute(assign, grad_out, pooled):
    count, slots, _ = grad_out.shape
    widths = (2 * PD, PD, WSUM)
    pieces = (((0, 0, 2 * PD), (1, 2 * PD, 3 * PD)), ((2, 0, WSUM),))
    return pl.pallas_call(
        functools.partial(permute_kernel, slots, pieces),
        out_shape=[jax.ShapeDtypeStruct((slots, count, width), jnp.bfloat16) for width in widths],
        grid_spec=pltpu.PrefetchScalarGridSpec(
            num_scalar_prefetch=1,
            grid=(count // STEP,),
            in_specs=[HBM] * 2,
            out_specs=[pl.BlockSpec((slots, STEP, width), lambda i, a: (0, i, 0)) for width in widths],
            scratch_shapes=[
                pltpu.VMEM((EB * slots, EB * slots), jnp.bfloat16),
                pltpu.VMEM(grad_out.shape, jnp.bfloat16),
                pltpu.VMEM(pooled.shape, jnp.bfloat16),
                pltpu.SemaphoreType.DMA((2, count // STEP)),
            ],
        ),
        compiler_params=params(1),
        cost_estimate=cost(1e7),
        name="permute_groups",
    )(assign, grad_out, pooled)


def fetch(ref, held, sems, blocks, pick=lambda i: i):
    size = held.shape[0] // blocks
    copies = [
        pltpu.make_async_copy(ref.at[pl.ds(pick(i) * size, size)], held.at[pl.ds(i * size, size)], sems.at[i])
        for i in range(blocks)
    ]
    for copy in copies:
        copy.start()
    return copies


def narrow_kernel(blocks, place_ref, g_ref, w_ref, *refs):
    out_ref, g_held, w_held, out_held, g_sems, w_sems, out_sems = refs[-7:]
    weights = fetch(w_ref, w_held, w_sems, 1)
    loads = fetch(g_ref, g_held, g_sems, blocks)
    slots, count, _ = g_held.shape
    step, half = slots // blocks, count // 2
    column = lax.broadcasted_iota(jnp.int32, (count, W12), 1)
    dims = (((1,), (1,)), ((), ()))
    weights[0].wait()
    stores = []
    for i, load in enumerate(loads):
        load.wait()
        for s in range(i * step, (i + 1) * step):
            w = w_held[place_ref[s]]
            first = lax.dot_general(g_held[s, :, :PD], w, dims, preferred_element_type=jnp.float32)
            second = lax.dot_general(g_held[s, :, PD:], w, dims, preferred_element_type=jnp.float32)
            d = jnp.where(column < W1, first, second)
            out_held[s] = jnp.concatenate([d[:half], d[half:]], axis=1).astype(jnp.bfloat16)
        at = pl.ds(i * step, step)
        stores.append(pltpu.make_async_copy(out_held.at[at], out_ref.at[at], out_sems.at[i]))
        stores[-1].start()
    for store in stores:
        store.wait()


def narrow_dpool(place, g12, w12, after=()):
    slots, count, _ = g12.shape
    blocks = 4
    shape = (slots, count // 2, 2 * W12)
    return pl.pallas_call(
        functools.partial(narrow_kernel, blocks),
        out_shape=jax.ShapeDtypeStruct(shape, jnp.bfloat16),
        grid_spec=pltpu.PrefetchScalarGridSpec(
            num_scalar_prefetch=1,
            grid=(1,),
            in_specs=[HBM] * 2 + [ANY] * len(after),
            out_specs=HBM,
            scratch_shapes=[
                pltpu.VMEM(g12.shape, jnp.bfloat16),
                pltpu.VMEM(w12.shape, jnp.bfloat16),
                pltpu.VMEM(shape, jnp.bfloat16),
                pltpu.SemaphoreType.DMA((blocks,)),
                pltpu.SemaphoreType.DMA((1,)),
                pltpu.SemaphoreType.DMA((blocks,)),
            ],
        ),
        compiler_params=params(1),
        cost_estimate=cost(1e7),
        name="narrow_dpool",
    )(place, g12, w12, *after)


def partial_kernel(ins, added, results, node_ref, line_ref, *refs):
    blocks, size = node_ref.shape[0], line_ref.shape[0]
    operands, others = refs[:ins], refs[ins : ins + added]
    outs, scratch = refs[-3 - 2 * results - ins - added :][:results], refs[-3 - results - ins - added :]
    held, other_held, out_held = scratch[:ins], scratch[ins : ins + added], scratch[ins + added : -3]
    in_sems, other_sems, out_sems = scratch[-3:]

    def block(arrays, i):
        per = blocks // len(arrays)
        return arrays[i // per].at[pl.ds(i % per * size, size)]

    loads = [
        fetch(ref, at, in_sems.at[n], blocks, lambda i: node_ref[i])
        for n, (ref, at) in enumerate(zip(operands, held))
    ]
    if added:
        loads.append(
            [
                pltpu.make_async_copy(block(others, i), block(other_held, i), other_sems.at[i])
                for i in range(blocks)
            ]
        )
        for copy in loads[-1]:
            copy.start()
    stores = []
    for i in range(blocks):
        for copies in loads:
            copies[i].wait()
        out = block(out_held, i)
        for l in range(size):
            slot = i * size + line_ref[l]
            q = held[0][slot].T
            narrow = jnp.dot(q[:W12], held[1][slot], preferred_element_type=jnp.float32)
            wide = jnp.dot(q[W12:], held[2][slot], preferred_element_type=jnp.float32)
            pieces = ((0, W1, narrow[:W1, :PD]), (W1, W12, narrow[W1:, PD:]), (W12, WSUM, wide))
            for start, end, piece in pieces:
                if added:
                    piece = piece + block(other_held, i)[l, start:end]
                out[l, start:end] = piece.astype(out.dtype)
        stores.append(pltpu.make_async_copy(out, block(outs, i), out_sems.at[i]))
        stores[-1].start()
    for store in stores:
        store.wait()


def partial_proj(nodes, lines, q, g12, g3, results, others=(), after=()):
    _, count, _ = q.shape
    blocks, size = nodes.shape[0], lines.shape[0]
    kinds = [jnp.bfloat16 if others and i else jnp.float32 for i in range(results)]
    shapes = [jax.ShapeDtypeStruct((blocks // results * size, WSUM, PD), kind) for kind in kinds]
    operands = (q, g12, g3)
    return pl.pallas_call(
        functools.partial(partial_kernel, len(operands), len(others), results),
        out_shape=shapes,
        grid_spec=pltpu.PrefetchScalarGridSpec(
            num_scalar_prefetch=2,
            grid=(1,),
            in_specs=[HBM] * (len(operands) + len(others)) + [ANY] * len(after),
            out_specs=[HBM] * results,
            scratch_shapes=[pltpu.VMEM((blocks * size, count, x.shape[2]), jnp.bfloat16) for x in operands]
            + [pltpu.VMEM(x.shape, x.dtype) for x in others]
            + [pltpu.VMEM(x.shape, x.dtype) for x in shapes]
            + [
                pltpu.SemaphoreType.DMA((len(operands), blocks)),
                pltpu.SemaphoreType.DMA((blocks,)),
                pltpu.SemaphoreType.DMA((blocks,)),
            ],
        ),
        compiler_params=params(1),
        cost_estimate=cost(1e7),
        name="partial_proj",
    )(nodes, lines, *operands, *others, *after)


def count_kernel(index_ref, length_ref, *refs):
    out_ref = refs[-1]
    bag, block = index_ref.shape[1], index_ref.shape[2]
    lanes, chunk, low = 256, 16, ROWS // 8

    def one(i, carry):
        at = pl.ds(pl.multiple_of(i * lanes, lanes), lanes)
        index = index_ref[0, :, at]
        which = lax.broadcasted_iota(jnp.int32, (bag, lanes), 0)
        key = jnp.where(which < length_ref[0, :, at], index & (low - 1), -1)
        unit = jnp.left_shift(jnp.int32(1), jnp.right_shift(index, 6) * 4)
        ids = lax.broadcasted_iota(jnp.int32, (chunk, lanes), 0)
        for c in range(low // chunk):
            total = jnp.zeros((chunk, lanes), jnp.int32)
            for j in range(bag):
                total = total + jnp.where(key[j : j + 1] == ids + c * chunk, unit[j : j + 1], 0)
            out_ref[0, c * chunk : (c + 1) * chunk, at] = total
        return carry

    lax.fori_loop(0, block // lanes, one, 0)


def count_hits(lookups, counts, after=()):
    tables, bag, examples = lookups.shape
    block = 4096
    return pl.pallas_call(
        count_kernel,
        out_shape=jax.ShapeDtypeStruct((tables, ROWS // 8, examples), jnp.int32),
        grid=(tables, examples // block),
        in_specs=[
            pl.BlockSpec((1, bag, block), lambda k, i: (k, 0, i)),
            pl.BlockSpec((1, 1, block), lambda k, i: (k, 0, i)),
        ]
        + [ANY] * len(after),
        out_specs=pl.BlockSpec((1, ROWS // 8, block), lambda k, i: (k, 0, i)),
        compiler_params=params(2),
        cost_estimate=cost(1e7),
        name="count_hits",
    )(lookups, counts, *after)


def unpacked(words):
    rows = [lax.shift_right_logical(words, jnp.int32(4 * n)) & 15 for n in range(8)]
    return jnp.concatenate([r.astype(jnp.float32).astype(jnp.bfloat16) for r in rows], axis=0)


def wide_kernel(hits_ref, g_ref, w_ref, *refs):
    out_ref = refs[-1]

    @pl.when(pl.program_id(0) == 0)
    def _():
        out_ref[...] = jnp.zeros_like(out_ref)

    block = g_ref.shape[0]
    column = lax.broadcasted_iota(jnp.int32, (block, WSUM), 1)
    d = lax.dot_general(g_ref[...], w_ref[...], (((1,), (1,)), ((), ())), preferred_element_type=jnp.float32)
    d = jnp.where(column < W12, 0.0, d).astype(jnp.bfloat16)
    out_ref[...] += jnp.dot(unpacked(hits_ref[0]), d, preferred_element_type=jnp.float32)


def wide_sum(hits, g3, weights, after=()):
    _, words, examples = hits.shape
    block = 1024
    return pl.pallas_call(
        wide_kernel,
        out_shape=jax.ShapeDtypeStruct((ROWS, WSUM), jnp.float32),
        grid=(examples // block,),
        in_specs=[
            pl.BlockSpec((1, words, block), lambda i: (2, 0, i)),
            pl.BlockSpec((block, PD), lambda i: (i, 0)),
            pl.BlockSpec((WSUM, PD), lambda i: (0, 0)),
        ]
        + [ANY] * len(after),
        out_specs=pl.BlockSpec((ROWS, WSUM), lambda i: (0, 0)),
        compiler_params=params(1),
        cost_estimate=cost(1e7),
        name="wide_sum",
    )(hits, g3, weights, *after)


def narrow_sum_kernel(hits_ref, d_ref, wide_ref, *refs):
    out_ref = refs[-1]

    @pl.when(pl.program_id(0) == 0)
    def _():
        out_ref[...] = wide_ref[...]

    sources = d_ref.shape[0]
    block = hits_ref.shape[2]
    column = lax.broadcasted_iota(jnp.int32, (block, PD), 1)
    pieces = []
    for d in range(sources):
        packed = d_ref[d].astype(jnp.float32)
        pieces += [packed, pltpu.roll(packed, PD - W12, 1)]
    both = jnp.concatenate(pieces, axis=0)
    d1 = jnp.where(column < W1, both, 0.0).astype(jnp.bfloat16)
    d2 = jnp.where((column >= W1) & (column < W12), both, 0.0).astype(jnp.bfloat16)
    out_ref[...] += jnp.dot(unpacked(hits_ref[0]), d1, preferred_element_type=jnp.float32) + jnp.dot(
        unpacked(hits_ref[1]), d2, preferred_element_type=jnp.float32
    )


def narrow_sum(hits, narrow, wide, after=()):
    _, words, examples = hits.shape
    sources, half, _ = narrow.shape
    block = 1024
    per = block // (2 * half)
    return pl.pallas_call(
        narrow_sum_kernel,
        out_shape=jax.ShapeDtypeStruct((ROWS, WSUM), jnp.float32),
        grid=(examples // block,),
        in_specs=[
            pl.BlockSpec((2, words, block), lambda i: (0, 0, i)),
            pl.BlockSpec((per, half, 2 * W12), lambda i: (i, 0, 0)),
            pl.BlockSpec((ROWS, PD), lambda i: (0, 0)),
        ]
        + [ANY] * len(after),
        out_specs=pl.BlockSpec((ROWS, PD), lambda i: (0, 0)),
        input_output_aliases={2: 0},
        compiler_params=params(1),
        cost_estimate=cost(1e7),
        name="narrow_sum",
    )(hits, narrow, wide, *after)


def swap(x, axis, size, bits):
    return lax.ppermute(x, axis, [(d, d ^ bits) for d in range(size)])


def local(sizes, grad_out, pooled, proj, assign, indices, lengths):
    count, slots, _ = grad_out.shape
    scale = 1.0 / math.sqrt(count * slots)
    n_node, n_local = sizes["node"], sizes["local"]
    n_plane = n_node // 2
    node, loc = lax.axis_index("node"), lax.axis_index("local")

    rows = proj[:, :W12]
    rows = jnp.concatenate([rows] + [swap(rows, "local", n_local, d) for d in range(1, n_local)])
    g12, g3, q = permute(assign, grad_out, pooled)
    rows, g3 = lax.optimization_barrier((rows, g3))
    g3_got = lax.all_to_all(g3, AXES, split_axis=0, concat_axis=0, tiled=True)

    plane = jnp.arange(n_plane, dtype=jnp.int32) ^ (node // 2)
    lines = jnp.arange(n_local, dtype=jnp.int32) ^ loc
    sent = partial_proj(plane * 2 + 1 - node % 2, lines, q, g12, g3, 2)
    got = [swap(x, "node", n_node, 1) for x in sent]

    rows, sent = lax.optimization_barrier((rows, sent))
    rows = jnp.concatenate([rows] + [swap(rows, "node", n_node, 2 * d) for d in range(1, n_plane)])
    hits = count_hits(indices[0].transpose(1, 2, 0), lengths[0].T[:, None, :], after=sent[:1])
    kept = partial_proj(plane * 2 + node % 2, lines, q, g12, g3, n_plane, got, after=[rows, hits])
    arrived = [swap(kept[d], "node", n_node, 2 * d) for d in range(1, n_plane)]

    rows = jnp.concatenate([rows, swap(rows, "node", n_node, 1)])
    slot = jnp.arange(slots, dtype=jnp.int32)
    slot_node = slot // n_local ^ node
    slot_place = slot_node % 2 * (slots // 2) + slot_node // 2 * n_local + (slot % n_local ^ loc)
    narrow = narrow_dpool(slot_place, g12, rows, after=kept[:1])
    narrow, g3_got, arrived = lax.optimization_barrier((narrow, g3_got, arrived))
    narrow_got = lax.all_to_all(narrow, AXES, split_axis=0, concat_axis=0, tiled=True)
    total = kept[0]
    for term in arrived:
        total = total + term.astype(jnp.float32)
    wide = wide_sum(hits, g3_got.reshape(-1, PD), proj[0])
    total, wide = lax.optimization_barrier((total, wide))
    rounded = total.astype(jnp.bfloat16)
    own, terms = total[:1], [swap(rounded[d : d + 1], "local", n_local, d) for d in range(1, n_local)]

    table_grad = narrow_sum(hits, narrow_got, wide)[None]
    terms, table_grad = lax.optimization_barrier((terms, table_grad))
    proj_grad = sum((term.astype(jnp.float32) for term in terms), own) * scale
    return (table_grad, proj_grad)


def solution(mesh):
    placed = (
        P(AXES, None, None),
        P(AXES, None, None),
        P(AXES, None, None),
        P(),
        P(AXES, None, None, None),
        P(AXES, None, None),
    )
    return jax.shard_map(
        functools.partial(local, dict(mesh.shape)),
        mesh=mesh,
        in_specs=placed,
        out_specs=(P(AXES, None, None), P(AXES, None, None)),
        check_vma=False,
    )
```

```python
import functools
import math

import jax
import jax.numpy as jnp
from jax import lax
from jax.experimental import pallas as pl
from jax.experimental.pallas import tpu as pltpu
from jax.sharding import PartitionSpec as P

ROWS = 512
W1 = 16
W2 = 48
W3 = 192
PD = 128
W12 = W1 + W2
WSUM = W12 + W3
AXES = ("node", "local")
EB = 8
STEP = 32
MIB = 1024 * 1024


def params(grid):
    return pltpu.CompilerParams(dimension_semantics=("arbitrary",) * grid, vmem_limit_bytes=58 * MIB)


HBM = pl.BlockSpec(memory_space=pltpu.HBM)
ANY = pl.BlockSpec(memory_space=pl.ANY)


def cost(flops):
    return pl.CostEstimate(flops=int(flops), bytes_accessed=1024, transcendentals=0)


def permute_kernel(slots, pieces, assign_ref, grad_ref, pool_ref, *refs):
    outs, (perm_ref, grad_held, pool_held, sems) = refs[:3], refs[3:]
    step = pl.program_id(0)
    sources = ((grad_ref, grad_held), (pool_ref, pool_held))

    def copies(i):
        at = pl.ds(i * STEP, STEP)
        return [
            pltpu.make_async_copy(ref.at[at], held.at[at], sems.at[n, i]) for n, (ref, held) in enumerate(sources)
        ]

    @pl.when(step == 0)
    def _():
        for i in range(grad_ref.shape[0] // STEP):
            for copy in copies(i):
                copy.start()
        width = EB * slots
        lane = lax.broadcasted_iota(jnp.int32, (2 * EB, width), 1)
        row = lax.broadcasted_iota(jnp.int32, (2 * EB, width), 0)
        for s in range(0, slots, 2):
            group = jnp.where(row < EB, assign_ref[s], assign_ref[s + 1])
            hit = lane == (row % EB) * slots + group
            perm_ref[s * EB : (s + 2) * EB, :] = jnp.where(hit, 1.0, 0.0).astype(jnp.bfloat16)

    for copy, (_, held), cuts in zip(copies(step), sources, pieces):
        copy.wait()
        width = held.shape[2]
        for start in range(0, STEP, 2 * EB):
            pair = []
            for at in (start, start + EB):
                block = held[pl.ds(step * STEP + at, EB)].reshape(EB * slots, width)
                moved = jnp.dot(perm_ref[...], block, preferred_element_type=jnp.float32)
                pair.append(moved.reshape(slots, EB, width))
            both = jnp.concatenate(pair, axis=1).astype(jnp.bfloat16)
            for n, low, high in cuts:
                outs[n][:, start : start + 2 * EB, :] = both[:, :, low:high]


def permute(assign, grad_out, pooled):
    count, slots, _ = grad_out.shape
    widths = (2 * PD, PD, WSUM)
    pieces = (((0, 0, 2 * PD), (1, 2 * PD, 3 * PD)), ((2, 0, WSUM),))
    return pl.pallas_call(
        functools.partial(permute_kernel, slots, pieces),
        out_shape=[jax.ShapeDtypeStruct((slots, count, width), jnp.bfloat16) for width in widths],
        grid_spec=pltpu.PrefetchScalarGridSpec(
            num_scalar_prefetch=1,
            grid=(count // STEP,),
            in_specs=[HBM] * 2,
            out_specs=[pl.BlockSpec((slots, STEP, width), lambda i, a: (0, i, 0)) for width in widths],
            scratch_shapes=[
                pltpu.VMEM((EB * slots, EB * slots), jnp.bfloat16),
                pltpu.VMEM(grad_out.shape, jnp.bfloat16),
                pltpu.VMEM(pooled.shape, jnp.bfloat16),
                pltpu.SemaphoreType.DMA((2, count // STEP)),
            ],
        ),
        compiler_params=params(1),
        cost_estimate=cost(1e7),
        name="permute_groups",
    )(assign, grad_out, pooled)


def fetch(ref, held, sems, blocks, pick=lambda i: i):
    size = held.shape[0] // blocks
    copies = [
        pltpu.make_async_copy(ref.at[pl.ds(pick(i) * size, size)], held.at[pl.ds(i * size, size)], sems.at[i])
        for i in range(blocks)
    ]
    for copy in copies:
        copy.start()
    return copies


def narrow_kernel(blocks, place_ref, g_ref, w_ref, *refs):
    out_ref, g_held, w_held, out_held, g_sems, w_sems, out_sems = refs[-7:]
    weights = fetch(w_ref, w_held, w_sems, 1)
    loads = fetch(g_ref, g_held, g_sems, blocks)
    slots, count, _ = g_held.shape
    step, half = slots // blocks, count // 2
    column = lax.broadcasted_iota(jnp.int32, (count, W12), 1)
    dims = (((1,), (1,)), ((), ()))
    weights[0].wait()
    stores = []
    for i, load in enumerate(loads):
        load.wait()
        for s in range(i * step, (i + 1) * step):
            w = w_held[place_ref[s]]
            first = lax.dot_general(g_held[s, :, :PD], w, dims, preferred_element_type=jnp.float32)
            second = lax.dot_general(g_held[s, :, PD:], w, dims, preferred_element_type=jnp.float32)
            d = jnp.where(column < W1, first, second)
            out_held[s] = jnp.concatenate([d[:half], d[half:]], axis=1).astype(jnp.bfloat16)
        at = pl.ds(i * step, step)
        stores.append(pltpu.make_async_copy(out_held.at[at], out_ref.at[at], out_sems.at[i]))
        stores[-1].start()
    for store in stores:
        store.wait()


def narrow_dpool(place, g12, w12, after=()):
    slots, count, _ = g12.shape
    blocks = 4
    shape = (slots, count // 2, 2 * W12)
    return pl.pallas_call(
        functools.partial(narrow_kernel, blocks),
        out_shape=jax.ShapeDtypeStruct(shape, jnp.bfloat16),
        grid_spec=pltpu.PrefetchScalarGridSpec(
            num_scalar_prefetch=1,
            grid=(1,),
            in_specs=[HBM] * 2 + [ANY] * len(after),
            out_specs=HBM,
            scratch_shapes=[
                pltpu.VMEM(g12.shape, jnp.bfloat16),
                pltpu.VMEM(w12.shape, jnp.bfloat16),
                pltpu.VMEM(shape, jnp.bfloat16),
                pltpu.SemaphoreType.DMA((blocks,)),
                pltpu.SemaphoreType.DMA((1,)),
                pltpu.SemaphoreType.DMA((blocks,)),
            ],
        ),
        compiler_params=params(1),
        cost_estimate=cost(1e7),
        name="narrow_dpool",
    )(place, g12, w12, *after)


def partial_kernel(ins, added, results, node_ref, line_ref, *refs):
    blocks, size = node_ref.shape[0], line_ref.shape[0]
    operands, others = refs[:ins], refs[ins : ins + added]
    outs, scratch = refs[-3 - 2 * results - ins - added :][:results], refs[-3 - results - ins - added :]
    held, other_held, out_held = scratch[:ins], scratch[ins : ins + added], scratch[ins + added : -3]
    in_sems, other_sems, out_sems = scratch[-3:]

    def block(arrays, i):
        per = blocks // len(arrays)
        return arrays[i // per].at[pl.ds(i % per * size, size)]

    loads = [
        fetch(ref, at, in_sems.at[n], blocks, lambda i: node_ref[i])
        for n, (ref, at) in enumerate(zip(operands, held))
    ]
    if added:
        loads.append(
            [
                pltpu.make_async_copy(block(others, i), block(other_held, i), other_sems.at[i])
                for i in range(blocks)
            ]
        )
        for copy in loads[-1]:
            copy.start()
    stores = []
    for i in range(blocks):
        for copies in loads:
            copies[i].wait()
        out = block(out_held, i)
        for l in range(size):
            slot = i * size + line_ref[l]
            q = held[0][slot].T
            narrow = jnp.dot(q[:W12], held[1][slot], preferred_element_type=jnp.float32)
            wide = jnp.dot(q[W12:], held[2][slot], preferred_element_type=jnp.float32)
            pieces = ((0, W1, narrow[:W1, :PD]), (W1, W12, narrow[W1:, PD:]), (W12, WSUM, wide))
            for start, end, piece in pieces:
                if added:
                    piece = piece + block(other_held, i)[l, start:end]
                out[l, start:end] = piece.astype(out.dtype)
        stores.append(pltpu.make_async_copy(out, block(outs, i), out_sems.at[i]))
        stores[-1].start()
    for store in stores:
        store.wait()


def partial_proj(nodes, lines, q, g12, g3, results, others=()):
    _, count, _ = q.shape
    blocks, size = nodes.shape[0], lines.shape[0]
    kinds = [jnp.bfloat16 if others and i else jnp.float32 for i in range(results)]
    shapes = [jax.ShapeDtypeStruct((blocks // results * size, WSUM, PD), kind) for kind in kinds]
    operands = (q, g12, g3)
    return pl.pallas_call(
        functools.partial(partial_kernel, len(operands), len(others), results),
        out_shape=shapes,
        grid_spec=pltpu.PrefetchScalarGridSpec(
            num_scalar_prefetch=2,
            grid=(1,),
            in_specs=[HBM] * (len(operands) + len(others)),
            out_specs=[HBM] * results,
            scratch_shapes=[pltpu.VMEM((blocks * size, count, x.shape[2]), jnp.bfloat16) for x in operands]
            + [pltpu.VMEM(x.shape, x.dtype) for x in others]
            + [pltpu.VMEM(x.shape, x.dtype) for x in shapes]
            + [
                pltpu.SemaphoreType.DMA((len(operands), blocks)),
                pltpu.SemaphoreType.DMA((blocks,)),
                pltpu.SemaphoreType.DMA((blocks,)),
            ],
        ),
        compiler_params=params(1),
        cost_estimate=cost(1e7),
        name="partial_proj",
    )(nodes, lines, *operands, *others)


def count_kernel(index_ref, length_ref, *refs):
    out_ref = refs[-1]
    bag, block = index_ref.shape[1], index_ref.shape[2]
    lanes, chunk, low = 256, 16, ROWS // 8

    def one(i, carry):
        at = pl.ds(pl.multiple_of(i * lanes, lanes), lanes)
        index = index_ref[0, :, at]
        which = lax.broadcasted_iota(jnp.int32, (bag, lanes), 0)
        key = jnp.where(which < length_ref[0, :, at], index & (low - 1), -1)
        unit = jnp.left_shift(jnp.int32(1), jnp.right_shift(index, 6) * 4)
        ids = lax.broadcasted_iota(jnp.int32, (chunk, lanes), 0)
        for c in range(low // chunk):
            total = jnp.zeros((chunk, lanes), jnp.int32)
            for j in range(bag):
                total = total + jnp.where(key[j : j + 1] == ids + c * chunk, unit[j : j + 1], 0)
            out_ref[0, c * chunk : (c + 1) * chunk, at] = total
        return carry

    lax.fori_loop(0, block // lanes, one, 0)


def count_hits(lookups, counts, after=()):
    tables, bag, examples = lookups.shape
    block = 4096
    return pl.pallas_call(
        count_kernel,
        out_shape=jax.ShapeDtypeStruct((tables, ROWS // 8, examples), jnp.int32),
        grid=(tables, examples // block),
        in_specs=[
            pl.BlockSpec((1, bag, block), lambda k, i: (k, 0, i)),
            pl.BlockSpec((1, 1, block), lambda k, i: (k, 0, i)),
        ]
        + [ANY] * len(after),
        out_specs=pl.BlockSpec((1, ROWS // 8, block), lambda k, i: (k, 0, i)),
        compiler_params=params(2),
        cost_estimate=cost(1e7),
        name="count_hits",
    )(lookups, counts, *after)


def unpacked(words):
    rows = [lax.shift_right_logical(words, jnp.int32(4 * n)) & 15 for n in range(8)]
    return jnp.concatenate([r.astype(jnp.float32).astype(jnp.bfloat16) for r in rows], axis=0)


def wide_kernel(hits_ref, g_ref, w_ref, *refs):
    out_ref = refs[-1]

    @pl.when(pl.program_id(0) == 0)
    def _():
        out_ref[...] = jnp.zeros_like(out_ref)

    block = g_ref.shape[0]
    column = lax.broadcasted_iota(jnp.int32, (block, WSUM), 1)
    d = lax.dot_general(g_ref[...], w_ref[...], (((1,), (1,)), ((), ())), preferred_element_type=jnp.float32)
    d = jnp.where(column < W12, 0.0, d).astype(jnp.bfloat16)
    out_ref[...] += jnp.dot(unpacked(hits_ref[0]), d, preferred_element_type=jnp.float32)


def wide_sum(hits, g3, weights, after=()):
    _, words, examples = hits.shape
    block = 1024
    return pl.pallas_call(
        wide_kernel,
        out_shape=jax.ShapeDtypeStruct((ROWS, WSUM), jnp.float32),
        grid=(examples // block,),
        in_specs=[
            pl.BlockSpec((1, words, block), lambda i: (2, 0, i)),
            pl.BlockSpec((block, PD), lambda i: (i, 0)),
            pl.BlockSpec((WSUM, PD), lambda i: (0, 0)),
        ]
        + [ANY] * len(after),
        out_specs=pl.BlockSpec((ROWS, WSUM), lambda i: (0, 0)),
        compiler_params=params(1),
        cost_estimate=cost(1e7),
        name="wide_sum",
    )(hits, g3, weights, *after)


def narrow_sum_kernel(hits_ref, d_ref, wide_ref, *refs):
    out_ref = refs[-1]

    @pl.when(pl.program_id(0) == 0)
    def _():
        out_ref[...] = wide_ref[...]

    sources = d_ref.shape[0]
    block = hits_ref.shape[2]
    column = lax.broadcasted_iota(jnp.int32, (block, PD), 1)
    pieces = []
    for d in range(sources):
        packed = d_ref[d].astype(jnp.float32)
        pieces += [packed, pltpu.roll(packed, PD - W12, 1)]
    both = jnp.concatenate(pieces, axis=0)
    d1 = jnp.where(column < W1, both, 0.0).astype(jnp.bfloat16)
    d2 = jnp.where((column >= W1) & (column < W12), both, 0.0).astype(jnp.bfloat16)
    out_ref[...] += jnp.dot(unpacked(hits_ref[0]), d1, preferred_element_type=jnp.float32) + jnp.dot(
        unpacked(hits_ref[1]), d2, preferred_element_type=jnp.float32
    )


def narrow_sum(hits, narrow, wide, after=()):
    _, words, examples = hits.shape
    sources, half, _ = narrow.shape
    block = 1024
    per = block // (2 * half)
    return pl.pallas_call(
        narrow_sum_kernel,
        out_shape=jax.ShapeDtypeStruct((ROWS, WSUM), jnp.float32),
        grid=(examples // block,),
        in_specs=[
            pl.BlockSpec((2, words, block), lambda i: (0, 0, i)),
            pl.BlockSpec((per, half, 2 * W12), lambda i: (i, 0, 0)),
            pl.BlockSpec((ROWS, PD), lambda i: (0, 0)),
        ]
        + [ANY] * len(after),
        out_specs=pl.BlockSpec((ROWS, PD), lambda i: (0, 0)),
        input_output_aliases={2: 0},
        compiler_params=params(1),
        cost_estimate=cost(1e7),
        name="narrow_sum",
    )(hits, narrow, wide, *after)


def swap(x, axis, size, bits):
    return lax.ppermute(x, axis, [(d, d ^ bits) for d in range(size)])


def local(sizes, grad_out, pooled, proj, assign, indices, lengths):
    count, slots, _ = grad_out.shape
    scale = 1.0 / math.sqrt(count * slots)
    n_node, n_local = sizes["node"], sizes["local"]
    n_plane = n_node // 2
    node, loc = lax.axis_index("node"), lax.axis_index("local")

    rows = proj[:, :W12]
    rows = jnp.concatenate([rows] + [swap(rows, "local", n_local, d) for d in range(1, n_local)])
    g12, g3, q = permute(assign, grad_out, pooled)
    rows, g3 = lax.optimization_barrier((rows, g3))
    g3_got = lax.all_to_all(g3, AXES, split_axis=0, concat_axis=0, tiled=True)

    plane = jnp.arange(n_plane, dtype=jnp.int32) ^ (node // 2)
    lines = jnp.arange(n_local, dtype=jnp.int32) ^ loc
    sent = partial_proj(plane * 2 + 1 - node % 2, lines, q, g12, g3, 2)
    got = [swap(x, "node", n_node, 1) for x in sent]

    rows, sent = lax.optimization_barrier((rows, sent))
    rows = jnp.concatenate([rows] + [swap(rows, "node", n_node, 2 * d) for d in range(1, n_plane)])
    kept = partial_proj(plane * 2 + node % 2, lines, q, g12, g3, n_plane, got)
    arrived = [swap(kept[d], "node", n_node, 2 * d) for d in range(1, n_plane)]

    rows = jnp.concatenate([rows, swap(rows, "node", n_node, 1)])
    slot = jnp.arange(slots, dtype=jnp.int32)
    slot_node = slot // n_local ^ node
    slot_place = slot_node % 2 * (slots // 2) + slot_node // 2 * n_local + (slot % n_local ^ loc)
    narrow = narrow_dpool(slot_place, g12, rows, after=kept[:1])
    hits = count_hits(indices[0].transpose(1, 2, 0), lengths[0].T[:, None, :], after=[narrow])

    narrow, hits, g3_got, arrived = lax.optimization_barrier((narrow, hits, g3_got, arrived))
    narrow_got = lax.all_to_all(narrow, AXES, split_axis=0, concat_axis=0, tiled=True)
    total = kept[0]
    for term in arrived:
        total = total + term.astype(jnp.float32)
    wide = wide_sum(hits, g3_got.reshape(-1, PD), proj[0])
    total, wide = lax.optimization_barrier((total, wide))
    rounded = total.astype(jnp.bfloat16)
    own, terms = total[:1], [swap(rounded[d : d + 1], "local", n_local, d) for d in range(1, n_local)]

    table_grad = narrow_sum(hits, narrow_got, wide)[None]
    terms, table_grad = lax.optimization_barrier((terms, table_grad))
    proj_grad = sum((term.astype(jnp.float32) for term in terms), own) * scale
    return (table_grad, proj_grad)


def solution(mesh):
    placed = (
        P(AXES, None, None),
        P(AXES, None, None),
        P(AXES, None, None),
        P(),
        P(AXES, None, None, None),
        P(AXES, None, None),
    )
    return jax.shard_map(
        functools.partial(local, dict(mesh.shape)),
        mesh=mesh,
        in_specs=placed,
        out_specs=(P(AXES, None, None), P(AXES, None, None)),
        check_vma=False,
    )
```

```python
import functools
import math

import jax
import jax.numpy as jnp
from jax import lax
from jax.experimental import pallas as pl
from jax.experimental.pallas import tpu as pltpu
from jax.sharding import PartitionSpec as P

ROWS = 512
W1 = 16
W2 = 48
W3 = 192
PD = 128
W12 = W1 + W2
WSUM = W12 + W3
AXES = ("node", "local")
EB = 8
STEP = 32
MIB = 1024 * 1024


def params(grid):
    return pltpu.CompilerParams(dimension_semantics=("arbitrary",) * grid, vmem_limit_bytes=58 * MIB)


HBM = pl.BlockSpec(memory_space=pltpu.HBM)
ANY = pl.BlockSpec(memory_space=pl.ANY)


def cost(flops):
    return pl.CostEstimate(flops=int(flops), bytes_accessed=1024, transcendentals=0)


def permute_kernel(slots, pieces, assign_ref, grad_ref, pool_ref, *refs):
    outs, (perm_ref, grad_held, pool_held, sems) = refs[:3], refs[3:]
    step = pl.program_id(0)
    sources = ((grad_ref, grad_held), (pool_ref, pool_held))

    def copies(i):
        at = pl.ds(i * STEP, STEP)
        return [
            pltpu.make_async_copy(ref.at[at], held.at[at], sems.at[n, i]) for n, (ref, held) in enumerate(sources)
        ]

    @pl.when(step == 0)
    def _():
        for i in range(grad_ref.shape[0] // STEP):
            for copy in copies(i):
                copy.start()
        width = EB * slots
        lane = lax.broadcasted_iota(jnp.int32, (2 * EB, width), 1)
        row = lax.broadcasted_iota(jnp.int32, (2 * EB, width), 0)
        for s in range(0, slots, 2):
            group = jnp.where(row < EB, assign_ref[s], assign_ref[s + 1])
            hit = lane == (row % EB) * slots + group
            perm_ref[s * EB : (s + 2) * EB, :] = jnp.where(hit, 1.0, 0.0).astype(jnp.bfloat16)

    for copy, (_, held), cuts in zip(copies(step), sources, pieces):
        copy.wait()
        width = held.shape[2]
        for start in range(0, STEP, 2 * EB):
            pair = []
            for at in (start, start + EB):
                block = held[pl.ds(step * STEP + at, EB)].reshape(EB * slots, width)
                moved = jnp.dot(perm_ref[...], block, preferred_element_type=jnp.float32)
                pair.append(moved.reshape(slots, EB, width))
            both = jnp.concatenate(pair, axis=1).astype(jnp.bfloat16)
            for n, low, high in cuts:
                outs[n][:, start : start + 2 * EB, :] = both[:, :, low:high]


def permute(assign, grad_out, pooled):
    count, slots, _ = grad_out.shape
    widths = (2 * PD, PD, WSUM)
    pieces = (((0, 0, 2 * PD), (1, 2 * PD, 3 * PD)), ((2, 0, WSUM),))
    return pl.pallas_call(
        functools.partial(permute_kernel, slots, pieces),
        out_shape=[jax.ShapeDtypeStruct((slots, count, width), jnp.bfloat16) for width in widths],
        grid_spec=pltpu.PrefetchScalarGridSpec(
            num_scalar_prefetch=1,
            grid=(count // STEP,),
            in_specs=[HBM] * 2,
            out_specs=[pl.BlockSpec((slots, STEP, width), lambda i, a: (0, i, 0)) for width in widths],
            scratch_shapes=[
                pltpu.VMEM((EB * slots, EB * slots), jnp.bfloat16),
                pltpu.VMEM(grad_out.shape, jnp.bfloat16),
                pltpu.VMEM(pooled.shape, jnp.bfloat16),
                pltpu.SemaphoreType.DMA((2, count // STEP)),
            ],
        ),
        compiler_params=params(1),
        cost_estimate=cost(1e7),
        name="permute_groups",
    )(assign, grad_out, pooled)


def fetch(ref, held, sems, blocks, pick=lambda i: i):
    size = held.shape[0] // blocks
    copies = [
        pltpu.make_async_copy(ref.at[pl.ds(pick(i) * size, size)], held.at[pl.ds(i * size, size)], sems.at[i])
        for i in range(blocks)
    ]
    for copy in copies:
        copy.start()
    return copies


def narrow_kernel(blocks, place_ref, g_ref, w_ref, *refs):
    out_ref, g_held, w_held, out_held, g_sems, w_sems, out_sems = refs[-7:]
    weights = fetch(w_ref, w_held, w_sems, 1)
    loads = fetch(g_ref, g_held, g_sems, blocks)
    slots, count, _ = g_held.shape
    step, half = slots // blocks, count // 2
    column = lax.broadcasted_iota(jnp.int32, (count, W12), 1)
    dims = (((1,), (1,)), ((), ()))
    weights[0].wait()
    stores = []
    for i, load in enumerate(loads):
        load.wait()
        for s in range(i * step, (i + 1) * step):
            w = w_held[place_ref[s]]
            first = lax.dot_general(g_held[s, :, :PD], w, dims, preferred_element_type=jnp.float32)
            second = lax.dot_general(g_held[s, :, PD:], w, dims, preferred_element_type=jnp.float32)
            d = jnp.where(column < W1, first, second)
            out_held[s] = jnp.concatenate([d[:half], d[half:]], axis=1).astype(jnp.bfloat16)
        at = pl.ds(i * step, step)
        stores.append(pltpu.make_async_copy(out_held.at[at], out_ref.at[at], out_sems.at[i]))
        stores[-1].start()
    for store in stores:
        store.wait()


def narrow_dpool(place, g12, w12, after=()):
    slots, count, _ = g12.shape
    blocks = 4
    shape = (slots, count // 2, 2 * W12)
    return pl.pallas_call(
        functools.partial(narrow_kernel, blocks),
        out_shape=jax.ShapeDtypeStruct(shape, jnp.bfloat16),
        grid_spec=pltpu.PrefetchScalarGridSpec(
            num_scalar_prefetch=1,
            grid=(1,),
            in_specs=[HBM] * 2 + [ANY] * len(after),
            out_specs=HBM,
            scratch_shapes=[
                pltpu.VMEM(g12.shape, jnp.bfloat16),
                pltpu.VMEM(w12.shape, jnp.bfloat16),
                pltpu.VMEM(shape, jnp.bfloat16),
                pltpu.SemaphoreType.DMA((blocks,)),
                pltpu.SemaphoreType.DMA((1,)),
                pltpu.SemaphoreType.DMA((blocks,)),
            ],
        ),
        compiler_params=params(1),
        cost_estimate=cost(1e7),
        name="narrow_dpool",
    )(place, g12, w12, *after)


def partial_kernel(ins, added, results, node_ref, line_ref, *refs):
    blocks, size = node_ref.shape[0], line_ref.shape[0]
    operands, others = refs[:ins], refs[ins : ins + added]
    outs, scratch = refs[-3 - 2 * results - ins - added :][:results], refs[-3 - results - ins - added :]
    held, other_held, out_held = scratch[:ins], scratch[ins : ins + added], scratch[ins + added : -3]
    in_sems, other_sems, out_sems = scratch[-3:]

    def block(arrays, i):
        per = blocks // len(arrays)
        return arrays[i // per].at[pl.ds(i % per * size, size)]

    loads = [
        fetch(ref, at, in_sems.at[n], blocks, lambda i: node_ref[i])
        for n, (ref, at) in enumerate(zip(operands, held))
    ]
    if added:
        loads.append(
            [
                pltpu.make_async_copy(block(others, i), block(other_held, i), other_sems.at[i])
                for i in range(blocks)
            ]
        )
        for copy in loads[-1]:
            copy.start()
    stores = []
    for i in range(blocks):
        for copies in loads:
            copies[i].wait()
        out = block(out_held, i)
        for l in range(size):
            slot = i * size + line_ref[l]
            q = held[0][slot].T
            narrow = jnp.dot(q[:W12], held[1][slot], preferred_element_type=jnp.float32)
            wide = jnp.dot(q[W12:], held[2][slot], preferred_element_type=jnp.float32)
            pieces = ((0, W1, narrow[:W1, :PD]), (W1, W12, narrow[W1:, PD:]), (W12, WSUM, wide))
            for start, end, piece in pieces:
                if added:
                    piece = piece + block(other_held, i)[l, start:end]
                out[l, start:end] = piece.astype(out.dtype)
        stores.append(pltpu.make_async_copy(out, block(outs, i), out_sems.at[i]))
        stores[-1].start()
    for store in stores:
        store.wait()


def partial_proj(nodes, lines, q, g12, g3, results, others=()):
    _, count, _ = q.shape
    blocks, size = nodes.shape[0], lines.shape[0]
    kinds = [jnp.bfloat16 if others and i else jnp.float32 for i in range(results)]
    shapes = [jax.ShapeDtypeStruct((blocks // results * size, WSUM, PD), kind) for kind in kinds]
    operands = (q, g12, g3)
    return pl.pallas_call(
        functools.partial(partial_kernel, len(operands), len(others), results),
        out_shape=shapes,
        grid_spec=pltpu.PrefetchScalarGridSpec(
            num_scalar_prefetch=2,
            grid=(1,),
            in_specs=[HBM] * len(operands) + [ANY] * len(others),
            out_specs=[HBM] * results,
            scratch_shapes=[pltpu.VMEM((blocks * size, count, x.shape[2]), jnp.bfloat16) for x in operands]
            + [pltpu.VMEM(x.shape, x.dtype) for x in others]
            + [pltpu.VMEM(x.shape, x.dtype) for x in shapes]
            + [
                pltpu.SemaphoreType.DMA((len(operands), blocks)),
                pltpu.SemaphoreType.DMA((blocks,)),
                pltpu.SemaphoreType.DMA((blocks,)),
            ],
        ),
        compiler_params=params(1),
        cost_estimate=cost(1e7),
        name="partial_proj",
    )(nodes, lines, *operands, *others)


def count_kernel(index_ref, length_ref, *refs):
    out_ref = refs[-1]
    bag, block = index_ref.shape[1], index_ref.shape[2]
    lanes, chunk, low = 256, 16, ROWS // 8

    def one(i, carry):
        at = pl.ds(pl.multiple_of(i * lanes, lanes), lanes)
        index = index_ref[0, :, at]
        which = lax.broadcasted_iota(jnp.int32, (bag, lanes), 0)
        key = jnp.where(which < length_ref[0, :, at], index & (low - 1), -1)
        unit = jnp.left_shift(jnp.int32(1), jnp.right_shift(index, 6) * 4)
        ids = lax.broadcasted_iota(jnp.int32, (chunk, lanes), 0)
        for c in range(low // chunk):
            total = jnp.zeros((chunk, lanes), jnp.int32)
            for j in range(bag):
                total = total + jnp.where(key[j : j + 1] == ids + c * chunk, unit[j : j + 1], 0)
            out_ref[0, c * chunk : (c + 1) * chunk, at] = total
        return carry

    lax.fori_loop(0, block // lanes, one, 0)


def count_hits(lookups, counts, after=()):
    tables, bag, examples = lookups.shape
    block = 4096
    return pl.pallas_call(
        count_kernel,
        out_shape=jax.ShapeDtypeStruct((tables, ROWS // 8, examples), jnp.int32),
        grid=(tables, examples // block),
        in_specs=[
            pl.BlockSpec((1, bag, block), lambda k, i: (k, 0, i)),
            pl.BlockSpec((1, 1, block), lambda k, i: (k, 0, i)),
        ]
        + [ANY] * len(after),
        out_specs=pl.BlockSpec((1, ROWS // 8, block), lambda k, i: (k, 0, i)),
        compiler_params=params(2),
        cost_estimate=cost(1e7),
        name="count_hits",
    )(lookups, counts, *after)


def unpacked(words):
    rows = [lax.shift_right_logical(words, jnp.int32(4 * n)) & 15 for n in range(8)]
    return jnp.concatenate([r.astype(jnp.float32).astype(jnp.bfloat16) for r in rows], axis=0)


def wide_kernel(hits_ref, g_ref, w_ref, *refs):
    out_ref = refs[-1]

    @pl.when(pl.program_id(0) == 0)
    def _():
        out_ref[...] = jnp.zeros_like(out_ref)

    block = g_ref.shape[0]
    column = lax.broadcasted_iota(jnp.int32, (block, WSUM), 1)
    d = lax.dot_general(g_ref[...], w_ref[...], (((1,), (1,)), ((), ())), preferred_element_type=jnp.float32)
    d = jnp.where(column < W12, 0.0, d).astype(jnp.bfloat16)
    out_ref[...] += jnp.dot(unpacked(hits_ref[0]), d, preferred_element_type=jnp.float32)


def wide_sum(hits, g3, weights, after=()):
    _, words, examples = hits.shape
    block = 1024
    return pl.pallas_call(
        wide_kernel,
        out_shape=jax.ShapeDtypeStruct((ROWS, WSUM), jnp.float32),
        grid=(examples // block,),
        in_specs=[
            pl.BlockSpec((1, words, block), lambda i: (2, 0, i)),
            pl.BlockSpec((block, PD), lambda i: (i, 0)),
            pl.BlockSpec((WSUM, PD), lambda i: (0, 0)),
        ]
        + [ANY] * len(after),
        out_specs=pl.BlockSpec((ROWS, WSUM), lambda i: (0, 0)),
        compiler_params=params(1),
        cost_estimate=cost(1e7),
        name="wide_sum",
    )(hits, g3, weights, *after)


def narrow_sum_kernel(hits_ref, d_ref, wide_ref, *refs):
    out_ref = refs[-1]

    @pl.when(pl.program_id(0) == 0)
    def _():
        out_ref[...] = wide_ref[...]

    sources = d_ref.shape[0]
    block = hits_ref.shape[2]
    column = lax.broadcasted_iota(jnp.int32, (block, PD), 1)
    pieces = []
    for d in range(sources):
        packed = d_ref[d].astype(jnp.float32)
        pieces += [packed, pltpu.roll(packed, PD - W12, 1)]
    both = jnp.concatenate(pieces, axis=0)
    d1 = jnp.where(column < W1, both, 0.0).astype(jnp.bfloat16)
    d2 = jnp.where((column >= W1) & (column < W12), both, 0.0).astype(jnp.bfloat16)
    out_ref[...] += jnp.dot(unpacked(hits_ref[0]), d1, preferred_element_type=jnp.float32) + jnp.dot(
        unpacked(hits_ref[1]), d2, preferred_element_type=jnp.float32
    )


def narrow_sum(hits, narrow, wide, after=()):
    _, words, examples = hits.shape
    sources, half, _ = narrow.shape
    block = 1024
    per = block // (2 * half)
    return pl.pallas_call(
        narrow_sum_kernel,
        out_shape=jax.ShapeDtypeStruct((ROWS, WSUM), jnp.float32),
        grid=(examples // block,),
        in_specs=[
            pl.BlockSpec((2, words, block), lambda i: (0, 0, i)),
            pl.BlockSpec((per, half, 2 * W12), lambda i: (i, 0, 0)),
            pl.BlockSpec((ROWS, PD), lambda i: (0, 0)),
        ]
        + [ANY] * len(after),
        out_specs=pl.BlockSpec((ROWS, PD), lambda i: (0, 0)),
        input_output_aliases={2: 0},
        compiler_params=params(1),
        cost_estimate=cost(1e7),
        name="narrow_sum",
    )(hits, narrow, wide, *after)


def swap(x, axis, size, bits):
    return lax.ppermute(x, axis, [(d, d ^ bits) for d in range(size)])


def local(sizes, grad_out, pooled, proj, assign, indices, lengths):
    count, slots, _ = grad_out.shape
    scale = 1.0 / math.sqrt(count * slots)
    n_node, n_local = sizes["node"], sizes["local"]
    n_plane = n_node // 2
    node, loc = lax.axis_index("node"), lax.axis_index("local")

    rows = proj[:, :W12]
    rows = jnp.concatenate([rows] + [swap(rows, "local", n_local, d) for d in range(1, n_local)])
    g12, g3, q = permute(assign, grad_out, pooled)
    rows, g3 = lax.optimization_barrier((rows, g3))
    g3_got = lax.all_to_all(g3, AXES, split_axis=0, concat_axis=0, tiled=True)

    plane = jnp.arange(n_plane, dtype=jnp.int32) ^ (node // 2)
    lines = jnp.arange(n_local, dtype=jnp.int32) ^ loc
    sent = partial_proj(plane * 2 + 1 - node % 2, lines, q, g12, g3, 2)
    got = [swap(x, "node", n_node, 1) for x in sent]

    rows, sent = lax.optimization_barrier((rows, sent))
    rows = jnp.concatenate([rows] + [swap(rows, "node", n_node, 2 * d) for d in range(1, n_plane)])
    kept = partial_proj(plane * 2 + node % 2, lines, q, g12, g3, n_plane, got)

    rows = jnp.concatenate([rows, swap(rows, "node", n_node, 1)])
    slot = jnp.arange(slots, dtype=jnp.int32)
    slot_node = slot // n_local ^ node
    slot_place = slot_node % 2 * (slots // 2) + slot_node // 2 * n_local + (slot % n_local ^ loc)
    narrow = narrow_dpool(slot_place, g12, rows, after=kept[:1])
    hits = count_hits(indices[0].transpose(1, 2, 0), lengths[0].T[:, None, :], after=[narrow])

    narrow, g3_got, kept = lax.optimization_barrier((narrow, g3_got, kept))
    narrow_got = lax.all_to_all(narrow, AXES, split_axis=0, concat_axis=0, tiled=True)
    total = kept[0]
    for d in range(1, n_plane):
        total = total + swap(kept[d], "node", n_node, 2 * d).astype(jnp.float32)
    wide = wide_sum(hits, g3_got.reshape(-1, PD), proj[0])
    total, wide = lax.optimization_barrier((total, wide))
    rounded = total.astype(jnp.bfloat16)
    own, terms = total[:1], [swap(rounded[d : d + 1], "local", n_local, d) for d in range(1, n_local)]

    table_grad = narrow_sum(hits, narrow_got, wide)[None]
    terms, table_grad = lax.optimization_barrier((terms, table_grad))
    proj_grad = sum((term.astype(jnp.float32) for term in terms), own) * scale
    return (table_grad, proj_grad)


def solution(mesh):
    placed = (
        P(AXES, None, None),
        P(AXES, None, None),
        P(AXES, None, None),
        P(),
        P(AXES, None, None, None),
        P(AXES, None, None),
    )
    return jax.shard_map(
        functools.partial(local, dict(mesh.shape)),
        mesh=mesh,
        in_specs=placed,
        out_specs=(P(AXES, None, None), P(AXES, None, None)),
        check_vma=False,
    )
```

```python
import functools
import math

import jax
import jax.numpy as jnp
from jax import lax
from jax.experimental import pallas as pl
from jax.experimental.pallas import tpu as pltpu
from jax.sharding import PartitionSpec as P

ROWS = 512
W1 = 16
W2 = 48
W3 = 192
PD = 128
W12 = W1 + W2
WSUM = W12 + W3
AXES = ("node", "local")
EB = 8
STEP = 32
MIB = 1024 * 1024


def params(grid):
    return pltpu.CompilerParams(dimension_semantics=("arbitrary",) * grid, vmem_limit_bytes=58 * MIB)


HBM = pl.BlockSpec(memory_space=pltpu.HBM)
ANY = pl.BlockSpec(memory_space=pl.ANY)


def cost(flops):
    return pl.CostEstimate(flops=int(flops), bytes_accessed=1024, transcendentals=0)


def permute_kernel(slots, pieces, assign_ref, grad_ref, pool_ref, *refs):
    outs, (perm_ref, grad_held, pool_held, sems) = refs[:3], refs[3:]
    step = pl.program_id(0)
    sources = ((grad_ref, grad_held), (pool_ref, pool_held))

    def copies(i):
        at = pl.ds(i * STEP, STEP)
        return [
            pltpu.make_async_copy(ref.at[at], held.at[at], sems.at[n, i]) for n, (ref, held) in enumerate(sources)
        ]

    @pl.when(step == 0)
    def _():
        for i in range(grad_ref.shape[0] // STEP):
            for copy in copies(i):
                copy.start()
        width = EB * slots
        lane = lax.broadcasted_iota(jnp.int32, (2 * EB, width), 1)
        row = lax.broadcasted_iota(jnp.int32, (2 * EB, width), 0)
        for s in range(0, slots, 2):
            group = jnp.where(row < EB, assign_ref[s], assign_ref[s + 1])
            hit = lane == (row % EB) * slots + group
            perm_ref[s * EB : (s + 2) * EB, :] = jnp.where(hit, 1.0, 0.0).astype(jnp.bfloat16)

    for copy, (_, held), cuts in zip(copies(step), sources, pieces):
        copy.wait()
        width = held.shape[2]
        for start in range(0, STEP, 2 * EB):
            pair = []
            for at in (start, start + EB):
                block = held[pl.ds(step * STEP + at, EB)].reshape(EB * slots, width)
                moved = jnp.dot(perm_ref[...], block, preferred_element_type=jnp.float32)
                pair.append(moved.reshape(slots, EB, width))
            both = jnp.concatenate(pair, axis=1).astype(jnp.bfloat16)
            for n, low, high in cuts:
                outs[n][:, start : start + 2 * EB, :] = both[:, :, low:high]


def permute(assign, grad_out, pooled):
    count, slots, _ = grad_out.shape
    widths = (2 * PD, PD, WSUM)
    pieces = (((0, 0, 2 * PD), (1, 2 * PD, 3 * PD)), ((2, 0, WSUM),))
    return pl.pallas_call(
        functools.partial(permute_kernel, slots, pieces),
        out_shape=[jax.ShapeDtypeStruct((slots, count, width), jnp.bfloat16) for width in widths],
        grid_spec=pltpu.PrefetchScalarGridSpec(
            num_scalar_prefetch=1,
            grid=(count // STEP,),
            in_specs=[HBM] * 2,
            out_specs=[pl.BlockSpec((slots, STEP, width), lambda i, a: (0, i, 0)) for width in widths],
            scratch_shapes=[
                pltpu.VMEM((EB * slots, EB * slots), jnp.bfloat16),
                pltpu.VMEM(grad_out.shape, jnp.bfloat16),
                pltpu.VMEM(pooled.shape, jnp.bfloat16),
                pltpu.SemaphoreType.DMA((2, count // STEP)),
            ],
        ),
        compiler_params=params(1),
        cost_estimate=cost(1e7),
        name="permute_groups",
    )(assign, grad_out, pooled)


def fetch(ref, held, sems, blocks, pick=lambda i: i):
    size = held.shape[0] // blocks
    copies = [
        pltpu.make_async_copy(ref.at[pl.ds(pick(i) * size, size)], held.at[pl.ds(i * size, size)], sems.at[i])
        for i in range(blocks)
    ]
    for copy in copies:
        copy.start()
    return copies


def narrow_kernel(blocks, place_ref, g_ref, w_ref, *refs):
    out_ref, g_held, w_held, out_held, g_sems, w_sems, out_sems = refs[-7:]
    weights = fetch(w_ref, w_held, w_sems, 1)
    loads = fetch(g_ref, g_held, g_sems, blocks)
    slots, count, _ = g_held.shape
    step, half = slots // blocks, count // 2
    column = lax.broadcasted_iota(jnp.int32, (count, W12), 1)
    dims = (((1,), (1,)), ((), ()))
    weights[0].wait()
    stores = []
    for i, load in enumerate(loads):
        load.wait()
        for s in range(i * step, (i + 1) * step):
            w = w_held[place_ref[s]]
            first = lax.dot_general(g_held[s, :, :PD], w, dims, preferred_element_type=jnp.float32)
            second = lax.dot_general(g_held[s, :, PD:], w, dims, preferred_element_type=jnp.float32)
            d = jnp.where(column < W1, first, second)
            out_held[s] = jnp.concatenate([d[:half], d[half:]], axis=1).astype(jnp.bfloat16)
        at = pl.ds(i * step, step)
        stores.append(pltpu.make_async_copy(out_held.at[at], out_ref.at[at], out_sems.at[i]))
        stores[-1].start()
    for store in stores:
        store.wait()


def narrow_dpool(place, g12, w12, after=()):
    slots, count, _ = g12.shape
    blocks = 4
    shape = (slots, count // 2, 2 * W12)
    return pl.pallas_call(
        functools.partial(narrow_kernel, blocks),
        out_shape=jax.ShapeDtypeStruct(shape, jnp.bfloat16),
        grid_spec=pltpu.PrefetchScalarGridSpec(
            num_scalar_prefetch=1,
            grid=(1,),
            in_specs=[HBM] * 2 + [ANY] * len(after),
            out_specs=HBM,
            scratch_shapes=[
                pltpu.VMEM(g12.shape, jnp.bfloat16),
                pltpu.VMEM(w12.shape, jnp.bfloat16),
                pltpu.VMEM(shape, jnp.bfloat16),
                pltpu.SemaphoreType.DMA((blocks,)),
                pltpu.SemaphoreType.DMA((1,)),
                pltpu.SemaphoreType.DMA((blocks,)),
            ],
        ),
        compiler_params=params(1),
        cost_estimate=cost(4e9),
        name="narrow_dpool",
    )(place, g12, w12, *after)


def partial_kernel(ins, added, results, node_ref, line_ref, *refs):
    blocks, size = node_ref.shape[0], line_ref.shape[0]
    operands, others = refs[:ins], refs[ins : ins + added]
    outs, scratch = refs[-3 - 2 * results - ins - added :][:results], refs[-3 - results - ins - added :]
    held, other_held, out_held = scratch[:ins], scratch[ins : ins + added], scratch[ins + added : -3]
    in_sems, other_sems, out_sems = scratch[-3:]

    def block(arrays, i):
        per = blocks // len(arrays)
        return arrays[i // per].at[pl.ds(i % per * size, size)]

    loads = [
        fetch(ref, at, in_sems.at[n], blocks, lambda i: node_ref[i])
        for n, (ref, at) in enumerate(zip(operands, held))
    ]
    if added:
        loads.append(
            [
                pltpu.make_async_copy(block(others, i), block(other_held, i), other_sems.at[i])
                for i in range(blocks)
            ]
        )
        for copy in loads[-1]:
            copy.start()
    stores = []
    for i in range(blocks):
        for copies in loads:
            copies[i].wait()
        out = block(out_held, i)
        for l in range(size):
            slot = i * size + line_ref[l]
            q = held[0][slot].T
            narrow = jnp.dot(q[:W12], held[1][slot], preferred_element_type=jnp.float32)
            wide = jnp.dot(q[W12:], held[2][slot], preferred_element_type=jnp.float32)
            pieces = ((0, W1, narrow[:W1, :PD]), (W1, W12, narrow[W1:, PD:]), (W12, WSUM, wide))
            for start, end, piece in pieces:
                if added:
                    piece = piece + block(other_held, i)[l, start:end]
                out[l, start:end] = piece.astype(out.dtype)
        stores.append(pltpu.make_async_copy(out, block(outs, i), out_sems.at[i]))
        stores[-1].start()
    for store in stores:
        store.wait()


def partial_proj(nodes, lines, q, g12, g3, results, others=()):
    _, count, _ = q.shape
    blocks, size = nodes.shape[0], lines.shape[0]
    kinds = [jnp.bfloat16 if others and i else jnp.float32 for i in range(results)]
    shapes = [jax.ShapeDtypeStruct((blocks // results * size, WSUM, PD), kind) for kind in kinds]
    operands = (q, g12, g3)
    return pl.pallas_call(
        functools.partial(partial_kernel, len(operands), len(others), results),
        out_shape=shapes,
        grid_spec=pltpu.PrefetchScalarGridSpec(
            num_scalar_prefetch=2,
            grid=(1,),
            in_specs=[HBM] * len(operands) + [ANY] * len(others),
            out_specs=[HBM] * results,
            scratch_shapes=[pltpu.VMEM((blocks * size, count, x.shape[2]), jnp.bfloat16) for x in operands]
            + [pltpu.VMEM(x.shape, x.dtype) for x in others]
            + [pltpu.VMEM(x.shape, x.dtype) for x in shapes]
            + [
                pltpu.SemaphoreType.DMA((len(operands), blocks)),
                pltpu.SemaphoreType.DMA((blocks,)),
                pltpu.SemaphoreType.DMA((blocks,)),
            ],
        ),
        compiler_params=params(1),
        cost_estimate=cost(4e9 if others else 1e7),
        name="partial_proj",
    )(nodes, lines, *operands, *others)


def count_kernel(index_ref, length_ref, *refs):
    out_ref = refs[-1]
    bag, block = index_ref.shape[1], index_ref.shape[2]
    lanes, chunk, low = 256, 16, ROWS // 8

    def one(i, carry):
        at = pl.ds(pl.multiple_of(i * lanes, lanes), lanes)
        index = index_ref[0, :, at]
        which = lax.broadcasted_iota(jnp.int32, (bag, lanes), 0)
        key = jnp.where(which < length_ref[0, :, at], index & (low - 1), -1)
        unit = jnp.left_shift(jnp.int32(1), jnp.right_shift(index, 6) * 4)
        ids = lax.broadcasted_iota(jnp.int32, (chunk, lanes), 0)
        for c in range(low // chunk):
            total = jnp.zeros((chunk, lanes), jnp.int32)
            for j in range(bag):
                total = total + jnp.where(key[j : j + 1] == ids + c * chunk, unit[j : j + 1], 0)
            out_ref[0, c * chunk : (c + 1) * chunk, at] = total
        return carry

    lax.fori_loop(0, block // lanes, one, 0)


def count_hits(lookups, counts, after=()):
    tables, bag, examples = lookups.shape
    block = 4096
    return pl.pallas_call(
        count_kernel,
        out_shape=jax.ShapeDtypeStruct((tables, ROWS // 8, examples), jnp.int32),
        grid=(tables, examples // block),
        in_specs=[
            pl.BlockSpec((1, bag, block), lambda k, i: (k, 0, i)),
            pl.BlockSpec((1, 1, block), lambda k, i: (k, 0, i)),
        ]
        + [ANY] * len(after),
        out_specs=pl.BlockSpec((1, ROWS // 8, block), lambda k, i: (k, 0, i)),
        compiler_params=params(2),
        cost_estimate=cost(5e9),
        name="count_hits",
    )(lookups, counts, *after)


def unpacked(words):
    rows = [lax.shift_right_logical(words, jnp.int32(4 * n)) & 15 for n in range(8)]
    return jnp.concatenate([r.astype(jnp.float32).astype(jnp.bfloat16) for r in rows], axis=0)


def wide_kernel(hits_ref, g_ref, w_ref, *refs):
    out_ref = refs[-1]

    @pl.when(pl.program_id(0) == 0)
    def _():
        out_ref[...] = jnp.zeros_like(out_ref)

    block = g_ref.shape[0]
    column = lax.broadcasted_iota(jnp.int32, (block, WSUM), 1)
    d = lax.dot_general(g_ref[...], w_ref[...], (((1,), (1,)), ((), ())), preferred_element_type=jnp.float32)
    d = jnp.where(column < W12, 0.0, d).astype(jnp.bfloat16)
    out_ref[...] += jnp.dot(unpacked(hits_ref[0]), d, preferred_element_type=jnp.float32)


def wide_sum(hits, g3, weights, after=()):
    _, words, examples = hits.shape
    block = 1024
    return pl.pallas_call(
        wide_kernel,
        out_shape=jax.ShapeDtypeStruct((ROWS, WSUM), jnp.float32),
        grid=(examples // block,),
        in_specs=[
            pl.BlockSpec((1, words, block), lambda i: (2, 0, i)),
            pl.BlockSpec((block, PD), lambda i: (i, 0)),
            pl.BlockSpec((WSUM, PD), lambda i: (0, 0)),
        ]
        + [ANY] * len(after),
        out_specs=pl.BlockSpec((ROWS, WSUM), lambda i: (0, 0)),
        compiler_params=params(1),
        cost_estimate=cost(1e7),
        name="wide_sum",
    )(hits, g3, weights, *after)


def narrow_sum_kernel(hits_ref, d_ref, wide_ref, *refs):
    out_ref = refs[-1]

    @pl.when(pl.program_id(0) == 0)
    def _():
        out_ref[...] = wide_ref[...]

    sources = d_ref.shape[0]
    block = hits_ref.shape[2]
    column = lax.broadcasted_iota(jnp.int32, (block, PD), 1)
    pieces = []
    for d in range(sources):
        packed = d_ref[d].astype(jnp.float32)
        pieces += [packed, pltpu.roll(packed, PD - W12, 1)]
    both = jnp.concatenate(pieces, axis=0)
    d1 = jnp.where(column < W1, both, 0.0).astype(jnp.bfloat16)
    d2 = jnp.where((column >= W1) & (column < W12), both, 0.0).astype(jnp.bfloat16)
    out_ref[...] += jnp.dot(unpacked(hits_ref[0]), d1, preferred_element_type=jnp.float32) + jnp.dot(
        unpacked(hits_ref[1]), d2, preferred_element_type=jnp.float32
    )


def narrow_sum(hits, narrow, wide, after=()):
    _, words, examples = hits.shape
    sources, half, _ = narrow.shape
    block = 1024
    per = block // (2 * half)
    return pl.pallas_call(
        narrow_sum_kernel,
        out_shape=jax.ShapeDtypeStruct((ROWS, WSUM), jnp.float32),
        grid=(examples // block,),
        in_specs=[
            pl.BlockSpec((2, words, block), lambda i: (0, 0, i)),
            pl.BlockSpec((per, half, 2 * W12), lambda i: (i, 0, 0)),
            pl.BlockSpec((ROWS, PD), lambda i: (0, 0)),
        ]
        + [ANY] * len(after),
        out_specs=pl.BlockSpec((ROWS, PD), lambda i: (0, 0)),
        input_output_aliases={2: 0},
        compiler_params=params(1),
        cost_estimate=cost(1e7),
        name="narrow_sum",
    )(hits, narrow, wide, *after)


def swap(x, axis, size, bits):
    return lax.ppermute(x, axis, [(d, d ^ bits) for d in range(size)])


def local(sizes, grad_out, pooled, proj, assign, indices, lengths):
    count, slots, _ = grad_out.shape
    scale = 1.0 / math.sqrt(count * slots)
    n_node, n_local = sizes["node"], sizes["local"]
    n_plane = n_node // 2
    node, loc = lax.axis_index("node"), lax.axis_index("local")

    rows = proj[:, :W12]
    rows = jnp.concatenate([rows] + [swap(rows, "local", n_local, d) for d in range(1, n_local)])
    g12, g3, q = permute(assign, grad_out, pooled)
    rows, g3 = lax.optimization_barrier((rows, g3))
    g3_got = lax.all_to_all(g3, AXES, split_axis=0, concat_axis=0, tiled=True)

    plane = jnp.arange(n_plane, dtype=jnp.int32) ^ (node // 2)
    lines = jnp.arange(n_local, dtype=jnp.int32) ^ loc
    sent = partial_proj(plane * 2 + 1 - node % 2, lines, q, g12, g3, 2)
    got = [swap(x, "node", n_node, 1) for x in sent]

    rows, sent = lax.optimization_barrier((rows, sent))
    rows = jnp.concatenate([rows] + [swap(rows, "node", n_node, 2 * d) for d in range(1, n_plane)])
    hits = count_hits(indices[0].transpose(1, 2, 0), lengths[0].T[:, None, :], after=sent[:1])
    kept = partial_proj(plane * 2 + node % 2, lines, q, g12, g3, n_plane, got)
    farthest = swap(kept[-1], "node", n_node, 2 * (n_plane - 1))

    rows = jnp.concatenate([rows, swap(rows, "node", n_node, 1)])
    slot = jnp.arange(slots, dtype=jnp.int32)
    slot_node = slot // n_local ^ node
    slot_place = slot_node % 2 * (slots // 2) + slot_node // 2 * n_local + (slot % n_local ^ loc)
    narrow = narrow_dpool(slot_place, g12, rows, after=kept[:1])

    narrow, hits, g3_got, kept, farthest = lax.optimization_barrier((narrow, hits, g3_got, kept, farthest))
    narrow_got = lax.all_to_all(narrow, AXES, split_axis=0, concat_axis=0, tiled=True)
    total = kept[0] + farthest.astype(jnp.float32)
    for d in range(1, n_plane - 1):
        total = total + swap(kept[d], "node", n_node, 2 * d).astype(jnp.float32)
    wide = wide_sum(hits, g3_got.reshape(-1, PD), proj[0])
    total, wide = lax.optimization_barrier((total, wide))
    rounded = total.astype(jnp.bfloat16)
    own, terms = total[:1], [swap(rounded[d : d + 1], "local", n_local, d) for d in range(1, n_local)]

    table_grad = narrow_sum(hits, narrow_got, wide)[None]
    terms, table_grad = lax.optimization_barrier((terms, table_grad))
    proj_grad = sum((term.astype(jnp.float32) for term in terms), own) * scale
    return (table_grad, proj_grad)


def solution(mesh):
    placed = (
        P(AXES, None, None),
        P(AXES, None, None),
        P(AXES, None, None),
        P(),
        P(AXES, None, None, None),
        P(AXES, None, None),
    )
    return jax.shard_map(
        functools.partial(local, dict(mesh.shape)),
        mesh=mesh,
        in_specs=placed,
        out_specs=(P(AXES, None, None), P(AXES, None, None)),
        check_vma=False,
    )
```

```python
import functools
import math

import jax
import jax.numpy as jnp
from jax import lax
from jax.experimental import pallas as pl
from jax.experimental.pallas import tpu as pltpu
from jax.sharding import PartitionSpec as P

ROWS = 512
W1 = 16
W2 = 48
W3 = 192
PD = 128
W12 = W1 + W2
WSUM = W12 + W3
AXES = ("node", "local")
EB = 8
STEP = 32
MIB = 1024 * 1024


def params(grid):
    return pltpu.CompilerParams(dimension_semantics=("arbitrary",) * grid, vmem_limit_bytes=58 * MIB)


HBM = pl.BlockSpec(memory_space=pltpu.HBM)
ANY = pl.BlockSpec(memory_space=pl.ANY)


def cost(flops):
    return pl.CostEstimate(flops=int(flops), bytes_accessed=1024, transcendentals=0)


def permute_kernel(slots, pieces, assign_ref, grad_ref, pool_ref, *refs):
    outs, (perm_ref, grad_held, pool_held, sems) = refs[:3], refs[3:]
    step = pl.program_id(0)
    sources = ((grad_ref, grad_held), (pool_ref, pool_held))

    def copies(i):
        at = pl.ds(i * STEP, STEP)
        return [
            pltpu.make_async_copy(ref.at[at], held.at[at], sems.at[n, i]) for n, (ref, held) in enumerate(sources)
        ]

    @pl.when(step == 0)
    def _():
        for i in range(grad_ref.shape[0] // STEP):
            for copy in copies(i):
                copy.start()
        width = EB * slots
        lane = lax.broadcasted_iota(jnp.int32, (2 * EB, width), 1)
        row = lax.broadcasted_iota(jnp.int32, (2 * EB, width), 0)
        for s in range(0, slots, 2):
            group = jnp.where(row < EB, assign_ref[s], assign_ref[s + 1])
            hit = lane == (row % EB) * slots + group
            perm_ref[s * EB : (s + 2) * EB, :] = jnp.where(hit, 1.0, 0.0).astype(jnp.bfloat16)

    for copy, (_, held), cuts in zip(copies(step), sources, pieces):
        copy.wait()
        width = held.shape[2]
        for start in range(0, STEP, 2 * EB):
            pair = []
            for at in (start, start + EB):
                block = held[pl.ds(step * STEP + at, EB)].reshape(EB * slots, width)
                moved = jnp.dot(perm_ref[...], block, preferred_element_type=jnp.float32)
                pair.append(moved.reshape(slots, EB, width))
            both = jnp.concatenate(pair, axis=1).astype(jnp.bfloat16)
            for n, low, high in cuts:
                outs[n][:, start : start + 2 * EB, :] = both[:, :, low:high]


def permute(assign, grad_out, pooled):
    count, slots, _ = grad_out.shape
    widths = (2 * PD, PD, WSUM)
    pieces = (((0, 0, 2 * PD), (1, 2 * PD, 3 * PD)), ((2, 0, WSUM),))
    return pl.pallas_call(
        functools.partial(permute_kernel, slots, pieces),
        out_shape=[
            jax.ShapeDtypeStruct((slots, count + (W12 if n == 1 else 0), width), jnp.bfloat16)
            for n, width in enumerate(widths)
        ],
        grid_spec=pltpu.PrefetchScalarGridSpec(
            num_scalar_prefetch=1,
            grid=(count // STEP,),
            in_specs=[HBM] * 2,
            out_specs=[pl.BlockSpec((slots, STEP, width), lambda i, a: (0, i, 0)) for width in widths],
            scratch_shapes=[
                pltpu.VMEM((EB * slots, EB * slots), jnp.bfloat16),
                pltpu.VMEM(grad_out.shape, jnp.bfloat16),
                pltpu.VMEM(pooled.shape, jnp.bfloat16),
                pltpu.SemaphoreType.DMA((2, count // STEP)),
            ],
        ),
        compiler_params=params(1),
        cost_estimate=cost(1e7),
        name="permute_groups",
    )(assign, grad_out, pooled)


def fetch(ref, held, sems, blocks, pick=lambda i: i):
    size, rows = held.shape[0] // blocks, pl.ds(0, held.shape[1])
    copies = [
        pltpu.make_async_copy(
            ref.at[pl.ds(pick(i) * size, size), rows], held.at[pl.ds(i * size, size)], sems.at[i]
        )
        for i in range(blocks)
    ]
    for copy in copies:
        copy.start()
    return copies


def narrow_kernel(blocks, place_ref, g_ref, w_ref, wide_ref, out_ref, g_held, w_held, out_held, g_sems, w_sems, out_sems):
    weights = fetch(w_ref, w_held, w_sems, 1)
    loads = fetch(g_ref, g_held, g_sems, blocks)
    slots, count, _ = g_held.shape
    step, half = slots // blocks, count // 2
    column = lax.broadcasted_iota(jnp.int32, (count, W12), 1)
    dims = (((1,), (1,)), ((), ()))
    weights[0].wait()
    stores = []
    for i, load in enumerate(loads):
        load.wait()
        for s in range(i * step, (i + 1) * step):
            w = w_held[place_ref[s]]
            first = lax.dot_general(g_held[s, :, :PD], w, dims, preferred_element_type=jnp.float32)
            second = lax.dot_general(g_held[s, :, PD:], w, dims, preferred_element_type=jnp.float32)
            d = jnp.where(column < W1, first, second)
            out_held[s] = jnp.concatenate([d[:half], d[half:]], axis=1).astype(jnp.bfloat16)
        at = pl.ds(i * step, step)
        stores.append(pltpu.make_async_copy(out_held.at[at], out_ref.at[at, pl.ds(count, half)], out_sems.at[i]))
        stores[-1].start()
    for store in stores:
        store.wait()


def narrow_dpool(place, g12, w12, wide):
    slots, count, _ = g12.shape
    blocks = 4
    return pl.pallas_call(
        functools.partial(narrow_kernel, blocks),
        out_shape=jax.ShapeDtypeStruct(wide.shape, jnp.bfloat16),
        grid_spec=pltpu.PrefetchScalarGridSpec(
            num_scalar_prefetch=1,
            grid=(1,),
            in_specs=[HBM] * 3,
            out_specs=HBM,
            scratch_shapes=[
                pltpu.VMEM(g12.shape, jnp.bfloat16),
                pltpu.VMEM(w12.shape, jnp.bfloat16),
                pltpu.VMEM((slots, count // 2, 2 * W12), jnp.bfloat16),
                pltpu.SemaphoreType.DMA((blocks,)),
                pltpu.SemaphoreType.DMA((1,)),
                pltpu.SemaphoreType.DMA((blocks,)),
            ],
        ),
        input_output_aliases={3: 0},
        compiler_params=params(1),
        cost_estimate=cost(1e7),
        name="narrow_dpool",
    )(place, g12, w12, wide)


def partial_kernel(ins, added, results, node_ref, line_ref, *refs):
    blocks, size = node_ref.shape[0], line_ref.shape[0]
    operands, others = refs[:ins], refs[ins : ins + added]
    outs, scratch = refs[-3 - 2 * results - ins - added :][:results], refs[-3 - results - ins - added :]
    held, other_held, out_held = scratch[:ins], scratch[ins : ins + added], scratch[ins + added : -3]
    in_sems, other_sems, out_sems = scratch[-3:]

    def block(arrays, i):
        per = blocks // len(arrays)
        return arrays[i // per].at[pl.ds(i % per * size, size)]

    loads = [
        fetch(ref, at, in_sems.at[n], blocks, lambda i: node_ref[i])
        for n, (ref, at) in enumerate(zip(operands, held))
    ]
    if added:
        loads.append(
            [
                pltpu.make_async_copy(block(others, i), block(other_held, i), other_sems.at[i])
                for i in range(blocks)
            ]
        )
        for copy in loads[-1]:
            copy.start()
    stores = []
    for i in range(blocks):
        for copies in loads:
            copies[i].wait()
        out = block(out_held, i)
        for l in range(size):
            slot = i * size + line_ref[l]
            q = held[0][slot].T
            narrow = jnp.dot(q[:W12], held[1][slot], preferred_element_type=jnp.float32)
            wide = jnp.dot(q[W12:], held[2][slot], preferred_element_type=jnp.float32)
            pieces = ((0, W1, narrow[:W1, :PD]), (W1, W12, narrow[W1:, PD:]), (W12, WSUM, wide))
            for start, end, piece in pieces:
                if added:
                    piece = piece + block(other_held, i)[l, start:end]
                out[l, start:end] = piece.astype(out.dtype)
        stores.append(pltpu.make_async_copy(out, block(outs, i), out_sems.at[i]))
        stores[-1].start()
    for store in stores:
        store.wait()


def partial_proj(nodes, lines, q, g12, g3, results, others=()):
    _, count, _ = q.shape
    blocks, size = nodes.shape[0], lines.shape[0]
    kinds = [jnp.bfloat16 if others and i else jnp.float32 for i in range(results)]
    shapes = [jax.ShapeDtypeStruct((blocks // results * size, WSUM, PD), kind) for kind in kinds]
    operands = (q, g12, g3)
    return pl.pallas_call(
        functools.partial(partial_kernel, len(operands), len(others), results),
        out_shape=shapes,
        grid_spec=pltpu.PrefetchScalarGridSpec(
            num_scalar_prefetch=2,
            grid=(1,),
            in_specs=[HBM] * len(operands) + [ANY] * len(others),
            out_specs=[HBM] * results,
            scratch_shapes=[pltpu.VMEM((blocks * size, count, x.shape[2]), jnp.bfloat16) for x in operands]
            + [pltpu.VMEM(x.shape, x.dtype) for x in others]
            + [pltpu.VMEM(x.shape, x.dtype) for x in shapes]
            + [
                pltpu.SemaphoreType.DMA((len(operands), blocks)),
                pltpu.SemaphoreType.DMA((blocks,)),
                pltpu.SemaphoreType.DMA((blocks,)),
            ],
        ),
        compiler_params=params(1),
        cost_estimate=cost(4e9 if others else 1e7),
        name="partial_proj",
    )(nodes, lines, *operands, *others)


def count_kernel(index_ref, length_ref, *refs):
    out_ref = refs[-1]
    bag, block = index_ref.shape[1], index_ref.shape[2]
    lanes, chunk, low = 256, 16, ROWS // 8

    def one(i, carry):
        at = pl.ds(pl.multiple_of(i * lanes, lanes), lanes)
        index = index_ref[0, :, at]
        which = lax.broadcasted_iota(jnp.int32, (bag, lanes), 0)
        key = jnp.where(which < length_ref[0, :, at], index & (low - 1), -1)
        unit = jnp.left_shift(jnp.int32(1), jnp.right_shift(index, 6) * 4)
        ids = lax.broadcasted_iota(jnp.int32, (chunk, lanes), 0)
        for c in range(low // chunk):
            total = jnp.zeros((chunk, lanes), jnp.int32)
            for j in range(bag):
                total = total + jnp.where(key[j : j + 1] == ids + c * chunk, unit[j : j + 1], 0)
            out_ref[0, c * chunk : (c + 1) * chunk, at] = total
        return carry

    lax.fori_loop(0, block // lanes, one, 0)


def count_hits(lookups, counts, after=()):
    tables, bag, examples = lookups.shape
    block = 4096
    return pl.pallas_call(
        count_kernel,
        out_shape=jax.ShapeDtypeStruct((tables, ROWS // 8, examples), jnp.int32),
        grid=(tables, examples // block),
        in_specs=[
            pl.BlockSpec((1, bag, block), lambda k, i: (k, 0, i)),
            pl.BlockSpec((1, 1, block), lambda k, i: (k, 0, i)),
        ]
        + [ANY] * len(after),
        out_specs=pl.BlockSpec((1, ROWS // 8, block), lambda k, i: (k, 0, i)),
        compiler_params=params(2),
        cost_estimate=cost(5e9),
        name="count_hits",
    )(lookups, counts, *after)


def unpacked(words):
    rows = [lax.shift_right_logical(words, jnp.int32(4 * n)) & 15 for n in range(8)]
    return jnp.concatenate([r.astype(jnp.float32).astype(jnp.bfloat16) for r in rows], axis=0)


def table_kernel(hits_ref, got_ref, w_ref, out_ref):
    @pl.when(pl.program_id(0) == 0)
    def _():
        out_ref[...] = jnp.zeros_like(out_ref)

    block = hits_ref.shape[2]
    sources, count = got_ref.shape[0], block // got_ref.shape[0]
    wide = got_ref[:, :count].reshape(block, PD)
    d = lax.dot_general(wide, w_ref[...], (((1,), (1,)), ((), ())), preferred_element_type=jnp.float32)
    column = lax.broadcasted_iota(jnp.int32, (block, WSUM), 1)
    d = jnp.where(column < W12, 0.0, d).astype(jnp.bfloat16)
    out_ref[...] += jnp.dot(unpacked(hits_ref[2]), d, preferred_element_type=jnp.float32)

    pieces = []
    for n in range(sources):
        packed = got_ref[n, count:].astype(jnp.float32)
        pieces += [packed, pltpu.roll(packed, PD - W12, 1)]
    both = jnp.concatenate(pieces, axis=0)
    column = lax.broadcasted_iota(jnp.int32, (block, PD), 1)
    d1 = jnp.where(column < W1, both, 0.0).astype(jnp.bfloat16)
    d2 = jnp.where((column >= W1) & (column < W12), both, 0.0).astype(jnp.bfloat16)
    out_ref[:, :PD] += jnp.dot(unpacked(hits_ref[0]), d1, preferred_element_type=jnp.float32) + jnp.dot(
        unpacked(hits_ref[1]), d2, preferred_element_type=jnp.float32
    )


def table_sum(hits, got, weights):
    tables, words, examples = hits.shape
    block = 1024
    per = block // (examples // got.shape[0])
    return pl.pallas_call(
        table_kernel,
        out_shape=jax.ShapeDtypeStruct((ROWS, WSUM), jnp.float32),
        grid=(examples // block,),
        in_specs=[
            pl.BlockSpec((tables, words, block), lambda i: (0, 0, i)),
            pl.BlockSpec((per,) + got.shape[1:], lambda i: (i, 0, 0)),
            pl.BlockSpec((WSUM, PD), lambda i: (0, 0)),
        ],
        out_specs=pl.BlockSpec((ROWS, WSUM), lambda i: (0, 0)),
        compiler_params=params(1),
        cost_estimate=cost(1e7),
        name="table_sum",
    )(hits, got, weights)


def swap(x, axis, size, bits):
    return lax.ppermute(x, axis, [(d, d ^ bits) for d in range(size)])


def local(sizes, grad_out, pooled, proj, assign, indices, lengths):
    count, slots, _ = grad_out.shape
    scale = 1.0 / math.sqrt(count * slots)
    n_node, n_local = sizes["node"], sizes["local"]
    n_plane = n_node // 2
    node, loc = lax.axis_index("node"), lax.axis_index("local")

    rows = proj[:, :W12]
    rows = jnp.concatenate([rows] + [swap(rows, "local", n_local, d) for d in range(1, n_local)])
    g12, g3, q = permute(assign, grad_out, pooled)
    rows, g3 = lax.optimization_barrier((rows, g3))
    rows = jnp.concatenate([rows] + [swap(rows, "node", n_node, 2 * d) for d in range(1, n_plane)])
    rows = jnp.concatenate([rows, swap(rows, "node", n_node, 1)])
    slot = jnp.arange(slots, dtype=jnp.int32)
    slot_node = slot // n_local ^ node
    slot_place = slot_node % 2 * (slots // 2) + slot_node // 2 * n_local + (slot % n_local ^ loc)
    payload = narrow_dpool(slot_place, g12, rows, g3)
    arrived = lax.all_to_all(payload, AXES, split_axis=0, concat_axis=0, tiled=True)

    plane = jnp.arange(n_plane, dtype=jnp.int32) ^ (node // 2)
    lines = jnp.arange(n_local, dtype=jnp.int32) ^ loc
    sent = partial_proj(plane * 2 + 1 - node % 2, lines, q, g12, payload, 2)
    got = [swap(x, "node", n_node, 1) for x in sent]
    kept = partial_proj(plane * 2 + node % 2, lines, q, g12, payload, n_plane, got)
    hits = count_hits(indices[0].transpose(1, 2, 0), lengths[0].T[:, None, :], after=kept[:1])
    total = kept[0]
    for d in range(1, n_plane):
        total = total + swap(kept[d], "node", n_node, 2 * d).astype(jnp.float32)
    rounded = total.astype(jnp.bfloat16)
    own, terms = total[:1], [swap(rounded[d : d + 1], "local", n_local, d) for d in range(1, n_local)]

    table_grad = table_sum(hits, arrived, proj[0])[None]
    terms, table_grad = lax.optimization_barrier((terms, table_grad))
    proj_grad = sum((term.astype(jnp.float32) for term in terms), own) * scale
    return (table_grad, proj_grad)


def solution(mesh):
    placed = (
        P(AXES, None, None),
        P(AXES, None, None),
        P(AXES, None, None),
        P(),
        P(AXES, None, None, None),
        P(AXES, None, None),
    )
    return jax.shard_map(
        functools.partial(local, dict(mesh.shape)),
        mesh=mesh,
        in_specs=placed,
        out_specs=(P(AXES, None, None), P(AXES, None, None)),
        check_vma=False,
    )
```

```python
import functools
import math

import jax
import jax.numpy as jnp
from jax import lax
from jax.experimental import pallas as pl
from jax.experimental.pallas import tpu as pltpu
from jax.sharding import PartitionSpec as P

ROWS = 512
W1 = 16
W2 = 48
W3 = 192
PD = 128
W12 = W1 + W2
WSUM = W12 + W3
AXES = ("node", "local")
EB = 8
STEP = 32
MIB = 1024 * 1024


def params(grid):
    return pltpu.CompilerParams(dimension_semantics=("arbitrary",) * grid, vmem_limit_bytes=58 * MIB)


HBM = pl.BlockSpec(memory_space=pltpu.HBM)
ANY = pl.BlockSpec(memory_space=pl.ANY)


def cost(flops):
    return pl.CostEstimate(flops=int(flops), bytes_accessed=1024, transcendentals=0)


def permute_kernel(slots, pieces, assign_ref, grad_ref, pool_ref, *refs):
    outs, (perm_ref, grad_held, pool_held, sems) = refs[:3], refs[3:]
    step = pl.program_id(0)
    sources = ((grad_ref, grad_held), (pool_ref, pool_held))

    def copies(i):
        at = pl.ds(i * STEP, STEP)
        return [
            pltpu.make_async_copy(ref.at[at], held.at[at], sems.at[n, i]) for n, (ref, held) in enumerate(sources)
        ]

    @pl.when(step == 0)
    def _():
        for i in range(grad_ref.shape[0] // STEP):
            for copy in copies(i):
                copy.start()
        width = EB * slots
        lane = lax.broadcasted_iota(jnp.int32, (2 * EB, width), 1)
        row = lax.broadcasted_iota(jnp.int32, (2 * EB, width), 0)
        for s in range(0, slots, 2):
            group = jnp.where(row < EB, assign_ref[s], assign_ref[s + 1])
            hit = lane == (row % EB) * slots + group
            perm_ref[s * EB : (s + 2) * EB, :] = jnp.where(hit, 1.0, 0.0).astype(jnp.bfloat16)

    for copy, (_, held), cuts in zip(copies(step), sources, pieces):
        copy.wait()
        width = held.shape[2]
        for start in range(0, STEP, 2 * EB):
            pair = []
            for at in (start, start + EB):
                block = held[pl.ds(step * STEP + at, EB)].reshape(EB * slots, width)
                moved = jnp.dot(perm_ref[...], block, preferred_element_type=jnp.float32)
                pair.append(moved.reshape(slots, EB, width))
            both = jnp.concatenate(pair, axis=1).astype(jnp.bfloat16)
            for n, low, high in cuts:
                outs[n][:, start : start + 2 * EB, :] = both[:, :, low:high]


def permute(assign, grad_out, pooled):
    count, slots, _ = grad_out.shape
    widths = (2 * PD, PD, WSUM)
    pieces = (((0, 0, 2 * PD), (1, 2 * PD, 3 * PD)), ((2, 0, WSUM),))
    return pl.pallas_call(
        functools.partial(permute_kernel, slots, pieces),
        out_shape=[jax.ShapeDtypeStruct((slots, count, width), jnp.bfloat16) for width in widths],
        grid_spec=pltpu.PrefetchScalarGridSpec(
            num_scalar_prefetch=1,
            grid=(count // STEP,),
            in_specs=[HBM] * 2,
            out_specs=[pl.BlockSpec((slots, STEP, width), lambda i, a: (0, i, 0)) for width in widths],
            scratch_shapes=[
                pltpu.VMEM((EB * slots, EB * slots), jnp.bfloat16),
                pltpu.VMEM(grad_out.shape, jnp.bfloat16),
                pltpu.VMEM(pooled.shape, jnp.bfloat16),
                pltpu.SemaphoreType.DMA((2, count // STEP)),
            ],
        ),
        compiler_params=params(1),
        cost_estimate=cost(1e7),
        name="permute_groups",
    )(assign, grad_out, pooled)


def fetch(ref, held, sems, blocks, pick=lambda i: i):
    size = held.shape[0] // blocks
    copies = [
        pltpu.make_async_copy(ref.at[pl.ds(pick(i) * size, size)], held.at[pl.ds(i * size, size)], sems.at[i])
        for i in range(blocks)
    ]
    for copy in copies:
        copy.start()
    return copies


def narrow_kernel(blocks, place_ref, g_ref, w_ref, *refs):
    out_ref, g_held, w_held, out_held, g_sems, w_sems, out_sems = refs[-7:]
    weights = fetch(w_ref, w_held, w_sems, 1)
    loads = fetch(g_ref, g_held, g_sems, blocks)
    slots, count, _ = g_held.shape
    step, half = slots // blocks, count // 2
    column = lax.broadcasted_iota(jnp.int32, (count, W12), 1)
    dims = (((1,), (1,)), ((), ()))
    weights[0].wait()
    stores = []
    for i, load in enumerate(loads):
        load.wait()
        for s in range(i * step, (i + 1) * step):
            w = w_held[place_ref[s]]
            first = lax.dot_general(g_held[s, :, :PD], w, dims, preferred_element_type=jnp.float32)
            second = lax.dot_general(g_held[s, :, PD:], w, dims, preferred_element_type=jnp.float32)
            d = jnp.where(column < W1, first, second)
            out_held[s] = jnp.concatenate([d[:half], d[half:]], axis=1).astype(jnp.bfloat16)
        at = pl.ds(i * step, step)
        stores.append(pltpu.make_async_copy(out_held.at[at], out_ref.at[at], out_sems.at[i]))
        stores[-1].start()
    for store in stores:
        store.wait()


def narrow_dpool(place, g12, w12, after=()):
    slots, count, _ = g12.shape
    blocks = 4
    shape = (slots, count // 2, 2 * W12)
    return pl.pallas_call(
        functools.partial(narrow_kernel, blocks),
        out_shape=jax.ShapeDtypeStruct(shape, jnp.bfloat16),
        grid_spec=pltpu.PrefetchScalarGridSpec(
            num_scalar_prefetch=1,
            grid=(1,),
            in_specs=[HBM] * 2 + [ANY] * len(after),
            out_specs=HBM,
            scratch_shapes=[
                pltpu.VMEM(g12.shape, jnp.bfloat16),
                pltpu.VMEM(w12.shape, jnp.bfloat16),
                pltpu.VMEM(shape, jnp.bfloat16),
                pltpu.SemaphoreType.DMA((blocks,)),
                pltpu.SemaphoreType.DMA((1,)),
                pltpu.SemaphoreType.DMA((blocks,)),
            ],
        ),
        compiler_params=params(1),
        cost_estimate=cost(4e9),
        name="narrow_dpool",
    )(place, g12, w12, *after)


def partial_kernel(ins, added, results, node_ref, line_ref, *refs):
    blocks, size = node_ref.shape[0], line_ref.shape[0]
    operands, others = refs[:ins], refs[ins : ins + added]
    outs, scratch = refs[-3 - 2 * results - ins - added :][:results], refs[-3 - results - ins - added :]
    held, other_held, out_held = scratch[:ins], scratch[ins : ins + added], scratch[ins + added : -3]
    in_sems, other_sems, out_sems = scratch[-3:]

    def block(arrays, i):
        per = blocks // len(arrays)
        return arrays[i // per].at[pl.ds(i % per * size, size)]

    loads = [
        fetch(ref, at, in_sems.at[n], blocks, lambda i: node_ref[i])
        for n, (ref, at) in enumerate(zip(operands, held))
    ]
    if added:
        loads.append(
            [
                pltpu.make_async_copy(block(others, i), block(other_held, i), other_sems.at[i])
                for i in range(blocks)
            ]
        )
        for copy in loads[-1]:
            copy.start()
    stores = []
    for i in range(blocks):
        for copies in loads:
            copies[i].wait()
        out = block(out_held, i)
        for l in range(size):
            slot = i * size + line_ref[l]
            q = held[0][slot].T
            narrow = jnp.dot(q[:W12], held[1][slot], preferred_element_type=jnp.float32)
            wide = jnp.dot(q[W12:], held[2][slot], preferred_element_type=jnp.float32)
            pieces = ((0, W1, narrow[:W1, :PD]), (W1, W12, narrow[W1:, PD:]), (W12, WSUM, wide))
            for start, end, piece in pieces:
                if added:
                    piece = piece + block(other_held, i)[l, start:end]
                out[l, start:end] = piece.astype(out.dtype)
        stores.append(pltpu.make_async_copy(out, block(outs, i), out_sems.at[i]))
        stores[-1].start()
    for store in stores:
        store.wait()


def partial_proj(nodes, lines, q, g12, g3, results, others=()):
    _, count, _ = q.shape
    blocks, size = nodes.shape[0], lines.shape[0]
    kinds = [jnp.bfloat16 if others and i else jnp.float32 for i in range(results)]
    shapes = [jax.ShapeDtypeStruct((blocks // results * size, WSUM, PD), kind) for kind in kinds]
    operands = (q, g12, g3)
    return pl.pallas_call(
        functools.partial(partial_kernel, len(operands), len(others), results),
        out_shape=shapes,
        grid_spec=pltpu.PrefetchScalarGridSpec(
            num_scalar_prefetch=2,
            grid=(1,),
            in_specs=[HBM] * len(operands) + [ANY] * len(others),
            out_specs=[HBM] * results,
            scratch_shapes=[pltpu.VMEM((blocks * size, count, x.shape[2]), jnp.bfloat16) for x in operands]
            + [pltpu.VMEM(x.shape, x.dtype) for x in others]
            + [pltpu.VMEM(x.shape, x.dtype) for x in shapes]
            + [
                pltpu.SemaphoreType.DMA((len(operands), blocks)),
                pltpu.SemaphoreType.DMA((blocks,)),
                pltpu.SemaphoreType.DMA((blocks,)),
            ],
        ),
        compiler_params=params(1),
        cost_estimate=cost(4e9 if others else 1e7),
        name="partial_proj",
    )(nodes, lines, *operands, *others)


def count_kernel(index_ref, length_ref, *refs):
    out_ref = refs[-1]
    bag, block = index_ref.shape[1], index_ref.shape[2]
    lanes, chunk, low = 256, 16, ROWS // 8

    def one(i, carry):
        at = pl.ds(pl.multiple_of(i * lanes, lanes), lanes)
        index = index_ref[0, :, at]
        which = lax.broadcasted_iota(jnp.int32, (bag, lanes), 0)
        key = jnp.where(which < length_ref[0, :, at], index & (low - 1), -1)
        unit = jnp.left_shift(jnp.int32(1), jnp.right_shift(index, 6) * 4)
        ids = lax.broadcasted_iota(jnp.int32, (chunk, lanes), 0)
        for c in range(low // chunk):
            total = jnp.zeros((chunk, lanes), jnp.int32)
            for j in range(bag):
                total = total + jnp.where(key[j : j + 1] == ids + c * chunk, unit[j : j + 1], 0)
            out_ref[0, c * chunk : (c + 1) * chunk, at] = total
        return carry

    lax.fori_loop(0, block // lanes, one, 0)


def count_hits(lookups, counts, after=()):
    tables, bag, examples = lookups.shape
    block = 4096
    return pl.pallas_call(
        count_kernel,
        out_shape=jax.ShapeDtypeStruct((tables, ROWS // 8, examples), jnp.int32),
        grid=(tables, examples // block),
        in_specs=[
            pl.BlockSpec((1, bag, block), lambda k, i: (k, 0, i)),
            pl.BlockSpec((1, 1, block), lambda k, i: (k, 0, i)),
        ]
        + [ANY] * len(after),
        out_specs=pl.BlockSpec((1, ROWS // 8, block), lambda k, i: (k, 0, i)),
        compiler_params=params(2),
        cost_estimate=cost(5e9),
        name="count_hits",
    )(lookups, counts, *after)


def unpacked(words):
    rows = [lax.shift_right_logical(words, jnp.int32(4 * n)) & 15 for n in range(8)]
    return jnp.concatenate([r.astype(jnp.float32).astype(jnp.bfloat16) for r in rows], axis=0)


def wide_kernel(hits_ref, g_ref, w_ref, *refs):
    out_ref = refs[-1]

    @pl.when(pl.program_id(0) == 0)
    def _():
        out_ref[...] = jnp.zeros_like(out_ref)

    block = g_ref.shape[0]
    column = lax.broadcasted_iota(jnp.int32, (block, WSUM), 1)
    d = lax.dot_general(g_ref[...], w_ref[...], (((1,), (1,)), ((), ())), preferred_element_type=jnp.float32)
    d = jnp.where(column < W12, 0.0, d).astype(jnp.bfloat16)
    out_ref[...] += jnp.dot(unpacked(hits_ref[0]), d, preferred_element_type=jnp.float32)


def wide_sum(hits, g3, weights, after=()):
    _, words, examples = hits.shape
    block = 1024
    return pl.pallas_call(
        wide_kernel,
        out_shape=jax.ShapeDtypeStruct((ROWS, WSUM), jnp.float32),
        grid=(examples // block,),
        in_specs=[
            pl.BlockSpec((1, words, block), lambda i: (2, 0, i)),
            pl.BlockSpec((block, PD), lambda i: (i, 0)),
            pl.BlockSpec((WSUM, PD), lambda i: (0, 0)),
        ]
        + [ANY] * len(after),
        out_specs=pl.BlockSpec((ROWS, WSUM), lambda i: (0, 0)),
        compiler_params=params(1),
        cost_estimate=cost(9e9),
        name="wide_sum",
    )(hits, g3, weights, *after)


def narrow_sum_kernel(hits_ref, d_ref, wide_ref, *refs):
    out_ref = refs[-1]

    @pl.when(pl.program_id(0) == 0)
    def _():
        out_ref[...] = wide_ref[...]

    sources = d_ref.shape[0]
    block = hits_ref.shape[2]
    column = lax.broadcasted_iota(jnp.int32, (block, PD), 1)
    pieces = []
    for d in range(sources):
        packed = d_ref[d].astype(jnp.float32)
        pieces += [packed, pltpu.roll(packed, PD - W12, 1)]
    both = jnp.concatenate(pieces, axis=0)
    d1 = jnp.where(column < W1, both, 0.0).astype(jnp.bfloat16)
    d2 = jnp.where((column >= W1) & (column < W12), both, 0.0).astype(jnp.bfloat16)
    out_ref[...] += jnp.dot(unpacked(hits_ref[0]), d1, preferred_element_type=jnp.float32) + jnp.dot(
        unpacked(hits_ref[1]), d2, preferred_element_type=jnp.float32
    )


def narrow_sum(hits, narrow, wide, after=()):
    _, words, examples = hits.shape
    sources, half, _ = narrow.shape
    block = 1024
    per = block // (2 * half)
    return pl.pallas_call(
        narrow_sum_kernel,
        out_shape=jax.ShapeDtypeStruct((ROWS, WSUM), jnp.float32),
        grid=(examples // block,),
        in_specs=[
            pl.BlockSpec((2, words, block), lambda i: (0, 0, i)),
            pl.BlockSpec((per, half, 2 * W12), lambda i: (i, 0, 0)),
            pl.BlockSpec((ROWS, PD), lambda i: (0, 0)),
        ]
        + [ANY] * len(after),
        out_specs=pl.BlockSpec((ROWS, PD), lambda i: (0, 0)),
        input_output_aliases={2: 0},
        compiler_params=params(1),
        cost_estimate=cost(1e7),
        name="narrow_sum",
    )(hits, narrow, wide, *after)


def swap(x, axis, size, bits):
    return lax.ppermute(x, axis, [(d, d ^ bits) for d in range(size)])


def local(sizes, grad_out, pooled, proj, assign, indices, lengths):
    count, slots, _ = grad_out.shape
    scale = 1.0 / math.sqrt(count * slots)
    n_node, n_local = sizes["node"], sizes["local"]
    n_plane = n_node // 2
    node, loc = lax.axis_index("node"), lax.axis_index("local")

    rows = proj[:, :W12]
    rows = jnp.concatenate([rows] + [swap(rows, "local", n_local, d) for d in range(1, n_local)])
    g12, g3, q = permute(assign, grad_out, pooled)
    rows, g3 = lax.optimization_barrier((rows, g3))
    g3_got = lax.all_to_all(g3, AXES, split_axis=0, concat_axis=0, tiled=True)

    plane = jnp.arange(n_plane, dtype=jnp.int32) ^ (node // 2)
    lines = jnp.arange(n_local, dtype=jnp.int32) ^ loc
    sent = partial_proj(plane * 2 + 1 - node % 2, lines, q, g12, g3, 2)
    got = [swap(x, "node", n_node, 1) for x in sent]

    rows, sent = lax.optimization_barrier((rows, sent))
    rows = jnp.concatenate([rows] + [swap(rows, "node", n_node, 2 * d) for d in range(1, n_plane)])
    hits = count_hits(indices[0].transpose(1, 2, 0), lengths[0].T[:, None, :], after=sent[:1])
    kept = partial_proj(plane * 2 + node % 2, lines, q, g12, g3, n_plane, got)
    rows = jnp.concatenate([rows, swap(rows, "node", n_node, 1)])
    slot = jnp.arange(slots, dtype=jnp.int32)
    slot_node = slot // n_local ^ node
    slot_place = slot_node % 2 * (slots // 2) + slot_node // 2 * n_local + (slot % n_local ^ loc)
    narrow = narrow_dpool(slot_place, g12, rows, after=kept[:1])

    narrow, hits, g3_got, kept = lax.optimization_barrier((narrow, hits, g3_got, kept))
    narrow_got = lax.all_to_all(narrow, AXES, split_axis=0, concat_axis=0, tiled=True)
    total = kept[0]
    for d in range(1, n_plane):
        total = total + swap(kept[d], "node", n_node, 2 * d).astype(jnp.float32)
    rounded = total.astype(jnp.bfloat16)
    own, terms = total[:1], [swap(rounded[d : d + 1], "local", n_local, d) for d in range(1, n_local)]

    wide = wide_sum(hits, g3_got.reshape(-1, PD), proj[0], after=[own])
    table_grad = narrow_sum(hits, narrow_got, wide)[None]
    terms, table_grad = lax.optimization_barrier((terms, table_grad))
    proj_grad = sum((term.astype(jnp.float32) for term in terms), own) * scale
    return (table_grad, proj_grad)


def solution(mesh):
    placed = (
        P(AXES, None, None),
        P(AXES, None, None),
        P(AXES, None, None),
        P(),
        P(AXES, None, None, None),
        P(AXES, None, None),
    )
    return jax.shard_map(
        functools.partial(local, dict(mesh.shape)),
        mesh=mesh,
        in_specs=placed,
        out_specs=(P(AXES, None, None), P(AXES, None, None)),
        check_vma=False,
    )
```

```python
import functools
import math

import jax
import jax.numpy as jnp
from jax import lax
from jax.experimental import pallas as pl
from jax.experimental.pallas import tpu as pltpu
from jax.sharding import PartitionSpec as P

ROWS = 512
W1 = 16
W2 = 48
W3 = 192
PD = 128
W12 = W1 + W2
WSUM = W12 + W3
AXES = ("node", "local")
EB = 8
STEP = 32
MIB = 1024 * 1024


def params(grid):
    return pltpu.CompilerParams(dimension_semantics=("arbitrary",) * grid, vmem_limit_bytes=58 * MIB)


HBM = pl.BlockSpec(memory_space=pltpu.HBM)
ANY = pl.BlockSpec(memory_space=pl.ANY)


def cost(flops):
    return pl.CostEstimate(flops=int(flops), bytes_accessed=1024, transcendentals=0)


def permute_kernel(slots, pieces, assign_ref, grad_ref, pool_ref, *refs):
    outs, (perm_ref, grad_held, pool_held, sems) = refs[:3], refs[3:]
    step = pl.program_id(0)
    sources = ((grad_ref, grad_held), (pool_ref, pool_held))

    def copies(i):
        at = pl.ds(i * STEP, STEP)
        return [
            pltpu.make_async_copy(ref.at[at], held.at[at], sems.at[n, i]) for n, (ref, held) in enumerate(sources)
        ]

    @pl.when(step == 0)
    def _():
        for i in range(grad_ref.shape[0] // STEP):
            for copy in copies(i):
                copy.start()
        width = EB * slots
        lane = lax.broadcasted_iota(jnp.int32, (2 * EB, width), 1)
        row = lax.broadcasted_iota(jnp.int32, (2 * EB, width), 0)
        for s in range(0, slots, 2):
            group = jnp.where(row < EB, assign_ref[s], assign_ref[s + 1])
            hit = lane == (row % EB) * slots + group
            perm_ref[s * EB : (s + 2) * EB, :] = jnp.where(hit, 1.0, 0.0).astype(jnp.bfloat16)

    for copy, (_, held), cuts in zip(copies(step), sources, pieces):
        copy.wait()
        width = held.shape[2]
        for start in range(0, STEP, 2 * EB):
            pair = []
            for at in (start, start + EB):
                block = held[pl.ds(step * STEP + at, EB)].reshape(EB * slots, width)
                moved = jnp.dot(perm_ref[...], block, preferred_element_type=jnp.float32)
                pair.append(moved.reshape(slots, EB, width))
            both = jnp.concatenate(pair, axis=1).astype(jnp.bfloat16)
            for n, low, high in cuts:
                outs[n][:, start : start + 2 * EB, :] = both[:, :, low:high]


def permute(assign, grad_out, pooled):
    count, slots, _ = grad_out.shape
    widths = (2 * PD, PD, WSUM)
    pieces = (((0, 0, 2 * PD), (1, 2 * PD, 3 * PD)), ((2, 0, WSUM),))
    return pl.pallas_call(
        functools.partial(permute_kernel, slots, pieces),
        out_shape=[jax.ShapeDtypeStruct((slots, count, width), jnp.bfloat16) for width in widths],
        grid_spec=pltpu.PrefetchScalarGridSpec(
            num_scalar_prefetch=1,
            grid=(count // STEP,),
            in_specs=[HBM] * 2,
            out_specs=[pl.BlockSpec((slots, STEP, width), lambda i, a: (0, i, 0)) for width in widths],
            scratch_shapes=[
                pltpu.VMEM((EB * slots, EB * slots), jnp.bfloat16),
                pltpu.VMEM(grad_out.shape, jnp.bfloat16),
                pltpu.VMEM(pooled.shape, jnp.bfloat16),
                pltpu.SemaphoreType.DMA((2, count // STEP)),
            ],
        ),
        compiler_params=params(1),
        cost_estimate=cost(1e7),
        name="permute_groups",
    )(assign, grad_out, pooled)


def fetch(ref, held, sems, blocks, pick=lambda i: i):
    size = held.shape[0] // blocks
    copies = [
        pltpu.make_async_copy(ref.at[pl.ds(pick(i) * size, size)], held.at[pl.ds(i * size, size)], sems.at[i])
        for i in range(blocks)
    ]
    for copy in copies:
        copy.start()
    return copies


def narrow_kernel(blocks, place_ref, g_ref, w_ref, *refs):
    out_ref, g_held, w_held, out_held, g_sems, w_sems, out_sems = refs[-7:]
    weights = fetch(w_ref, w_held, w_sems, 1)
    loads = fetch(g_ref, g_held, g_sems, blocks)
    slots, count, _ = g_held.shape
    step, half = slots // blocks, count // 2
    column = lax.broadcasted_iota(jnp.int32, (count, W12), 1)
    dims = (((1,), (1,)), ((), ()))
    weights[0].wait()
    stores = []
    for i, load in enumerate(loads):
        load.wait()
        for s in range(i * step, (i + 1) * step):
            w = w_held[place_ref[s]]
            first = lax.dot_general(g_held[s, :, :PD], w, dims, preferred_element_type=jnp.float32)
            second = lax.dot_general(g_held[s, :, PD:], w, dims, preferred_element_type=jnp.float32)
            d = jnp.where(column < W1, first, second)
            out_held[s] = jnp.concatenate([d[:half], d[half:]], axis=1).astype(jnp.bfloat16)
        at = pl.ds(i * step, step)
        stores.append(pltpu.make_async_copy(out_held.at[at], out_ref.at[at], out_sems.at[i]))
        stores[-1].start()
    for store in stores:
        store.wait()


def narrow_dpool(place, g12, w12, after=()):
    slots, count, _ = g12.shape
    blocks = 4
    shape = (slots, count // 2, 2 * W12)
    return pl.pallas_call(
        functools.partial(narrow_kernel, blocks),
        out_shape=jax.ShapeDtypeStruct(shape, jnp.bfloat16),
        grid_spec=pltpu.PrefetchScalarGridSpec(
            num_scalar_prefetch=1,
            grid=(1,),
            in_specs=[HBM] * 2 + [ANY] * len(after),
            out_specs=HBM,
            scratch_shapes=[
                pltpu.VMEM(g12.shape, jnp.bfloat16),
                pltpu.VMEM(w12.shape, jnp.bfloat16),
                pltpu.VMEM(shape, jnp.bfloat16),
                pltpu.SemaphoreType.DMA((blocks,)),
                pltpu.SemaphoreType.DMA((1,)),
                pltpu.SemaphoreType.DMA((blocks,)),
            ],
        ),
        compiler_params=params(1),
        cost_estimate=cost(4e9),
        name="narrow_dpool",
    )(place, g12, w12, *after)


def partial_kernel(ins, added, results, node_ref, line_ref, *refs):
    blocks, size = node_ref.shape[0], line_ref.shape[0]
    operands, others = refs[:ins], refs[ins : ins + added]
    outs, scratch = refs[-3 - 2 * results - ins - added :][:results], refs[-3 - results - ins - added :]
    held, other_held, out_held = scratch[:ins], scratch[ins : ins + added], scratch[ins + added : -3]
    in_sems, other_sems, out_sems = scratch[-3:]

    def block(arrays, i):
        per = blocks // len(arrays)
        return arrays[i // per].at[pl.ds(i % per * size, size)]

    loads = [
        fetch(ref, at, in_sems.at[n], blocks, lambda i: node_ref[i])
        for n, (ref, at) in enumerate(zip(operands, held))
    ]
    if added:
        loads.append(
            [
                pltpu.make_async_copy(block(others, i), block(other_held, i), other_sems.at[i])
                for i in range(blocks)
            ]
        )
        for copy in loads[-1]:
            copy.start()
    stores = []
    for i in range(blocks):
        for copies in loads:
            copies[i].wait()
        out = block(out_held, i)
        for l in range(size):
            slot = i * size + line_ref[l]
            q = held[0][slot].T
            narrow = jnp.dot(q[:W12], held[1][slot], preferred_element_type=jnp.float32)
            wide = jnp.dot(q[W12:], held[2][slot], preferred_element_type=jnp.float32)
            pieces = ((0, W1, narrow[:W1, :PD]), (W1, W12, narrow[W1:, PD:]), (W12, WSUM, wide))
            for start, end, piece in pieces:
                if added:
                    piece = piece + block(other_held, i)[l, start:end]
                out[l, start:end] = piece.astype(out.dtype)
        stores.append(pltpu.make_async_copy(out, block(outs, i), out_sems.at[i]))
        stores[-1].start()
    for store in stores:
        store.wait()


def partial_proj(nodes, lines, q, g12, g3, results, others=()):
    _, count, _ = q.shape
    blocks, size = nodes.shape[0], lines.shape[0]
    kinds = [jnp.bfloat16 if others and i else jnp.float32 for i in range(results)]
    shapes = [jax.ShapeDtypeStruct((blocks // results * size, WSUM, PD), kind) for kind in kinds]
    operands = (q, g12, g3)
    return pl.pallas_call(
        functools.partial(partial_kernel, len(operands), len(others), results),
        out_shape=shapes,
        grid_spec=pltpu.PrefetchScalarGridSpec(
            num_scalar_prefetch=2,
            grid=(1,),
            in_specs=[HBM] * len(operands) + [ANY] * len(others),
            out_specs=[HBM] * results,
            scratch_shapes=[pltpu.VMEM((blocks * size, count, x.shape[2]), jnp.bfloat16) for x in operands]
            + [pltpu.VMEM(x.shape, x.dtype) for x in others]
            + [pltpu.VMEM(x.shape, x.dtype) for x in shapes]
            + [
                pltpu.SemaphoreType.DMA((len(operands), blocks)),
                pltpu.SemaphoreType.DMA((blocks,)),
                pltpu.SemaphoreType.DMA((blocks,)),
            ],
        ),
        compiler_params=params(1),
        cost_estimate=cost(4e9 if others else 1e7),
        name="partial_proj",
    )(nodes, lines, *operands, *others)


def count_kernel(index_ref, length_ref, *refs):
    out_ref = refs[-1]
    bag, block = index_ref.shape[1], index_ref.shape[2]
    lanes, chunk, low = 256, 16, ROWS // 8

    def one(i, carry):
        at = pl.ds(pl.multiple_of(i * lanes, lanes), lanes)
        index = index_ref[0, :, at]
        which = lax.broadcasted_iota(jnp.int32, (bag, lanes), 0)
        key = jnp.where(which < length_ref[0, :, at], index & (low - 1), -1)
        unit = jnp.left_shift(jnp.int32(1), jnp.right_shift(index, 6) * 4)
        ids = lax.broadcasted_iota(jnp.int32, (chunk, lanes), 0)
        for c in range(low // chunk):
            total = jnp.zeros((chunk, lanes), jnp.int32)
            for j in range(bag):
                total = total + jnp.where(key[j : j + 1] == ids + c * chunk, unit[j : j + 1], 0)
            out_ref[0, c * chunk : (c + 1) * chunk, at] = total
        return carry

    lax.fori_loop(0, block // lanes, one, 0)


def count_hits(lookups, counts, after=()):
    tables, bag, examples = lookups.shape
    block = 4096
    return pl.pallas_call(
        count_kernel,
        out_shape=jax.ShapeDtypeStruct((tables, ROWS // 8, examples), jnp.int32),
        grid=(tables, examples // block),
        in_specs=[
            pl.BlockSpec((1, bag, block), lambda k, i: (k, 0, i)),
            pl.BlockSpec((1, 1, block), lambda k, i: (k, 0, i)),
        ]
        + [ANY] * len(after),
        out_specs=pl.BlockSpec((1, ROWS // 8, block), lambda k, i: (k, 0, i)),
        compiler_params=params(2),
        cost_estimate=cost(5e9),
        name="count_hits",
    )(lookups, counts, *after)


def unpacked(words):
    rows = [lax.shift_right_logical(words, jnp.int32(4 * n)) & 15 for n in range(8)]
    return jnp.concatenate([r.astype(jnp.float32).astype(jnp.bfloat16) for r in rows], axis=0)


def wide_kernel(hits_ref, g_ref, w_ref, *refs):
    out_ref = refs[-1]

    @pl.when(pl.program_id(0) == 0)
    def _():
        out_ref[...] = jnp.zeros_like(out_ref)

    block = g_ref.shape[0]
    column = lax.broadcasted_iota(jnp.int32, (block, WSUM), 1)
    d = lax.dot_general(g_ref[...], w_ref[...], (((1,), (1,)), ((), ())), preferred_element_type=jnp.float32)
    d = jnp.where(column < W12, 0.0, d).astype(jnp.bfloat16)
    out_ref[...] += jnp.dot(unpacked(hits_ref[0]), d, preferred_element_type=jnp.float32)


def wide_sum(hits, g3, weights, after=()):
    _, words, examples = hits.shape
    block = 1024
    return pl.pallas_call(
        wide_kernel,
        out_shape=jax.ShapeDtypeStruct((ROWS, WSUM), jnp.float32),
        grid=(examples // block,),
        in_specs=[
            pl.BlockSpec((1, words, block), lambda i: (2, 0, i)),
            pl.BlockSpec((block, PD), lambda i: (i, 0)),
            pl.BlockSpec((WSUM, PD), lambda i: (0, 0)),
        ]
        + [ANY] * len(after),
        out_specs=pl.BlockSpec((ROWS, WSUM), lambda i: (0, 0)),
        compiler_params=params(1),
        cost_estimate=cost(1e7),
        name="wide_sum",
    )(hits, g3, weights, *after)


def narrow_sum_kernel(hits_ref, d_ref, wide_ref, *refs):
    out_ref = refs[-1]

    @pl.when(pl.program_id(0) == 0)
    def _():
        out_ref[...] = wide_ref[...]

    sources = d_ref.shape[0]
    block = hits_ref.shape[2]
    column = lax.broadcasted_iota(jnp.int32, (block, PD), 1)
    pieces = []
    for d in range(sources):
        packed = d_ref[d].astype(jnp.float32)
        pieces += [packed, pltpu.roll(packed, PD - W12, 1)]
    both = jnp.concatenate(pieces, axis=0)
    d1 = jnp.where(column < W1, both, 0.0).astype(jnp.bfloat16)
    d2 = jnp.where((column >= W1) & (column < W12), both, 0.0).astype(jnp.bfloat16)
    out_ref[...] += jnp.dot(unpacked(hits_ref[0]), d1, preferred_element_type=jnp.float32) + jnp.dot(
        unpacked(hits_ref[1]), d2, preferred_element_type=jnp.float32
    )


def narrow_sum(hits, narrow, wide, after=()):
    _, words, examples = hits.shape
    sources, half, _ = narrow.shape
    block = 1024
    per = block // (2 * half)
    return pl.pallas_call(
        narrow_sum_kernel,
        out_shape=jax.ShapeDtypeStruct((ROWS, WSUM), jnp.float32),
        grid=(examples // block,),
        in_specs=[
            pl.BlockSpec((2, words, block), lambda i: (0, 0, i)),
            pl.BlockSpec((per, half, 2 * W12), lambda i: (i, 0, 0)),
            pl.BlockSpec((ROWS, PD), lambda i: (0, 0)),
        ]
        + [ANY] * len(after),
        out_specs=pl.BlockSpec((ROWS, PD), lambda i: (0, 0)),
        input_output_aliases={2: 0},
        compiler_params=params(1),
        cost_estimate=cost(1e7),
        name="narrow_sum",
    )(hits, narrow, wide, *after)


def plane_kernel(terms, kept_ref, *refs):
    own_ref, outs = refs[terms + 1], refs[terms + 2 :]
    for i in range(kept_ref.shape[0]):
        total = kept_ref[i]
        for term in refs[:terms]:
            total = total + term[i].astype(jnp.float32)
        if i == 0:
            own_ref[0] = total
        else:
            outs[i - 1][0] = total.astype(jnp.bfloat16)


def plane_sum(kept, arrived, after):
    vmem = pl.BlockSpec(memory_space=pltpu.VMEM)
    others = kept.shape[0] - 1
    shape = (1,) + kept.shape[1:]
    return pl.pallas_call(
        functools.partial(plane_kernel, len(arrived)),
        out_shape=[jax.ShapeDtypeStruct(shape, jnp.float32)] + [jax.ShapeDtypeStruct(shape, jnp.bfloat16)] * others,
        in_specs=[vmem] * (1 + len(arrived)) + [ANY],
        out_specs=[vmem] * (1 + others),
        compiler_params=pltpu.CompilerParams(vmem_limit_bytes=16 * MIB),
        cost_estimate=cost(9e9),
        name="plane_sum",
    )(kept, *arrived, after)


def swap(x, axis, size, bits):
    return lax.ppermute(x, axis, [(d, d ^ bits) for d in range(size)])


def local(sizes, grad_out, pooled, proj, assign, indices, lengths):
    count, slots, _ = grad_out.shape
    scale = 1.0 / math.sqrt(count * slots)
    n_node, n_local = sizes["node"], sizes["local"]
    n_plane = n_node // 2
    node, loc = lax.axis_index("node"), lax.axis_index("local")

    rows = proj[:, :W12]
    rows = jnp.concatenate([rows] + [swap(rows, "local", n_local, d) for d in range(1, n_local)])
    g12, g3, q = permute(assign, grad_out, pooled)
    rows, g3 = lax.optimization_barrier((rows, g3))
    g3_got = lax.all_to_all(g3, AXES, split_axis=0, concat_axis=0, tiled=True)

    plane = jnp.arange(n_plane, dtype=jnp.int32) ^ (node // 2)
    lines = jnp.arange(n_local, dtype=jnp.int32) ^ loc
    sent = partial_proj(plane * 2 + 1 - node % 2, lines, q, g12, g3, 2)
    got = [swap(x, "node", n_node, 1) for x in sent]

    rows, sent = lax.optimization_barrier((rows, sent))
    rows = jnp.concatenate([rows] + [swap(rows, "node", n_node, 2 * d) for d in range(1, n_plane)])
    hits = count_hits(indices[0].transpose(1, 2, 0), lengths[0].T[:, None, :], after=sent[:1])
    kept = partial_proj(plane * 2 + node % 2, lines, q, g12, g3, n_plane, got)
    rows = jnp.concatenate([rows, swap(rows, "node", n_node, 1)])
    slot = jnp.arange(slots, dtype=jnp.int32)
    slot_node = slot // n_local ^ node
    slot_place = slot_node % 2 * (slots // 2) + slot_node // 2 * n_local + (slot % n_local ^ loc)
    narrow = narrow_dpool(slot_place, g12, rows, after=kept[:1])

    narrow, hits, g3_got, kept = lax.optimization_barrier((narrow, hits, g3_got, kept))
    narrow_got = lax.all_to_all(narrow, AXES, split_axis=0, concat_axis=0, tiled=True)
    wide = wide_sum(hits, g3_got.reshape(-1, PD), proj[0])
    arrived = [swap(kept[d], "node", n_node, 2 * d) for d in range(1, n_plane)]
    own, *sums = plane_sum(kept[0], arrived, wide)
    terms = [swap(x, "local", n_local, d) for d, x in enumerate(sums, 1)]

    table_grad = narrow_sum(hits, narrow_got, wide)[None]
    terms, table_grad = lax.optimization_barrier((terms, table_grad))
    proj_grad = sum((term.astype(jnp.float32) for term in terms), own) * scale
    return (table_grad, proj_grad)


def solution(mesh):
    placed = (
        P(AXES, None, None),
        P(AXES, None, None),
        P(AXES, None, None),
        P(),
        P(AXES, None, None, None),
        P(AXES, None, None),
    )
    return jax.shard_map(
        functools.partial(local, dict(mesh.shape)),
        mesh=mesh,
        in_specs=placed,
        out_specs=(P(AXES, None, None), P(AXES, None, None)),
        check_vma=False,
    )
```

```python
import functools
import math

import jax
import jax.numpy as jnp
from jax import lax
from jax.experimental import pallas as pl
from jax.experimental.pallas import tpu as pltpu
from jax.sharding import PartitionSpec as P

ROWS = 512
W1 = 16
W2 = 48
W3 = 192
PD = 128
W12 = W1 + W2
WSUM = W12 + W3
AXES = ("node", "local")
EB = 8
STEP = 32
MIB = 1024 * 1024


def params(grid, mib=58):
    return pltpu.CompilerParams(dimension_semantics=("arbitrary",) * grid, vmem_limit_bytes=mib * MIB)


HBM = pl.BlockSpec(memory_space=pltpu.HBM)
ANY = pl.BlockSpec(memory_space=pl.ANY)


def cost(flops):
    return pl.CostEstimate(flops=int(flops), bytes_accessed=1024, transcendentals=0)


def permute_kernel(slots, pieces, assign_ref, grad_ref, pool_ref, *refs):
    outs, (perm_ref, grad_held, pool_held, sems) = refs[:3], refs[3:]
    step = pl.program_id(0)
    sources = ((grad_ref, grad_held), (pool_ref, pool_held))

    def copies(i):
        at = pl.ds(i * STEP, STEP)
        return [
            pltpu.make_async_copy(ref.at[at], held.at[at], sems.at[n, i]) for n, (ref, held) in enumerate(sources)
        ]

    @pl.when(step == 0)
    def _():
        for i in range(grad_ref.shape[0] // STEP):
            for copy in copies(i):
                copy.start()
        width = EB * slots
        lane = lax.broadcasted_iota(jnp.int32, (2 * EB, width), 1)
        row = lax.broadcasted_iota(jnp.int32, (2 * EB, width), 0)
        for s in range(0, slots, 2):
            group = jnp.where(row < EB, assign_ref[s], assign_ref[s + 1])
            hit = lane == (row % EB) * slots + group
            perm_ref[s * EB : (s + 2) * EB, :] = jnp.where(hit, 1.0, 0.0).astype(jnp.bfloat16)

    for copy, (_, held), cuts in zip(copies(step), sources, pieces):
        copy.wait()
        width = held.shape[2]
        for start in range(0, STEP, 2 * EB):
            pair = []
            for at in (start, start + EB):
                block = held[pl.ds(step * STEP + at, EB)].reshape(EB * slots, width)
                moved = jnp.dot(perm_ref[...], block, preferred_element_type=jnp.float32)
                pair.append(moved.reshape(slots, EB, width))
            both = jnp.concatenate(pair, axis=1).astype(jnp.bfloat16)
            for n, low, high in cuts:
                outs[n][:, start : start + 2 * EB, :] = both[:, :, low:high]


def permute(assign, grad_out, pooled):
    count, slots, _ = grad_out.shape
    widths = (2 * PD, PD, WSUM)
    pieces = (((0, 0, 2 * PD), (1, 2 * PD, 3 * PD)), ((2, 0, WSUM),))
    return pl.pallas_call(
        functools.partial(permute_kernel, slots, pieces),
        out_shape=[jax.ShapeDtypeStruct((slots, count, width), jnp.bfloat16) for width in widths],
        grid_spec=pltpu.PrefetchScalarGridSpec(
            num_scalar_prefetch=1,
            grid=(count // STEP,),
            in_specs=[HBM] * 2,
            out_specs=[pl.BlockSpec((slots, STEP, width), lambda i, a: (0, i, 0)) for width in widths],
            scratch_shapes=[
                pltpu.VMEM((EB * slots, EB * slots), jnp.bfloat16),
                pltpu.VMEM(grad_out.shape, jnp.bfloat16),
                pltpu.VMEM(pooled.shape, jnp.bfloat16),
                pltpu.SemaphoreType.DMA((2, count // STEP)),
            ],
        ),
        compiler_params=params(1),
        cost_estimate=cost(1e7),
        name="permute_groups",
    )(assign, grad_out, pooled)


def fetch(ref, held, sems, blocks, pick=lambda i: i):
    size = held.shape[0] // blocks
    copies = [
        pltpu.make_async_copy(ref.at[pl.ds(pick(i) * size, size)], held.at[pl.ds(i * size, size)], sems.at[i])
        for i in range(blocks)
    ]
    for copy in copies:
        copy.start()
    return copies


def narrow_kernel(base, blocks, index_ref, g_ref, w_ref, *refs):
    out_ref, g_held, w_held, out_held, g_sems, w_sems, out_sems = refs[-7:]
    weights = fetch(w_ref, w_held, w_sems, 1)
    loads = fetch(g_ref, g_held, g_sems, blocks)
    slots, count, _ = g_held.shape
    step, half = slots // blocks, count // 2
    column = lax.broadcasted_iota(jnp.int32, (count, W12), 1)
    dims = (((1,), (1,)), ((), ()))
    weights[0].wait()
    stores = []
    for i, load in enumerate(loads):
        load.wait()
        for s in range(i * step, (i + 1) * step):
            w = w_held[index_ref[base + s]]
            first = lax.dot_general(g_held[s, :, :PD], w, dims, preferred_element_type=jnp.float32)
            second = lax.dot_general(g_held[s, :, PD:], w, dims, preferred_element_type=jnp.float32)
            d = jnp.where(column < W1, first, second)
            out_held[s] = jnp.concatenate([d[:half], d[half:]], axis=1).astype(jnp.bfloat16)
        at = pl.ds(i * step, step)
        stores.append(pltpu.make_async_copy(out_held.at[at], out_ref.at[at], out_sems.at[i]))
        stores[-1].start()
    for store in stores:
        store.wait()


def narrow_dpool(index, first, g12, w12, after=()):
    slots, count, _ = g12.shape
    blocks = 4
    shape = (slots, count // 2, 2 * W12)
    return pl.pallas_call(
        functools.partial(narrow_kernel, first, blocks),
        out_shape=jax.ShapeDtypeStruct(shape, jnp.bfloat16),
        grid_spec=pltpu.PrefetchScalarGridSpec(
            num_scalar_prefetch=1,
            grid=(1,),
            in_specs=[HBM] * 2 + [ANY] * len(after),
            out_specs=HBM,
            scratch_shapes=[
                pltpu.VMEM(g12.shape, jnp.bfloat16),
                pltpu.VMEM(w12.shape, jnp.bfloat16),
                pltpu.VMEM(shape, jnp.bfloat16),
                pltpu.SemaphoreType.DMA((blocks,)),
                pltpu.SemaphoreType.DMA((1,)),
                pltpu.SemaphoreType.DMA((blocks,)),
            ],
        ),
        compiler_params=params(1),
        cost_estimate=cost(4e9),
        name="narrow_dpool",
    )(index, g12, w12, *after)


def partial_kernel(first, blocks, size, ins, added, results, index_ref, *refs):
    operands, others = refs[:ins], refs[ins : ins + added]
    outs, scratch = refs[-3 - 2 * results - ins - added :][:results], refs[-3 - results - ins - added :]
    held, other_held, out_held = scratch[:ins], scratch[ins : ins + added], scratch[ins + added : -3]
    in_sems, other_sems, out_sems = scratch[-3:]

    def block(arrays, i):
        per = blocks // len(arrays)
        return arrays[i // per].at[pl.ds(i % per * size, size)]

    loads = [
        fetch(ref, at, in_sems.at[n], blocks, lambda i: index_ref[first + i])
        for n, (ref, at) in enumerate(zip(operands, held))
    ]
    if added:
        loads.append(
            [
                pltpu.make_async_copy(block(others, i), block(other_held, i), other_sems.at[i])
                for i in range(blocks)
            ]
        )
        for copy in loads[-1]:
            copy.start()
    stores = []
    for i in range(blocks):
        for copies in loads:
            copies[i].wait()
        out = block(out_held, i)
        for l in range(size):
            slot = i * size + index_ref[l]
            q = held[0][slot].T
            narrow = jnp.dot(q[:W12], held[1][slot], preferred_element_type=jnp.float32)
            wide = jnp.dot(q[W12:], held[2][slot], preferred_element_type=jnp.float32)
            pieces = ((0, W1, narrow[:W1, :PD]), (W1, W12, narrow[W1:, PD:]), (W12, WSUM, wide))
            for start, end, piece in pieces:
                if added:
                    piece = piece + block(other_held, i)[l, start:end]
                out[l, start:end] = piece.astype(out.dtype)
        stores.append(pltpu.make_async_copy(out, block(outs, i), out_sems.at[i]))
        stores[-1].start()
    for store in stores:
        store.wait()


def partial_proj(index, first, blocks, size, q, g12, g3, results, others=()):
    _, count, _ = q.shape
    kinds = [jnp.bfloat16 if others and i else jnp.float32 for i in range(results)]
    shapes = [jax.ShapeDtypeStruct((blocks // results * size, WSUM, PD), kind) for kind in kinds]
    operands = (q, g12, g3)
    return pl.pallas_call(
        functools.partial(partial_kernel, first, blocks, size, len(operands), len(others), results),
        out_shape=shapes,
        grid_spec=pltpu.PrefetchScalarGridSpec(
            num_scalar_prefetch=1,
            grid=(1,),
            in_specs=[HBM] * len(operands) + [ANY] * len(others),
            out_specs=[HBM] * results,
            scratch_shapes=[pltpu.VMEM((blocks * size, count, x.shape[2]), jnp.bfloat16) for x in operands]
            + [pltpu.VMEM(x.shape, x.dtype) for x in others]
            + [pltpu.VMEM(x.shape, x.dtype) for x in shapes]
            + [
                pltpu.SemaphoreType.DMA((len(operands), blocks)),
                pltpu.SemaphoreType.DMA((blocks,)),
                pltpu.SemaphoreType.DMA((blocks,)),
            ],
        ),
        compiler_params=params(1, 57),
        cost_estimate=cost(4e9 if others else 1e7),
        name="partial_proj",
    )(index, *operands, *others)


def count_kernel(index_ref, length_ref, *refs):
    out_ref = refs[-1]
    bag, block = index_ref.shape[1], index_ref.shape[2]
    lanes, chunk, low = 256, 16, ROWS // 8

    def one(i, carry):
        at = pl.ds(pl.multiple_of(i * lanes, lanes), lanes)
        index = index_ref[0, :, at]
        which = lax.broadcasted_iota(jnp.int32, (bag, lanes), 0)
        key = jnp.where(which < length_ref[0, :, at], index & (low - 1), -1)
        unit = jnp.left_shift(jnp.int32(1), jnp.right_shift(index, 6) * 4)
        ids = lax.broadcasted_iota(jnp.int32, (chunk, lanes), 0)
        for c in range(low // chunk):
            total = jnp.zeros((chunk, lanes), jnp.int32)
            for j in range(bag):
                total = total + jnp.where(key[j : j + 1] == ids + c * chunk, unit[j : j + 1], 0)
            out_ref[0, c * chunk : (c + 1) * chunk, at] = total
        return carry

    lax.fori_loop(0, block // lanes, one, 0)


def count_hits(lookups, counts, after=()):
    tables, bag, examples = lookups.shape
    block = 4096
    return pl.pallas_call(
        count_kernel,
        out_shape=jax.ShapeDtypeStruct((tables, ROWS // 8, examples), jnp.int32),
        grid=(tables, examples // block),
        in_specs=[
            pl.BlockSpec((1, bag, block), lambda k, i: (k, 0, i)),
            pl.BlockSpec((1, 1, block), lambda k, i: (k, 0, i)),
        ]
        + [ANY] * len(after),
        out_specs=pl.BlockSpec((1, ROWS // 8, block), lambda k, i: (k, 0, i)),
        compiler_params=params(2),
        cost_estimate=cost(5e9),
        name="count_hits",
    )(lookups, counts, *after)


def unpacked(words):
    rows = [lax.shift_right_logical(words, jnp.int32(4 * n)) & 15 for n in range(8)]
    return jnp.concatenate([r.astype(jnp.float32).astype(jnp.bfloat16) for r in rows], axis=0)


def wide_kernel(hits_ref, g_ref, w_ref, *refs):
    out_ref = refs[-1]

    @pl.when(pl.program_id(0) == 0)
    def _():
        out_ref[...] = jnp.zeros_like(out_ref)

    block = g_ref.shape[0]
    column = lax.broadcasted_iota(jnp.int32, (block, WSUM), 1)
    d = lax.dot_general(g_ref[...], w_ref[...], (((1,), (1,)), ((), ())), preferred_element_type=jnp.float32)
    d = jnp.where(column < W12, 0.0, d).astype(jnp.bfloat16)
    out_ref[...] += jnp.dot(unpacked(hits_ref[0]), d, preferred_element_type=jnp.float32)


def wide_sum(hits, g3, weights, after=()):
    _, words, examples = hits.shape
    block = 1024
    return pl.pallas_call(
        wide_kernel,
        out_shape=jax.ShapeDtypeStruct((ROWS, WSUM), jnp.float32),
        grid=(examples // block,),
        in_specs=[
            pl.BlockSpec((1, words, block), lambda i: (2, 0, i)),
            pl.BlockSpec((block, PD), lambda i: (i, 0)),
            pl.BlockSpec((WSUM, PD), lambda i: (0, 0)),
        ]
        + [ANY] * len(after),
        out_specs=pl.BlockSpec((ROWS, WSUM), lambda i: (0, 0)),
        compiler_params=params(1),
        cost_estimate=cost(1e7),
        name="wide_sum",
    )(hits, g3, weights, *after)


def narrow_sum_kernel(hits_ref, d_ref, wide_ref, *refs):
    out_ref = refs[-1]

    @pl.when(pl.program_id(0) == 0)
    def _():
        out_ref[...] = wide_ref[...]

    sources = d_ref.shape[0]
    block = hits_ref.shape[2]
    column = lax.broadcasted_iota(jnp.int32, (block, PD), 1)
    pieces = []
    for d in range(sources):
        packed = d_ref[d].astype(jnp.float32)
        pieces += [packed, pltpu.roll(packed, PD - W12, 1)]
    both = jnp.concatenate(pieces, axis=0)
    d1 = jnp.where(column < W1, both, 0.0).astype(jnp.bfloat16)
    d2 = jnp.where((column >= W1) & (column < W12), both, 0.0).astype(jnp.bfloat16)
    out_ref[...] += jnp.dot(unpacked(hits_ref[0]), d1, preferred_element_type=jnp.float32) + jnp.dot(
        unpacked(hits_ref[1]), d2, preferred_element_type=jnp.float32
    )


def narrow_sum(hits, narrow, wide, after=()):
    _, words, examples = hits.shape
    sources, half, _ = narrow.shape
    block = 1024
    per = block // (2 * half)
    return pl.pallas_call(
        narrow_sum_kernel,
        out_shape=jax.ShapeDtypeStruct((ROWS, WSUM), jnp.float32),
        grid=(examples // block,),
        in_specs=[
            pl.BlockSpec((2, words, block), lambda i: (0, 0, i)),
            pl.BlockSpec((per, half, 2 * W12), lambda i: (i, 0, 0)),
            pl.BlockSpec((ROWS, PD), lambda i: (0, 0)),
        ]
        + [ANY] * len(after),
        out_specs=pl.BlockSpec((ROWS, PD), lambda i: (0, 0)),
        input_output_aliases={2: 0},
        compiler_params=params(1),
        cost_estimate=cost(1e7),
        name="narrow_sum",
    )(hits, narrow, wide, *after)


def plane_kernel(terms, kept_ref, *refs):
    own_ref, outs = refs[terms + 1], refs[terms + 2 :]
    for i in range(kept_ref.shape[0]):
        total = kept_ref[i]
        for term in refs[:terms]:
            total = total + term[i].astype(jnp.float32)
        if i == 0:
            own_ref[0] = total
        else:
            outs[i - 1][0] = total.astype(jnp.bfloat16)


def plane_sum(kept, arrived, after):
    vmem = pl.BlockSpec(memory_space=pltpu.VMEM)
    others = kept.shape[0] - 1
    shape = (1,) + kept.shape[1:]
    return pl.pallas_call(
        functools.partial(plane_kernel, len(arrived)),
        out_shape=[jax.ShapeDtypeStruct(shape, jnp.float32)] + [jax.ShapeDtypeStruct(shape, jnp.bfloat16)] * others,
        in_specs=[vmem] * (1 + len(arrived)) + [ANY],
        out_specs=[vmem] * (1 + others),
        compiler_params=pltpu.CompilerParams(vmem_limit_bytes=16 * MIB),
        cost_estimate=cost(9e9),
        name="plane_sum",
    )(kept, *arrived, after)


def swap(x, axis, size, bits):
    return lax.ppermute(x, axis, [(d, d ^ bits) for d in range(size)])


def local(sizes, grad_out, pooled, proj, assign, indices, lengths):
    count, slots, _ = grad_out.shape
    scale = 1.0 / math.sqrt(count * slots)
    n_node, n_local = sizes["node"], sizes["local"]
    n_plane = n_node // 2
    node, loc = lax.axis_index("node"), lax.axis_index("local")

    entry = jnp.arange(n_local + 2 * n_plane + slots, dtype=jnp.int32)
    plane = entry - n_local
    slot = plane - 2 * n_plane
    other = slot // n_local ^ node
    index = jnp.where(
        plane < 0,
        entry ^ loc,
        jnp.where(
            slot < 0,
            ((plane % n_plane) ^ (node // 2)) * 2 + (node + 1 + plane // n_plane) % 2,
            other % 2 * (slots // 2) + other // 2 * n_local + (slot % n_local ^ loc),
        ),
    ).astype(jnp.int32)

    rows = proj[:, :W12]
    rows = jnp.concatenate([rows] + [swap(rows, "local", n_local, d) for d in range(1, n_local)])
    g12, g3, q = permute(assign, grad_out, pooled)
    rows, g3 = lax.optimization_barrier((rows, g3))
    g3_got = lax.all_to_all(g3, AXES, split_axis=0, concat_axis=0, tiled=True)

    sent = partial_proj(index, n_local, n_plane, n_local, q, g12, g3, 2)
    got = [swap(x, "node", n_node, 1) for x in sent]

    rows, sent = lax.optimization_barrier((rows, sent))
    rows = jnp.concatenate([rows] + [swap(rows, "node", n_node, 2 * d) for d in range(1, n_plane)])
    hits = count_hits(indices[0].transpose(1, 2, 0), lengths[0].T[:, None, :], after=sent[:1])
    kept = partial_proj(index, n_local + n_plane, n_plane, n_local, q, g12, g3, n_plane, got)
    rows = jnp.concatenate([rows, swap(rows, "node", n_node, 1)])
    narrow = narrow_dpool(index, n_local + 2 * n_plane, g12, rows, after=kept[:1])

    narrow, hits, g3_got, kept = lax.optimization_barrier((narrow, hits, g3_got, kept))
    narrow_got = lax.all_to_all(narrow, AXES, split_axis=0, concat_axis=0, tiled=True)
    wide = wide_sum(hits, g3_got.reshape(-1, PD), proj[0])
    arrived = [swap(kept[d], "node", n_node, 2 * d) for d in range(1, n_plane)]
    own, *sums = plane_sum(kept[0], arrived, wide)
    terms = [swap(x, "local", n_local, d) for d, x in enumerate(sums, 1)]

    table_grad = narrow_sum(hits, narrow_got, wide)[None]
    terms, table_grad = lax.optimization_barrier((terms, table_grad))
    proj_grad = sum((term.astype(jnp.float32) for term in terms), own) * scale
    return (table_grad, proj_grad)


def solution(mesh):
    placed = (
        P(AXES, None, None),
        P(AXES, None, None),
        P(AXES, None, None),
        P(),
        P(AXES, None, None, None),
        P(AXES, None, None),
    )
    return jax.shard_map(
        functools.partial(local, dict(mesh.shape)),
        mesh=mesh,
        in_specs=placed,
        out_specs=(P(AXES, None, None), P(AXES, None, None)),
        check_vma=False,
    )
```

```python
import functools
import math

import jax
import jax.numpy as jnp
from jax import lax
from jax.experimental import pallas as pl
from jax.experimental.pallas import tpu as pltpu
from jax.sharding import PartitionSpec as P

ROWS = 512
W1 = 16
W2 = 48
W3 = 192
PD = 128
W12 = W1 + W2
WSUM = W12 + W3
AXES = ("node", "local")
EB = 8
STEP = 32
MIB = 1024 * 1024


def params(grid, mib=58):
    return pltpu.CompilerParams(dimension_semantics=("arbitrary",) * grid, vmem_limit_bytes=mib * MIB)


HBM = pl.BlockSpec(memory_space=pltpu.HBM)
ANY = pl.BlockSpec(memory_space=pl.ANY)


def cost(flops):
    return pl.CostEstimate(flops=int(flops), bytes_accessed=1024, transcendentals=0)


def permute_kernel(slots, pieces, assign_ref, grad_ref, pool_ref, *refs):
    outs, (perm_ref, grad_held, pool_held, sems) = refs[:3], refs[3:]
    step = pl.program_id(0)
    sources = ((grad_ref, grad_held), (pool_ref, pool_held))

    def copies(i):
        at = pl.ds(i * STEP, STEP)
        return [
            pltpu.make_async_copy(ref.at[at], held.at[at], sems.at[n, i]) for n, (ref, held) in enumerate(sources)
        ]

    @pl.when(step == 0)
    def _():
        for i in range(grad_ref.shape[0] // STEP):
            for copy in copies(i):
                copy.start()
        width = EB * slots
        lane = lax.broadcasted_iota(jnp.int32, (2 * EB, width), 1)
        row = lax.broadcasted_iota(jnp.int32, (2 * EB, width), 0)
        for s in range(0, slots, 2):
            group = jnp.where(row < EB, assign_ref[s], assign_ref[s + 1])
            hit = lane == (row % EB) * slots + group
            perm_ref[s * EB : (s + 2) * EB, :] = jnp.where(hit, 1.0, 0.0).astype(jnp.bfloat16)

    for copy, (_, held), cuts in zip(copies(step), sources, pieces):
        copy.wait()
        width = held.shape[2]
        for start in range(0, STEP, 2 * EB):
            pair = []
            for at in (start, start + EB):
                block = held[pl.ds(step * STEP + at, EB)].reshape(EB * slots, width)
                moved = jnp.dot(perm_ref[...], block, preferred_element_type=jnp.float32)
                pair.append(moved.reshape(slots, EB, width))
            both = jnp.concatenate(pair, axis=1).astype(jnp.bfloat16)
            for n, low, high in cuts:
                outs[n][:, start : start + 2 * EB, :] = both[:, :, low:high]


def permute(assign, grad_out, pooled):
    count, slots, _ = grad_out.shape
    widths = (2 * PD, PD, WSUM)
    pieces = (((0, 0, 2 * PD), (1, 2 * PD, 3 * PD)), ((2, 0, WSUM),))
    return pl.pallas_call(
        functools.partial(permute_kernel, slots, pieces),
        out_shape=[jax.ShapeDtypeStruct((slots, count, width), jnp.bfloat16) for width in widths],
        grid_spec=pltpu.PrefetchScalarGridSpec(
            num_scalar_prefetch=1,
            grid=(count // STEP,),
            in_specs=[HBM] * 2,
            out_specs=[pl.BlockSpec((slots, STEP, width), lambda i, a: (0, i, 0)) for width in widths],
            scratch_shapes=[
                pltpu.VMEM((EB * slots, EB * slots), jnp.bfloat16),
                pltpu.VMEM(grad_out.shape, jnp.bfloat16),
                pltpu.VMEM(pooled.shape, jnp.bfloat16),
                pltpu.SemaphoreType.DMA((2, count // STEP)),
            ],
        ),
        compiler_params=params(1),
        cost_estimate=cost(1e7),
        name="permute_groups",
    )(assign, grad_out, pooled)


def fetch(ref, held, sems, blocks, pick=lambda i: i):
    size = held.shape[0] // blocks
    copies = [
        pltpu.make_async_copy(ref.at[pl.ds(pick(i) * size, size)], held.at[pl.ds(i * size, size)], sems.at[i])
        for i in range(blocks)
    ]
    for copy in copies:
        copy.start()
    return copies


def narrow_kernel(base, blocks, index_ref, g_ref, w_ref, *refs):
    out_ref, g_held, w_held, out_held, g_sems, w_sems, out_sems = refs[-7:]
    weights = fetch(w_ref, w_held, w_sems, 1)
    loads = fetch(g_ref, g_held, g_sems, blocks)
    slots, count, _ = g_held.shape
    step, half = slots // blocks, count // 2
    column = lax.broadcasted_iota(jnp.int32, (count, W12), 1)
    dims = (((1,), (1,)), ((), ()))
    weights[0].wait()
    stores = []
    for i, load in enumerate(loads):
        load.wait()
        for s in range(i * step, (i + 1) * step):
            w = w_held[index_ref[base + s]]
            first = lax.dot_general(g_held[s, :, :PD], w, dims, preferred_element_type=jnp.float32)
            second = lax.dot_general(g_held[s, :, PD:], w, dims, preferred_element_type=jnp.float32)
            d = jnp.where(column < W1, first, second)
            out_held[s] = jnp.concatenate([d[:half], d[half:]], axis=1).astype(jnp.bfloat16)
        at = pl.ds(i * step, step)
        stores.append(pltpu.make_async_copy(out_held.at[at], out_ref.at[at], out_sems.at[i]))
        stores[-1].start()
    for store in stores:
        store.wait()


def narrow_dpool(index, first, g12, w12, after=()):
    slots, count, _ = g12.shape
    blocks = 4
    shape = (slots, count // 2, 2 * W12)
    return pl.pallas_call(
        functools.partial(narrow_kernel, first, blocks),
        out_shape=jax.ShapeDtypeStruct(shape, jnp.bfloat16),
        grid_spec=pltpu.PrefetchScalarGridSpec(
            num_scalar_prefetch=1,
            grid=(1,),
            in_specs=[HBM] * 2 + [ANY] * len(after),
            out_specs=HBM,
            scratch_shapes=[
                pltpu.VMEM(g12.shape, jnp.bfloat16),
                pltpu.VMEM(w12.shape, jnp.bfloat16),
                pltpu.VMEM(shape, jnp.bfloat16),
                pltpu.SemaphoreType.DMA((blocks,)),
                pltpu.SemaphoreType.DMA((1,)),
                pltpu.SemaphoreType.DMA((blocks,)),
            ],
        ),
        compiler_params=params(1),
        cost_estimate=cost(4e9),
        name="narrow_dpool",
    )(index, g12, w12, *after)


def partial_kernel(first, blocks, size, ins, added, results, index_ref, *refs):
    operands, others = refs[:ins], refs[ins : ins + added]
    outs, scratch = refs[-3 - 2 * results - ins - added :][:results], refs[-3 - results - ins - added :]
    held, other_held, out_held = scratch[:ins], scratch[ins : ins + added], scratch[ins + added : -3]
    in_sems, other_sems, out_sems = scratch[-3:]

    def block(arrays, i):
        per = blocks // len(arrays)
        return arrays[i // per].at[pl.ds(i % per * size, size)]

    loads = [
        fetch(ref, at, in_sems.at[n], blocks, lambda i: index_ref[first + i])
        for n, (ref, at) in enumerate(zip(operands, held))
    ]
    if added:
        loads.append(
            [
                pltpu.make_async_copy(block(others, i), block(other_held, i), other_sems.at[i])
                for i in range(blocks)
            ]
        )
        for copy in loads[-1]:
            copy.start()
    stores = []
    for i in range(blocks):
        for copies in loads:
            copies[i].wait()
        out = block(out_held, i)
        for l in range(size):
            slot = i * size + index_ref[l]
            q = held[0][slot].T
            narrow = jnp.dot(q[:W12], held[1][slot], preferred_element_type=jnp.float32)
            wide = jnp.dot(q[W12:], held[2][slot], preferred_element_type=jnp.float32)
            pieces = ((0, W1, narrow[:W1, :PD]), (W1, W12, narrow[W1:, PD:]), (W12, WSUM, wide))
            for start, end, piece in pieces:
                if added:
                    piece = piece + block(other_held, i)[l, start:end]
                out[l, start:end] = piece.astype(out.dtype)
        stores.append(pltpu.make_async_copy(out, block(outs, i), out_sems.at[i]))
        stores[-1].start()
    for store in stores:
        store.wait()


def partial_proj(index, first, blocks, size, q, g12, g3, results, others=()):
    _, count, _ = q.shape
    kinds = [jnp.bfloat16 if others and i else jnp.float32 for i in range(results)]
    shapes = [jax.ShapeDtypeStruct((blocks // results * size, WSUM, PD), kind) for kind in kinds]
    operands = (q, g12, g3)
    return pl.pallas_call(
        functools.partial(partial_kernel, first, blocks, size, len(operands), len(others), results),
        out_shape=shapes,
        grid_spec=pltpu.PrefetchScalarGridSpec(
            num_scalar_prefetch=1,
            grid=(1,),
            in_specs=[HBM] * len(operands) + [ANY] * len(others),
            out_specs=[HBM] * results,
            scratch_shapes=[pltpu.VMEM((blocks * size, count, x.shape[2]), jnp.bfloat16) for x in operands]
            + [pltpu.VMEM(x.shape, x.dtype) for x in others]
            + [pltpu.VMEM(x.shape, x.dtype) for x in shapes]
            + [
                pltpu.SemaphoreType.DMA((len(operands), blocks)),
                pltpu.SemaphoreType.DMA((blocks,)),
                pltpu.SemaphoreType.DMA((blocks,)),
            ],
        ),
        compiler_params=params(1),
        cost_estimate=cost(4e9 if others else 1e7),
        name="partial_proj",
    )(index, *operands, *others)


def count_kernel(index_ref, length_ref, *refs):
    out_ref = refs[-1]
    bag, block = index_ref.shape[1], index_ref.shape[2]
    lanes, chunk, low = 256, 16, ROWS // 8

    def one(i, carry):
        at = pl.ds(pl.multiple_of(i * lanes, lanes), lanes)
        index = index_ref[0, :, at]
        which = lax.broadcasted_iota(jnp.int32, (bag, lanes), 0)
        key = jnp.where(which < length_ref[0, :, at], index & (low - 1), -1)
        unit = jnp.left_shift(jnp.int32(1), jnp.right_shift(index, 6) * 4)
        ids = lax.broadcasted_iota(jnp.int32, (chunk, lanes), 0)
        for c in range(low // chunk):
            total = jnp.zeros((chunk, lanes), jnp.int32)
            for j in range(bag):
                total = total + jnp.where(key[j : j + 1] == ids + c * chunk, unit[j : j + 1], 0)
            out_ref[0, c * chunk : (c + 1) * chunk, at] = total
        return carry

    lax.fori_loop(0, block // lanes, one, 0)


def count_hits(lookups, counts, after=()):
    tables, bag, examples = lookups.shape
    block = 4096
    return pl.pallas_call(
        count_kernel,
        out_shape=jax.ShapeDtypeStruct((tables, ROWS // 8, examples), jnp.int32),
        grid=(tables, examples // block),
        in_specs=[
            pl.BlockSpec((1, bag, block), lambda k, i: (k, 0, i)),
            pl.BlockSpec((1, 1, block), lambda k, i: (k, 0, i)),
        ]
        + [ANY] * len(after),
        out_specs=pl.BlockSpec((1, ROWS // 8, block), lambda k, i: (k, 0, i)),
        compiler_params=params(2, 60),
        cost_estimate=cost(5e9),
        name="count_hits",
    )(lookups, counts, *after)


def unpacked(words):
    rows = [lax.shift_right_logical(words, jnp.int32(4 * n)) & 15 for n in range(8)]
    return jnp.concatenate([r.astype(jnp.float32).astype(jnp.bfloat16) for r in rows], axis=0)


def wide_kernel(hits_ref, g_ref, w_ref, *refs):
    out_ref = refs[-1]

    @pl.when(pl.program_id(0) == 0)
    def _():
        out_ref[...] = jnp.zeros_like(out_ref)

    block = g_ref.shape[0]
    column = lax.broadcasted_iota(jnp.int32, (block, WSUM), 1)
    d = lax.dot_general(g_ref[...], w_ref[...], (((1,), (1,)), ((), ())), preferred_element_type=jnp.float32)
    d = jnp.where(column < W12, 0.0, d).astype(jnp.bfloat16)
    out_ref[...] += jnp.dot(unpacked(hits_ref[0]), d, preferred_element_type=jnp.float32)


def wide_sum(hits, g3, weights, after=()):
    _, words, examples = hits.shape
    block = 1024
    return pl.pallas_call(
        wide_kernel,
        out_shape=jax.ShapeDtypeStruct((ROWS, WSUM), jnp.float32),
        grid=(examples // block,),
        in_specs=[
            pl.BlockSpec((1, words, block), lambda i: (2, 0, i)),
            pl.BlockSpec((block, PD), lambda i: (i, 0)),
            pl.BlockSpec((WSUM, PD), lambda i: (0, 0)),
        ]
        + [ANY] * len(after),
        out_specs=pl.BlockSpec((ROWS, WSUM), lambda i: (0, 0)),
        compiler_params=params(1, 52),
        cost_estimate=cost(1e7),
        name="wide_sum",
    )(hits, g3, weights, *after)


def narrow_sum_kernel(hits_ref, d_ref, wide_ref, *refs):
    out_ref = refs[-1]

    @pl.when(pl.program_id(0) == 0)
    def _():
        out_ref[...] = wide_ref[...]

    sources = d_ref.shape[0]
    block = hits_ref.shape[2]
    column = lax.broadcasted_iota(jnp.int32, (block, PD), 1)
    pieces = []
    for d in range(sources):
        packed = d_ref[d].astype(jnp.float32)
        pieces += [packed, pltpu.roll(packed, PD - W12, 1)]
    both = jnp.concatenate(pieces, axis=0)
    d1 = jnp.where(column < W1, both, 0.0).astype(jnp.bfloat16)
    d2 = jnp.where((column >= W1) & (column < W12), both, 0.0).astype(jnp.bfloat16)
    out_ref[...] += jnp.dot(unpacked(hits_ref[0]), d1, preferred_element_type=jnp.float32) + jnp.dot(
        unpacked(hits_ref[1]), d2, preferred_element_type=jnp.float32
    )


def narrow_sum(hits, narrow, wide, after=()):
    _, words, examples = hits.shape
    sources, half, _ = narrow.shape
    block = 1024
    per = block // (2 * half)
    return pl.pallas_call(
        narrow_sum_kernel,
        out_shape=jax.ShapeDtypeStruct((ROWS, WSUM), jnp.float32),
        grid=(examples // block,),
        in_specs=[
            pl.BlockSpec((2, words, block), lambda i: (0, 0, i)),
            pl.BlockSpec((per, half, 2 * W12), lambda i: (i, 0, 0)),
            pl.BlockSpec((ROWS, PD), lambda i: (0, 0)),
        ]
        + [ANY] * len(after),
        out_specs=pl.BlockSpec((ROWS, PD), lambda i: (0, 0)),
        input_output_aliases={2: 0},
        compiler_params=params(1),
        cost_estimate=cost(1e7),
        name="narrow_sum",
    )(hits, narrow, wide, *after)


def plane_kernel(terms, kept_ref, *refs):
    own_ref, outs = refs[terms + 1], refs[terms + 2 :]
    for i in range(kept_ref.shape[0]):
        total = kept_ref[i]
        for term in refs[:terms]:
            total = total + term[i].astype(jnp.float32)
        if i == 0:
            own_ref[0] = total
        else:
            outs[i - 1][0] = total.astype(jnp.bfloat16)


def plane_sum(kept, arrived, after):
    vmem = pl.BlockSpec(memory_space=pltpu.VMEM)
    others = kept.shape[0] - 1
    shape = (1,) + kept.shape[1:]
    return pl.pallas_call(
        functools.partial(plane_kernel, len(arrived)),
        out_shape=[jax.ShapeDtypeStruct(shape, jnp.float32)] + [jax.ShapeDtypeStruct(shape, jnp.bfloat16)] * others,
        in_specs=[vmem] * (1 + len(arrived)) + [ANY],
        out_specs=[vmem] * (1 + others),
        compiler_params=pltpu.CompilerParams(vmem_limit_bytes=16 * MIB),
        cost_estimate=cost(9e9),
        name="plane_sum",
    )(kept, *arrived, after)


def swap(x, axis, size, bits):
    return lax.ppermute(x, axis, [(d, d ^ bits) for d in range(size)])


def local(sizes, grad_out, pooled, proj, assign, indices, lengths):
    count, slots, _ = grad_out.shape
    scale = 1.0 / math.sqrt(count * slots)
    n_node, n_local = sizes["node"], sizes["local"]
    n_plane = n_node // 2
    node, loc = lax.axis_index("node"), lax.axis_index("local")

    entry = jnp.arange(n_local + 2 * n_plane + slots, dtype=jnp.int32)
    plane = entry - n_local
    slot = plane - 2 * n_plane
    other = slot // n_local ^ node
    index = jnp.where(
        plane < 0,
        entry ^ loc,
        jnp.where(
            slot < 0,
            ((plane % n_plane) ^ (node // 2)) * 2 + (node + 1 + plane // n_plane) % 2,
            other % 2 * (slots // 2) + other // 2 * n_local + (slot % n_local ^ loc),
        ),
    ).astype(jnp.int32)

    rows = proj[:, :W12]
    rows = jnp.concatenate([rows] + [swap(rows, "local", n_local, d) for d in range(1, n_local)])
    g12, g3, q = permute(assign, grad_out, pooled)
    rows, g3 = lax.optimization_barrier((rows, g3))
    g3_got = lax.all_to_all(g3, AXES, split_axis=0, concat_axis=0, tiled=True)

    sent = partial_proj(index, n_local, n_plane, n_local, q, g12, g3, 2)
    got = [swap(x, "node", n_node, 1) for x in sent]

    rows, sent = lax.optimization_barrier((rows, sent))
    rows = jnp.concatenate([rows] + [swap(rows, "node", n_node, 2 * d) for d in range(1, n_plane)])
    hits = count_hits(indices[0].transpose(1, 2, 0), lengths.transpose(2, 0, 1), after=sent[:1])
    kept = partial_proj(index, n_local + n_plane, n_plane, n_local, q, g12, g3, n_plane, got)
    rows = jnp.concatenate([rows, swap(rows, "node", n_node, 1)])
    narrow = narrow_dpool(index, n_local + 2 * n_plane, g12, rows, after=kept[:1])

    narrow, hits, g3_got, kept = lax.optimization_barrier((narrow, hits, g3_got, kept))
    narrow_got = lax.all_to_all(narrow, AXES, split_axis=0, concat_axis=0, tiled=True)
    wide = wide_sum(hits, g3_got.reshape(-1, PD), proj[0])
    arrived = [swap(kept[d], "node", n_node, 2 * d) for d in range(1, n_plane)]
    own, *sums = plane_sum(kept[0], arrived, wide)
    terms = [swap(x, "local", n_local, d) for d, x in enumerate(sums, 1)]

    table_grad = narrow_sum(hits, narrow_got, wide)[None]
    terms, table_grad = lax.optimization_barrier((terms, table_grad))
    proj_grad = sum((term.astype(jnp.float32) for term in terms), own) * scale
    return (table_grad, proj_grad)


def solution(mesh):
    placed = (
        P(AXES, None, None),
        P(AXES, None, None),
        P(AXES, None, None),
        P(),
        P(AXES, None, None, None),
        P(AXES, None, None),
    )
    return jax.shard_map(
        functools.partial(local, dict(mesh.shape)),
        mesh=mesh,
        in_specs=placed,
        out_specs=(P(AXES, None, None), P(AXES, None, None)),
        check_vma=False,
    )
```

```python
import functools
import math

import jax
import jax.numpy as jnp
from jax import lax
from jax.experimental import pallas as pl
from jax.experimental.pallas import tpu as pltpu
from jax.sharding import PartitionSpec as P

ROWS = 512
W1 = 16
W2 = 48
W3 = 192
PD = 128
W12 = W1 + W2
WSUM = W12 + W3
AXES = ("node", "local")
EB = 8
STEP = 32
MIB = 1024 * 1024


def params(grid, mib=58):
    return pltpu.CompilerParams(dimension_semantics=("arbitrary",) * grid, vmem_limit_bytes=mib * MIB)


HBM = pl.BlockSpec(memory_space=pltpu.HBM)
ANY = pl.BlockSpec(memory_space=pl.ANY)


def cost(flops):
    return pl.CostEstimate(flops=int(flops), bytes_accessed=1024, transcendentals=0)


def permute_kernel(slots, pieces, assign_ref, grad_ref, pool_ref, *refs):
    outs, (perm_ref, grad_held, pool_held, sems) = refs[:3], refs[3:]
    step = pl.program_id(0)
    sources = ((grad_ref, grad_held), (pool_ref, pool_held))

    def copies(i):
        at = pl.ds(i * STEP, STEP)
        return [
            pltpu.make_async_copy(ref.at[at], held.at[at], sems.at[n, i]) for n, (ref, held) in enumerate(sources)
        ]

    @pl.when(step == 0)
    def _():
        for i in range(grad_ref.shape[0] // STEP):
            for copy in copies(i):
                copy.start()
        width = EB * slots
        lane = lax.broadcasted_iota(jnp.int32, (2 * EB, width), 1)
        row = lax.broadcasted_iota(jnp.int32, (2 * EB, width), 0)
        for s in range(0, slots, 2):
            group = jnp.where(row < EB, assign_ref[s], assign_ref[s + 1])
            hit = lane == (row % EB) * slots + group
            perm_ref[s * EB : (s + 2) * EB, :] = jnp.where(hit, 1.0, 0.0).astype(jnp.bfloat16)

    for copy, (_, held), cuts in zip(copies(step), sources, pieces):
        copy.wait()
        width = held.shape[2]
        for start in range(0, STEP, 2 * EB):
            pair = []
            for at in (start, start + EB):
                block = held[pl.ds(step * STEP + at, EB)].reshape(EB * slots, width)
                moved = jnp.dot(perm_ref[...], block, preferred_element_type=jnp.float32)
                pair.append(moved.reshape(slots, EB, width))
            both = jnp.concatenate(pair, axis=1).astype(jnp.bfloat16)
            for n, low, high in cuts:
                outs[n][:, start : start + 2 * EB, :] = both[:, :, low:high]


def permute(assign, grad_out, pooled):
    count, slots, _ = grad_out.shape
    widths = (2 * PD, PD, WSUM)
    pieces = (((0, 0, 2 * PD), (1, 2 * PD, 3 * PD)), ((2, 0, WSUM),))
    return pl.pallas_call(
        functools.partial(permute_kernel, slots, pieces),
        out_shape=[jax.ShapeDtypeStruct((slots, count, width), jnp.bfloat16) for width in widths],
        grid_spec=pltpu.PrefetchScalarGridSpec(
            num_scalar_prefetch=1,
            grid=(count // STEP,),
            in_specs=[HBM] * 2,
            out_specs=[pl.BlockSpec((slots, STEP, width), lambda i, a: (0, i, 0)) for width in widths],
            scratch_shapes=[
                pltpu.VMEM((EB * slots, EB * slots), jnp.bfloat16),
                pltpu.VMEM(grad_out.shape, jnp.bfloat16),
                pltpu.VMEM(pooled.shape, jnp.bfloat16),
                pltpu.SemaphoreType.DMA((2, count // STEP)),
            ],
        ),
        compiler_params=params(1),
        cost_estimate=cost(1e7),
        name="permute_groups",
    )(assign, grad_out, pooled)


def fetch(ref, held, sems, blocks, pick=lambda i: i):
    size = held.shape[0] // blocks
    copies = [
        pltpu.make_async_copy(ref.at[pl.ds(pick(i) * size, size)], held.at[pl.ds(i * size, size)], sems.at[i])
        for i in range(blocks)
    ]
    for copy in copies:
        copy.start()
    return copies


def narrow_kernel(base, blocks, index_ref, g_ref, w_ref, *refs):
    out_ref, g_held, w_held, out_held, g_sems, w_sems, out_sems = refs[-7:]
    weights = fetch(w_ref, w_held, w_sems, 1)
    loads = fetch(g_ref, g_held, g_sems, blocks)
    slots, count, _ = g_held.shape
    step, half = slots // blocks, count // 2
    column = lax.broadcasted_iota(jnp.int32, (count, W12), 1)
    dims = (((1,), (1,)), ((), ()))
    weights[0].wait()
    stores = []
    for i, load in enumerate(loads):
        load.wait()
        for s in range(i * step, (i + 1) * step):
            w = w_held[index_ref[base + s]]
            first = lax.dot_general(g_held[s, :, :PD], w, dims, preferred_element_type=jnp.float32)
            second = lax.dot_general(g_held[s, :, PD:], w, dims, preferred_element_type=jnp.float32)
            d = jnp.where(column < W1, first, second)
            out_held[s] = jnp.concatenate([d[:half], d[half:]], axis=1).astype(jnp.bfloat16)
        at = pl.ds(i * step, step)
        stores.append(pltpu.make_async_copy(out_held.at[at], out_ref.at[at], out_sems.at[i]))
        stores[-1].start()
    for store in stores:
        store.wait()


def narrow_dpool(index, first, g12, w12, after=()):
    slots, count, _ = g12.shape
    blocks = 4
    shape = (slots, count // 2, 2 * W12)
    return pl.pallas_call(
        functools.partial(narrow_kernel, first, blocks),
        out_shape=jax.ShapeDtypeStruct(shape, jnp.bfloat16),
        grid_spec=pltpu.PrefetchScalarGridSpec(
            num_scalar_prefetch=1,
            grid=(1,),
            in_specs=[HBM] * 2 + [ANY] * len(after),
            out_specs=HBM,
            scratch_shapes=[
                pltpu.VMEM(g12.shape, jnp.bfloat16),
                pltpu.VMEM(w12.shape, jnp.bfloat16),
                pltpu.VMEM(shape, jnp.bfloat16),
                pltpu.SemaphoreType.DMA((blocks,)),
                pltpu.SemaphoreType.DMA((1,)),
                pltpu.SemaphoreType.DMA((blocks,)),
            ],
        ),
        compiler_params=params(1),
        cost_estimate=cost(4e9),
        name="narrow_dpool",
    )(index, g12, w12, *after)


def partial_kernel(first, blocks, size, ins, added, results, index_ref, *refs):
    operands, others, outs = refs[:ins], refs[ins : ins + added], refs[ins + added : ins + added + results]
    held, out_held, (in_sems, out_sems) = refs[-2 - results - ins : -2 - results], refs[-2 - results : -2], refs[-2:]

    def block(arrays, i):
        per = blocks // len(arrays)
        return arrays[i // per].at[pl.ds(i % per * size, size)]

    loads = [
        fetch(ref, at, in_sems.at[n], blocks, lambda i: index_ref[first + i])
        for n, (ref, at) in enumerate(zip(operands, held))
    ]
    stores = []
    for i in range(blocks):
        for copies in loads:
            copies[i].wait()
        out = block(out_held, i)
        for l in range(size):
            slot = i * size + index_ref[l]
            q = held[0][slot].T
            narrow = jnp.dot(q[:W12], held[1][slot], preferred_element_type=jnp.float32)
            wide = jnp.dot(q[W12:], held[2][slot], preferred_element_type=jnp.float32)
            pieces = ((0, W1, narrow[:W1, :PD]), (W1, W12, narrow[W1:, PD:]), (W12, WSUM, wide))
            for start, end, piece in pieces:
                if added:
                    piece = piece + block(others, i)[l, start:end]
                out[l, start:end] = piece.astype(out.dtype)
        stores.append(pltpu.make_async_copy(out, block(outs, i), out_sems.at[i]))
        stores[-1].start()
    for store in stores:
        store.wait()


def partial_proj(index, first, blocks, size, q, g12, g3, results, others=()):
    _, count, _ = q.shape
    kinds = [jnp.bfloat16 if others and i else jnp.float32 for i in range(results)]
    shapes = [jax.ShapeDtypeStruct((blocks // results * size, WSUM, PD), kind) for kind in kinds]
    operands = (q, g12, g3)
    beside = sum(4 * x.size for x in others) // MIB
    return pl.pallas_call(
        functools.partial(partial_kernel, first, blocks, size, len(operands), len(others), results),
        out_shape=shapes,
        in_specs=[pl.BlockSpec(memory_space=pltpu.SMEM)]
        + [HBM] * len(operands)
        + [pl.BlockSpec(memory_space=pltpu.VMEM)] * len(others),
        out_specs=[HBM] * results,
        scratch_shapes=[pltpu.VMEM((blocks * size, count, x.shape[2]), jnp.bfloat16) for x in operands]
        + [pltpu.VMEM(x.shape, x.dtype) for x in shapes]
        + [pltpu.SemaphoreType.DMA((len(operands), blocks)), pltpu.SemaphoreType.DMA((blocks,))],
        compiler_params=params(0, 58 - beside),
        cost_estimate=cost(4e9 if others else 1e7),
        name="partial_proj",
    )(index, *operands, *others)


def count_kernel(index_ref, length_ref, *refs):
    out_ref = refs[-1]
    bag, block = index_ref.shape[1], index_ref.shape[2]
    lanes, chunk, low = 256, 16, ROWS // 8

    def one(i, carry):
        at = pl.ds(pl.multiple_of(i * lanes, lanes), lanes)
        index = index_ref[0, :, at]
        which = lax.broadcasted_iota(jnp.int32, (bag, lanes), 0)
        key = jnp.where(which < length_ref[0, :, at], index & (low - 1), -1)
        unit = jnp.left_shift(jnp.int32(1), jnp.right_shift(index, 6) * 4)
        ids = lax.broadcasted_iota(jnp.int32, (chunk, lanes), 0)
        for c in range(low // chunk):
            total = jnp.zeros((chunk, lanes), jnp.int32)
            for j in range(bag):
                total = total + jnp.where(key[j : j + 1] == ids + c * chunk, unit[j : j + 1], 0)
            out_ref[0, c * chunk : (c + 1) * chunk, at] = total
        return carry

    lax.fori_loop(0, block // lanes, one, 0)


def count_hits(lookups, counts, after=()):
    tables, bag, examples = lookups.shape
    block = 4096
    return pl.pallas_call(
        count_kernel,
        out_shape=jax.ShapeDtypeStruct((tables, ROWS // 8, examples), jnp.int32),
        grid=(tables, examples // block),
        in_specs=[
            pl.BlockSpec((1, bag, block), lambda k, i: (k, 0, i)),
            pl.BlockSpec((1, 1, block), lambda k, i: (k, 0, i)),
        ]
        + [ANY] * len(after),
        out_specs=pl.BlockSpec((1, ROWS // 8, block), lambda k, i: (k, 0, i)),
        compiler_params=params(2, 60),
        cost_estimate=cost(5e9),
        name="count_hits",
    )(lookups, counts, *after)


def unpacked(words):
    rows = [lax.shift_right_logical(words, jnp.int32(4 * n)) & 15 for n in range(8)]
    return jnp.concatenate([r.astype(jnp.float32).astype(jnp.bfloat16) for r in rows], axis=0)


def wide_kernel(hits_ref, g_ref, w_ref, *refs):
    out_ref = refs[-1]

    @pl.when(pl.program_id(0) == 0)
    def _():
        out_ref[...] = jnp.zeros_like(out_ref)

    block = g_ref.shape[0]
    column = lax.broadcasted_iota(jnp.int32, (block, WSUM), 1)
    d = lax.dot_general(g_ref[...], w_ref[...], (((1,), (1,)), ((), ())), preferred_element_type=jnp.float32)
    d = jnp.where(column < W12, 0.0, d).astype(jnp.bfloat16)
    out_ref[...] += jnp.dot(unpacked(hits_ref[0]), d, preferred_element_type=jnp.float32)


def wide_sum(hits, g3, weights, after=()):
    _, words, examples = hits.shape
    block = 1024
    return pl.pallas_call(
        wide_kernel,
        out_shape=jax.ShapeDtypeStruct((ROWS, WSUM), jnp.float32),
        grid=(examples // block,),
        in_specs=[
            pl.BlockSpec((1, words, block), lambda i: (2, 0, i)),
            pl.BlockSpec((block, PD), lambda i: (i, 0)),
            pl.BlockSpec((WSUM, PD), lambda i: (0, 0)),
        ]
        + [ANY] * len(after),
        out_specs=pl.BlockSpec((ROWS, WSUM), lambda i: (0, 0)),
        compiler_params=params(1, 52),
        cost_estimate=cost(1e7),
        name="wide_sum",
    )(hits, g3, weights, *after)


def narrow_sum_kernel(hits_ref, d_ref, wide_ref, *refs):
    out_ref = refs[-1]

    @pl.when(pl.program_id(0) == 0)
    def _():
        out_ref[...] = wide_ref[...]

    sources = d_ref.shape[0]
    block = hits_ref.shape[2]
    column = lax.broadcasted_iota(jnp.int32, (block, PD), 1)
    pieces = []
    for d in range(sources):
        packed = d_ref[d].astype(jnp.float32)
        pieces += [packed, pltpu.roll(packed, PD - W12, 1)]
    both = jnp.concatenate(pieces, axis=0)
    d1 = jnp.where(column < W1, both, 0.0).astype(jnp.bfloat16)
    d2 = jnp.where((column >= W1) & (column < W12), both, 0.0).astype(jnp.bfloat16)
    out_ref[...] += jnp.dot(unpacked(hits_ref[0]), d1, preferred_element_type=jnp.float32) + jnp.dot(
        unpacked(hits_ref[1]), d2, preferred_element_type=jnp.float32
    )


def narrow_sum(hits, narrow, wide, after=()):
    _, words, examples = hits.shape
    sources, half, _ = narrow.shape
    block = 1024
    per = block // (2 * half)
    return pl.pallas_call(
        narrow_sum_kernel,
        out_shape=jax.ShapeDtypeStruct((ROWS, WSUM), jnp.float32),
        grid=(examples // block,),
        in_specs=[
            pl.BlockSpec((2, words, block), lambda i: (0, 0, i)),
            pl.BlockSpec((per, half, 2 * W12), lambda i: (i, 0, 0)),
            pl.BlockSpec((ROWS, PD), lambda i: (0, 0)),
        ]
        + [ANY] * len(after),
        out_specs=pl.BlockSpec((ROWS, PD), lambda i: (0, 0)),
        input_output_aliases={2: 0},
        compiler_params=params(1),
        cost_estimate=cost(1e7),
        name="narrow_sum",
    )(hits, narrow, wide, *after)


def plane_kernel(terms, kept_ref, *refs):
    own_ref, outs = refs[terms + 1], refs[terms + 2 :]
    for i in range(kept_ref.shape[0]):
        total = kept_ref[i]
        for term in refs[:terms]:
            total = total + term[i].astype(jnp.float32)
        if i == 0:
            own_ref[0] = total
        else:
            outs[i - 1][0] = total.astype(jnp.bfloat16)


def plane_sum(kept, arrived, after):
    vmem = pl.BlockSpec(memory_space=pltpu.VMEM)
    others = kept.shape[0] - 1
    shape = (1,) + kept.shape[1:]
    return pl.pallas_call(
        functools.partial(plane_kernel, len(arrived)),
        out_shape=[jax.ShapeDtypeStruct(shape, jnp.float32)] + [jax.ShapeDtypeStruct(shape, jnp.bfloat16)] * others,
        in_specs=[vmem] * (1 + len(arrived)) + [ANY],
        out_specs=[vmem] * (1 + others),
        compiler_params=pltpu.CompilerParams(vmem_limit_bytes=16 * MIB),
        cost_estimate=cost(9e9),
        name="plane_sum",
    )(kept, *arrived, after)


def swap(x, axis, size, bits):
    return lax.ppermute(x, axis, [(d, d ^ bits) for d in range(size)])


def local(sizes, grad_out, pooled, proj, assign, indices, lengths):
    count, slots, _ = grad_out.shape
    scale = 1.0 / math.sqrt(count * slots)
    n_node, n_local = sizes["node"], sizes["local"]
    n_plane = n_node // 2
    node, loc = lax.axis_index("node"), lax.axis_index("local")

    entry = jnp.arange(n_local + 2 * n_plane + slots, dtype=jnp.int32)
    plane = entry - n_local
    slot = plane - 2 * n_plane
    other = slot // n_local ^ node
    index = jnp.where(
        plane < 0,
        entry ^ loc,
        jnp.where(
            slot < 0,
            ((plane % n_plane) ^ (node // 2)) * 2 + (node + 1 + plane // n_plane) % 2,
            other % 2 * (slots // 2) + other // 2 * n_local + (slot % n_local ^ loc),
        ),
    ).astype(jnp.int32)

    rows = proj[:, :W12]
    rows = jnp.concatenate([rows] + [swap(rows, "local", n_local, d) for d in range(1, n_local)])
    g12, g3, q = permute(assign, grad_out, pooled)
    rows, g3 = lax.optimization_barrier((rows, g3))
    g3_got = lax.all_to_all(g3, AXES, split_axis=0, concat_axis=0, tiled=True)

    sent = partial_proj(index, n_local, n_plane, n_local, q, g12, g3, 2)
    got = [swap(x, "node", n_node, 1) for x in sent]

    rows, sent = lax.optimization_barrier((rows, sent))
    rows = jnp.concatenate([rows] + [swap(rows, "node", n_node, 2 * d) for d in range(1, n_plane)])
    hits = count_hits(indices[0].transpose(1, 2, 0), lengths.transpose(2, 0, 1), after=sent[:1])
    kept = partial_proj(index, n_local + n_plane, n_plane, n_local, q, g12, g3, n_plane, got)
    rows = jnp.concatenate([rows, swap(rows, "node", n_node, 1)])
    narrow = narrow_dpool(index, n_local + 2 * n_plane, g12, rows, after=kept[:1])

    narrow, hits, g3_got, kept = lax.optimization_barrier((narrow, hits, g3_got, kept))
    narrow_got = lax.all_to_all(narrow, AXES, split_axis=0, concat_axis=0, tiled=True)
    wide = wide_sum(hits, g3_got.reshape(-1, PD), proj[0])
    arrived = [swap(kept[d], "node", n_node, 2 * d) for d in range(1, n_plane)]
    own, *sums = plane_sum(kept[0], arrived, wide)
    terms = [swap(x, "local", n_local, d) for d, x in enumerate(sums, 1)]

    table_grad = narrow_sum(hits, narrow_got, wide)[None]
    terms, table_grad = lax.optimization_barrier((terms, table_grad))
    proj_grad = sum((term.astype(jnp.float32) for term in terms), own) * scale
    return (table_grad, proj_grad)


def solution(mesh):
    placed = (
        P(AXES, None, None),
        P(AXES, None, None),
        P(AXES, None, None),
        P(),
        P(AXES, None, None, None),
        P(AXES, None, None),
    )
    return jax.shard_map(
        functools.partial(local, dict(mesh.shape)),
        mesh=mesh,
        in_specs=placed,
        out_specs=(P(AXES, None, None), P(AXES, None, None)),
        check_vma=False,
    )
```

```python
import functools
import math

import jax
import jax.numpy as jnp
from jax import lax
from jax.experimental import pallas as pl
from jax.experimental.pallas import tpu as pltpu
from jax.sharding import PartitionSpec as P

ROWS = 512
W1 = 16
W2 = 48
W3 = 192
PD = 128
W12 = W1 + W2
WSUM = W12 + W3
AXES = ("node", "local")
EB = 8
STEP = 32
MIB = 1024 * 1024


def params(grid, mib=58):
    return pltpu.CompilerParams(dimension_semantics=("arbitrary",) * grid, vmem_limit_bytes=mib * MIB)


HBM = pl.BlockSpec(memory_space=pltpu.HBM)
ANY = pl.BlockSpec(memory_space=pl.ANY)


def cost(flops):
    return pl.CostEstimate(flops=int(flops), bytes_accessed=1024, transcendentals=0)


def permute_kernel(slots, pieces, assign_ref, grad_ref, pool_ref, *refs):
    outs, (perm_ref, grad_held, pool_held, sems) = refs[:3], refs[3:]
    step = pl.program_id(0)
    sources = ((grad_ref, grad_held), (pool_ref, pool_held))

    def copies(i):
        at = pl.ds(i * STEP, STEP)
        return [
            pltpu.make_async_copy(ref.at[at], held.at[at], sems.at[n, i]) for n, (ref, held) in enumerate(sources)
        ]

    @pl.when(step == 0)
    def _():
        for i in range(grad_ref.shape[0] // STEP):
            for copy in copies(i):
                copy.start()
        width = EB * slots
        lane = lax.broadcasted_iota(jnp.int32, (2 * EB, width), 1)
        row = lax.broadcasted_iota(jnp.int32, (2 * EB, width), 0)
        for s in range(0, slots, 2):
            group = jnp.where(row < EB, assign_ref[s], assign_ref[s + 1])
            hit = lane == (row % EB) * slots + group
            perm_ref[s * EB : (s + 2) * EB, :] = jnp.where(hit, 1.0, 0.0).astype(jnp.bfloat16)

    for copy, (_, held), cuts in zip(copies(step), sources, pieces):
        copy.wait()
        width = held.shape[2]
        for start in range(0, STEP, 2 * EB):
            pair = []
            for at in (start, start + EB):
                block = held[pl.ds(step * STEP + at, EB)].reshape(EB * slots, width)
                moved = jnp.dot(perm_ref[...], block, preferred_element_type=jnp.float32)
                pair.append(moved.reshape(slots, EB, width))
            both = jnp.concatenate(pair, axis=1).astype(jnp.bfloat16)
            for n, low, high in cuts:
                outs[n][:, start : start + 2 * EB, :] = both[:, :, low:high]


def permute(assign, grad_out, pooled):
    count, slots, _ = grad_out.shape
    widths = (2 * PD, PD, WSUM)
    pieces = (((0, 0, 2 * PD), (1, 2 * PD, 3 * PD)), ((2, 0, WSUM),))
    return pl.pallas_call(
        functools.partial(permute_kernel, slots, pieces),
        out_shape=[jax.ShapeDtypeStruct((slots, count, width), jnp.bfloat16) for width in widths],
        grid_spec=pltpu.PrefetchScalarGridSpec(
            num_scalar_prefetch=1,
            grid=(count // STEP,),
            in_specs=[HBM] * 2,
            out_specs=[pl.BlockSpec((slots, STEP, width), lambda i, a: (0, i, 0)) for width in widths],
            scratch_shapes=[
                pltpu.VMEM((EB * slots, EB * slots), jnp.bfloat16),
                pltpu.VMEM(grad_out.shape, jnp.bfloat16),
                pltpu.VMEM(pooled.shape, jnp.bfloat16),
                pltpu.SemaphoreType.DMA((2, count // STEP)),
            ],
        ),
        compiler_params=params(1),
        cost_estimate=cost(1e7),
        name="permute_groups",
    )(assign, grad_out, pooled)


def fetch(ref, held, sems, blocks, pick=lambda i: i):
    size = held.shape[0] // blocks
    copies = [
        pltpu.make_async_copy(ref.at[pl.ds(pick(i) * size, size)], held.at[pl.ds(i * size, size)], sems.at[i])
        for i in range(blocks)
    ]
    for copy in copies:
        copy.start()
    return copies


def narrow_kernel(base, blocks, index_ref, g_ref, w_ref, *refs):
    out_ref, g_held, w_held, out_held, g_sems, w_sems, out_sems = refs[-7:]
    weights = fetch(w_ref, w_held, w_sems, 1)
    loads = fetch(g_ref, g_held, g_sems, blocks)
    slots, count, _ = g_held.shape
    step, half = slots // blocks, count // 2
    column = lax.broadcasted_iota(jnp.int32, (count, W12), 1)
    dims = (((1,), (1,)), ((), ()))
    weights[0].wait()
    stores = []
    for i, load in enumerate(loads):
        load.wait()
        for s in range(i * step, (i + 1) * step):
            w = w_held[index_ref[base + s]]
            first = lax.dot_general(g_held[s, :, :PD], w, dims, preferred_element_type=jnp.float32)
            second = lax.dot_general(g_held[s, :, PD:], w, dims, preferred_element_type=jnp.float32)
            d = jnp.where(column < W1, first, second)
            out_held[s] = jnp.concatenate([d[:half], d[half:]], axis=1).astype(jnp.bfloat16)
        at = pl.ds(i * step, step)
        stores.append(pltpu.make_async_copy(out_held.at[at], out_ref.at[at], out_sems.at[i]))
        stores[-1].start()
    for store in stores:
        store.wait()


def narrow_dpool(index, first, g12, w12, after=()):
    slots, count, _ = g12.shape
    blocks = 4
    shape = (slots, count // 2, 2 * W12)
    return pl.pallas_call(
        functools.partial(narrow_kernel, first, blocks),
        out_shape=jax.ShapeDtypeStruct(shape, jnp.bfloat16),
        grid_spec=pltpu.PrefetchScalarGridSpec(
            num_scalar_prefetch=1,
            grid=(1,),
            in_specs=[HBM] * 2 + [ANY] * len(after),
            out_specs=HBM,
            scratch_shapes=[
                pltpu.VMEM(g12.shape, jnp.bfloat16),
                pltpu.VMEM(w12.shape, jnp.bfloat16),
                pltpu.VMEM(shape, jnp.bfloat16),
                pltpu.SemaphoreType.DMA((blocks,)),
                pltpu.SemaphoreType.DMA((1,)),
                pltpu.SemaphoreType.DMA((blocks,)),
            ],
        ),
        compiler_params=params(1),
        cost_estimate=cost(4e9),
        name="narrow_dpool",
    )(index, g12, w12, *after)


def partial_kernel(first, blocks, size, ins, added, results, index_ref, *refs):
    operands, others = refs[:ins], refs[ins : ins + added]
    outs, scratch = refs[-3 - 2 * results - ins - added :][:results], refs[-3 - results - ins - added :]
    held, other_held, out_held = scratch[:ins], scratch[ins : ins + added], scratch[ins + added : -3]
    in_sems, other_sems, out_sems = scratch[-3:]

    def block(arrays, i):
        per = blocks // len(arrays)
        return arrays[i // per].at[pl.ds(i % per * size, size)]

    loads = [
        fetch(ref, at, in_sems.at[n], blocks, lambda i: index_ref[first + i])
        for n, (ref, at) in enumerate(zip(operands, held))
    ]
    if added:
        loads.append(
            [
                pltpu.make_async_copy(block(others, i), block(other_held, i), other_sems.at[i])
                for i in range(blocks)
            ]
        )
        for copy in loads[-1]:
            copy.start()
    stores = []
    for i in range(blocks):
        for copies in loads:
            copies[i].wait()
        out = block(out_held, i)
        for l in range(size):
            slot = i * size + index_ref[l]
            q = held[0][slot].T
            narrow = jnp.dot(q[:W12], held[1][slot], preferred_element_type=jnp.float32)
            wide = jnp.dot(q[W12:], held[2][slot], preferred_element_type=jnp.float32)
            pieces = ((0, W1, narrow[:W1, :PD]), (W1, W12, narrow[W1:, PD:]), (W12, WSUM, wide))
            for start, end, piece in pieces:
                if added:
                    piece = piece + block(other_held, i)[l, start:end]
                out[l, start:end] = piece.astype(out.dtype)
        stores.append(pltpu.make_async_copy(out, block(outs, i), out_sems.at[i]))
        stores[-1].start()
    for store in stores:
        store.wait()


def partial_proj(index, first, blocks, size, q, g12, g3, results, others=()):
    _, count, _ = q.shape
    kinds = [jnp.bfloat16 if others and i else jnp.float32 for i in range(results)]
    shapes = [jax.ShapeDtypeStruct((blocks // results * size, WSUM, PD), kind) for kind in kinds]
    operands = (q, g12, g3)
    return pl.pallas_call(
        functools.partial(partial_kernel, first, blocks, size, len(operands), len(others), results),
        out_shape=shapes,
        grid_spec=pltpu.PrefetchScalarGridSpec(
            num_scalar_prefetch=1,
            grid=(1,),
            in_specs=[HBM] * len(operands) + [ANY] * len(others),
            out_specs=[HBM] * results,
            scratch_shapes=[pltpu.VMEM((blocks * size, count, x.shape[2]), jnp.bfloat16) for x in operands]
            + [pltpu.VMEM(x.shape, x.dtype) for x in others]
            + [pltpu.VMEM(x.shape, x.dtype) for x in shapes]
            + [
                pltpu.SemaphoreType.DMA((len(operands), blocks)),
                pltpu.SemaphoreType.DMA((blocks,)),
                pltpu.SemaphoreType.DMA((blocks,)),
            ],
        ),
        compiler_params=params(1, 50),
        cost_estimate=cost(4e9 if others else 1e7),
        name="partial_proj",
    )(index, *operands, *others)


def count_kernel(index_ref, length_ref, *refs):
    out_ref = refs[-1]
    bag, block = index_ref.shape[1], index_ref.shape[2]
    lanes, chunk, low = 256, 16, ROWS // 8

    def one(i, carry):
        at = pl.ds(pl.multiple_of(i * lanes, lanes), lanes)
        index = index_ref[0, :, at]
        which = lax.broadcasted_iota(jnp.int32, (bag, lanes), 0)
        key = jnp.where(which < length_ref[0, :, at], index & (low - 1), -1)
        unit = jnp.left_shift(jnp.int32(1), jnp.right_shift(index, 6) * 4)
        ids = lax.broadcasted_iota(jnp.int32, (chunk, lanes), 0)
        for c in range(low // chunk):
            total = jnp.zeros((chunk, lanes), jnp.int32)
            for j in range(bag):
                total = total + jnp.where(key[j : j + 1] == ids + c * chunk, unit[j : j + 1], 0)
            out_ref[0, c * chunk : (c + 1) * chunk, at] = total
        return carry

    lax.fori_loop(0, block // lanes, one, 0)


def count_hits(lookups, counts, after=()):
    tables, bag, examples = lookups.shape
    block = 4096
    return pl.pallas_call(
        count_kernel,
        out_shape=jax.ShapeDtypeStruct((tables, ROWS // 8, examples), jnp.int32),
        grid=(tables, examples // block),
        in_specs=[
            pl.BlockSpec((1, bag, block), lambda k, i: (k, 0, i)),
            pl.BlockSpec((1, 1, block), lambda k, i: (k, 0, i)),
        ]
        + [ANY] * len(after),
        out_specs=pl.BlockSpec((1, ROWS // 8, block), lambda k, i: (k, 0, i)),
        compiler_params=params(2, 60),
        cost_estimate=cost(5e9),
        name="count_hits",
    )(lookups, counts, *after)


def unpacked(words):
    rows = [lax.shift_right_logical(words, jnp.int32(4 * n)) & 15 for n in range(8)]
    return jnp.concatenate([r.astype(jnp.float32).astype(jnp.bfloat16) for r in rows], axis=0)


def wide_kernel(hits_ref, g_ref, w_ref, *refs):
    out_ref = refs[-1]

    @pl.when(pl.program_id(0) == 0)
    def _():
        out_ref[...] = jnp.zeros_like(out_ref)

    block = g_ref.shape[0]
    column = lax.broadcasted_iota(jnp.int32, (block, WSUM), 1)
    d = lax.dot_general(g_ref[...], w_ref[...], (((1,), (1,)), ((), ())), preferred_element_type=jnp.float32)
    d = jnp.where(column < W12, 0.0, d).astype(jnp.bfloat16)
    out_ref[...] += jnp.dot(unpacked(hits_ref[0]), d, preferred_element_type=jnp.float32)


def wide_sum(hits, g3, weights, after=()):
    _, words, examples = hits.shape
    block = 1024
    return pl.pallas_call(
        wide_kernel,
        out_shape=jax.ShapeDtypeStruct((ROWS, WSUM), jnp.float32),
        grid=(examples // block,),
        in_specs=[
            pl.BlockSpec((1, words, block), lambda i: (2, 0, i)),
            pl.BlockSpec((block, PD), lambda i: (i, 0)),
            pl.BlockSpec((WSUM, PD), lambda i: (0, 0)),
        ]
        + [ANY] * len(after),
        out_specs=pl.BlockSpec((ROWS, WSUM), lambda i: (0, 0)),
        compiler_params=params(1, 52),
        cost_estimate=cost(1e7),
        name="wide_sum",
    )(hits, g3, weights, *after)


def narrow_sum_kernel(hits_ref, d_ref, wide_ref, *refs):
    out_ref = refs[-1]

    @pl.when(pl.program_id(0) == 0)
    def _():
        out_ref[...] = wide_ref[...]

    sources = d_ref.shape[0]
    block = hits_ref.shape[2]
    column = lax.broadcasted_iota(jnp.int32, (block, PD), 1)
    pieces = []
    for d in range(sources):
        packed = d_ref[d].astype(jnp.float32)
        pieces += [packed, pltpu.roll(packed, PD - W12, 1)]
    both = jnp.concatenate(pieces, axis=0)
    d1 = jnp.where(column < W1, both, 0.0).astype(jnp.bfloat16)
    d2 = jnp.where((column >= W1) & (column < W12), both, 0.0).astype(jnp.bfloat16)
    out_ref[...] += jnp.dot(unpacked(hits_ref[0]), d1, preferred_element_type=jnp.float32) + jnp.dot(
        unpacked(hits_ref[1]), d2, preferred_element_type=jnp.float32
    )


def narrow_sum(hits, narrow, wide, after=()):
    _, words, examples = hits.shape
    sources, half, _ = narrow.shape
    block = 1024
    per = block // (2 * half)
    return pl.pallas_call(
        narrow_sum_kernel,
        out_shape=jax.ShapeDtypeStruct((ROWS, WSUM), jnp.float32),
        grid=(examples // block,),
        in_specs=[
            pl.BlockSpec((2, words, block), lambda i: (0, 0, i)),
            pl.BlockSpec((per, half, 2 * W12), lambda i: (i, 0, 0)),
            pl.BlockSpec((ROWS, PD), lambda i: (0, 0)),
        ]
        + [ANY] * len(after),
        out_specs=pl.BlockSpec((ROWS, PD), lambda i: (0, 0)),
        input_output_aliases={2: 0},
        compiler_params=params(1),
        cost_estimate=cost(1e7),
        name="narrow_sum",
    )(hits, narrow, wide, *after)


def plane_kernel(terms, kept_ref, *refs):
    own_ref, outs = refs[terms + 1], refs[terms + 2 :]
    for i in range(kept_ref.shape[0]):
        total = kept_ref[i]
        for term in refs[:terms]:
            total = total + term[i].astype(jnp.float32)
        if i == 0:
            own_ref[0] = total
        else:
            outs[i - 1][0] = total.astype(jnp.bfloat16)


def plane_sum(kept, arrived, after):
    vmem = pl.BlockSpec(memory_space=pltpu.VMEM)
    others = kept.shape[0] - 1
    shape = (1,) + kept.shape[1:]
    return pl.pallas_call(
        functools.partial(plane_kernel, len(arrived)),
        out_shape=[jax.ShapeDtypeStruct(shape, jnp.float32)] + [jax.ShapeDtypeStruct(shape, jnp.bfloat16)] * others,
        in_specs=[vmem] * (1 + len(arrived)) + [ANY],
        out_specs=[vmem] * (1 + others),
        compiler_params=pltpu.CompilerParams(vmem_limit_bytes=16 * MIB),
        cost_estimate=cost(9e9),
        name="plane_sum",
    )(kept, *arrived, after)


def swap(x, axis, size, bits):
    return lax.ppermute(x, axis, [(d, d ^ bits) for d in range(size)])


def local(sizes, grad_out, pooled, proj, assign, indices, lengths):
    count, slots, _ = grad_out.shape
    scale = 1.0 / math.sqrt(count * slots)
    n_node, n_local = sizes["node"], sizes["local"]
    n_plane = n_node // 2
    node, loc = lax.axis_index("node"), lax.axis_index("local")

    entry = jnp.arange(n_local + 2 * n_plane + slots, dtype=jnp.int32)
    plane = entry - n_local
    slot = plane - 2 * n_plane
    other = slot // n_local ^ node
    index = jnp.where(
        plane < 0,
        entry ^ loc,
        jnp.where(
            slot < 0,
            ((plane % n_plane) ^ (node // 2)) * 2 + (node + 1 + plane // n_plane) % 2,
            other % 2 * (slots // 2) + other // 2 * n_local + (slot % n_local ^ loc),
        ),
    ).astype(jnp.int32)

    rows = proj[:, :W12]
    rows = jnp.concatenate([rows] + [swap(rows, "local", n_local, d) for d in range(1, n_local)])
    g12, g3, q = permute(assign, grad_out, pooled)
    rows, g3 = lax.optimization_barrier((rows, g3))
    g3_got = lax.all_to_all(g3, AXES, split_axis=0, concat_axis=0, tiled=True)

    sent = partial_proj(index, n_local, n_plane, n_local, q, g12, g3, 2)
    got = [swap(x, "node", n_node, 1) for x in sent]

    rows, sent = lax.optimization_barrier((rows, sent))
    rows = jnp.concatenate([rows] + [swap(rows, "node", n_node, 2 * d) for d in range(1, n_plane)])
    hits = count_hits(indices[0].transpose(1, 2, 0), lengths.transpose(2, 0, 1), after=sent[:1])
    kept = partial_proj(index, n_local + n_plane, n_plane, n_local, q, g12, g3, n_plane, got)
    rows = jnp.concatenate([rows, swap(rows, "node", n_node, 1)])
    narrow = narrow_dpool(index, n_local + 2 * n_plane, g12, rows, after=kept[:1])

    narrow, hits, g3_got, kept = lax.optimization_barrier((narrow, hits, g3_got, kept))
    narrow_got = lax.all_to_all(narrow, AXES, split_axis=0, concat_axis=0, tiled=True)
    wide = wide_sum(hits, g3_got.reshape(-1, PD), proj[0])
    arrived = [swap(kept[d], "node", n_node, 2 * d) for d in range(1, n_plane)]
    own, *sums = plane_sum(kept[0], arrived, wide)
    terms = [swap(x, "local", n_local, d) for d, x in enumerate(sums, 1)]

    table_grad = narrow_sum(hits, narrow_got, wide)[None]
    terms, table_grad = lax.optimization_barrier((terms, table_grad))
    proj_grad = sum((term.astype(jnp.float32) for term in terms), own) * scale
    return (table_grad, proj_grad)


def solution(mesh):
    placed = (
        P(AXES, None, None),
        P(AXES, None, None),
        P(AXES, None, None),
        P(),
        P(AXES, None, None, None),
        P(AXES, None, None),
    )
    return jax.shard_map(
        functools.partial(local, dict(mesh.shape)),
        mesh=mesh,
        in_specs=placed,
        out_specs=(P(AXES, None, None), P(AXES, None, None)),
        check_vma=False,
    )
```

```python
import functools
import math

import jax
import jax.numpy as jnp
from jax import lax
from jax.experimental import pallas as pl
from jax.experimental.pallas import tpu as pltpu
from jax.sharding import PartitionSpec as P

ROWS = 512
W1 = 16
W2 = 48
W3 = 192
PD = 128
W12 = W1 + W2
WSUM = W12 + W3
AXES = ("node", "local")
EB = 8
STEP = 32
MIB = 1024 * 1024


def params(grid, mib=58):
    return pltpu.CompilerParams(dimension_semantics=("arbitrary",) * grid, vmem_limit_bytes=mib * MIB)


HBM = pl.BlockSpec(memory_space=pltpu.HBM)
ANY = pl.BlockSpec(memory_space=pl.ANY)


def cost(flops):
    return pl.CostEstimate(flops=int(flops), bytes_accessed=1024, transcendentals=0)


def permute_kernel(slots, pieces, assign_ref, grad_ref, pool_ref, *refs):
    outs, (perm_ref, grad_held, pool_held, sems) = refs[:3], refs[3:]
    step = pl.program_id(0)
    sources = ((grad_ref, grad_held), (pool_ref, pool_held))

    def copies(i):
        at = pl.ds(i * STEP, STEP)
        return [
            pltpu.make_async_copy(ref.at[at], held.at[at], sems.at[n, i]) for n, (ref, held) in enumerate(sources)
        ]

    @pl.when(step == 0)
    def _():
        for i in range(grad_ref.shape[0] // STEP):
            for copy in copies(i):
                copy.start()
        width = EB * slots
        lane = lax.broadcasted_iota(jnp.int32, (2 * EB, width), 1)
        row = lax.broadcasted_iota(jnp.int32, (2 * EB, width), 0)
        for s in range(0, slots, 2):
            group = jnp.where(row < EB, assign_ref[s], assign_ref[s + 1])
            hit = lane == (row % EB) * slots + group
            perm_ref[s * EB : (s + 2) * EB, :] = jnp.where(hit, 1.0, 0.0).astype(jnp.bfloat16)

    for copy, (_, held), cuts in zip(copies(step), sources, pieces):
        copy.wait()
        width = held.shape[2]
        for start in range(0, STEP, 2 * EB):
            pair = []
            for at in (start, start + EB):
                block = held[pl.ds(step * STEP + at, EB)].reshape(EB * slots, width)
                moved = jnp.dot(perm_ref[...], block, preferred_element_type=jnp.float32)
                pair.append(moved.reshape(slots, EB, width))
            both = jnp.concatenate(pair, axis=1).astype(jnp.bfloat16)
            for n, low, high in cuts:
                outs[n][:, start : start + 2 * EB, :] = both[:, :, low:high]


def permute(assign, grad_out, pooled):
    count, slots, _ = grad_out.shape
    widths = (2 * PD, PD, WSUM)
    pieces = (((0, 0, 2 * PD), (1, 2 * PD, 3 * PD)), ((2, 0, WSUM),))
    return pl.pallas_call(
        functools.partial(permute_kernel, slots, pieces),
        out_shape=[jax.ShapeDtypeStruct((slots, count, width), jnp.bfloat16) for width in widths],
        grid_spec=pltpu.PrefetchScalarGridSpec(
            num_scalar_prefetch=1,
            grid=(count // STEP,),
            in_specs=[HBM] * 2,
            out_specs=[pl.BlockSpec((slots, STEP, width), lambda i, a: (0, i, 0)) for width in widths],
            scratch_shapes=[
                pltpu.VMEM((EB * slots, EB * slots), jnp.bfloat16),
                pltpu.VMEM(grad_out.shape, jnp.bfloat16),
                pltpu.VMEM(pooled.shape, jnp.bfloat16),
                pltpu.SemaphoreType.DMA((2, count // STEP)),
            ],
        ),
        compiler_params=params(1),
        cost_estimate=cost(1e7),
        name="permute_groups",
    )(assign, grad_out, pooled)


def fetch(ref, held, sems, blocks, pick=lambda i: i):
    size = held.shape[0] // blocks
    copies = [
        pltpu.make_async_copy(ref.at[pl.ds(pick(i) * size, size)], held.at[pl.ds(i * size, size)], sems.at[i])
        for i in range(blocks)
    ]
    for copy in copies:
        copy.start()
    return copies


def narrow_kernel(base, blocks, index_ref, g_ref, w_ref, *refs):
    out_ref, g_held, w_held, out_held, g_sems, w_sems, out_sems = refs[-7:]
    weights = fetch(w_ref, w_held, w_sems, 1)
    loads = fetch(g_ref, g_held, g_sems, blocks)
    slots, count, _ = g_held.shape
    step, half = slots // blocks, count // 2
    column = lax.broadcasted_iota(jnp.int32, (count, W12), 1)
    dims = (((1,), (1,)), ((), ()))
    weights[0].wait()
    stores = []
    for i, load in enumerate(loads):
        load.wait()
        for s in range(i * step, (i + 1) * step):
            w = w_held[index_ref[base + s]]
            first = lax.dot_general(g_held[s, :, :PD], w, dims, preferred_element_type=jnp.float32)
            second = lax.dot_general(g_held[s, :, PD:], w, dims, preferred_element_type=jnp.float32)
            d = jnp.where(column < W1, first, second)
            out_held[s] = jnp.concatenate([d[:half], d[half:]], axis=1).astype(jnp.bfloat16)
        at = pl.ds(i * step, step)
        stores.append(pltpu.make_async_copy(out_held.at[at], out_ref.at[at], out_sems.at[i]))
        stores[-1].start()
    for store in stores:
        store.wait()


def narrow_dpool(index, first, g12, w12, after=()):
    slots, count, _ = g12.shape
    blocks = 4
    shape = (slots, count // 2, 2 * W12)
    return pl.pallas_call(
        functools.partial(narrow_kernel, first, blocks),
        out_shape=jax.ShapeDtypeStruct(shape, jnp.bfloat16),
        grid_spec=pltpu.PrefetchScalarGridSpec(
            num_scalar_prefetch=1,
            grid=(1,),
            in_specs=[HBM] * 2 + [ANY] * len(after),
            out_specs=HBM,
            scratch_shapes=[
                pltpu.VMEM(g12.shape, jnp.bfloat16),
                pltpu.VMEM(w12.shape, jnp.bfloat16),
                pltpu.VMEM(shape, jnp.bfloat16),
                pltpu.SemaphoreType.DMA((blocks,)),
                pltpu.SemaphoreType.DMA((1,)),
                pltpu.SemaphoreType.DMA((blocks,)),
            ],
        ),
        compiler_params=params(1, 50),
        cost_estimate=cost(4e9),
        name="narrow_dpool",
    )(index, g12, w12, *after)


def partial_kernel(first, blocks, size, ins, added, results, index_ref, *refs):
    operands, others = refs[:ins], refs[ins : ins + added]
    outs, scratch = refs[-3 - 2 * results - ins - added :][:results], refs[-3 - results - ins - added :]
    held, other_held, out_held = scratch[:ins], scratch[ins : ins + added], scratch[ins + added : -3]
    in_sems, other_sems, out_sems = scratch[-3:]

    def block(arrays, i):
        per = blocks // len(arrays)
        return arrays[i // per].at[pl.ds(i % per * size, size)]

    loads = [
        fetch(ref, at, in_sems.at[n], blocks, lambda i: index_ref[first + i])
        for n, (ref, at) in enumerate(zip(operands, held))
    ]
    if added:
        loads.append(
            [
                pltpu.make_async_copy(block(others, i), block(other_held, i), other_sems.at[i])
                for i in range(blocks)
            ]
        )
        for copy in loads[-1]:
            copy.start()
    stores = []
    for i in range(blocks):
        for copies in loads:
            copies[i].wait()
        out = block(out_held, i)
        for l in range(size):
            slot = i * size + index_ref[l]
            q = held[0][slot].T
            narrow = jnp.dot(q[:W12], held[1][slot], preferred_element_type=jnp.float32)
            wide = jnp.dot(q[W12:], held[2][slot], preferred_element_type=jnp.float32)
            pieces = ((0, W1, narrow[:W1, :PD]), (W1, W12, narrow[W1:, PD:]), (W12, WSUM, wide))
            for start, end, piece in pieces:
                if added:
                    piece = piece + block(other_held, i)[l, start:end]
                out[l, start:end] = piece.astype(out.dtype)
        stores.append(pltpu.make_async_copy(out, block(outs, i), out_sems.at[i]))
        stores[-1].start()
    for store in stores:
        store.wait()


def partial_proj(index, first, blocks, size, q, g12, g3, results, others=()):
    _, count, _ = q.shape
    kinds = [jnp.bfloat16 if others and i else jnp.float32 for i in range(results)]
    shapes = [jax.ShapeDtypeStruct((blocks // results * size, WSUM, PD), kind) for kind in kinds]
    operands = (q, g12, g3)
    return pl.pallas_call(
        functools.partial(partial_kernel, first, blocks, size, len(operands), len(others), results),
        out_shape=shapes,
        grid_spec=pltpu.PrefetchScalarGridSpec(
            num_scalar_prefetch=1,
            grid=(1,),
            in_specs=[HBM] * len(operands) + [ANY] * len(others),
            out_specs=[HBM] * results,
            scratch_shapes=[pltpu.VMEM((blocks * size, count, x.shape[2]), jnp.bfloat16) for x in operands]
            + [pltpu.VMEM(x.shape, x.dtype) for x in others]
            + [pltpu.VMEM(x.shape, x.dtype) for x in shapes]
            + [
                pltpu.SemaphoreType.DMA((len(operands), blocks)),
                pltpu.SemaphoreType.DMA((blocks,)),
                pltpu.SemaphoreType.DMA((blocks,)),
            ],
        ),
        compiler_params=params(1, 50),
        cost_estimate=cost(4e9 if others else 1e7),
        name="partial_proj",
    )(index, *operands, *others)


def count_kernel(index_ref, length_ref, *refs):
    out_ref = refs[-1]
    bag, block = index_ref.shape[1], index_ref.shape[2]
    lanes, chunk, low = 256, 16, ROWS // 8

    def one(i, carry):
        at = pl.ds(pl.multiple_of(i * lanes, lanes), lanes)
        index = index_ref[0, :, at]
        which = lax.broadcasted_iota(jnp.int32, (bag, lanes), 0)
        key = jnp.where(which < length_ref[0, :, at], index & (low - 1), -1)
        unit = jnp.left_shift(jnp.int32(1), jnp.right_shift(index, 6) * 4)
        ids = lax.broadcasted_iota(jnp.int32, (chunk, lanes), 0)
        for c in range(low // chunk):
            total = jnp.zeros((chunk, lanes), jnp.int32)
            for j in range(bag):
                total = total + jnp.where(key[j : j + 1] == ids + c * chunk, unit[j : j + 1], 0)
            out_ref[0, c * chunk : (c + 1) * chunk, at] = total
        return carry

    lax.fori_loop(0, block // lanes, one, 0)


def count_hits(lookups, counts, after=()):
    tables, bag, examples = lookups.shape
    block = 4096
    return pl.pallas_call(
        count_kernel,
        out_shape=jax.ShapeDtypeStruct((tables, ROWS // 8, examples), jnp.int32),
        grid=(tables, examples // block),
        in_specs=[
            pl.BlockSpec((1, bag, block), lambda k, i: (k, 0, i)),
            pl.BlockSpec((1, 1, block), lambda k, i: (k, 0, i)),
        ]
        + [ANY] * len(after),
        out_specs=pl.BlockSpec((1, ROWS // 8, block), lambda k, i: (k, 0, i)),
        compiler_params=params(2, 60),
        cost_estimate=cost(5e9),
        name="count_hits",
    )(lookups, counts, *after)


def unpacked(words):
    rows = [lax.shift_right_logical(words, jnp.int32(4 * n)) & 15 for n in range(8)]
    return jnp.concatenate([r.astype(jnp.float32).astype(jnp.bfloat16) for r in rows], axis=0)


def wide_kernel(hits_ref, g_ref, w_ref, *refs):
    out_ref = refs[-1]

    @pl.when(pl.program_id(0) == 0)
    def _():
        out_ref[...] = jnp.zeros_like(out_ref)

    block = g_ref.shape[0]
    column = lax.broadcasted_iota(jnp.int32, (block, WSUM), 1)
    d = lax.dot_general(g_ref[...], w_ref[...], (((1,), (1,)), ((), ())), preferred_element_type=jnp.float32)
    d = jnp.where(column < W12, 0.0, d).astype(jnp.bfloat16)
    out_ref[...] += jnp.dot(unpacked(hits_ref[0]), d, preferred_element_type=jnp.float32)


def wide_sum(hits, g3, weights, after=()):
    _, words, examples = hits.shape
    block = 1024
    return pl.pallas_call(
        wide_kernel,
        out_shape=jax.ShapeDtypeStruct((ROWS, WSUM), jnp.float32),
        grid=(examples // block,),
        in_specs=[
            pl.BlockSpec((1, words, block), lambda i: (2, 0, i)),
            pl.BlockSpec((block, PD), lambda i: (i, 0)),
            pl.BlockSpec((WSUM, PD), lambda i: (0, 0)),
        ]
        + [ANY] * len(after),
        out_specs=pl.BlockSpec((ROWS, WSUM), lambda i: (0, 0)),
        compiler_params=params(1, 52),
        cost_estimate=cost(1e7),
        name="wide_sum",
    )(hits, g3, weights, *after)


def narrow_sum_kernel(hits_ref, d_ref, wide_ref, *refs):
    out_ref = refs[-1]

    @pl.when(pl.program_id(0) == 0)
    def _():
        out_ref[...] = wide_ref[...]

    sources = d_ref.shape[0]
    block = hits_ref.shape[2]
    column = lax.broadcasted_iota(jnp.int32, (block, PD), 1)
    pieces = []
    for d in range(sources):
        packed = d_ref[d].astype(jnp.float32)
        pieces += [packed, pltpu.roll(packed, PD - W12, 1)]
    both = jnp.concatenate(pieces, axis=0)
    d1 = jnp.where(column < W1, both, 0.0).astype(jnp.bfloat16)
    d2 = jnp.where((column >= W1) & (column < W12), both, 0.0).astype(jnp.bfloat16)
    out_ref[...] += jnp.dot(unpacked(hits_ref[0]), d1, preferred_element_type=jnp.float32) + jnp.dot(
        unpacked(hits_ref[1]), d2, preferred_element_type=jnp.float32
    )


def narrow_sum(hits, narrow, wide, after=()):
    _, words, examples = hits.shape
    sources, half, _ = narrow.shape
    block = 1024
    per = block // (2 * half)
    return pl.pallas_call(
        narrow_sum_kernel,
        out_shape=jax.ShapeDtypeStruct((ROWS, WSUM), jnp.float32),
        grid=(examples // block,),
        in_specs=[
            pl.BlockSpec((2, words, block), lambda i: (0, 0, i)),
            pl.BlockSpec((per, half, 2 * W12), lambda i: (i, 0, 0)),
            pl.BlockSpec((ROWS, PD), lambda i: (0, 0)),
        ]
        + [ANY] * len(after),
        out_specs=pl.BlockSpec((ROWS, PD), lambda i: (0, 0)),
        input_output_aliases={2: 0},
        compiler_params=params(1, 54),
        cost_estimate=cost(1e7),
        name="narrow_sum",
    )(hits, narrow, wide, *after)


def plane_kernel(terms, kept_ref, *refs):
    own_ref, outs = refs[terms + 1], refs[terms + 2 :]
    for i in range(kept_ref.shape[0]):
        total = kept_ref[i]
        for term in refs[:terms]:
            total = total + term[i].astype(jnp.float32)
        if i == 0:
            own_ref[0] = total
        else:
            outs[i - 1][0] = total.astype(jnp.bfloat16)


def plane_sum(kept, arrived, after):
    vmem = pl.BlockSpec(memory_space=pltpu.VMEM)
    others = kept.shape[0] - 1
    shape = (1,) + kept.shape[1:]
    return pl.pallas_call(
        functools.partial(plane_kernel, len(arrived)),
        out_shape=[jax.ShapeDtypeStruct(shape, jnp.float32)] + [jax.ShapeDtypeStruct(shape, jnp.bfloat16)] * others,
        in_specs=[vmem] * (1 + len(arrived)) + [ANY],
        out_specs=[vmem] * (1 + others),
        compiler_params=pltpu.CompilerParams(vmem_limit_bytes=16 * MIB),
        cost_estimate=cost(9e9),
        name="plane_sum",
    )(kept, *arrived, after)


def swap(x, axis, size, bits):
    return lax.ppermute(x, axis, [(d, d ^ bits) for d in range(size)])


def local(sizes, grad_out, pooled, proj, assign, indices, lengths):
    count, slots, _ = grad_out.shape
    scale = 1.0 / math.sqrt(count * slots)
    n_node, n_local = sizes["node"], sizes["local"]
    n_plane = n_node // 2
    node, loc = lax.axis_index("node"), lax.axis_index("local")

    entry = jnp.arange(n_local + 2 * n_plane + slots, dtype=jnp.int32)
    plane = entry - n_local
    slot = plane - 2 * n_plane
    other = slot // n_local ^ node
    index = jnp.where(
        plane < 0,
        entry ^ loc,
        jnp.where(
            slot < 0,
            ((plane % n_plane) ^ (node // 2)) * 2 + (node + 1 + plane // n_plane) % 2,
            other % 2 * (slots // 2) + other // 2 * n_local + (slot % n_local ^ loc),
        ),
    ).astype(jnp.int32)

    rows = proj[:, :W12]
    rows = jnp.concatenate([rows] + [swap(rows, "local", n_local, d) for d in range(1, n_local)])
    g12, g3, q = permute(assign, grad_out, pooled)
    rows, g3 = lax.optimization_barrier((rows, g3))
    g3_got = lax.all_to_all(g3, AXES, split_axis=0, concat_axis=0, tiled=True)

    sent = partial_proj(index, n_local, n_plane, n_local, q, g12, g3, 2)
    got = [swap(x, "node", n_node, 1) for x in sent]

    rows, sent = lax.optimization_barrier((rows, sent))
    rows = jnp.concatenate([rows] + [swap(rows, "node", n_node, 2 * d) for d in range(1, n_plane)])
    hits = count_hits(indices[0].transpose(1, 2, 0), lengths.transpose(2, 0, 1), after=sent[:1])
    kept = partial_proj(index, n_local + n_plane, n_plane, n_local, q, g12, g3, n_plane, got)
    rows = jnp.concatenate([rows, swap(rows, "node", n_node, 1)])
    narrow = narrow_dpool(index, n_local + 2 * n_plane, g12, rows, after=kept[:1])

    narrow, hits, g3_got, kept = lax.optimization_barrier((narrow, hits, g3_got, kept))
    narrow_got = lax.all_to_all(narrow, AXES, split_axis=0, concat_axis=0, tiled=True)
    wide = wide_sum(hits, g3_got.reshape(-1, PD), proj[0])
    arrived = [swap(kept[d], "node", n_node, 2 * d) for d in range(1, n_plane)]
    own, *sums = plane_sum(kept[0], arrived, wide)
    terms = [swap(x, "local", n_local, d) for d, x in enumerate(sums, 1)]

    table_grad = narrow_sum(hits, narrow_got, wide)[None]
    terms, table_grad = lax.optimization_barrier((terms, table_grad))
    proj_grad = sum((term.astype(jnp.float32) for term in terms), own) * scale
    return (table_grad, proj_grad)


def solution(mesh):
    placed = (
        P(AXES, None, None),
        P(AXES, None, None),
        P(AXES, None, None),
        P(),
        P(AXES, None, None, None),
        P(AXES, None, None),
    )
    return jax.shard_map(
        functools.partial(local, dict(mesh.shape)),
        mesh=mesh,
        in_specs=placed,
        out_specs=(P(AXES, None, None), P(AXES, None, None)),
        check_vma=False,
    )
```

```python
import functools
import math

import jax
import jax.numpy as jnp
from jax import lax
from jax.experimental import pallas as pl
from jax.experimental.pallas import tpu as pltpu
from jax.sharding import PartitionSpec as P

ROWS = 512
W1 = 16
W2 = 48
W3 = 192
PD = 128
W12 = W1 + W2
WSUM = W12 + W3
AXES = ("node", "local")
EB = 8
STEP = 32
MIB = 1024 * 1024


def params(grid, mib=58):
    return pltpu.CompilerParams(dimension_semantics=("arbitrary",) * grid, vmem_limit_bytes=mib * MIB)


HBM = pl.BlockSpec(memory_space=pltpu.HBM)
ANY = pl.BlockSpec(memory_space=pl.ANY)


def cost(flops):
    return pl.CostEstimate(flops=int(flops), bytes_accessed=1024, transcendentals=0)


def permute_kernel(slots, pieces, assign_ref, grad_ref, pool_ref, *refs):
    outs, (perm_ref, grad_held, pool_held, sems) = refs[:3], refs[3:]
    step = pl.program_id(0)
    sources = ((grad_ref, grad_held), (pool_ref, pool_held))

    def copies(i):
        at = pl.ds(i * STEP, STEP)
        return [
            pltpu.make_async_copy(ref.at[at], held.at[at], sems.at[n, i]) for n, (ref, held) in enumerate(sources)
        ]

    @pl.when(step == 0)
    def _():
        for i in range(grad_ref.shape[0] // STEP):
            for copy in copies(i):
                copy.start()
        width = EB * slots
        lane = lax.broadcasted_iota(jnp.int32, (2 * EB, width), 1)
        row = lax.broadcasted_iota(jnp.int32, (2 * EB, width), 0)
        for s in range(0, slots, 2):
            group = jnp.where(row < EB, assign_ref[s], assign_ref[s + 1])
            hit = lane == (row % EB) * slots + group
            perm_ref[s * EB : (s + 2) * EB, :] = jnp.where(hit, 1.0, 0.0).astype(jnp.bfloat16)

    for copy, (_, held), cuts in zip(copies(step), sources, pieces):
        copy.wait()
        width = held.shape[2]
        for start in range(0, STEP, 2 * EB):
            pair = []
            for at in (start, start + EB):
                block = held[pl.ds(step * STEP + at, EB)].reshape(EB * slots, width)
                moved = jnp.dot(perm_ref[...], block, preferred_element_type=jnp.float32)
                pair.append(moved.reshape(slots, EB, width))
            both = jnp.concatenate(pair, axis=1).astype(jnp.bfloat16)
            for n, low, high in cuts:
                outs[n][:, start : start + 2 * EB, :] = both[:, :, low:high]


def permute(assign, grad_out, pooled):
    count, slots, _ = grad_out.shape
    widths = (2 * PD, PD, WSUM)
    pieces = (((0, 0, 2 * PD), (1, 2 * PD, 3 * PD)), ((2, 0, WSUM),))
    return pl.pallas_call(
        functools.partial(permute_kernel, slots, pieces),
        out_shape=[jax.ShapeDtypeStruct((slots, count, width), jnp.bfloat16) for width in widths],
        grid_spec=pltpu.PrefetchScalarGridSpec(
            num_scalar_prefetch=1,
            grid=(count // STEP,),
            in_specs=[HBM] * 2,
            out_specs=[pl.BlockSpec((slots, STEP, width), lambda i, a: (0, i, 0)) for width in widths],
            scratch_shapes=[
                pltpu.VMEM((EB * slots, EB * slots), jnp.bfloat16),
                pltpu.VMEM(grad_out.shape, jnp.bfloat16),
                pltpu.VMEM(pooled.shape, jnp.bfloat16),
                pltpu.SemaphoreType.DMA((2, count // STEP)),
            ],
        ),
        compiler_params=params(1),
        cost_estimate=cost(1e7),
        name="permute_groups",
    )(assign, grad_out, pooled)


def fetch(ref, held, sems, blocks, pick=lambda i: i):
    size = held.shape[0] // blocks
    copies = [
        pltpu.make_async_copy(ref.at[pl.ds(pick(i) * size, size)], held.at[pl.ds(i * size, size)], sems.at[i])
        for i in range(blocks)
    ]
    for copy in copies:
        copy.start()
    return copies


def narrow_kernel(base, blocks, index_ref, g_ref, w_ref, *refs):
    out_ref, g_held, w_held, out_held, g_sems, w_sems, out_sems = refs[-7:]
    weights = fetch(w_ref, w_held, w_sems, 1)
    loads = fetch(g_ref, g_held, g_sems, blocks)
    slots, count, _ = g_held.shape
    step, half = slots // blocks, count // 2
    column = lax.broadcasted_iota(jnp.int32, (count, W12), 1)
    dims = (((1,), (1,)), ((), ()))
    weights[0].wait()
    stores = []
    for i, load in enumerate(loads):
        load.wait()
        for s in range(i * step, (i + 1) * step):
            w = w_held[index_ref[base + s]]
            first = lax.dot_general(g_held[s, :, :PD], w, dims, preferred_element_type=jnp.float32)
            second = lax.dot_general(g_held[s, :, PD:], w, dims, preferred_element_type=jnp.float32)
            d = jnp.where(column < W1, first, second)
            out_held[s] = jnp.concatenate([d[:half], d[half:]], axis=1).astype(jnp.bfloat16)
        at = pl.ds(i * step, step)
        stores.append(pltpu.make_async_copy(out_held.at[at], out_ref.at[at], out_sems.at[i]))
        stores[-1].start()
    for store in stores:
        store.wait()


def narrow_dpool(index, first, g12, w12, after=()):
    slots, count, _ = g12.shape
    blocks = 4
    shape = (slots, count // 2, 2 * W12)
    return pl.pallas_call(
        functools.partial(narrow_kernel, first, blocks),
        out_shape=jax.ShapeDtypeStruct(shape, jnp.bfloat16),
        grid_spec=pltpu.PrefetchScalarGridSpec(
            num_scalar_prefetch=1,
            grid=(1,),
            in_specs=[HBM] * 2 + [ANY] * len(after),
            out_specs=HBM,
            scratch_shapes=[
                pltpu.VMEM(g12.shape, jnp.bfloat16),
                pltpu.VMEM(w12.shape, jnp.bfloat16),
                pltpu.VMEM(shape, jnp.bfloat16),
                pltpu.SemaphoreType.DMA((blocks,)),
                pltpu.SemaphoreType.DMA((1,)),
                pltpu.SemaphoreType.DMA((blocks,)),
            ],
        ),
        compiler_params=params(1, 50),
        cost_estimate=cost(4e9),
        name="narrow_dpool",
    )(index, g12, w12, *after)


def partial_kernel(first, blocks, size, ins, added, results, index_ref, *refs):
    operands, others = refs[:ins], refs[ins : ins + added]
    outs, scratch = refs[-3 - 2 * results - ins - added :][:results], refs[-3 - results - ins - added :]
    held, other_held, out_held = scratch[:ins], scratch[ins : ins + added], scratch[ins + added : -3]
    in_sems, other_sems, out_sems = scratch[-3:]

    def block(arrays, i):
        per = blocks // len(arrays)
        return arrays[i // per].at[pl.ds(i % per * size, size)]

    loads = [
        fetch(ref, at, in_sems.at[n], blocks, lambda i: index_ref[first + i])
        for n, (ref, at) in enumerate(zip(operands, held))
    ]
    if added:
        loads.append(
            [
                pltpu.make_async_copy(block(others, i), block(other_held, i), other_sems.at[i])
                for i in range(blocks)
            ]
        )
        for copy in loads[-1]:
            copy.start()
    stores = []
    for i in range(blocks):
        for copies in loads:
            copies[i].wait()
        out = block(out_held, i)
        for l in range(size):
            slot = i * size + index_ref[l]
            q = held[0][slot].T
            narrow = jnp.dot(q[:W12], held[1][slot], preferred_element_type=jnp.float32)
            wide = jnp.dot(q[W12:], held[2][slot], preferred_element_type=jnp.float32)
            pieces = ((0, W1, narrow[:W1, :PD]), (W1, W12, narrow[W1:, PD:]), (W12, WSUM, wide))
            for start, end, piece in pieces:
                if added:
                    piece = piece + block(other_held, i)[l, start:end]
                out[l, start:end] = piece.astype(out.dtype)
        stores.append(pltpu.make_async_copy(out, block(outs, i), out_sems.at[i]))
        stores[-1].start()
    for store in stores:
        store.wait()


def partial_proj(index, first, blocks, size, q, g12, g3, results, others=()):
    _, count, _ = q.shape
    kinds = [jnp.bfloat16 if others and i else jnp.float32 for i in range(results)]
    shapes = [jax.ShapeDtypeStruct((blocks // results * size, WSUM, PD), kind) for kind in kinds]
    operands = (q, g12, g3)
    return pl.pallas_call(
        functools.partial(partial_kernel, first, blocks, size, len(operands), len(others), results),
        out_shape=shapes,
        grid_spec=pltpu.PrefetchScalarGridSpec(
            num_scalar_prefetch=1,
            grid=(1,),
            in_specs=[HBM] * len(operands) + [ANY] * len(others),
            out_specs=[HBM] * results,
            scratch_shapes=[pltpu.VMEM((blocks * size, count, x.shape[2]), jnp.bfloat16) for x in operands]
            + [pltpu.VMEM(x.shape, x.dtype) for x in others]
            + [pltpu.VMEM(x.shape, x.dtype) for x in shapes]
            + [
                pltpu.SemaphoreType.DMA((len(operands), blocks)),
                pltpu.SemaphoreType.DMA((blocks,)),
                pltpu.SemaphoreType.DMA((blocks,)),
            ],
        ),
        compiler_params=params(1, 50),
        cost_estimate=cost(4e9 if others else 1e7),
        name="partial_proj",
    )(index, *operands, *others)


def count_kernel(index_ref, length_ref, *refs):
    out_ref = refs[-1]
    bag, block = index_ref.shape[1], index_ref.shape[2]
    lanes, chunk, low = 256, 16, ROWS // 8

    def one(i, carry):
        at = pl.ds(pl.multiple_of(i * lanes, lanes), lanes)
        index = index_ref[0, :, at]
        which = lax.broadcasted_iota(jnp.int32, (bag, lanes), 0)
        key = jnp.where(which < length_ref[0, :, at], index & (low - 1), -1)
        unit = jnp.left_shift(jnp.int32(1), jnp.right_shift(index, 6) * 4)
        ids = lax.broadcasted_iota(jnp.int32, (chunk, lanes), 0)
        for c in range(low // chunk):
            total = jnp.zeros((chunk, lanes), jnp.int32)
            for j in range(bag):
                total = total + jnp.where(key[j : j + 1] == ids + c * chunk, unit[j : j + 1], 0)
            out_ref[0, c * chunk : (c + 1) * chunk, at] = total
        return carry

    lax.fori_loop(0, block // lanes, one, 0)


def count_hits(lookups, counts, after=()):
    tables, bag, examples = lookups.shape
    block = 4096
    return pl.pallas_call(
        count_kernel,
        out_shape=jax.ShapeDtypeStruct((tables, ROWS // 8, examples), jnp.int32),
        grid=(tables, examples // block),
        in_specs=[
            pl.BlockSpec((1, bag, block), lambda k, i: (k, 0, i)),
            pl.BlockSpec((1, 1, block), lambda k, i: (k, 0, i)),
        ]
        + [ANY] * len(after),
        out_specs=pl.BlockSpec((1, ROWS // 8, block), lambda k, i: (k, 0, i)),
        compiler_params=params(2, 60),
        cost_estimate=cost(5e9),
        name="count_hits",
    )(lookups, counts, *after)


def unpacked(words):
    rows = [lax.shift_right_logical(words, jnp.int32(4 * n)) & 15 for n in range(8)]
    return jnp.concatenate([r.astype(jnp.float32).astype(jnp.bfloat16) for r in rows], axis=0)


def wide_kernel(hits_ref, g_ref, w_ref, *refs):
    out_ref = refs[-1]

    @pl.when(pl.program_id(0) == 0)
    def _():
        out_ref[...] = jnp.zeros_like(out_ref)

    block = g_ref.shape[0]
    column = lax.broadcasted_iota(jnp.int32, (block, WSUM), 1)
    d = lax.dot_general(g_ref[...], w_ref[...], (((1,), (1,)), ((), ())), preferred_element_type=jnp.float32)
    d = jnp.where(column < W12, 0.0, d).astype(jnp.bfloat16)
    out_ref[...] += jnp.dot(unpacked(hits_ref[0]), d, preferred_element_type=jnp.float32)


def wide_sum(hits, g3, weights, after=()):
    _, words, examples = hits.shape
    block = 1024
    return pl.pallas_call(
        wide_kernel,
        out_shape=jax.ShapeDtypeStruct((ROWS, WSUM), jnp.float32),
        grid=(examples // block,),
        in_specs=[
            pl.BlockSpec((1, words, block), lambda i: (2, 0, i)),
            pl.BlockSpec((block, PD), lambda i: (i, 0)),
            pl.BlockSpec((WSUM, PD), lambda i: (0, 0)),
        ]
        + [ANY] * len(after),
        out_specs=pl.BlockSpec((ROWS, WSUM), lambda i: (0, 0)),
        compiler_params=params(1, 52),
        cost_estimate=cost(1e7),
        name="wide_sum",
    )(hits, g3, weights, *after)


def narrow_sum_kernel(hits_ref, d_ref, wide_ref, *refs):
    out_ref = refs[-1]

    @pl.when(pl.program_id(0) == 0)
    def _():
        out_ref[...] = wide_ref[...]

    sources = d_ref.shape[0]
    block = hits_ref.shape[2]
    column = lax.broadcasted_iota(jnp.int32, (block, PD), 1)
    pieces = []
    for d in range(sources):
        packed = d_ref[d].astype(jnp.float32)
        pieces += [packed, pltpu.roll(packed, PD - W12, 1)]
    both = jnp.concatenate(pieces, axis=0)
    d1 = jnp.where(column < W1, both, 0.0).astype(jnp.bfloat16)
    d2 = jnp.where((column >= W1) & (column < W12), both, 0.0).astype(jnp.bfloat16)
    out_ref[...] += jnp.dot(unpacked(hits_ref[0]), d1, preferred_element_type=jnp.float32) + jnp.dot(
        unpacked(hits_ref[1]), d2, preferred_element_type=jnp.float32
    )


def narrow_sum(hits, narrow, wide, after=()):
    _, words, examples = hits.shape
    sources, half, _ = narrow.shape
    block = 1024
    per = block // (2 * half)
    return pl.pallas_call(
        narrow_sum_kernel,
        out_shape=jax.ShapeDtypeStruct((ROWS, WSUM), jnp.float32),
        grid=(examples // block,),
        in_specs=[
            pl.BlockSpec((2, words, block), lambda i: (0, 0, i)),
            pl.BlockSpec((per, half, 2 * W12), lambda i: (i, 0, 0)),
            pl.BlockSpec((ROWS, PD), lambda i: (0, 0)),
        ]
        + [ANY] * len(after),
        out_specs=pl.BlockSpec((ROWS, PD), lambda i: (0, 0)),
        input_output_aliases={2: 0},
        compiler_params=params(1, 54),
        cost_estimate=cost(1e7),
        name="narrow_sum",
    )(hits, narrow, wide, *after)


def plane_kernel(terms, kept_ref, *refs):
    own_ref, outs = refs[terms + 1], refs[terms + 2 :]
    for i in range(kept_ref.shape[0]):
        total = kept_ref[i]
        for term in refs[:terms]:
            total = total + term[i].astype(jnp.float32)
        if i == 0:
            own_ref[0] = total
        else:
            outs[i - 1][0] = total.astype(jnp.bfloat16)


def plane_sum(kept, arrived, after):
    vmem = pl.BlockSpec(memory_space=pltpu.VMEM)
    others = kept.shape[0] - 1
    shape = (1,) + kept.shape[1:]
    return pl.pallas_call(
        functools.partial(plane_kernel, len(arrived)),
        out_shape=[jax.ShapeDtypeStruct(shape, jnp.float32)] + [jax.ShapeDtypeStruct(shape, jnp.bfloat16)] * others,
        in_specs=[vmem] * (1 + len(arrived)) + [ANY],
        out_specs=[vmem] * (1 + others),
        compiler_params=pltpu.CompilerParams(vmem_limit_bytes=16 * MIB),
        cost_estimate=cost(9e9),
        name="plane_sum",
    )(kept, *arrived, after)


def swap(x, axis, size, bits):
    return lax.ppermute(x, axis, [(d, d ^ bits) for d in range(size)])


def local(sizes, grad_out, pooled, proj, assign, indices, lengths):
    count, slots, _ = grad_out.shape
    scale = 1.0 / math.sqrt(count * slots)
    n_node, n_local = sizes["node"], sizes["local"]
    n_plane = n_node // 2
    node, loc = lax.axis_index("node"), lax.axis_index("local")

    entry = jnp.arange(n_local + 2 * n_plane + slots, dtype=jnp.int32)
    plane = entry - n_local
    slot = plane - 2 * n_plane
    other = slot // n_local ^ node
    index = jnp.where(
        plane < 0,
        entry ^ loc,
        jnp.where(
            slot < 0,
            ((plane % n_plane) ^ (node // 2)) * 2 + (node + 1 + plane // n_plane) % 2,
            other % 2 * (slots // 2) + other // 2 * n_local + (slot % n_local ^ loc),
        ),
    ).astype(jnp.int32)

    rows = proj[:, :W12]
    rows = jnp.concatenate([rows] + [swap(rows, "local", n_local, d) for d in range(1, n_local)])
    g12, g3, q = permute(assign, grad_out, pooled)
    rows, g3 = lax.optimization_barrier((rows, g3))
    g3_got = lax.all_to_all(g3, AXES, split_axis=0, concat_axis=0, tiled=True)

    sent = partial_proj(index, n_local, n_plane, n_local, q, g12, g3, 2)
    got = [swap(x, "node", n_node, 1) for x in sent]

    rows, sent = lax.optimization_barrier((rows, sent))
    rows = jnp.concatenate([rows] + [swap(rows, "node", n_node, 2 * d) for d in range(1, n_plane)])
    hits = count_hits(indices[0].transpose(1, 2, 0), lengths.transpose(2, 0, 1), after=sent[:1])
    kept = partial_proj(index, n_local + n_plane, n_plane, n_local, q, g12, g3, n_plane, got)
    rows = jnp.concatenate([rows, swap(rows, "node", n_node, 1)])
    narrow = narrow_dpool(index, n_local + 2 * n_plane, g12, rows, after=kept[:1])

    narrow, hits, g3_got, _ = lax.optimization_barrier((narrow, hits, g3_got, kept))
    narrow_got = lax.all_to_all(narrow, AXES, split_axis=0, concat_axis=0, tiled=True)
    wide = wide_sum(hits, g3_got.reshape(-1, PD), proj[0])
    arrived = [swap(kept[d], "node", n_node, 2 * d) for d in range(1, n_plane)]
    own, *sums = plane_sum(kept[0], arrived, wide)
    terms = [swap(x, "local", n_local, d) for d, x in enumerate(sums, 1)]

    table_grad = narrow_sum(hits, narrow_got, wide)[None]
    terms, table_grad = lax.optimization_barrier((terms, table_grad))
    proj_grad = sum((term.astype(jnp.float32) for term in terms), own) * scale
    return (table_grad, proj_grad)


def solution(mesh):
    placed = (
        P(AXES, None, None),
        P(AXES, None, None),
        P(AXES, None, None),
        P(),
        P(AXES, None, None, None),
        P(AXES, None, None),
    )
    return jax.shard_map(
        functools.partial(local, dict(mesh.shape)),
        mesh=mesh,
        in_specs=placed,
        out_specs=(P(AXES, None, None), P(AXES, None, None)),
        check_vma=False,
    )
```
